32 devices in a mesh: design: 2 (over y), node: 16 (over z, x, core).
Axes of the slice: x: 2, y: 2, z: 4, core: 2. Of those that a mesh axis runs over, the one named last changes fastest.
Arguments:
- feats: bfloat16 [131072, 256], P(('design', 'node')), parts along dimension 0, as said below
- cotangent: bfloat16 [131072, 256], P(('design', 'node')), parts along dimension 0, may hold values from -6 to 6
- valid: int32 [131072], P(('design', 'node')), parts along dimension 0, may hold values 0 or 1
- owned: int32 [32], P(('design', 'node')), parts along dimension 0, may hold values from 2048 to 4096, as said below
- w_mid: bfloat16 [256, 256], replicated, may hold values from -0.375 to 0.375
- w_slice: bfloat16 [32, 32], replicated, may hold values from -1 to 1
- temp_vec: bfloat16 [32], replicated, may hold values from -2 to 2
- w_qkv: bfloat16 [3, 32, 32], replicated, may hold values from -1 to 1
- w_out: bfloat16 [256, 256], replicated, may hold values from -0.375 to 0.375
Outputs:
- attended: bfloat16 [131072, 256], P(('design', 'node')), parts along dimension 0
- feats_grad: bfloat16 [131072, 256], P(('design', 'node')), parts along dimension 0
- grad_w_mid: float32 [512, 256], P('design'), parts along dimension 0
- grad_w_out: float32 [512, 256], P('design'), parts along dimension 0
- grad_w_slice: float32 [64, 32], P('design'), parts along dimension 0
- grad_temp: float32 [64], P('design'), parts along dimension 0
- grad_qkv: float32 [6, 32, 32], P('design'), parts along dimension 0
The draws below stay inside these ranges and needn't reach their ends.
There are 2 independent parts, one for each index of `design`. The reference program is written for one: setup_inputs(seed, part) draws one part's arguments, and reference() takes and returns one part's arrays. A program takes and returns all parts, laid end to end along the dimension named above; an argument that names none is the same for every part. Nothing has to cross between parts.
Inputs may be any that keep to these rules, and one draw needn't show every extreme that they name: `feats`: node features of order one. `owned`: rows of a device at or past its count are padding; some device owns all 4096 rows.
All inputs are finite; a program needn't handle non-finite values. No bound on the sum of `valid` on one device may be relied on, other than what follows from the above.
Results may differ from the reference program's by a relative error of at most 0.04.
The reference program's roundings to bfloat16 on the way count: a program that leaves them out, or rounds other values in their place, can miss the bound.
Values sent between devices are 32-bit elements; how exact they have to be, the bound alone decides.
No kernel may reach another device: no remote copies, remote signals or barrier semaphores. Data moves between devices by JAX's collectives and lax.ppermute only.
A program may use at most 128 MiB of HBM per device.

```python
import math
import jax
import jax.numpy as jnp
from jax import lax

HEAD_COUNT = 8
HEAD_FEATURES = 32
SLICES = 32
C = 256
NODE_DEV = 4096
NODES = 65536
N_NODE = 16


def draw_feats(key, part):
    key = jax.random.fold_in(key, 11)
    key_base, key_rough = jax.random.split(key, 2)
    ramp = 1.0 + 2.0 * jnp.arange(NODES, dtype=jnp.float32)[:, None] / NODES
    rough = jnp.exp(jax.random.uniform(key_rough, (NODES, 1), jnp.float32, -0.7, 0.7))
    values = jax.random.normal(key_base, (NODES, C), jnp.float32) * ramp * rough
    return values.astype(jnp.bfloat16)


def draw_owned(key, part):
    key = jax.random.fold_in(key, 23)
    key_count, key_pick = jax.random.split(key)
    counts = jax.random.randint(key_count, (N_NODE,), NODE_DEV // 2, NODE_DEV + 1)
    chosen = jax.random.randint(key_pick, (), 0, N_NODE)
    return jnp.where(jnp.arange(N_NODE) == chosen, NODE_DEV, counts).astype(jnp.int32)


def set_ends(result, own_key, smallest, top_value):
    spot = [jax.random.randint(jax.random.fold_in(own_key, axis), (), 0, length) for axis, length in enumerate(result.shape)]
    main_axis = result.shape.index(max(result.shape))
    neighbour = spot[:main_axis] + [(spot[main_axis] + 1) % result.shape[main_axis]] + spot[main_axis + 1:]
    return result.at[tuple(spot)].set(smallest).at[tuple(neighbour)].set(top_value)


def level_of(key, shape, cuts, low, high):
    def one(dim, shards_of):
        draws = jax.random.uniform(jax.random.fold_in(jax.random.fold_in(key, 6), dim), (shards_of,), jnp.float32, low / len(cuts), high / len(cuts))
        return jnp.repeat(jnp.exp(draws), shape[dim] // shards_of).reshape((-1,) + (1,) * (len(shape) - dim - 1))

    level = one(*cuts[0])
    for cut in cuts[1:]:
        level = level * one(*cut)
    return level


def scatter_about(rng, dims, spread, bound, cuts=(), kind=jnp.bfloat16):
    result = jax.random.normal(rng, dims, jnp.float32) * spread
    if len(cuts) > 0:
        result = level_of(rng, dims, cuts, -0.22, 0.18) * result
    return jnp.clip(result, min=-bound, max=bound).astype(kind)


def setup_inputs(seed: int = 0, part: int = 0) -> dict:
    arg_keys = jax.random.split(jax.random.key(seed), 10)
    own_keys = jax.random.split(jax.random.fold_in(arg_keys[9], part), 10)
    feats = draw_feats(jax.random.fold_in(jax.random.fold_in(arg_keys[9], part), 71), part)
    cotangent = scatter_about(own_keys[1], (NODES, C), 1.0, 6.0, ((0, 16),))
    valid = set_ends((jax.random.randint(own_keys[2], (NODES,), 0, 8) < 7).astype(jnp.int32), jax.random.fold_in(own_keys[2], 1), 0, 1)
    owned = draw_owned(jax.random.fold_in(jax.random.fold_in(arg_keys[9], part), 71), part)
    w_mid = scatter_about(arg_keys[4], (C, C), C ** -0.5, 0.375)
    w_slice = scatter_about(arg_keys[5], (HEAD_FEATURES, SLICES), HEAD_FEATURES ** -0.5, 1.0)
    temp_vec = scatter_about(arg_keys[6], (HEAD_FEATURES,), (HEAD_FEATURES // 4) ** -0.5, 2.0)
    w_qkv = scatter_about(arg_keys[7], (3, HEAD_FEATURES, HEAD_FEATURES), HEAD_FEATURES ** -0.5, 1.0)
    w_out = scatter_about(arg_keys[8], (C, C), C ** -0.5, 0.375)
    return {"feats": feats, "cotangent": cotangent, "valid": valid, "owned": owned, "w_mid": w_mid, "w_slice": w_slice, "temp_vec": temp_vec, "w_qkv": w_qkv, "w_out": w_out}


top_precision = lax.Precision.HIGHEST
eps_norm = 1e-05

def mix_slices(token_rows, matrices):
    query_rows = jnp.einsum('nir,ry->niy', token_rows, matrices[0], precision=top_precision)
    every_key = jnp.einsum('nir,ry->niy', token_rows, matrices[1], precision=top_precision)
    every_value = jnp.einsum('nir,ry->niy', token_rows, matrices[2], precision=top_precision)
    scores = jnp.einsum('hme,hke->hmk', query_rows, every_key, precision=top_precision) / math.sqrt(query_rows.shape[-1])
    scores = scores - lax.stop_gradient(lax.optimization_barrier(jnp.max(scores, axis=-1, keepdims=True)))
    expo_vals = jnp.exp(scores)
    attn_probs = expo_vals / lax.optimization_barrier(jnp.sum(expo_vals, axis=-1, keepdims=True))
    return jnp.einsum('hmk,hke->hme', attn_probs, every_value, precision=top_precision)

def reference(feats, cotangent, valid, owned, w_mid, w_slice, temp_vec, w_qkv, w_out):
    f32 = jnp.float32
    brain_float_sixteen = jnp.bfloat16
    mesh_point_count = feats.shape[0]
    mid = jnp.dot(feats, w_mid, preferred_element_type=f32).astype(brain_float_sixteen)
    position = jnp.arange(mesh_point_count, dtype=jnp.int32)
    device_of = (position // NODE_DEV).astype(jnp.int32)
    live = ((valid > 0) & (position % NODE_DEV < owned[device_of])).astype(f32)
    head_triple3 = mid.astype(f32).reshape(mesh_point_count, HEAD_COUNT, HEAD_FEATURES)
    slice_f = w_slice.astype(f32)
    temp_f = temp_vec.astype(f32)
    raw_score = jnp.einsum('nhd,dm->nhm', head_triple3, slice_f)
    zsum = jnp.einsum('nhd,d->nh', head_triple3, temp_f)
    tau = (0.5 + jax.nn.softplus(zsum))[:, :, None]
    logits = raw_score / tau
    peak_value = lax.optimization_barrier(jnp.max(logits, axis=-1, keepdims=True))
    expo_vals = jnp.exp(logits - peak_value)
    probs = expo_vals / lax.optimization_barrier(jnp.sum(expo_vals, axis=-1, keepdims=True))
    weights = probs * live[:, None, None]
    weights_b = weights.astype(brain_float_sixteen)
    weight_wide = weights_b.astype(f32)
    unscaled_scores = jnp.einsum('vsx,vsq->sxq', weight_wide, head_triple3)
    norm = lax.optimization_barrier(jnp.sum(weights, axis=0))
    token_rows = unscaled_scores / (norm[:, :, None] + eps_norm)
    matrices = w_qkv.astype(f32)
    mixed, mix_back = jax.vjp(mix_slices, token_rows, matrices)
    mixed_b = mixed.astype(brain_float_sixteen)
    mixture_wide = mixed_b.astype(f32)
    combined_heads = jnp.einsum('jgo,gov->jgv', weight_wide, mixture_wide).astype(brain_float_sixteen).reshape(mesh_point_count, HEAD_COUNT * HEAD_FEATURES)
    attended = jnp.dot(combined_heads, w_out, preferred_element_type=f32).astype(brain_float_sixteen)
    d_merged = jnp.dot(cotangent, w_out.T, preferred_element_type=f32).astype(brain_float_sixteen)
    grad_w_out = jnp.dot(combined_heads.T, cotangent, preferred_element_type=f32)
    combined_gradient3 = d_merged.astype(f32).reshape(mesh_point_count, HEAD_COUNT, HEAD_FEATURES)
    mixture_gradient = jnp.einsum('vsx,vsq->sxq', weight_wide, combined_gradient3)
    d_tokens, grad_qkv = mix_back(mixture_gradient)
    d_raw = d_tokens / (norm[:, :, None] + eps_norm)
    norm_gradient = -lax.optimization_barrier(jnp.sum(d_tokens * unscaled_scores, axis=-1)) / (norm + eps_norm) ** 2
    raw_gradient_wide = d_raw.astype(brain_float_sixteen).astype(f32)
    weight_cotangents = jnp.einsum('wxr,xzr->wxz', combined_gradient3, mixture_wide)
    weight_cotangents = weight_cotangents + jnp.einsum('wxr,xzr->wxz', head_triple3, raw_gradient_wide) + norm_gradient[None]
    d_logits = live[:, None, None] * probs * (weight_cotangents - lax.optimization_barrier(jnp.sum(probs * weight_cotangents, axis=-1, keepdims=True)))
    u_f = (d_logits / tau).astype(brain_float_sixteen).astype(f32)
    c_f = (-d_logits * logits / tau * jax.nn.sigmoid(zsum)[:, :, None]).astype(brain_float_sixteen).astype(f32)
    middle_gradient = jnp.einsum('jgo,gov->jgv', weight_wide, raw_gradient_wide)
    middle_gradient = middle_gradient + jnp.einsum('nhm,dm->nhd', u_f, slice_f)
    middle_gradient = middle_gradient + jnp.einsum('nhm,d->nhd', c_f, temp_f)
    d_mid_b = middle_gradient.reshape(mesh_point_count, HEAD_COUNT * HEAD_FEATURES).astype(brain_float_sixteen)
    feats_grad = jnp.dot(d_mid_b, w_mid.T, preferred_element_type=f32).astype(brain_float_sixteen)
    grad_w_mid = jnp.dot(feats.T, d_mid_b, preferred_element_type=f32)
    grad_w_slice = jnp.einsum('nhd,nhm->dm', head_triple3, u_f)
    grad_temp = jnp.einsum('nhd,nhm->d', head_triple3, c_f)
    return (attended, feats_grad, grad_w_mid, grad_w_out, grad_w_slice, grad_temp, grad_qkv)
```

```python
import functools
import math

import jax
import jax.numpy as jnp
from jax import lax
from jax.experimental import pallas as pl
from jax.experimental.pallas import tpu as pltpu
from jax.sharding import PartitionSpec as P

f32 = jnp.float32
bf16 = jnp.bfloat16
eps_norm = 1e-05
exact = lax.Precision.HIGHEST
group = 4
vmem_bytes = 56 * 1024 * 1024


def nn(a, b, precision=None):
    return lax.dot_general(
        a, b, (((1,), (0,)), ((), ())), preferred_element_type=f32, precision=precision
    )


def nt(a, b, precision=None):
    return lax.dot_general(
        a, b, (((1,), (1,)), ((), ())), preferred_element_type=f32, precision=precision
    )


def tn(a, b, precision=None):
    return lax.dot_general(
        a, b, (((0,), (0,)), ((), ())), preferred_element_type=f32, precision=precision
    )


def rows_of(shape):
    return lax.broadcasted_iota(jnp.int32, shape, 0)


def cols_of(shape):
    return lax.broadcasted_iota(jnp.int32, shape, 1)


def spread_matrix(width, small):
    shape = (width, small)
    return jnp.where(rows_of(shape) % small == cols_of(shape), 1.0, 0.0).astype(bf16)


def same_block(rows, cols, row_size, col_size):
    shape = (rows, cols)
    return rows_of(shape) // row_size == cols_of(shape) // col_size


def two_pieces(x):
    high = x.astype(bf16)
    return high, (x - high.astype(f32)).astype(bf16)


def fold_rows(x, heads, size):
    total = x[0:size]
    for h in range(1, heads):
        total = total + x[h * size : (h + 1) * size]
    return total


def group_place():
    return lax.axis_index("node") % group


def stats_kernel(
    heads,
    slices,
    owned_ref,
    valid_ref,
    feats_ref,
    cot_ref,
    w_mid_ref,
    w_slice_ref,
    temp_ref,
    w_out_ref,
    mid_ref,
    wt_ref,
    aux_ref,
    sw_ref,
    sb_ref,
    wc_ref,
    send0,
    send1,
    send2,
    send3,
    raw_acc,
    norm_acc,
    pack,
):
    step = pl.program_id(0)
    width = w_mid_ref.shape[0]
    depth = width // heads
    hm = heads * slices
    block = feats_ref.shape[0]

    @pl.when(step == 0)
    def _():
        spread_d = spread_matrix(width, depth)
        spread_m = spread_matrix(hm, slices)
        w_slice = w_slice_ref[...]
        half = nt(spread_m, w_slice).astype(bf16)
        full = nt(half, spread_d)
        sw_ref[0:hm, :] = jnp.where(same_block(hm, width, slices, depth), full, 0.0).astype(bf16)
        half = nn(spread_d, w_slice).astype(bf16)
        full = nt(half, spread_m)
        sb_ref[...] = jnp.where(same_block(width, hm, depth, slices), full, 0.0).astype(bf16)
        temp = jnp.broadcast_to(temp_ref[...].astype(f32), (16, depth)).astype(bf16)
        full = nt(temp, spread_d)
        sw_ref[hm : hm + 16, :] = jnp.where(same_block(16, width, 1, depth), full, 0.0).astype(
            bf16
        )
        raw_acc[...] = jnp.zeros_like(raw_acc)
        norm_acc[...] = jnp.zeros_like(norm_acc)
        wc_ref[...] = jnp.zeros_like(wc_ref)

    mid = nn(feats_ref[...], w_mid_ref[...]).astype(bf16)
    mid_ref[...] = mid
    scores = nt(sw_ref[...], mid)
    zsum = scores[hm : hm + heads]
    small = jnp.exp(-jnp.abs(zsum))
    inv_tau = 1.0 / (0.5 + (jnp.maximum(zsum, 0.0) + jnp.log(1.0 + small)))
    sig = jnp.where(zsum >= 0.0, 1.0, small) / (1.0 + small)
    position = step * block + cols_of((1, block))
    live = (valid_ref[...] > 0) & (position < owned_ref[0])
    live_f = live.astype(f32)
    aux_ref[0:heads, :] = inv_tau
    aux_ref[2 * heads : 3 * heads, :] = sig * inv_tau
    for h in range(heads):
        span = slice(h * slices, (h + 1) * slices)
        logits = scores[span] * inv_tau[h : h + 1]
        peak = jnp.max(logits, axis=0, keepdims=True)
        expo = jnp.exp(logits - peak)
        total = jnp.sum(expo, axis=0, keepdims=True)
        weights = expo * (live_f / total)
        wt_ref[span, :] = weights.astype(bf16)
        lanes = weights[:, 0:128]
        for c in range(1, block // 128):
            lanes = lanes + weights[:, c * 128 : (c + 1) * 128]
        norm_acc[span, :] += lanes
        aux_ref[heads + h : heads + h + 1, :] = jnp.where(live, peak + jnp.log(total), jnp.inf)
    wt = wt_ref[...]
    raw_acc[...] += nn(wt, mid)
    wc_ref[...] += nn(wt, cot_ref[...])

    @pl.when(step == pl.num_programs(0) - 1)
    def _():
        diagonal = same_block(hm, width, slices, depth)
        raw = fold_rows(jnp.where(diagonal, raw_acc[...], 0.0), heads, slices)
        high, low = two_pieces(wc_ref[...])
        w_out = w_out_ref[...]
        mixed = nt(high, w_out) + nt(low, w_out)
        mixed = fold_rows(jnp.where(diagonal, mixed, 0.0), heads, slices)
        norm = jnp.sum(norm_acc[...].T, axis=0, keepdims=True)
        halves = width // 128
        for j in range(halves):
            part = slice(j * 128, (j + 1) * 128)
            pack[j * slices : (j + 1) * slices, :] = raw[:, part]
            pack[(halves + j) * slices : (halves + j + 1) * slices, :] = mixed[:, part]
        base = 2 * halves * slices
        rest = pack.shape[0] - base
        where_row = rows_of((rest, 128))
        tail = jnp.zeros((rest, 128), f32)
        for j in range(hm // 128):
            tail = jnp.where(where_row == j, norm[:, j * 128 : (j + 1) * 128], tail)
        pack[base:, :] = tail
        place = group_place()
        size = pack.shape[0] // group
        for k, send in enumerate((send0, send1, send2, send3)):
            send[...] = pack[pl.ds(pl.multiple_of((place ^ k) * size, 8), size), :]


def tokens_kernel(
    heads,
    slices,
    own_ref,
    got1,
    got2,
    got3,
    w_qkv_ref,
    w_out_ref,
    sw_ref,
    sb_ref,
    wc_ref,
    lhs_ref,
    mw_ref,
    yt_ref,
    dn_ref,
    grad_qkv_ref,
    send0,
    send1,
    send2,
    send3,
    pack,
    gwo,
):
    width = w_out_ref.shape[0]
    depth = width // heads
    hm = heads * slices
    halves = width // 128
    place = group_place()
    size = own_ref.shape[0]
    for k, got in enumerate((own_ref, got1, got2, got3)):
        pack[pl.ds(pl.multiple_of((place ^ k) * size, 8), size), :] = got[...]

    def compact(first):
        pieces = []
        for h in range(heads):
            per = 128 // depth
            x = pack[(first + h // per) * slices : (first + h // per + 1) * slices, :]
            shift = (h % per) * depth
            pieces.append(pltpu.roll(x, 128 - shift, 1) if shift else x)
        return jnp.concatenate(pieces, axis=0)[:, 0:depth]

    raw = compact(0)
    d_mixed = compact(halves)
    base = 2 * halves * slices
    columns = pack[base : base + 8, :].T
    norm = jnp.concatenate([columns[:, j : j + 1] for j in range(hm // 128)], axis=0)
    inverse = 1.0 / (norm + eps_norm)
    tokens = raw * inverse
    w_q, w_k, w_v = (w_qkv_ref[i].astype(f32) for i in range(3))
    q, k, v = (nn(tokens, w, exact) for w in (w_q, w_k, w_v))
    blocks = same_block(hm, hm, slices, slices)
    scale = 1.0 / math.sqrt(depth)
    scores = jnp.where(blocks, nt(q, k, exact) * scale, -jnp.inf)
    expo = jnp.exp(scores - jnp.max(scores, axis=1, keepdims=True))
    probs = expo / jnp.sum(expo, axis=1, keepdims=True)
    mixed_b = nn(probs, v, exact).astype(bf16)

    spread_d = spread_matrix(width, depth)
    diagonal = same_block(hm, width, slices, depth)
    diagonal_t = same_block(width, hm, depth, slices)
    w_out = w_out_ref[...]
    mixed_block = jnp.where(diagonal, nt(mixed_b, spread_d), 0.0).astype(bf16)
    mw_ref[...] = nn(mixed_block, w_out).astype(bf16)

    d_probs = nt(d_mixed, v, exact)
    d_v = tn(probs, d_mixed, exact)
    d_scores = probs * (d_probs - jnp.sum(probs * d_probs, axis=1, keepdims=True)) * scale
    d_q = nn(d_scores, k, exact)
    d_k = tn(d_scores, q, exact)
    d_tokens = nt(d_q, w_q, exact) + nt(d_k, w_k, exact) + nt(d_v, w_v, exact)
    d_raw_b = (d_tokens * inverse).astype(bf16)
    d_norm = -jnp.sum(d_tokens * raw, axis=1, keepdims=True) * inverse * inverse
    dn_ref[...] = jnp.broadcast_to(d_norm, dn_ref.shape)
    top = sw_ref.shape[0]
    lhs_ref[0:top, :] = sw_ref[...]
    lhs_ref[top : top + hm, :] = jnp.where(diagonal, nt(d_raw_b, spread_d), 0.0).astype(bf16)
    yt_ref[:, 0:hm] = jnp.where(diagonal_t, nt(spread_d, d_raw_b), 0.0).astype(bf16)
    yt_ref[:, hm : 2 * hm] = sb_ref[...]

    for i, grad in enumerate((d_q, d_k, d_v)):
        grad_qkv_ref[i] = tn(tokens, grad, exact)
    mixed_t = jnp.where(diagonal_t, nt(spread_d, mixed_b), 0.0).astype(bf16)
    high, low = two_pieces(wc_ref[...])
    gwo[...] = nn(mixed_t, high) + nn(mixed_t, low)
    rows = width // group
    for k, send in enumerate((send0, send1, send2, send3)):
        send[...] = gwo[pl.ds(pl.multiple_of((place ^ k) * rows, 8), rows), :]


def backward_kernel(
    heads,
    slices,
    aux_ref,
    mid_ref,
    cot_ref,
    feats_ref,
    lhs_ref,
    mw_ref,
    yt_ref,
    dn_ref,
    temp_ref,
    dmt_ref,
    send0,
    send1,
    send2,
    send3,
    stack,
    grad_acc,
    small_acc,
    pack,
):
    step = pl.program_id(0)
    width = mid_ref.shape[1]
    depth = width // heads
    hm = heads * slices
    block = mid_ref.shape[0]

    @pl.when(step == 0)
    def _():
        grad_acc[...] = jnp.zeros_like(grad_acc)
        small_acc[...] = jnp.zeros_like(small_acc)

    mid = mid_ref[...]
    from_mid = nt(lhs_ref[...], mid)
    from_cot = nt(mw_ref[...], cot_ref[...])
    aux = aux_ref[...]
    sums = []
    for h in range(heads):
        span = slice(h * slices, (h + 1) * slices)
        inv_tau = aux[h : h + 1]
        logits = from_mid[span] * inv_tau
        weights = jnp.exp(logits - aux[heads + h : heads + h + 1])
        d_weights = from_cot[span] + from_mid[hm + 16 + h * slices : hm + 16 + (h + 1) * slices]
        d_weights = d_weights + dn_ref[span, 0:1]
        mean = jnp.sum(weights * d_weights, axis=0, keepdims=True)
        d_logits = weights * (d_weights - mean)
        d_tau = jnp.sum(d_logits * logits, axis=0, keepdims=True)
        sums.append(-d_tau * aux[2 * heads + h : 2 * heads + h + 1])
        stack[span, :] = weights.astype(bf16)
        stack[hm + h * slices : hm + (h + 1) * slices, :] = (d_logits * inv_tau).astype(bf16)
    c_sum = jnp.concatenate(sums, axis=0)
    c_high = c_sum.astype(bf16).astype(f32)
    stack[2 * hm : 2 * hm + 2 * heads, :] = jnp.concatenate([c_high, c_sum - c_high], axis=0).astype(bf16)
    d_mid = nn(yt_ref[...], stack[0 : 2 * hm, :])
    temp = temp_ref[...].astype(f32)
    for h in range(heads):
        span = slice(h * depth, (h + 1) * depth)
        dmt_ref[span, :] = (d_mid[span] + temp * sums[h]).astype(bf16)
    grad_acc[...] += nn(dmt_ref[...], feats_ref[...])
    small_acc[...] += nn(stack[hm : 2 * hm + 2 * heads, :], mid)

    @pl.when(step == pl.num_programs(0) - 1)
    def _():
        grad = grad_acc[...].T
        u_part = jnp.where(same_block(hm, width, slices, depth), small_acc[0:hm, :], 0.0)
        u_part = fold_rows(u_part, heads, slices)
        c_part = small_acc[hm : hm + heads, :] + small_acc[hm + heads : hm + 2 * heads, :]
        c_part = jnp.where(same_block(heads, width, 1, depth), c_part, 0.0)
        c_part = jnp.sum(c_part, axis=0, keepdims=True)

        def fold_lanes(x):
            total = x[:, 0:128]
            for j in range(1, width // 128):
                total = total + x[:, j * 128 : (j + 1) * 128]
            shift = 64
            while shift >= depth:
                total = total + pltpu.roll(total, shift, 1)
                shift //= 2
            return total

        u_part = fold_lanes(u_part)
        c_part = fold_lanes(jnp.broadcast_to(c_part, (slices, width)))
        where_lane = cols_of((slices, 128))
        extra = jnp.where(where_lane < depth, u_part, c_part)
        rows = width // group
        more = slices // group
        for j in range(group):
            pack[j, 0:rows, :] = grad[j * rows : (j + 1) * rows]
            pack[j, rows : rows + more, 0:128] = extra[j * more : (j + 1) * more]
            pack[j, rows : rows + more, 128:] = jnp.zeros((more, width - 128), f32)
        place = group_place()
        for k, send in enumerate((send0, send1, send2, send3)):
            send[...] = pack[place ^ k]


def rows_kernel(wt_ref, dmt_ref, mw_ref, w_mid_ref, attended_ref, feats_grad_ref):
    attended_ref[...] = tn(wt_ref[...], mw_ref[...]).astype(bf16)
    feats_grad_ref[...] = lax.dot_general(
        dmt_ref[...], w_mid_ref[...], (((0,), (1,)), ((), ())), preferred_element_type=f32
    ).astype(bf16)


def finish_kernel(
    depth, o0, o1, o2, o3, m0, m1, m2, m3, grad_mid_ref, grad_out_ref, slice_ref, temp_ref, extra
):
    place = group_place()
    rows = o0.shape[0]
    more = m0.shape[0] - rows
    for k, (out_part, mid_part) in enumerate(((o0, m0), (o1, m1), (o2, m2), (o3, m3))):
        at = pl.ds(pl.multiple_of((place ^ k) * rows, 8), rows)
        grad_out_ref[at, :] = out_part[...]
        grad_mid_ref[at, :] = mid_part[0:rows, :]
        extra[pl.ds(pl.multiple_of((place ^ k) * more, 8), more), :] = mid_part[rows:, 0:128]
    slices = slice_ref.shape[1]
    turned = extra[...].T
    slice_ref[...] = turned[0:depth, 0:slices]
    temp_ref[...] = extra[0:1, depth : 2 * depth]


def full(shape):
    zeros = (0,) * len(shape)
    return pl.BlockSpec(shape, lambda *_: zeros)


def params(grid=True):
    if grid:
        return pltpu.CompilerParams(
            dimension_semantics=("arbitrary",), vmem_limit_bytes=vmem_bytes
        )
    return pltpu.CompilerParams(vmem_limit_bytes=vmem_bytes)


def cost(flops, moved, transcendentals=0):
    return pl.CostEstimate(flops=flops, bytes_accessed=moved, transcendentals=transcendentals)


def exchange(x, k, count):
    return lax.ppermute(x, "node", [(i, i ^ k) for i in range(count)])


def sum_over_groups(parts, count):
    got = [parts[0]] + [exchange(parts[k], k, count) for k in range(1, group)]
    total = (got[0] + got[1]) + (got[2] + got[3])
    stride = group
    while stride < count:
        if count // stride % 4 == 0:
            r1, r2, r3 = (exchange(total, stride * j, count) for j in (1, 2, 3))
            total = (total + r1) + (r2 + r3)
            stride *= 4
        else:
            total = total + exchange(total, stride, count)
            stride *= 2
    return total


def gather_group(total, count):
    return [total] + [exchange(total, k, count) for k in range(1, group)]


def shards(count, feats, cotangent, valid, owned, w_mid, w_slice, temp_vec, w_qkv, w_out):
    rows, width = feats.shape
    depth, slices = w_slice.shape
    heads = width // depth
    hm = heads * slices
    block = min(1024, rows)
    grid = (rows // block,)
    unit = 2 * rows * width * width
    smem = pl.BlockSpec(memory_space=pltpu.SMEM)
    by_rows = pl.BlockSpec((block, width), lambda i: (i, 0))
    by_cols = pl.BlockSpec((hm, block), lambda i: (0, i))
    aux_spec = pl.BlockSpec((3 * heads, block), lambda i: (0, i))
    pack_rows = 2 * (width // 128) * slices + 32
    piece = (pack_rows // group, 128)

    def like(shape, dtype):
        return jax.ShapeDtypeStruct(shape, dtype)

    mid, wt, aux, sw, sb, wc, *sends = pl.pallas_call(
        functools.partial(stats_kernel, heads, slices),
        grid=grid,
        in_specs=[
            smem,
            pl.BlockSpec((1, block), lambda i: (0, i)),
            by_rows,
            by_rows,
            full((width, width)),
            full((depth, slices)),
            full((1, depth)),
            full((width, width)),
        ],
        out_specs=[
            by_rows,
            by_cols,
            aux_spec,
            full((hm + 16, width)),
            full((width, hm)),
            full((hm, width)),
        ]
        + [full(piece)] * group,
        out_shape=[
            like((rows, width), bf16),
            like((hm, rows), bf16),
            like((3 * heads, rows), f32),
            like((hm + 16, width), bf16),
            like((width, hm), bf16),
            like((hm, width), f32),
        ]
        + [like(piece, f32)] * group,
        scratch_shapes=[
            pltpu.VMEM((hm, width), f32),
            pltpu.VMEM((hm, 128), f32),
            pltpu.VMEM((pack_rows, 128), f32),
        ],
        compiler_params=params(),
        cost_estimate=cost(4 * unit, rows * width * 8, rows * hm),
    )(owned, valid.reshape(1, rows), feats, cotangent, w_mid, w_slice, temp_vec.reshape(1, depth), w_out)

    pieces = gather_group(sum_over_groups(sends, count), count)

    quarter = (width // group, width)
    lhs, mw, yt, dn, grad_qkv, *sends = pl.pallas_call(
        functools.partial(tokens_kernel, heads, slices),
        out_shape=[
            like((2 * hm + 16, width), bf16),
            like((hm, width), bf16),
            like((width, 2 * hm), bf16),
            like((hm, 128), f32),
            like((3, depth, depth), f32),
        ]
        + [like(quarter, f32)] * group,
        scratch_shapes=[pltpu.VMEM((pack_rows, 128), f32), pltpu.VMEM((width, width), f32)],
        compiler_params=params(False),
        cost_estimate=cost(30 * width**3, 4 * width * width * 4, hm * hm),
    )(*pieces, w_qkv, w_out, sw, sb, wc)

    out_parts = gather_group(sum_over_groups(sends, count), count)

    more = slices // group
    larger = (width // group + more, width)
    dmt, *sends = pl.pallas_call(
        functools.partial(backward_kernel, heads, slices),
        grid=grid,
        in_specs=[
            aux_spec,
            by_rows,
            by_rows,
            by_rows,
            full((2 * hm + 16, width)),
            full((hm, width)),
            full((width, 2 * hm)),
            full((hm, 128)),
            full((depth, 1)),
        ],
        out_specs=[by_cols] + [full(larger)] * group,
        out_shape=[like((width, rows), bf16)] + [like(larger, f32)] * group,
        scratch_shapes=[
            pltpu.VMEM((2 * hm + 16, block), bf16),
            pltpu.VMEM((width, width), f32),
            pltpu.VMEM((hm + 16, width), f32),
            pltpu.VMEM((group,) + larger, f32),
        ],
        compiler_params=params(),
        cost_estimate=cost(8 * unit, rows * width * 8, rows * hm),
    )(aux, mid, cotangent, feats, lhs, mw, yt, dn, temp_vec.reshape(depth, 1))

    mid_parts = gather_group(sum_over_groups(sends, count), count)

    attended, feats_grad = pl.pallas_call(
        rows_kernel,
        grid=grid,
        in_specs=[by_cols, by_cols, full((hm, width)), full((width, width))],
        out_specs=[by_rows, by_rows],
        out_shape=[like((rows, width), bf16)] * 2,
        compiler_params=params(),
        cost_estimate=cost(2 * unit, rows * width * 8),
    )(wt, dmt, mw, w_mid)

    grad_w_mid, grad_w_out, grad_w_slice, grad_temp = pl.pallas_call(
        functools.partial(finish_kernel, depth),
        out_shape=[
            like((width, width), f32),
            like((width, width), f32),
            like((depth, slices), f32),
            like((1, depth), f32),
        ],
        scratch_shapes=[pltpu.VMEM((slices, 128), f32)],
        compiler_params=params(False),
        cost_estimate=cost(0, 4 * width * width * 4),
    )(*out_parts, *mid_parts)
    return (
        attended,
        feats_grad,
        grad_w_mid,
        grad_w_out,
        grad_w_slice,
        grad_temp.reshape(depth),
        grad_qkv,
    )


def solution(mesh):
    in_specs = (
        P(("design", "node"), None),
        P(("design", "node"), None),
        P(("design", "node")),
        P(("design", "node")),
        P(),
        P(),
        P(),
        P(),
        P(),
    )
    out_specs = (
        P(("design", "node"), None),
        P(("design", "node"), None),
        P("design", None),
        P("design", None),
        P("design", None),
        P("design"),
        P("design", None, None),
    )
    return jax.shard_map(
        functools.partial(shards, mesh.shape["node"]),
        mesh=mesh,
        in_specs=in_specs,
        out_specs=out_specs,
        check_vma=False,
    )
```

```python
import functools
import math

import jax
import jax.numpy as jnp
from jax import lax
from jax.experimental import pallas as pl
from jax.experimental.pallas import tpu as pltpu
from jax.sharding import PartitionSpec as P

f32 = jnp.float32
bf16 = jnp.bfloat16
eps_norm = 1e-05
exact = lax.Precision.HIGHEST
group = 4
vmem_bytes = 56 * 1024 * 1024


def nn(a, b, precision=None):
    return lax.dot_general(
        a, b, (((1,), (0,)), ((), ())), preferred_element_type=f32, precision=precision
    )


def nt(a, b, precision=None):
    return lax.dot_general(
        a, b, (((1,), (1,)), ((), ())), preferred_element_type=f32, precision=precision
    )


def tn(a, b, precision=None):
    return lax.dot_general(
        a, b, (((0,), (0,)), ((), ())), preferred_element_type=f32, precision=precision
    )


def rows_of(shape):
    return lax.broadcasted_iota(jnp.int32, shape, 0)


def cols_of(shape):
    return lax.broadcasted_iota(jnp.int32, shape, 1)


def spread_matrix(width, small):
    shape = (width, small)
    return jnp.where(rows_of(shape) % small == cols_of(shape), 1.0, 0.0).astype(bf16)


def same_block(rows, cols, row_size, col_size):
    shape = (rows, cols)
    return rows_of(shape) // row_size == cols_of(shape) // col_size


def two_pieces(x):
    high = x.astype(bf16)
    return high, (x - high.astype(f32)).astype(bf16)


def fold_rows(x, heads, size):
    total = x[0:size]
    for h in range(1, heads):
        total = total + x[h * size : (h + 1) * size]
    return total


def group_place():
    return lax.axis_index("node") % group


def stats_kernel(
    heads,
    slices,
    owned_ref,
    valid_ref,
    feats_ref,
    cot_ref,
    w_mid_ref,
    w_slice_ref,
    temp_ref,
    w_out_ref,
    mid_ref,
    wt_ref,
    aux_ref,
    sw_ref,
    sb_ref,
    wc_ref,
    pack_ref,
    raw_acc,
    norm_acc,
):
    step = pl.program_id(0)
    width = w_mid_ref.shape[0]
    depth = width // heads
    hm = heads * slices
    block = feats_ref.shape[0]

    @pl.when(step == 0)
    def _():
        spread_d = spread_matrix(width, depth)
        spread_m = spread_matrix(hm, slices)
        w_slice = w_slice_ref[...]
        half = nt(spread_m, w_slice).astype(bf16)
        full = nt(half, spread_d)
        sw_ref[0:hm, :] = jnp.where(same_block(hm, width, slices, depth), full, 0.0).astype(bf16)
        half = nn(spread_d, w_slice).astype(bf16)
        full = nt(half, spread_m)
        sb_ref[...] = jnp.where(same_block(width, hm, depth, slices), full, 0.0).astype(bf16)
        temp = jnp.broadcast_to(temp_ref[...].astype(f32), (16, depth)).astype(bf16)
        full = nt(temp, spread_d)
        sw_ref[hm : hm + 16, :] = jnp.where(same_block(16, width, 1, depth), full, 0.0).astype(
            bf16
        )
        raw_acc[...] = jnp.zeros_like(raw_acc)
        norm_acc[...] = jnp.zeros_like(norm_acc)
        wc_ref[...] = jnp.zeros_like(wc_ref)

    mid = nn(feats_ref[...], w_mid_ref[...]).astype(bf16)
    mid_ref[...] = mid
    scores = nt(sw_ref[...], mid)
    zsum = scores[hm : hm + heads]
    small = jnp.exp(-jnp.abs(zsum))
    inv_tau = 1.0 / (0.5 + (jnp.maximum(zsum, 0.0) + jnp.log(1.0 + small)))
    sig = jnp.where(zsum >= 0.0, 1.0, small) / (1.0 + small)
    position = step * block + cols_of((1, block))
    live = (valid_ref[...] > 0) & (position < owned_ref[0])
    live_f = live.astype(f32)
    aux_ref[0:heads, :] = inv_tau
    aux_ref[2 * heads : 3 * heads, :] = sig * inv_tau
    for h in range(heads):
        span = slice(h * slices, (h + 1) * slices)
        logits = scores[span] * inv_tau[h : h + 1]
        peak = jnp.max(logits, axis=0, keepdims=True)
        expo = jnp.exp(logits - peak)
        total = jnp.sum(expo, axis=0, keepdims=True)
        weights = expo * (live_f / total)
        wt_ref[span, :] = weights.astype(bf16)
        lanes = weights[:, 0:128]
        for c in range(1, block // 128):
            lanes = lanes + weights[:, c * 128 : (c + 1) * 128]
        norm_acc[span, :] += lanes
        aux_ref[heads + h : heads + h + 1, :] = jnp.where(live, peak + jnp.log(total), jnp.inf)
    wt = wt_ref[...]
    raw_acc[...] += nn(wt, mid)
    wc_ref[...] += nn(wt, cot_ref[...])

    @pl.when(step == pl.num_programs(0) - 1)
    def _():
        diagonal = same_block(hm, width, slices, depth)
        raw = fold_rows(jnp.where(diagonal, raw_acc[...], 0.0), heads, slices)
        high, low = two_pieces(wc_ref[...])
        w_out = w_out_ref[...]
        mixed = nt(high, w_out) + nt(low, w_out)
        mixed = fold_rows(jnp.where(diagonal, mixed, 0.0), heads, slices)
        norm = jnp.sum(norm_acc[...].T, axis=0, keepdims=True)
        tiles = slices // 8
        count = pack_ref.shape[0] // 2
        below = rows_of((8, 128))
        for j in range(count):
            part = slice(j // tiles * 128, (j // tiles + 1) * 128)
            at = slice(j % tiles * 8, (j % tiles + 1) * 8)
            pack_ref[j, 0:8, :] = raw[at, part]
            pack_ref[count + j, 0:8, :] = mixed[at, part]
            if j < hm // 128:
                row = norm[:, j * 128 : (j + 1) * 128]
                pack_ref[j, 8:16, :] = jnp.where(below == 0, row, 0.0)
            else:
                pack_ref[j, 8:16, :] = jnp.zeros((8, 128), f32)
            pack_ref[count + j, 8:16, :] = jnp.zeros((8, 128), f32)


def tokens_kernel(
    heads,
    slices,
    pack_ref,
    w_qkv_ref,
    w_out_ref,
    sw_ref,
    sb_ref,
    wc_ref,
    lhs_ref,
    mw_ref,
    yt_ref,
    dn_ref,
    grad_qkv_ref,
    send0,
    send1,
    send2,
    send3,
    gwo,
):
    width = w_out_ref.shape[0]
    depth = width // heads
    hm = heads * slices
    place = group_place()
    tiles = slices // 8
    count = pack_ref.shape[0] // 2

    def compact(first):
        pieces = []
        for h in range(heads):
            per = 128 // depth
            at = first + h // per * tiles
            x = pack_ref[at : at + tiles, 0:8, :].reshape(slices, 128)
            shift = (h % per) * depth
            pieces.append(pltpu.roll(x, 128 - shift, 1) if shift else x)
        return jnp.concatenate(pieces, axis=0)[:, 0:depth]

    raw = compact(0)
    d_mixed = compact(count)
    norm = [pack_ref[j, 8:16, :].T[:, 0:1] for j in range(hm // 128)]
    norm = jnp.concatenate(norm, axis=0)
    inverse = 1.0 / (norm + eps_norm)
    tokens = raw * inverse
    w_q, w_k, w_v = (w_qkv_ref[i].astype(f32) for i in range(3))
    q, k, v = (nn(tokens, w, exact) for w in (w_q, w_k, w_v))
    blocks = same_block(hm, hm, slices, slices)
    scale = 1.0 / math.sqrt(depth)
    scores = jnp.where(blocks, nt(q, k, exact) * scale, -jnp.inf)
    expo = jnp.exp(scores - jnp.max(scores, axis=1, keepdims=True))
    probs = expo / jnp.sum(expo, axis=1, keepdims=True)
    mixed_b = nn(probs, v, exact).astype(bf16)

    spread_d = spread_matrix(width, depth)
    diagonal = same_block(hm, width, slices, depth)
    diagonal_t = same_block(width, hm, depth, slices)
    w_out = w_out_ref[...]
    mixed_block = jnp.where(diagonal, nt(mixed_b, spread_d), 0.0).astype(bf16)
    mw_ref[...] = nn(mixed_block, w_out).astype(bf16)

    d_probs = nt(d_mixed, v, exact)
    d_v = tn(probs, d_mixed, exact)
    d_scores = probs * (d_probs - jnp.sum(probs * d_probs, axis=1, keepdims=True)) * scale
    d_q = nn(d_scores, k, exact)
    d_k = tn(d_scores, q, exact)
    d_tokens = nt(d_q, w_q, exact) + nt(d_k, w_k, exact) + nt(d_v, w_v, exact)
    d_raw_b = (d_tokens * inverse).astype(bf16)
    d_norm = -jnp.sum(d_tokens * raw, axis=1, keepdims=True) * inverse * inverse
    dn_ref[...] = jnp.broadcast_to(d_norm, dn_ref.shape)
    top = sw_ref.shape[0]
    lhs_ref[0:top, :] = sw_ref[...]
    lhs_ref[top : top + hm, :] = jnp.where(diagonal, nt(d_raw_b, spread_d), 0.0).astype(bf16)
    yt_ref[:, 0:hm] = jnp.where(diagonal_t, nt(spread_d, d_raw_b), 0.0).astype(bf16)
    yt_ref[:, hm : 2 * hm] = sb_ref[...]

    for i, grad in enumerate((d_q, d_k, d_v)):
        grad_qkv_ref[i] = tn(tokens, grad, exact)
    mixed_t = jnp.where(diagonal_t, nt(spread_d, mixed_b), 0.0).astype(bf16)
    high, low = two_pieces(wc_ref[...])
    gwo[...] = nn(mixed_t, high) + nn(mixed_t, low)
    rows = width // group
    for k, send in enumerate((send0, send1, send2, send3)):
        send[...] = gwo[pl.ds(pl.multiple_of((place ^ k) * rows, 8), rows), :]


def backward_kernel(
    heads,
    slices,
    aux_ref,
    mid_ref,
    cot_ref,
    feats_ref,
    lhs_ref,
    mw_ref,
    yt_ref,
    dn_ref,
    temp_ref,
    dmt_ref,
    send0,
    send1,
    send2,
    send3,
    stack,
    grad_acc,
    small_acc,
    pack,
):
    step = pl.program_id(0)
    width = mid_ref.shape[1]
    depth = width // heads
    hm = heads * slices
    block = mid_ref.shape[0]

    @pl.when(step == 0)
    def _():
        grad_acc[...] = jnp.zeros_like(grad_acc)
        small_acc[...] = jnp.zeros_like(small_acc)

    mid = mid_ref[...]
    from_mid = nt(lhs_ref[...], mid)
    from_cot = nt(mw_ref[...], cot_ref[...])
    aux = aux_ref[...]
    sums = []
    for h in range(heads):
        span = slice(h * slices, (h + 1) * slices)
        inv_tau = aux[h : h + 1]
        logits = from_mid[span] * inv_tau
        weights = jnp.exp(logits - aux[heads + h : heads + h + 1])
        d_weights = from_cot[span] + from_mid[hm + 16 + h * slices : hm + 16 + (h + 1) * slices]
        d_weights = d_weights + dn_ref[span, 0:1]
        mean = jnp.sum(weights * d_weights, axis=0, keepdims=True)
        d_logits = weights * (d_weights - mean)
        d_tau = jnp.sum(d_logits * logits, axis=0, keepdims=True)
        sums.append(-d_tau * aux[2 * heads + h : 2 * heads + h + 1])
        stack[span, :] = weights.astype(bf16)
        stack[hm + h * slices : hm + (h + 1) * slices, :] = (d_logits * inv_tau).astype(bf16)
    c_sum = jnp.concatenate(sums, axis=0)
    c_high = c_sum.astype(bf16).astype(f32)
    stack[2 * hm : 2 * hm + 2 * heads, :] = jnp.concatenate([c_high, c_sum - c_high], axis=0).astype(bf16)
    d_mid = nn(yt_ref[...], stack[0 : 2 * hm, :])
    temp = temp_ref[...].astype(f32)
    for h in range(heads):
        span = slice(h * depth, (h + 1) * depth)
        dmt_ref[span, :] = (d_mid[span] + temp * sums[h]).astype(bf16)
    grad_acc[...] += nn(dmt_ref[...], feats_ref[...])
    small_acc[...] += nn(stack[hm : 2 * hm + 2 * heads, :], mid)

    @pl.when(step == pl.num_programs(0) - 1)
    def _():
        grad = grad_acc[...].T
        u_part = jnp.where(same_block(hm, width, slices, depth), small_acc[0:hm, :], 0.0)
        u_part = fold_rows(u_part, heads, slices)
        c_part = small_acc[hm : hm + heads, :] + small_acc[hm + heads : hm + 2 * heads, :]
        c_part = jnp.where(same_block(heads, width, 1, depth), c_part, 0.0)
        c_part = jnp.sum(c_part, axis=0, keepdims=True)

        def fold_lanes(x):
            total = x[:, 0:128]
            for j in range(1, width // 128):
                total = total + x[:, j * 128 : (j + 1) * 128]
            shift = 64
            while shift >= depth:
                total = total + pltpu.roll(total, shift, 1)
                shift //= 2
            return total

        u_part = fold_lanes(u_part)
        c_part = fold_lanes(jnp.broadcast_to(c_part, (slices, width)))
        where_lane = cols_of((slices, 128))
        extra = jnp.where(where_lane < depth, u_part, c_part)
        rows = width // group
        more = slices // group
        for j in range(group):
            pack[j, 0:rows, :] = grad[j * rows : (j + 1) * rows]
            pack[j, rows : rows + more, 0:128] = extra[j * more : (j + 1) * more]
            pack[j, rows : rows + more, 128:] = jnp.zeros((more, width - 128), f32)
        place = group_place()
        for k, send in enumerate((send0, send1, send2, send3)):
            send[...] = pack[place ^ k]


def rows_kernel(wt_ref, dmt_ref, mw_ref, w_mid_ref, attended_ref, feats_grad_ref):
    attended_ref[...] = tn(wt_ref[...], mw_ref[...]).astype(bf16)
    feats_grad_ref[...] = lax.dot_general(
        dmt_ref[...], w_mid_ref[...], (((0,), (1,)), ((), ())), preferred_element_type=f32
    ).astype(bf16)


def finish_kernel(
    depth, o0, o1, o2, o3, m0, m1, m2, m3, grad_mid_ref, grad_out_ref, slice_ref, temp_ref, extra
):
    place = group_place()
    rows = o0.shape[0]
    more = m0.shape[0] - rows
    for k, (out_part, mid_part) in enumerate(((o0, m0), (o1, m1), (o2, m2), (o3, m3))):
        at = pl.ds(pl.multiple_of((place ^ k) * rows, 8), rows)
        grad_out_ref[at, :] = out_part[...]
        grad_mid_ref[at, :] = mid_part[0:rows, :]
        extra[pl.ds(pl.multiple_of((place ^ k) * more, 8), more), :] = mid_part[rows:, 0:128]
    slices = slice_ref.shape[1]
    turned = extra[...].T
    slice_ref[...] = turned[0:depth, 0:slices]
    temp_ref[...] = extra[0:1, depth : 2 * depth]


def full(shape):
    zeros = (0,) * len(shape)
    return pl.BlockSpec(shape, lambda *_: zeros)


def params(grid=True):
    if grid:
        return pltpu.CompilerParams(
            dimension_semantics=("arbitrary",), vmem_limit_bytes=vmem_bytes
        )
    return pltpu.CompilerParams(vmem_limit_bytes=vmem_bytes)


def cost(flops, moved, transcendentals=0):
    return pl.CostEstimate(flops=flops, bytes_accessed=moved, transcendentals=transcendentals)


def exchange(x, k, count):
    return lax.ppermute(x, "node", [(i, i ^ k) for i in range(count)])


def sum_over_groups(parts, count):
    got = [parts[0]] + [exchange(parts[k], k, count) for k in range(1, group)]
    total = (got[0] + got[1]) + (got[2] + got[3])
    stride = group
    while stride < count:
        if count // stride % 4 == 0:
            r1, r2, r3 = (exchange(total, stride * j, count) for j in (1, 2, 3))
            total = (total + r1) + (r2 + r3)
            stride *= 4
        else:
            total = total + exchange(total, stride, count)
            stride *= 2
    return total


def sum_everywhere(x, count):
    pieces = x.shape[0]
    groups = None
    if count > pieces:
        groups = [list(range(i, i + pieces)) for i in range(0, count, pieces)]

    def swap(y):
        return lax.all_to_all(y, "node", 0, 0, axis_index_groups=groups, tiled=True)

    total = jnp.sum(swap(x), axis=0)
    stride = pieces
    while stride < count:
        total = total + exchange(total, stride, count)
        stride *= 2
    return swap(jnp.broadcast_to(total, x.shape))


def gather_group(total, count):
    return [total] + [exchange(total, k, count) for k in range(1, group)]


def shards(count, feats, cotangent, valid, owned, w_mid, w_slice, temp_vec, w_qkv, w_out):
    rows, width = feats.shape
    depth, slices = w_slice.shape
    heads = width // depth
    hm = heads * slices
    block = min(1024, rows)
    grid = (rows // block,)
    unit = 2 * rows * width * width
    smem = pl.BlockSpec(memory_space=pltpu.SMEM)
    by_rows = pl.BlockSpec((block, width), lambda i: (i, 0))
    by_cols = pl.BlockSpec((hm, block), lambda i: (0, i))
    aux_spec = pl.BlockSpec((3 * heads, block), lambda i: (0, i))
    pack = (2 * (slices // 8) * (width // 128), 16, 128)

    def like(shape, dtype):
        return jax.ShapeDtypeStruct(shape, dtype)

    mid, wt, aux, sw, sb, wc, sums = pl.pallas_call(
        functools.partial(stats_kernel, heads, slices),
        grid=grid,
        in_specs=[
            smem,
            pl.BlockSpec((1, block), lambda i: (0, i)),
            by_rows,
            by_rows,
            full((width, width)),
            full((depth, slices)),
            full((1, depth)),
            full((width, width)),
        ],
        out_specs=[
            by_rows,
            by_cols,
            aux_spec,
            full((hm + 16, width)),
            full((width, hm)),
            full((hm, width)),
            full(pack),
        ],
        out_shape=[
            like((rows, width), bf16),
            like((hm, rows), bf16),
            like((3 * heads, rows), f32),
            like((hm + 16, width), bf16),
            like((width, hm), bf16),
            like((hm, width), f32),
            like(pack, f32),
        ],
        scratch_shapes=[pltpu.VMEM((hm, width), f32), pltpu.VMEM((hm, 128), f32)],
        compiler_params=params(),
        cost_estimate=cost(4 * unit, rows * width * 8, rows * hm),
    )(owned, valid.reshape(1, rows), feats, cotangent, w_mid, w_slice, temp_vec.reshape(1, depth), w_out)

    sums = sum_everywhere(sums, count)

    quarter = (width // group, width)
    lhs, mw, yt, dn, grad_qkv, *sends = pl.pallas_call(
        functools.partial(tokens_kernel, heads, slices),
        out_shape=[
            like((2 * hm + 16, width), bf16),
            like((hm, width), bf16),
            like((width, 2 * hm), bf16),
            like((hm, 128), f32),
            like((3, depth, depth), f32),
        ]
        + [like(quarter, f32)] * group,
        scratch_shapes=[pltpu.VMEM((width, width), f32)],
        compiler_params=params(False),
        cost_estimate=cost(30 * width**3, 4 * width * width * 4, hm * hm),
    )(sums, w_qkv, w_out, sw, sb, wc)

    out_parts = gather_group(sum_over_groups(sends, count), count)

    more = slices // group
    larger = (width // group + more, width)
    dmt, *sends = pl.pallas_call(
        functools.partial(backward_kernel, heads, slices),
        grid=grid,
        in_specs=[
            aux_spec,
            by_rows,
            by_rows,
            by_rows,
            full((2 * hm + 16, width)),
            full((hm, width)),
            full((width, 2 * hm)),
            full((hm, 128)),
            full((depth, 1)),
        ],
        out_specs=[by_cols] + [full(larger)] * group,
        out_shape=[like((width, rows), bf16)] + [like(larger, f32)] * group,
        scratch_shapes=[
            pltpu.VMEM((2 * hm + 16, block), bf16),
            pltpu.VMEM((width, width), f32),
            pltpu.VMEM((hm + 16, width), f32),
            pltpu.VMEM((group,) + larger, f32),
        ],
        compiler_params=params(),
        cost_estimate=cost(8 * unit, rows * width * 8, rows * hm),
    )(aux, mid, cotangent, feats, lhs, mw, yt, dn, temp_vec.reshape(depth, 1))

    mid_parts = gather_group(sum_over_groups(sends, count), count)

    attended, feats_grad = pl.pallas_call(
        rows_kernel,
        grid=grid,
        in_specs=[by_cols, by_cols, full((hm, width)), full((width, width))],
        out_specs=[by_rows, by_rows],
        out_shape=[like((rows, width), bf16)] * 2,
        compiler_params=params(),
        cost_estimate=cost(2 * unit, rows * width * 8),
    )(wt, dmt, mw, w_mid)

    grad_w_mid, grad_w_out, grad_w_slice, grad_temp = pl.pallas_call(
        functools.partial(finish_kernel, depth),
        out_shape=[
            like((width, width), f32),
            like((width, width), f32),
            like((depth, slices), f32),
            like((1, depth), f32),
        ],
        scratch_shapes=[pltpu.VMEM((slices, 128), f32)],
        compiler_params=params(False),
        cost_estimate=cost(0, 4 * width * width * 4),
    )(*out_parts, *mid_parts)
    return (
        attended,
        feats_grad,
        grad_w_mid,
        grad_w_out,
        grad_w_slice,
        grad_temp.reshape(depth),
        grad_qkv,
    )


def solution(mesh):
    in_specs = (
        P(("design", "node"), None),
        P(("design", "node"), None),
        P(("design", "node")),
        P(("design", "node")),
        P(),
        P(),
        P(),
        P(),
        P(),
    )
    out_specs = (
        P(("design", "node"), None),
        P(("design", "node"), None),
        P("design", None),
        P("design", None),
        P("design", None),
        P("design"),
        P("design", None, None),
    )
    return jax.shard_map(
        functools.partial(shards, mesh.shape["node"]),
        mesh=mesh,
        in_specs=in_specs,
        out_specs=out_specs,
        check_vma=False,
    )
```

```python
import functools
import math

import jax
import jax.numpy as jnp
from jax import lax
from jax.experimental import pallas as pl
from jax.experimental.pallas import tpu as pltpu
from jax.sharding import PartitionSpec as P

f32 = jnp.float32
bf16 = jnp.bfloat16
eps_norm = 1e-05
exact = lax.Precision.HIGHEST
group = 4
mib = 1024 * 1024


def nn(a, b, precision=None):
    return lax.dot_general(
        a, b, (((1,), (0,)), ((), ())), preferred_element_type=f32, precision=precision
    )


def nt(a, b, precision=None):
    return lax.dot_general(
        a, b, (((1,), (1,)), ((), ())), preferred_element_type=f32, precision=precision
    )


def tn(a, b, precision=None):
    return lax.dot_general(
        a, b, (((0,), (0,)), ((), ())), preferred_element_type=f32, precision=precision
    )


def rows_of(shape):
    return lax.broadcasted_iota(jnp.int32, shape, 0)


def cols_of(shape):
    return lax.broadcasted_iota(jnp.int32, shape, 1)


def spread_matrix(width, small):
    shape = (width, small)
    return jnp.where(rows_of(shape) % small == cols_of(shape), 1.0, 0.0).astype(bf16)


def same_block(rows, cols, row_size, col_size):
    shape = (rows, cols)
    return rows_of(shape) // row_size == cols_of(shape) // col_size


def two_pieces(x):
    high = x.astype(bf16)
    return high, (x - high.astype(f32)).astype(bf16)


def fold_rows(x, heads, size):
    total = x[0:size]
    for h in range(1, heads):
        total = total + x[h * size : (h + 1) * size]
    return total


def group_place():
    return lax.axis_index("node") % group


def stats_kernel(
    heads,
    slices,
    owned_ref,
    valid_ref,
    feats_ref,
    cot_ref,
    w_mid_ref,
    w_slice_ref,
    temp_ref,
    w_out_ref,
    w_qkv_ref,
    mid_ref,
    wt_ref,
    aux_ref,
    sw_ref,
    sb_ref,
    w_cat_ref,
    keep_ref,
    send_ref,
    wc0,
    wc1,
    wc2,
    wc3,
    raw_acc,
    norm_acc,
    wc_acc,
    pack,
):
    step = pl.program_id(0)
    width = w_mid_ref.shape[0]
    depth = width // heads
    hm = heads * slices
    block = feats_ref.shape[0]

    @pl.when(step == 0)
    def _():
        spread_d = spread_matrix(width, depth)
        spread_m = spread_matrix(hm, slices)
        w_slice = w_slice_ref[...]
        half = nt(spread_m, w_slice).astype(bf16)
        full = nt(half, spread_d)
        sw_ref[0:hm, :] = jnp.where(same_block(hm, width, slices, depth), full, 0.0).astype(bf16)
        half = nn(spread_d, w_slice).astype(bf16)
        full = nt(half, spread_m)
        sb_ref[...] = jnp.where(same_block(width, hm, depth, slices), full, 0.0).astype(bf16)
        temp = jnp.broadcast_to(temp_ref[...].astype(f32), (16, depth)).astype(bf16)
        full = nt(temp, spread_d)
        sw_ref[hm : hm + 16, :] = jnp.where(same_block(16, width, 1, depth), full, 0.0).astype(
            bf16
        )
        w_cat = jnp.zeros((depth, 128), f32)
        for i in range(3):
            place_at = jnp.where(rows_of((depth, 128)) + i * depth == cols_of((depth, 128)), 1.0, 0.0)
            w_cat = w_cat + nn(w_qkv_ref[i], place_at.astype(bf16))
        w_cat_ref[...] = w_cat.astype(bf16)
        raw_acc[...] = jnp.zeros_like(raw_acc)
        norm_acc[...] = jnp.zeros_like(norm_acc)
        wc_acc[...] = jnp.zeros_like(wc_acc)

    mid = nn(feats_ref[...], w_mid_ref[...]).astype(bf16)
    mid_ref[...] = mid
    scores = nt(sw_ref[...], mid)
    zsum = scores[hm : hm + heads]
    small = jnp.exp(-jnp.abs(zsum))
    inv_tau = 1.0 / (0.5 + (jnp.maximum(zsum, 0.0) + jnp.log(1.0 + small)))
    sig = jnp.where(zsum >= 0.0, 1.0, small) / (1.0 + small)
    position = step * block + cols_of((1, block))
    live = (valid_ref[...] > 0) & (position < owned_ref[0])
    live_f = live.astype(f32)
    aux_ref[0:heads, :] = inv_tau
    aux_ref[2 * heads : 3 * heads, :] = sig * inv_tau
    for h in range(heads):
        span = slice(h * slices, (h + 1) * slices)
        logits = scores[span] * inv_tau[h : h + 1]
        peak = jnp.max(logits, axis=0, keepdims=True)
        expo = jnp.exp(logits - peak)
        total = jnp.sum(expo, axis=0, keepdims=True)
        weights = expo * (live_f / total)
        wt_ref[span, :] = weights.astype(bf16)
        lanes = weights[:, 0:128]
        for c in range(1, block // 128):
            lanes = lanes + weights[:, c * 128 : (c + 1) * 128]
        norm_acc[span, :] += lanes
        aux_ref[heads + h : heads + h + 1, :] = jnp.where(live, peak + jnp.log(total), jnp.inf)
    wt = wt_ref[...]
    raw_acc[...] += nn(wt, mid)
    wc_acc[...] += nn(wt, cot_ref[...])

    @pl.when(step == pl.num_programs(0) - 1)
    def _():
        diagonal = same_block(hm, width, slices, depth)
        raw = fold_rows(jnp.where(diagonal, raw_acc[...], 0.0), heads, slices)
        high, low = two_pieces(wc_acc[...])
        w_out = w_out_ref[...]
        mixed = nt(high, w_out) + nt(low, w_out)
        mixed = fold_rows(jnp.where(diagonal, mixed, 0.0), heads, slices)
        norm = jnp.sum(norm_acc[...].T, axis=0, keepdims=True)
        first = rows_of((8, 128)) == 0
        for j in range(2):
            part = slice(j * 128, (j + 1) * 128)
            pack[j, 0:slices, :] = raw[:, part]
            pack[j, slices : 2 * slices, :] = mixed[:, part]
            pack[j, 2 * slices :, :] = jnp.where(first, norm[:, part], 0.0)
        place = group_place()
        keep_ref[...] = pack[place & 1]
        send_ref[...] = pack[(place & 1) ^ 1]
        rows = hm // group
        for k, send in enumerate((wc0, wc1, wc2, wc3)):
            send[...] = wc_acc[pl.ds(pl.multiple_of((place ^ k) * rows, 8), rows), :]


def lanes_at(x, lane, *where):
    place = cols_of(x.shape) // lane
    total = jnp.zeros_like(x)
    for value, at, to in where:
        shift = (to - at) * lane % 128
        moved = pltpu.roll(value, shift, 1) if shift else value
        total = jnp.where(place == to, moved, total)
    return total.astype(bf16)


def split(x):
    high = x.astype(bf16).astype(f32)
    return high, x - high


def tokens_kernel(
    heads,
    slices,
    own_ref,
    got_ref,
    w_cat_ref,
    w_out_ref,
    sw_ref,
    sb_ref,
    lhs_ref,
    mw_ref,
    mixed_t_ref,
    yt_ref,
    dn_ref,
    grad_qkv_ref,
    pack,
):
    width = w_out_ref.shape[0]
    depth = width // heads
    hm = heads * slices
    place = group_place() & 1
    pack[place] = own_ref[...]
    pack[place ^ 1] = got_ref[...]
    per = 128 // depth

    def compact(first):
        pieces = []
        for h in range(heads):
            x = pack[h // per, first : first + slices, :]
            shift = (h % per) * depth
            pieces.append(pltpu.roll(x, 128 - shift, 1) if shift else x)
        x = jnp.concatenate(pieces, axis=0)
        return jnp.where(cols_of(x.shape) < depth, x, 0.0)

    raw = compact(0)
    d_mixed = compact(slices)
    norm = jnp.concatenate([pack[j, 2 * slices :, :].T[:, 0:1] for j in range(2)], axis=0)
    inverse = 1.0 / (norm + eps_norm)
    tokens = raw * inverse
    w_cat = w_cat_ref[...]

    t_high, rest = split(tokens)
    t_low, rest = split(rest)
    left = lanes_at(tokens, depth, (t_high, 0, 0), (t_low, 0, 1), (rest, 0, 2))
    blank = jnp.zeros((128 - 3 * depth, 128), bf16)
    qkv = nn(left, jnp.concatenate([w_cat, w_cat, w_cat, blank], axis=0))
    high, low = split(qkv)
    q_left = lanes_at(qkv, depth, (high, 0, 0), (high, 0, 1), (low, 0, 2))
    k_right = lanes_at(qkv, depth, (high, 1, 0), (low, 1, 1), (high, 1, 2))
    v_right = lanes_at(qkv, depth, (high, 2, 0), (low, 2, 1), (high, 2, 2))
    q_pair = lanes_at(qkv, depth, (high, 0, 0), (low, 0, 1))
    k_pair = lanes_at(qkv, depth, (high, 1, 0), (low, 1, 1))
    v_pair = lanes_at(qkv, depth, (high, 2, 0), (low, 2, 1))
    g_high, g_low = split(d_mixed)
    g_left = lanes_at(qkv, depth, (g_high, 0, 0), (g_high, 0, 1), (g_low, 0, 2))
    g_pair = lanes_at(qkv, depth, (g_high, 0, 0), (g_low, 0, 1))

    def times_pair(dot, x, pair):
        x_high, x_low = two_pieces(x)
        both = dot(x_high, pair)
        low_part = dot(x_low, pair)
        total = both + pltpu.roll(both, 128 - depth, 1) + low_part
        return jnp.where(cols_of(total.shape) < depth, total, 0.0)

    blocks = same_block(hm, hm, slices, slices)
    scale = 1.0 / math.sqrt(depth)
    scores = jnp.where(blocks, nt(q_left, k_right) * scale, -jnp.inf)
    expo = jnp.exp(scores - jnp.max(scores, axis=1, keepdims=True))
    probs = expo * (1.0 / jnp.sum(expo, axis=1, keepdims=True))
    mixed_b = times_pair(nn, probs, v_pair).astype(bf16)

    spread_d = jnp.where(
        (rows_of((width, 128)) % depth == cols_of((width, 128))), 1.0, 0.0
    ).astype(bf16)
    diagonal = same_block(hm, width, slices, depth)
    diagonal_t = same_block(width, hm, depth, slices)
    mixed_block = jnp.where(diagonal, nt(mixed_b, spread_d), 0.0).astype(bf16)
    mw_ref[...] = nn(mixed_block, w_out_ref[...]).astype(bf16)
    mixed_t_ref[...] = jnp.where(diagonal_t, nt(spread_d, mixed_b), 0.0).astype(bf16)

    d_probs = nt(g_left, v_right)
    d_v = times_pair(tn, probs, g_pair)
    d_scores = probs * (d_probs - jnp.sum(probs * d_probs, axis=1, keepdims=True)) * scale
    d_q = times_pair(nn, d_scores, k_pair)
    d_k = times_pair(tn, d_scores, q_pair)
    d_qkv = d_q + pltpu.roll(d_k, depth, 1) + pltpu.roll(d_v, 2 * depth, 1)
    d_high, d_low = two_pieces(d_qkv)
    d_tokens = nt(d_high, w_cat) + nt(d_low, w_cat)
    raw = raw[:, 0:depth]
    d_raw_b = (d_tokens * inverse).astype(bf16)
    d_norm = -jnp.sum(d_tokens * raw, axis=1, keepdims=True) * inverse * inverse
    dn_ref[...] = jnp.broadcast_to(d_norm, dn_ref.shape)
    top = sw_ref.shape[0]
    lhs_ref[0:top, :] = sw_ref[...]
    spread_d = spread_matrix(width, depth)
    lhs_ref[top : top + hm, :] = jnp.where(diagonal, nt(d_raw_b, spread_d), 0.0).astype(bf16)
    yt_ref[:, 0:hm] = jnp.where(diagonal_t, nt(spread_d, d_raw_b), 0.0).astype(bf16)
    yt_ref[:, hm : 2 * hm] = sb_ref[...]

    t_high, t_low = two_pieces(tokens)
    grads = tn(t_high, d_high) + tn(t_high, d_low) + tn(t_low, d_high)
    for i in range(3):
        at = pltpu.roll(grads, 128 - i * depth, 1) if i else grads
        grad_qkv_ref[i] = at[0:depth, 0:depth]


def backward_kernel(
    heads,
    slices,
    aux_ref,
    mid_ref,
    cot_ref,
    feats_ref,
    lhs_ref,
    mw_ref,
    yt_ref,
    dn_ref,
    temp_ref,
    _,
    dmt_ref,
    send0,
    send1,
    send2,
    send3,
    stack,
    grad_acc,
    small_acc,
    pack,
):
    step = pl.program_id(0)
    width = mid_ref.shape[1]
    depth = width // heads
    hm = heads * slices
    block = mid_ref.shape[0]

    @pl.when(step == 0)
    def _():
        grad_acc[...] = jnp.zeros_like(grad_acc)
        small_acc[...] = jnp.zeros_like(small_acc)

    mid = mid_ref[...]
    from_mid = nt(lhs_ref[...], mid)
    from_cot = nt(mw_ref[...], cot_ref[...])
    aux = aux_ref[...]
    sums = []
    for h in range(heads):
        span = slice(h * slices, (h + 1) * slices)
        inv_tau = aux[h : h + 1]
        logits = from_mid[span] * inv_tau
        weights = jnp.exp(logits - aux[heads + h : heads + h + 1])
        d_weights = from_cot[span] + from_mid[hm + 16 + h * slices : hm + 16 + (h + 1) * slices]
        d_weights = d_weights + dn_ref[span, 0:1]
        mean = jnp.sum(weights * d_weights, axis=0, keepdims=True)
        d_logits = weights * (d_weights - mean)
        d_tau = jnp.sum(d_logits * logits, axis=0, keepdims=True)
        sums.append(-d_tau * aux[2 * heads + h : 2 * heads + h + 1])
        stack[span, :] = weights.astype(bf16)
        stack[hm + h * slices : hm + (h + 1) * slices, :] = (d_logits * inv_tau).astype(bf16)
    c_sum = jnp.concatenate(sums, axis=0)
    c_high = c_sum.astype(bf16).astype(f32)
    stack[2 * hm : 2 * hm + 2 * heads, :] = jnp.concatenate([c_high, c_sum - c_high], axis=0).astype(bf16)
    d_mid = nn(yt_ref[...], stack[0 : 2 * hm, :])
    temp = jnp.broadcast_to(temp_ref[...].astype(f32), (16, depth)).astype(bf16)
    same = (rows_of((depth, depth)) == cols_of((depth, depth))).astype(f32).astype(bf16)
    temp = nt(same, temp)[:, 0:1]
    for h in range(heads):
        span = slice(h * depth, (h + 1) * depth)
        dmt_ref[span, :] = (d_mid[span] + temp * sums[h]).astype(bf16)
    grad_acc[...] += nn(dmt_ref[...], feats_ref[...])
    small_acc[...] += nn(stack[hm : 2 * hm + 2 * heads, :], mid)

    @pl.when(step == pl.num_programs(0) - 1)
    def _():
        grad = grad_acc[...].T
        u_part = jnp.where(same_block(hm, width, slices, depth), small_acc[0:hm, :], 0.0)
        u_part = fold_rows(u_part, heads, slices)
        c_part = small_acc[hm : hm + heads, :] + small_acc[hm + heads : hm + 2 * heads, :]
        c_part = jnp.where(same_block(heads, width, 1, depth), c_part, 0.0)
        c_part = jnp.sum(c_part, axis=0, keepdims=True)

        def fold_lanes(x):
            total = x[:, 0:128]
            for j in range(1, width // 128):
                total = total + x[:, j * 128 : (j + 1) * 128]
            shift = 64
            while shift >= depth:
                total = total + pltpu.roll(total, shift, 1)
                shift //= 2
            return total

        u_part = fold_lanes(u_part)
        c_part = fold_lanes(jnp.broadcast_to(c_part, (slices, width)))
        where_lane = cols_of((slices, 128))
        extra = jnp.where(where_lane < depth, u_part, c_part)
        rows = width // group
        more = slices // group
        for j in range(group):
            pack[j, 0:rows, :] = grad[j * rows : (j + 1) * rows]
            pack[j, rows : rows + more, 0:128] = extra[j * more : (j + 1) * more]
            pack[j, rows : rows + more, 128:] = jnp.zeros((more, width - 128), f32)
        place = group_place()
        for k, send in enumerate((send0, send1, send2, send3)):
            send[...] = pack[place ^ k]


def rows_kernel(wt_ref, dmt_ref, mw_ref, w_mid_ref, _, attended_ref, feats_grad_ref, token_ref):
    token_ref[...] = jnp.zeros_like(token_ref)
    attended_ref[...] = tn(wt_ref[...], mw_ref[...]).astype(bf16)
    feats_grad_ref[...] = lax.dot_general(
        dmt_ref[...], w_mid_ref[...], (((0,), (1,)), ((), ())), preferred_element_type=f32
    ).astype(bf16)


def grad_out_kernel(o0, o1, o2, o3, mixed_t_ref, grad_out_ref, whole):
    place = group_place()
    rows = o0.shape[0]
    for k, part in enumerate((o0, o1, o2, o3)):
        whole[pl.ds(pl.multiple_of((place ^ k) * rows, 8), rows), :] = part[...]
    high, low = two_pieces(whole[...])
    mixed_t = mixed_t_ref[...]
    grad_out_ref[...] = nn(mixed_t, high) + nn(mixed_t, low)


def finish_kernel(depth, m0, m1, m2, m3, grad_mid_ref, slice_ref, temp_ref, extra):
    place = group_place()
    slices = slice_ref.shape[1]
    more = slices // group
    rows = m0.shape[0] - more
    for k, part in enumerate((m0, m1, m2, m3)):
        at = pl.ds(pl.multiple_of((place ^ k) * rows, 8), rows)
        grad_mid_ref[at, :] = part[0:rows, :]
        extra[pl.ds(pl.multiple_of((place ^ k) * more, 8), more), :] = part[rows:, 0:128]
    turned = extra[...].T
    slice_ref[...] = turned[0:depth, 0:slices]
    temp_ref[...] = extra[0:1, depth : 2 * depth]


def full(shape):
    zeros = (0,) * len(shape)
    return pl.BlockSpec(shape, lambda *_: zeros)


def params(mebibytes, grid=True):
    semantics = ("arbitrary",) if grid else None
    return pltpu.CompilerParams(
        dimension_semantics=semantics, vmem_limit_bytes=mebibytes * mib
    )


def cost(flops, moved, transcendentals=0):
    return pl.CostEstimate(flops=flops, bytes_accessed=moved, transcendentals=transcendentals)


def exchange(x, k, count):
    return lax.ppermute(x, "node", [(i, i ^ k) for i in range(count)])


def sum_kernel(r0, r1, r2, r3, *rest):
    rest[-1][...] = (r0[...] + r1[...]) + (r2[...] + r3[...])


def sum_four(parts, *before):
    return pl.pallas_call(
        sum_kernel,
        out_shape=jax.ShapeDtypeStruct(parts[0].shape, f32),
        in_specs=[pl.BlockSpec(memory_space=pltpu.VMEM)] * 4
        + [pl.BlockSpec(memory_space=pl.ANY)] * len(before),
        out_specs=pl.BlockSpec(memory_space=pltpu.VMEM),
        compiler_params=params(2, False),
        cost_estimate=cost(3 * parts[0].size, 5 * parts[0].size * 4),
    )(*parts, *before)


def scatter_group(parts, count):
    return sum_four([parts[0]] + [exchange(parts[k], k, count) for k in range(1, group)])


def sum_over_groups(total, count, *before):
    stride = group
    while stride < count:
        if count // stride % 4 == 0:
            got = [total] + [exchange(total, stride * j, count) for j in (1, 2, 3)]
            total = sum_four(got, *before)
            stride *= 4
        else:
            total = total + exchange(total, stride, count)
            stride *= 2
    return total


def gather_group(total, count):
    return [total] + [exchange(total, k, count) for k in range(1, group)]


def shards(count, feats, cotangent, valid, owned, w_mid, w_slice, temp_vec, w_qkv, w_out):
    rows, width = feats.shape
    depth, slices = w_slice.shape
    heads = width // depth
    hm = heads * slices
    unit = 2 * rows * width * width
    smem = pl.BlockSpec(memory_space=pltpu.SMEM)

    def blocks(size):
        return (
            (rows // size,),
            pl.BlockSpec((size, width), lambda i: (i, 0)),
            pl.BlockSpec((hm, size), lambda i: (0, i)),
            pl.BlockSpec((3 * heads, size), lambda i: (0, i)),
        )

    def like(shape, dtype):
        return jax.ShapeDtypeStruct(shape, dtype)

    temp = temp_vec.reshape(1, depth)
    half = (2 * slices + 8, 128)
    quarter = (width // group, width)
    block = min(2048, rows)
    grid, by_rows, by_cols, aux_spec = blocks(block)
    mid, wt, aux, sw, sb, w_cat, keep, send, *wc = pl.pallas_call(
        functools.partial(stats_kernel, heads, slices),
        grid=grid,
        in_specs=[
            smem,
            pl.BlockSpec((1, block), lambda i: (0, i)),
            by_rows,
            by_rows,
            full((width, width)),
            full((depth, slices)),
            full((1, depth)),
            full((width, width)),
            full((3, depth, depth)),
        ],
        out_specs=[
            by_rows,
            by_cols,
            aux_spec,
            full((hm + 16, width)),
            full((width, hm)),
            full((depth, 128)),
            full(half),
            full(half),
        ]
        + [full(quarter)] * group,
        out_shape=[
            like((rows, width), bf16),
            like((hm, rows), bf16),
            like((3 * heads, rows), f32),
            like((hm + 16, width), bf16),
            like((width, hm), bf16),
            like((depth, 128), bf16),
            like(half, f32),
            like(half, f32),
        ]
        + [like(quarter, f32)] * group,
        scratch_shapes=[
            pltpu.VMEM((hm, width), f32),
            pltpu.VMEM((hm, 128), f32),
            pltpu.VMEM((hm, width), f32),
            pltpu.VMEM((2,) + half, f32),
        ],
        compiler_params=params(56),
        cost_estimate=cost(4 * unit, rows * width * 8, rows * hm),
    )(owned, valid.reshape(1, rows), feats, cotangent, w_mid, w_slice, temp, w_out, w_qkv)

    own = keep + exchange(send, 1, count)
    stride = 2
    while stride < count:
        own = own + exchange(own, stride, count)
        stride *= 2
    other = exchange(own, 1, count)

    parts = lax.optimization_barrier((*wc, other))
    wc_total = scatter_group(parts[:group], count)
    lhs, mw, mixed_t, yt, dn, grad_qkv = pl.pallas_call(
        functools.partial(tokens_kernel, heads, slices),
        out_shape=[
            like((2 * hm + 16, width), bf16),
            like((hm, width), bf16),
            like((width, hm), bf16),
            like((width, 2 * hm), bf16),
            like((hm, 128), f32),
            like((3, depth, depth), f32),
        ],
        scratch_shapes=[pltpu.VMEM((2,) + half, f32)],
        compiler_params=params(8, False),
        cost_estimate=cost(30 * width**3, 4 * width * width * 4, hm * hm),
    )(own, other, w_cat, w_out, sw, sb)

    larger = (width // group + slices // group, width)
    block = min(512, rows)
    grid, by_rows, by_cols, aux_spec = blocks(block)
    dmt, *sends = pl.pallas_call(
        functools.partial(backward_kernel, heads, slices),
        grid=grid,
        in_specs=[
            aux_spec,
            by_rows,
            by_rows,
            by_rows,
            full((2 * hm + 16, width)),
            full((hm, width)),
            full((width, 2 * hm)),
            full((hm, 128)),
            full((1, depth)),
            pl.BlockSpec(memory_space=pl.ANY),
        ],
        out_specs=[by_cols] + [full(larger)] * group,
        out_shape=[like((width, rows), bf16)] + [like(larger, f32)] * group,
        scratch_shapes=[
            pltpu.VMEM((2 * hm + 16, block), bf16),
            pltpu.VMEM((width, width), f32),
            pltpu.VMEM((hm + 16, width), f32),
            pltpu.VMEM((group,) + larger, f32),
        ],
        compiler_params=params(56),
        cost_estimate=cost(8 * unit, rows * width * 8, rows * hm),
    )(aux, mid, cotangent, feats, lhs, mw, yt, dn, temp, wc_total)

    mid_total = scatter_group(sends, count)
    wc_total = sum_over_groups(wc_total, count, sends[1])
    out_parts = gather_group(wc_total, count)

    block = min(1024, rows)
    grid, by_rows, by_cols, aux_spec = blocks(block)
    attended, feats_grad, token = pl.pallas_call(
        rows_kernel,
        grid=grid,
        in_specs=[
            by_cols,
            by_cols,
            full((hm, width)),
            full((width, width)),
            pl.BlockSpec(memory_space=pl.ANY),
        ],
        out_specs=[by_rows, by_rows, full((8, 128))],
        out_shape=[like((rows, width), bf16)] * 2 + [like((8, 128), f32)],
        compiler_params=params(56),
        cost_estimate=cost(2 * unit, rows * width * 8),
    )(wt, dmt, mw, w_mid, mid_total)

    mid_total = sum_over_groups(mid_total, count, token)
    grad_w_out = pl.pallas_call(
        grad_out_kernel,
        out_shape=like((width, width), f32),
        scratch_shapes=[pltpu.VMEM((hm, width), f32)],
        compiler_params=params(8, False),
        cost_estimate=cost(4 * width**3, 3 * width * width * 4),
    )(*out_parts, mixed_t)

    mid_parts = gather_group(mid_total, count)
    grad_w_mid, grad_w_slice, grad_temp = pl.pallas_call(
        functools.partial(finish_kernel, depth),
        out_shape=[
            like((width, width), f32),
            like((depth, slices), f32),
            like((1, depth), f32),
        ],
        scratch_shapes=[pltpu.VMEM((slices, 128), f32)],
        compiler_params=params(8, False),
        cost_estimate=cost(0, 2 * width * width * 4),
    )(*mid_parts)
    return (
        attended,
        feats_grad,
        grad_w_mid,
        grad_w_out,
        grad_w_slice,
        grad_temp.reshape(depth),
        grad_qkv,
    )


def solution(mesh):
    in_specs = (
        P(("design", "node"), None),
        P(("design", "node"), None),
        P(("design", "node")),
        P(("design", "node")),
        P(),
        P(),
        P(),
        P(),
        P(),
    )
    out_specs = (
        P(("design", "node"), None),
        P(("design", "node"), None),
        P("design", None),
        P("design", None),
        P("design", None),
        P("design"),
        P("design", None, None),
    )
    return jax.shard_map(
        functools.partial(shards, mesh.shape["node"]),
        mesh=mesh,
        in_specs=in_specs,
        out_specs=out_specs,
        check_vma=False,
    )
```

```python
import functools
import math

import jax
import jax.numpy as jnp
from jax import lax
from jax.experimental import pallas as pl
from jax.experimental.pallas import tpu as pltpu
from jax.sharding import PartitionSpec as P

f32 = jnp.float32
bf16 = jnp.bfloat16
eps_norm = 1e-05
exact = lax.Precision.HIGHEST
group = 4
sub_block = 512
mib = 1024 * 1024


def nn(a, b, precision=None):
    return lax.dot_general(
        a, b, (((1,), (0,)), ((), ())), preferred_element_type=f32, precision=precision
    )


def nt(a, b, precision=None):
    return lax.dot_general(
        a, b, (((1,), (1,)), ((), ())), preferred_element_type=f32, precision=precision
    )


def tn(a, b, precision=None):
    return lax.dot_general(
        a, b, (((0,), (0,)), ((), ())), preferred_element_type=f32, precision=precision
    )


def rows_of(shape):
    return lax.broadcasted_iota(jnp.int32, shape, 0)


def cols_of(shape):
    return lax.broadcasted_iota(jnp.int32, shape, 1)


def spread_matrix(width, small):
    shape = (width, small)
    return jnp.where(rows_of(shape) % small == cols_of(shape), 1.0, 0.0).astype(bf16)


def same_block(rows, cols, row_size, col_size):
    shape = (rows, cols)
    return rows_of(shape) // row_size == cols_of(shape) // col_size


def two_pieces(x):
    high = x.astype(bf16)
    return high, (x - high.astype(f32)).astype(bf16)


def fold_rows(x, heads, size):
    total = x[0:size]
    for h in range(1, heads):
        total = total + x[h * size : (h + 1) * size]
    return total


def group_place():
    return lax.axis_index("node") % group


def stats_kernel(
    heads,
    slices,
    owned_ref,
    valid_ref,
    feats_ref,
    cot_ref,
    w_mid_ref,
    w_slice_ref,
    temp_ref,
    w_out_ref,
    w_qkv_ref,
    mid_ref,
    wt_ref,
    aux_ref,
    sw_ref,
    sb_ref,
    w_cat_ref,
    keep_ref,
    send_ref,
    wc_keep_ref,
    wc_send_ref,
    raw_acc,
    norm_acc,
    wc_acc,
    pack,
):
    step = pl.program_id(0)
    width = w_mid_ref.shape[0]
    depth = width // heads
    hm = heads * slices
    block = feats_ref.shape[0]

    @pl.when(step == 0)
    def _():
        spread_d = spread_matrix(width, depth)
        spread_m = spread_matrix(hm, slices)
        w_slice = w_slice_ref[...]
        half = nt(spread_m, w_slice).astype(bf16)
        full = nt(half, spread_d)
        sw_ref[0:hm, :] = jnp.where(same_block(hm, width, slices, depth), full, 0.0).astype(bf16)
        half = nn(spread_d, w_slice).astype(bf16)
        full = nt(half, spread_m)
        sb_ref[...] = jnp.where(same_block(width, hm, depth, slices), full, 0.0).astype(bf16)
        temp = jnp.broadcast_to(temp_ref[...].astype(f32), (16, depth)).astype(bf16)
        full = nt(temp, spread_d)
        sw_ref[hm : hm + 16, :] = jnp.where(same_block(16, width, 1, depth), full, 0.0).astype(
            bf16
        )
        w_cat = jnp.zeros((depth, 128), f32)
        for i in range(3):
            place_at = jnp.where(rows_of((depth, 128)) + i * depth == cols_of((depth, 128)), 1.0, 0.0)
            w_cat = w_cat + nn(w_qkv_ref[i], place_at.astype(bf16))
        w_cat_ref[...] = w_cat.astype(bf16)
        raw_acc[...] = jnp.zeros_like(raw_acc)
        norm_acc[...] = jnp.zeros_like(norm_acc)
        wc_acc[...] = jnp.zeros_like(wc_acc)

    mid = nn(feats_ref[...], w_mid_ref[...]).astype(bf16)
    mid_ref[...] = mid
    scores = nt(sw_ref[...], mid)
    zsum = scores[hm : hm + heads]
    small = jnp.exp(-jnp.abs(zsum))
    inv_tau = 1.0 / (0.5 + (jnp.maximum(zsum, 0.0) + jnp.log(1.0 + small)))
    sig = jnp.where(zsum >= 0.0, 1.0, small) / (1.0 + small)
    position = step * block + cols_of((1, block))
    live = (valid_ref[...] > 0) & (position < owned_ref[0])
    live_f = live.astype(f32)
    aux_ref[0:heads, :] = inv_tau
    aux_ref[2 * heads : 3 * heads, :] = sig * inv_tau
    for h in range(heads):
        span = slice(h * slices, (h + 1) * slices)
        logits = scores[span] * inv_tau[h : h + 1]
        peak = jnp.max(logits, axis=0, keepdims=True)
        expo = jnp.exp(logits - peak)
        total = jnp.sum(expo, axis=0, keepdims=True)
        weights = expo * (live_f / total)
        wt_ref[span, :] = weights.astype(bf16)
        lanes = weights[:, 0:128]
        for c in range(1, block // 128):
            lanes = lanes + weights[:, c * 128 : (c + 1) * 128]
        norm_acc[span, :] += lanes
        aux_ref[heads + h : heads + h + 1, :] = jnp.where(live, peak + jnp.log(total), jnp.inf)
    wt = wt_ref[...]
    raw_acc[...] += nn(wt, mid)
    wc_acc[...] += nn(wt, cot_ref[...])

    @pl.when(step == pl.num_programs(0) - 1)
    def _():
        diagonal = same_block(hm, width, slices, depth)
        raw = fold_rows(jnp.where(diagonal, raw_acc[...], 0.0), heads, slices)
        high, low = two_pieces(wc_acc[...])
        w_out = w_out_ref[...]
        mixed = nt(high, w_out) + nt(low, w_out)
        mixed = fold_rows(jnp.where(diagonal, mixed, 0.0), heads, slices)
        norm = jnp.sum(norm_acc[...].T, axis=0, keepdims=True)
        first = rows_of((8, 128)) == 0
        for j in range(2):
            part = slice(j * 128, (j + 1) * 128)
            pack[j, 0:slices, :] = raw[:, part]
            pack[j, slices : 2 * slices, :] = mixed[:, part]
            pack[j, 2 * slices :, :] = jnp.where(first, norm[:, part], 0.0)
        place = group_place()
        keep_ref[...] = pack[place & 1]
        send_ref[...] = pack[(place & 1) ^ 1]
        rows = hm // 2
        for k, out in enumerate((wc_keep_ref, wc_send_ref)):
            out[...] = wc_acc[pl.ds(pl.multiple_of(((place & 1) ^ k) * rows, 8), rows), :]


def lanes_at(x, lane, *where):
    place = cols_of(x.shape) // lane
    total = jnp.zeros_like(x)
    for value, at, to in where:
        shift = (to - at) * lane % 128
        moved = pltpu.roll(value, shift, 1) if shift else value
        total = jnp.where(place == to, moved, total)
    return total.astype(bf16)


def split(x):
    high = x.astype(bf16).astype(f32)
    return high, x - high


def tokens_kernel(
    heads,
    slices,
    own_ref,
    got_ref,
    w_cat_ref,
    w_out_ref,
    mw_ref,
    mixed_t_ref,
    dr_ref,
    drt_ref,
    dn_ref,
    grad_qkv_ref,
    pack,
):
    width = w_out_ref.shape[0]
    depth = width // heads
    hm = heads * slices
    place = group_place() & 1
    pack[place] = own_ref[...]
    pack[place ^ 1] = got_ref[...]
    per = 128 // depth

    def compact(first):
        pieces = []
        for h in range(heads):
            x = pack[h // per, first : first + slices, :]
            shift = (h % per) * depth
            pieces.append(pltpu.roll(x, 128 - shift, 1) if shift else x)
        x = jnp.concatenate(pieces, axis=0)
        return jnp.where(cols_of(x.shape) < depth, x, 0.0)

    raw = compact(0)
    d_mixed = compact(slices)
    norm = jnp.concatenate([pack[j, 2 * slices :, :].T[:, 0:1] for j in range(2)], axis=0)
    inverse = 1.0 / (norm + eps_norm)
    tokens = raw * inverse
    w_cat = w_cat_ref[...]

    t_high, rest = split(tokens)
    t_low, rest = split(rest)
    left = lanes_at(tokens, depth, (t_high, 0, 0), (t_low, 0, 1), (rest, 0, 2))
    blank = jnp.zeros((128 - 3 * depth, 128), bf16)
    qkv = nn(left, jnp.concatenate([w_cat, w_cat, w_cat, blank], axis=0))
    high, low = split(qkv)
    q_left = lanes_at(qkv, depth, (high, 0, 0), (high, 0, 1), (low, 0, 2))
    k_right = lanes_at(qkv, depth, (high, 1, 0), (low, 1, 1), (high, 1, 2))
    v_right = lanes_at(qkv, depth, (high, 2, 0), (low, 2, 1), (high, 2, 2))
    q_pair = lanes_at(qkv, depth, (high, 0, 0), (low, 0, 1))
    k_pair = lanes_at(qkv, depth, (high, 1, 0), (low, 1, 1))
    v_pair = lanes_at(qkv, depth, (high, 2, 0), (low, 2, 1))
    g_high, g_low = split(d_mixed)
    g_left = lanes_at(qkv, depth, (g_high, 0, 0), (g_high, 0, 1), (g_low, 0, 2))
    g_pair = lanes_at(qkv, depth, (g_high, 0, 0), (g_low, 0, 1))

    def times_pair(dot, x, pair):
        x_high, x_low = two_pieces(x)
        both = dot(x_high, pair)
        low_part = dot(x_low, pair)
        total = both + pltpu.roll(both, 128 - depth, 1) + low_part
        return jnp.where(cols_of(total.shape) < depth, total, 0.0)

    blocks = same_block(hm, hm, slices, slices)
    scale = 1.0 / math.sqrt(depth)
    scores = jnp.where(blocks, nt(q_left, k_right) * scale, -jnp.inf)
    expo = jnp.exp(scores - jnp.max(scores, axis=1, keepdims=True))
    probs = expo * (1.0 / jnp.sum(expo, axis=1, keepdims=True))
    mixed_b = times_pair(nn, probs, v_pair).astype(bf16)

    spread_d = jnp.where(
        (rows_of((width, 128)) % depth == cols_of((width, 128))), 1.0, 0.0
    ).astype(bf16)
    diagonal = same_block(hm, width, slices, depth)
    diagonal_t = same_block(width, hm, depth, slices)
    mixed_block = jnp.where(diagonal, nt(mixed_b, spread_d), 0.0).astype(bf16)
    mw_ref[...] = nn(mixed_block, w_out_ref[...]).astype(bf16)
    mixed_t_ref[...] = jnp.where(diagonal_t, nt(spread_d, mixed_b), 0.0).astype(bf16)

    d_probs = nt(g_left, v_right)
    d_v = times_pair(tn, probs, g_pair)
    d_scores = probs * (d_probs - jnp.sum(probs * d_probs, axis=1, keepdims=True)) * scale
    d_q = times_pair(nn, d_scores, k_pair)
    d_k = times_pair(tn, d_scores, q_pair)
    d_qkv = d_q + pltpu.roll(d_k, depth, 1) + pltpu.roll(d_v, 2 * depth, 1)
    d_high, d_low = two_pieces(d_qkv)
    d_tokens = nt(d_high, w_cat) + nt(d_low, w_cat)
    raw = raw[:, 0:depth]
    d_raw_b = (d_tokens * inverse).astype(bf16)
    d_norm = -jnp.sum(d_tokens * raw, axis=1, keepdims=True) * inverse * inverse
    dn_ref[...] = jnp.broadcast_to(d_norm, dn_ref.shape)
    spread_d = spread_matrix(width, depth)
    dr_ref[...] = jnp.where(diagonal, nt(d_raw_b, spread_d), 0.0).astype(bf16)
    drt_ref[...] = jnp.where(diagonal_t, nt(spread_d, d_raw_b), 0.0).astype(bf16)

    t_high, t_low = two_pieces(tokens)
    grads = tn(t_high, d_high) + tn(t_high, d_low) + tn(t_low, d_high)
    for i in range(3):
        at = pltpu.roll(grads, 128 - i * depth, 1) if i else grads
        grad_qkv_ref[i] = at[0:depth, 0:depth]


def backward_kernel(
    heads,
    slices,
    aux_ref,
    mid_ref,
    cot_ref,
    feats_ref,
    sw_ref,
    sb_ref,
    mw_ref,
    dr_ref,
    drt_ref,
    dn_ref,
    temp_ref,
    _,
    dmt_ref,
    send0,
    send1,
    send2,
    send3,
    lhs,
    yt,
    grad_acc,
    small_acc,
    pack,
):
    step = pl.program_id(0)
    width = mid_ref.shape[1]
    depth = width // heads
    hm = heads * slices
    block = mid_ref.shape[0]
    top = hm + 16

    @pl.when(step == 0)
    def _():
        grad_acc[...] = jnp.zeros_like(grad_acc)
        small_acc[...] = jnp.zeros_like(small_acc)
        lhs[0:top, :] = sw_ref[...]
        lhs[top:, :] = dr_ref[...]
        yt[:, 0:hm] = drt_ref[...]
        yt[:, hm:] = sb_ref[...]

    temp = jnp.broadcast_to(temp_ref[...].astype(f32), (16, depth)).astype(bf16)
    same = (rows_of((depth, depth)) == cols_of((depth, depth))).astype(f32).astype(bf16)
    temp = nt(same, temp)[:, 0:1]
    piece = min(sub_block, block)
    pieces = [slice(i * piece, (i + 1) * piece) for i in range(block // piece)]

    def products(at):
        return nt(lhs[...], mid_ref[at, :]), nt(mw_ref[...], cot_ref[at, :])

    def per_head(at, from_mid, from_cot):
        weights_b, u_b, sums = [], [], []
        for h in range(heads):
            span = slice(h * slices, (h + 1) * slices)
            inv_tau = aux_ref[h : h + 1, at]
            logits = from_mid[span] * inv_tau
            weights = jnp.exp(logits - aux_ref[heads + h : heads + h + 1, at])
            d_weights = from_cot[span] + from_mid[top + h * slices : top + (h + 1) * slices]
            d_weights = d_weights + dn_ref[span, 0:1]
            mean = jnp.sum(weights * d_weights, axis=0, keepdims=True)
            d_logits = weights * (d_weights - mean)
            d_tau = jnp.sum(d_logits * logits, axis=0, keepdims=True)
            sums.append(-d_tau * aux_ref[2 * heads + h : 2 * heads + h + 1, at])
            weights_b.append(weights.astype(bf16))
            u_b.append((d_logits * inv_tau).astype(bf16))
        c_sum = jnp.concatenate(sums, axis=0)
        c_high = c_sum.astype(bf16).astype(f32)
        u_b.append(jnp.concatenate([c_high, c_sum - c_high], axis=0).astype(bf16))
        return jnp.concatenate(weights_b, axis=0), jnp.concatenate(u_b, axis=0), sums

    def outputs(at, weights_b, u_b, sums):
        d_mid = nn(yt[...], jnp.concatenate([weights_b, u_b[0:hm]], axis=0))
        for h in range(heads):
            span = slice(h * depth, (h + 1) * depth)
            dmt_ref[span, at] = (d_mid[span] + temp * sums[h]).astype(bf16)
        grad_acc[...] += nn(dmt_ref[:, at], feats_ref[at, :])
        small_acc[...] += nn(u_b, mid_ref[at, :])

    ready = products(pieces[0])
    for i, at in enumerate(pieces):
        current = ready
        if i + 1 < len(pieces):
            ready = products(pieces[i + 1])
        outputs(at, *per_head(at, *current))

    @pl.when(step == pl.num_programs(0) - 1)
    def _():
        grad = grad_acc[...].T
        u_part = jnp.where(same_block(hm, width, slices, depth), small_acc[0:hm, :], 0.0)
        u_part = fold_rows(u_part, heads, slices)
        c_part = small_acc[hm : hm + heads, :] + small_acc[hm + heads : hm + 2 * heads, :]
        c_part = jnp.where(same_block(heads, width, 1, depth), c_part, 0.0)
        c_part = jnp.sum(c_part, axis=0, keepdims=True)

        def fold_lanes(x):
            total = x[:, 0:128]
            for j in range(1, width // 128):
                total = total + x[:, j * 128 : (j + 1) * 128]
            shift = 64
            while shift >= depth:
                total = total + pltpu.roll(total, shift, 1)
                shift //= 2
            return total

        u_part = fold_lanes(u_part)
        c_part = fold_lanes(jnp.broadcast_to(c_part, (slices, width)))
        where_lane = cols_of((slices, 128))
        extra = jnp.where(where_lane < depth, u_part, c_part)
        rows = width // group
        more = slices // group
        for j in range(group):
            pack[j, 0:rows, :] = grad[j * rows : (j + 1) * rows]
            pack[j, rows : rows + more, 0:128] = extra[j * more : (j + 1) * more]
            pack[j, rows : rows + more, 128:] = jnp.zeros((more, width - 128), f32)
        place = group_place()
        for k, send in enumerate((send0, send1, send2, send3)):
            send[...] = pack[place ^ k]


def rows_kernel(wt_ref, dmt_ref, mw_ref, w_mid_ref, _, attended_ref, feats_grad_ref, token_ref):
    token_ref[...] = jnp.zeros_like(token_ref)
    attended_ref[...] = tn(wt_ref[...], mw_ref[...]).astype(bf16)
    feats_grad_ref[...] = lax.dot_general(
        dmt_ref[...], w_mid_ref[...], (((0,), (1,)), ((), ())), preferred_element_type=f32
    ).astype(bf16)


def grad_out_kernel(own_ref, other_ref, mixed_t_ref, grad_out_ref, whole):
    place = group_place() & 1
    rows = own_ref.shape[0]
    for k, part in enumerate((own_ref, other_ref)):
        whole[pl.ds(pl.multiple_of((place ^ k) * rows, 8), rows), :] = part[...]
    high, low = two_pieces(whole[...])
    mixed_t = mixed_t_ref[...]
    grad_out_ref[...] = nn(mixed_t, high) + nn(mixed_t, low)


def finish_kernel(depth, m0, m1, m2, m3, grad_mid_ref, slice_ref, temp_ref, extra):
    place = group_place()
    slices = slice_ref.shape[1]
    more = slices // group
    rows = m0.shape[0] - more
    for k, part in enumerate((m0, m1, m2, m3)):
        at = pl.ds(pl.multiple_of((place ^ k) * rows, 8), rows)
        grad_mid_ref[at, :] = part[0:rows, :]
        extra[pl.ds(pl.multiple_of((place ^ k) * more, 8), more), :] = part[rows:, 0:128]
    turned = extra[...].T
    slice_ref[...] = turned[0:depth, 0:slices]
    temp_ref[...] = extra[0:1, depth : 2 * depth]


def full(shape):
    zeros = (0,) * len(shape)
    return pl.BlockSpec(shape, lambda *_: zeros)


def params(mebibytes, grid=True):
    semantics = ("arbitrary",) if grid else None
    return pltpu.CompilerParams(
        dimension_semantics=semantics, vmem_limit_bytes=mebibytes * mib
    )


def cost(flops, moved, transcendentals=0):
    return pl.CostEstimate(flops=flops, bytes_accessed=moved, transcendentals=transcendentals)


def exchange(x, k, count):
    return lax.ppermute(x, "node", [(i, i ^ k) for i in range(count)])


def sum_kernel(count, *refs):
    total = refs[0][...] + refs[1][...]
    if count == 4:
        total = total + (refs[2][...] + refs[3][...])
    refs[-1][...] = total


def sum_behind(parts, *before):
    return pl.pallas_call(
        functools.partial(sum_kernel, len(parts)),
        out_shape=jax.ShapeDtypeStruct(parts[0].shape, f32),
        in_specs=[pl.BlockSpec(memory_space=pltpu.VMEM)] * len(parts)
        + [pl.BlockSpec(memory_space=pl.ANY)] * len(before),
        out_specs=pl.BlockSpec(memory_space=pltpu.VMEM),
        compiler_params=params(2, False),
        cost_estimate=cost(3 * parts[0].size, 5 * parts[0].size * 4),
    )(*parts, *before)


def scatter_group(parts, count):
    got = [parts[0]] + [exchange(parts[k], k, count) for k in range(1, group)]
    return (got[0] + got[1]) + (got[2] + got[3])


def sum_over_groups(total, count, *before):
    stride = group
    while stride < count:
        if count // stride % 4 == 0:
            got = [total] + [exchange(total, stride * j, count) for j in (1, 2, 3)]
            if before:
                total = sum_behind(got, *before)
            else:
                total = (got[0] + got[1]) + (got[2] + got[3])
            stride *= 4
        else:
            total = total + exchange(total, stride, count)
            stride *= 2
    return total


def gather_group(total, count):
    return [total] + [exchange(total, k, count) for k in range(1, group)]


def shards(count, feats, cotangent, valid, owned, w_mid, w_slice, temp_vec, w_qkv, w_out):
    rows, width = feats.shape
    depth, slices = w_slice.shape
    heads = width // depth
    hm = heads * slices
    unit = 2 * rows * width * width
    smem = pl.BlockSpec(memory_space=pltpu.SMEM)

    def blocks(size):
        return (
            (rows // size,),
            pl.BlockSpec((size, width), lambda i: (i, 0)),
            pl.BlockSpec((hm, size), lambda i: (0, i)),
            pl.BlockSpec((3 * heads, size), lambda i: (0, i)),
        )

    def like(shape, dtype):
        return jax.ShapeDtypeStruct(shape, dtype)

    temp = temp_vec.reshape(1, depth)
    half = (2 * slices + 8, 128)
    wide = (hm // 2, width)
    block = min(2048, rows)
    grid, by_rows, by_cols, aux_spec = blocks(block)
    mid, wt, aux, sw, sb, w_cat, keep, send, wc_keep, wc_send = pl.pallas_call(
        functools.partial(stats_kernel, heads, slices),
        grid=grid,
        in_specs=[
            smem,
            pl.BlockSpec((1, block), lambda i: (0, i)),
            by_rows,
            by_rows,
            full((width, width)),
            full((depth, slices)),
            full((1, depth)),
            full((width, width)),
            full((3, depth, depth)),
        ],
        out_specs=[
            by_rows,
            by_cols,
            aux_spec,
            full((hm + 16, width)),
            full((width, hm)),
            full((depth, 128)),
            full(half),
            full(half),
            full(wide),
            full(wide),
        ],
        out_shape=[
            like((rows, width), bf16),
            like((hm, rows), bf16),
            like((3 * heads, rows), f32),
            like((hm + 16, width), bf16),
            like((width, hm), bf16),
            like((depth, 128), bf16),
            like(half, f32),
            like(half, f32),
            like(wide, f32),
            like(wide, f32),
        ],
        scratch_shapes=[
            pltpu.VMEM((hm, width), f32),
            pltpu.VMEM((hm, 128), f32),
            pltpu.VMEM((hm, width), f32),
            pltpu.VMEM((2,) + half, f32),
        ],
        compiler_params=params(60),
        cost_estimate=cost(4 * unit, rows * width * 8, rows * hm),
    )(owned, valid.reshape(1, rows), feats, cotangent, w_mid, w_slice, temp, w_out, w_qkv)

    own = keep + exchange(send, 1, count)
    wc_got = exchange(wc_send, 1, count)
    own = own + exchange(own, 2, count)
    wc_sum = sum_behind([wc_keep, wc_got], own)
    wc_got = exchange(wc_sum, 2, count)
    own = sum_over_groups(own, count)
    wc_sum = sum_behind([wc_sum, wc_got], own)
    other = exchange(own, 1, count)
    strides = [stride for stride in (1 << i for i in range(2, 30)) if stride < count]
    for stride in strides[:-1]:
        wc_got = exchange(wc_sum, stride, count)
        if stride != strides[-2]:
            wc_sum = wc_sum + wc_got

    mw, mixed_t, dr, drt, dn, grad_qkv = pl.pallas_call(
        functools.partial(tokens_kernel, heads, slices),
        out_shape=[
            like((hm, width), bf16),
            like((width, hm), bf16),
            like((hm, width), bf16),
            like((width, hm), bf16),
            like((hm, 128), f32),
            like((3, depth, depth), f32),
        ],
        scratch_shapes=[pltpu.VMEM((2,) + half, f32)],
        compiler_params=params(16, False),
        cost_estimate=cost(30 * width**3, 4 * width * width * 4, hm * hm),
    )(own, other, w_cat, w_out)
    wc_sum = sum_behind([wc_sum, wc_got], mw)
    wc_got = exchange(wc_sum, strides[-1], count)

    larger = (width // group + slices // group, width)
    block = min(2048, rows)
    grid, by_rows, by_cols, aux_spec = blocks(block)
    dmt, *sends = pl.pallas_call(
        functools.partial(backward_kernel, heads, slices),
        grid=grid,
        in_specs=[
            aux_spec,
            by_rows,
            by_rows,
            by_rows,
            full((hm + 16, width)),
            full((width, hm)),
            full((hm, width)),
            full((hm, width)),
            full((width, hm)),
            full((hm, 128)),
            full((1, depth)),
            pl.BlockSpec(memory_space=pl.ANY),
        ],
        out_specs=[by_cols] + [full(larger)] * group,
        out_shape=[like((width, rows), bf16)] + [like(larger, f32)] * group,
        scratch_shapes=[
            pltpu.VMEM((2 * hm + 16, width), bf16),
            pltpu.VMEM((width, 2 * hm), bf16),
            pltpu.VMEM((width, width), f32),
            pltpu.VMEM((hm + 16, width), f32),
            pltpu.VMEM((group,) + larger, f32),
        ],
        compiler_params=params(32),
        cost_estimate=cost(8 * unit, rows * width * 8, rows * hm),
    )(aux, mid, cotangent, feats, sw, sb, mw, dr, drt, dn, temp, wc_sum)

    mid_total = scatter_group(sends, count)
    wc_sum = sum_behind([wc_sum, wc_got], sends[1])
    wc_other = exchange(wc_sum, 1, count)

    block = min(1024, rows)
    grid, by_rows, by_cols, aux_spec = blocks(block)
    attended, feats_grad, token = pl.pallas_call(
        rows_kernel,
        grid=grid,
        in_specs=[
            by_cols,
            by_cols,
            full((hm, width)),
            full((width, width)),
            pl.BlockSpec(memory_space=pl.ANY),
        ],
        out_specs=[by_rows, by_rows, full((8, 128))],
        out_shape=[like((rows, width), bf16)] * 2 + [like((8, 128), f32)],
        compiler_params=params(20),
        cost_estimate=cost(2 * unit, rows * width * 8),
    )(wt, dmt, mw, w_mid, mid_total)

    mid_total = sum_over_groups(mid_total, count, token)
    grad_w_out = pl.pallas_call(
        grad_out_kernel,
        out_shape=like((width, width), f32),
        scratch_shapes=[pltpu.VMEM((hm, width), f32)],
        compiler_params=params(8, False),
        cost_estimate=cost(4 * width**3, 3 * width * width * 4),
    )(wc_sum, wc_other, mixed_t)

    mid_parts = gather_group(mid_total, count)
    grad_w_mid, grad_w_slice, grad_temp = pl.pallas_call(
        functools.partial(finish_kernel, depth),
        out_shape=[
            like((width, width), f32),
            like((depth, slices), f32),
            like((1, depth), f32),
        ],
        scratch_shapes=[pltpu.VMEM((slices, 128), f32)],
        compiler_params=params(8, False),
        cost_estimate=cost(0, 2 * width * width * 4),
    )(*mid_parts)
    return (
        attended,
        feats_grad,
        grad_w_mid,
        grad_w_out,
        grad_w_slice,
        grad_temp.reshape(depth),
        grad_qkv,
    )


def solution(mesh):
    in_specs = (
        P(("design", "node"), None),
        P(("design", "node"), None),
        P(("design", "node")),
        P(("design", "node")),
        P(),
        P(),
        P(),
        P(),
        P(),
    )
    out_specs = (
        P(("design", "node"), None),
        P(("design", "node"), None),
        P("design", None),
        P("design", None),
        P("design", None),
        P("design"),
        P("design", None, None),
    )
    return jax.shard_map(
        functools.partial(shards, mesh.shape["node"]),
        mesh=mesh,
        in_specs=in_specs,
        out_specs=out_specs,
        check_vma=False,
    )
```

```python
import functools
import math

import jax
import jax.numpy as jnp
from jax import lax
from jax.experimental import pallas as pl
from jax.experimental.pallas import tpu as pltpu
from jax.sharding import PartitionSpec as P

f32 = jnp.float32
bf16 = jnp.bfloat16
eps_norm = 1e-05
exact = lax.Precision.HIGHEST
group = 4
sub_block = 512
mib = 1024 * 1024


def nn(a, b, precision=None):
    return lax.dot_general(
        a, b, (((1,), (0,)), ((), ())), preferred_element_type=f32, precision=precision
    )


def nt(a, b, precision=None):
    return lax.dot_general(
        a, b, (((1,), (1,)), ((), ())), preferred_element_type=f32, precision=precision
    )


def tn(a, b, precision=None):
    return lax.dot_general(
        a, b, (((0,), (0,)), ((), ())), preferred_element_type=f32, precision=precision
    )


def rows_of(shape):
    return lax.broadcasted_iota(jnp.int32, shape, 0)


def cols_of(shape):
    return lax.broadcasted_iota(jnp.int32, shape, 1)


def spread_matrix(width, small):
    shape = (width, small)
    return jnp.where(rows_of(shape) % small == cols_of(shape), 1.0, 0.0).astype(bf16)


def same_block(rows, cols, row_size, col_size):
    shape = (rows, cols)
    return rows_of(shape) // row_size == cols_of(shape) // col_size


def two_pieces(x):
    high = x.astype(bf16)
    return high, (x - high.astype(f32)).astype(bf16)


def fold_rows(x, heads, size):
    total = x[0:size]
    for h in range(1, heads):
        total = total + x[h * size : (h + 1) * size]
    return total


def group_place():
    return lax.axis_index("node") % group


def stats_kernel(
    heads,
    slices,
    owned_ref,
    valid_ref,
    feats_ref,
    cot_ref,
    w_mid_ref,
    w_slice_ref,
    temp_ref,
    w_out_ref,
    w_qkv_ref,
    mid_ref,
    wt_ref,
    aux_ref,
    sw_ref,
    sb_ref,
    w_cat_ref,
    keep_ref,
    send_ref,
    wc_keep_ref,
    wc_send_ref,
    raw_acc,
    norm_acc,
    wc_acc,
    pack,
):
    step = pl.program_id(0)
    width = w_mid_ref.shape[0]
    depth = width // heads
    hm = heads * slices
    block = feats_ref.shape[0]

    @pl.when(step == 0)
    def _():
        spread_d = spread_matrix(width, depth)
        spread_m = spread_matrix(hm, slices)
        w_slice = w_slice_ref[...]
        half = nt(spread_m, w_slice).astype(bf16)
        full = nt(half, spread_d)
        sw_ref[0:hm, :] = jnp.where(same_block(hm, width, slices, depth), full, 0.0).astype(bf16)
        half = nn(spread_d, w_slice).astype(bf16)
        full = nt(half, spread_m)
        sb_ref[...] = jnp.where(same_block(width, hm, depth, slices), full, 0.0).astype(bf16)
        temp = jnp.broadcast_to(temp_ref[...].astype(f32), (16, depth)).astype(bf16)
        full = nt(temp, spread_d)
        sw_ref[hm : hm + 16, :] = jnp.where(same_block(16, width, 1, depth), full, 0.0).astype(
            bf16
        )
        w_cat = jnp.zeros((depth, 128), f32)
        for i in range(3):
            place_at = jnp.where(rows_of((depth, 128)) + i * depth == cols_of((depth, 128)), 1.0, 0.0)
            w_cat = w_cat + nn(w_qkv_ref[i], place_at.astype(bf16))
        w_cat_ref[...] = w_cat.astype(bf16)
        raw_acc[...] = jnp.zeros_like(raw_acc)
        norm_acc[...] = jnp.zeros_like(norm_acc)
        wc_acc[...] = jnp.zeros_like(wc_acc)

    piece = min(sub_block, block)
    base = step * block
    owned = owned_ref[0]

    def products(i):
        at = slice(i * piece, (i + 1) * piece)
        mid = nn(feats_ref[at, :], w_mid_ref[...]).astype(bf16)
        mid_ref[pl.ds(pl.multiple_of(base + i * piece, piece), piece), :] = mid
        return mid, nt(sw_ref[...], mid)

    def statistics(i, mid, scores):
        at = slice(i * piece, (i + 1) * piece)
        span_all = pl.ds(pl.multiple_of(base + i * piece, piece), piece)
        zsum = scores[hm : hm + heads]
        small = jnp.exp(-jnp.abs(zsum))
        inv_tau = 1.0 / (0.5 + (jnp.maximum(zsum, 0.0) + jnp.log(1.0 + small)))
        sig = jnp.where(zsum >= 0.0, 1.0, small) / (1.0 + small)
        position = base + i * piece + cols_of((1, piece))
        live = (valid_ref[:, at] > 0) & (position < owned)
        live_f = live.astype(f32)
        rounded, sums, logs = [], [], []
        for h in range(heads):
            span = slice(h * slices, (h + 1) * slices)
            logits = scores[span] * inv_tau[h : h + 1]
            peak = jnp.max(logits, axis=0, keepdims=True)
            expo = jnp.exp(logits - peak)
            total = jnp.sum(expo, axis=0, keepdims=True)
            weights = expo * (live_f / total)
            rounded.append(weights.astype(bf16))
            lanes = weights[:, 0:128]
            for c in range(1, piece // 128):
                lanes = lanes + weights[:, c * 128 : (c + 1) * 128]
            sums.append(lanes)
            logs.append(jnp.where(live, peak + jnp.log(total), jnp.inf))
        wt = jnp.concatenate(rounded, axis=0)
        wt_ref[:, span_all] = wt
        norm_acc[...] += jnp.concatenate(sums, axis=0)
        aux_ref[:, span_all] = jnp.concatenate([inv_tau] + logs + [sig * inv_tau], axis=0)
        raw_acc[...] += nn(wt, mid)
        wc_acc[...] += nn(wt, cot_ref[at, :])

    ready = products(0)
    for i in range(block // piece):
        current = ready
        if (i + 1) * piece < block:
            ready = products(i + 1)
        statistics(i, *current)

    @pl.when(step == pl.num_programs(0) - 1)
    def _():
        diagonal = same_block(hm, width, slices, depth)
        raw = fold_rows(jnp.where(diagonal, raw_acc[...], 0.0), heads, slices)
        high, low = two_pieces(wc_acc[...])
        w_out = w_out_ref[...]
        mixed = nt(high, w_out) + nt(low, w_out)
        mixed = fold_rows(jnp.where(diagonal, mixed, 0.0), heads, slices)
        norm = jnp.sum(norm_acc[...].T, axis=0, keepdims=True)
        first = rows_of((8, 128)) == 0
        for j in range(2):
            part = slice(j * 128, (j + 1) * 128)
            pack[j, 0:slices, :] = raw[:, part]
            pack[j, slices : 2 * slices, :] = mixed[:, part]
            pack[j, 2 * slices :, :] = jnp.where(first, norm[:, part], 0.0)
        place = group_place()
        keep_ref[...] = pack[place & 1]
        send_ref[...] = pack[(place & 1) ^ 1]
        rows = hm // 2
        for k, out in enumerate((wc_keep_ref, wc_send_ref)):
            out[...] = wc_acc[pl.ds(pl.multiple_of(((place & 1) ^ k) * rows, 8), rows), :]


def lanes_at(x, lane, *where):
    place = cols_of(x.shape) // lane
    total = jnp.zeros_like(x)
    for value, at, to in where:
        shift = (to - at) * lane % 128
        moved = pltpu.roll(value, shift, 1) if shift else value
        total = jnp.where(place == to, moved, total)
    return total.astype(bf16)


def split(x):
    high = x.astype(bf16).astype(f32)
    return high, x - high


def tokens_kernel(
    heads,
    slices,
    own_ref,
    got_ref,
    w_cat_ref,
    w_out_ref,
    mw_ref,
    mixed_t_ref,
    dr_ref,
    drt_ref,
    dn_ref,
    grad_qkv_ref,
    pack,
):
    width = w_out_ref.shape[0]
    depth = width // heads
    hm = heads * slices
    place = group_place() & 1
    pack[place] = own_ref[...]
    pack[place ^ 1] = got_ref[...]
    per = 128 // depth

    def compact(first):
        pieces = []
        for h in range(heads):
            x = pack[h // per, first : first + slices, :]
            shift = (h % per) * depth
            pieces.append(pltpu.roll(x, 128 - shift, 1) if shift else x)
        x = jnp.concatenate(pieces, axis=0)
        return jnp.where(cols_of(x.shape) < depth, x, 0.0)

    raw = compact(0)
    d_mixed = compact(slices)
    norm = jnp.concatenate([pack[j, 2 * slices :, :].T[:, 0:1] for j in range(2)], axis=0)
    inverse = 1.0 / (norm + eps_norm)
    tokens = raw * inverse
    w_cat = w_cat_ref[...]

    t_high, rest = split(tokens)
    t_low, rest = split(rest)
    left = lanes_at(tokens, depth, (t_high, 0, 0), (t_low, 0, 1), (rest, 0, 2))
    blank = jnp.zeros((128 - 3 * depth, 128), bf16)
    qkv = nn(left, jnp.concatenate([w_cat, w_cat, w_cat, blank], axis=0))
    high, low = split(qkv)
    q_left = lanes_at(qkv, depth, (high, 0, 0), (high, 0, 1), (low, 0, 2))
    k_right = lanes_at(qkv, depth, (high, 1, 0), (low, 1, 1), (high, 1, 2))
    v_right = lanes_at(qkv, depth, (high, 2, 0), (low, 2, 1), (high, 2, 2))
    q_pair = lanes_at(qkv, depth, (high, 0, 0), (low, 0, 1))
    k_pair = lanes_at(qkv, depth, (high, 1, 0), (low, 1, 1))
    v_pair = lanes_at(qkv, depth, (high, 2, 0), (low, 2, 1))
    g_high, g_low = split(d_mixed)
    g_left = lanes_at(qkv, depth, (g_high, 0, 0), (g_high, 0, 1), (g_low, 0, 2))
    g_pair = lanes_at(qkv, depth, (g_high, 0, 0), (g_low, 0, 1))

    def times_pair(dot, x, pair):
        x_high, x_low = two_pieces(x)
        both = dot(x_high, pair)
        low_part = dot(x_low, pair)
        total = both + pltpu.roll(both, 128 - depth, 1) + low_part
        return jnp.where(cols_of(total.shape) < depth, total, 0.0)

    blocks = same_block(hm, hm, slices, slices)
    scale = 1.0 / math.sqrt(depth)
    scores = jnp.where(blocks, nt(q_left, k_right) * scale, -jnp.inf)
    expo = jnp.exp(scores - jnp.max(scores, axis=1, keepdims=True))
    probs = expo * (1.0 / jnp.sum(expo, axis=1, keepdims=True))
    mixed_b = times_pair(nn, probs, v_pair).astype(bf16)

    spread_d = jnp.where(
        (rows_of((width, 128)) % depth == cols_of((width, 128))), 1.0, 0.0
    ).astype(bf16)
    diagonal = same_block(hm, width, slices, depth)
    diagonal_t = same_block(width, hm, depth, slices)
    mixed_block = jnp.where(diagonal, nt(mixed_b, spread_d), 0.0).astype(bf16)
    mw_ref[...] = nn(mixed_block, w_out_ref[...]).astype(bf16)
    mixed_t_ref[...] = jnp.where(diagonal_t, nt(spread_d, mixed_b), 0.0).astype(bf16)

    d_probs = nt(g_left, v_right)
    d_v = times_pair(tn, probs, g_pair)
    d_scores = probs * (d_probs - jnp.sum(probs * d_probs, axis=1, keepdims=True)) * scale
    d_q = times_pair(nn, d_scores, k_pair)
    d_k = times_pair(tn, d_scores, q_pair)
    d_qkv = d_q + pltpu.roll(d_k, depth, 1) + pltpu.roll(d_v, 2 * depth, 1)
    d_high, d_low = two_pieces(d_qkv)
    d_tokens = nt(d_high, w_cat) + nt(d_low, w_cat)
    raw = raw[:, 0:depth]
    d_raw_b = (d_tokens * inverse).astype(bf16)
    d_norm = -jnp.sum(d_tokens * raw, axis=1, keepdims=True) * inverse * inverse
    dn_ref[...] = jnp.broadcast_to(d_norm, dn_ref.shape)
    spread_d = spread_matrix(width, depth)
    dr_ref[...] = jnp.where(diagonal, nt(d_raw_b, spread_d), 0.0).astype(bf16)
    drt_ref[...] = jnp.where(diagonal_t, nt(spread_d, d_raw_b), 0.0).astype(bf16)

    t_high, t_low = two_pieces(tokens)
    grads = tn(t_high, d_high) + tn(t_high, d_low) + tn(t_low, d_high)
    for i in range(3):
        at = pltpu.roll(grads, 128 - i * depth, 1) if i else grads
        grad_qkv_ref[i] = at[0:depth, 0:depth]


def backward_kernel(
    heads,
    slices,
    aux_ref,
    mid_ref,
    cot_ref,
    feats_ref,
    sw_ref,
    sb_ref,
    mw_ref,
    dr_ref,
    drt_ref,
    dn_ref,
    temp_ref,
    _,
    dmt_ref,
    send0,
    send1,
    send2,
    send3,
    lhs,
    yt,
    grad_acc,
    small_acc,
    pack,
):
    step = pl.program_id(0)
    width = mid_ref.shape[1]
    depth = width // heads
    hm = heads * slices
    block = feats_ref.shape[0]
    top = hm + 16

    @pl.when(step == 0)
    def _():
        grad_acc[...] = jnp.zeros_like(grad_acc)
        small_acc[...] = jnp.zeros_like(small_acc)
        lhs[0:top, :] = sw_ref[...]
        lhs[top:, :] = dr_ref[...]
        yt[:, 0:hm] = drt_ref[...]
        yt[:, hm:] = sb_ref[...]

    temp = jnp.broadcast_to(temp_ref[...].astype(f32), (16, depth)).astype(bf16)
    same = (rows_of((depth, depth)) == cols_of((depth, depth))).astype(f32).astype(bf16)
    temp = nt(same, temp)[:, 0:1]
    piece = min(sub_block, block)
    pieces = [slice(i * piece, (i + 1) * piece) for i in range(block // piece)]

    def whole(at):
        return pl.ds(pl.multiple_of(step * block + at.start, piece), piece)

    def products(at):
        return nt(lhs[...], mid_ref[whole(at), :]), nt(mw_ref[...], cot_ref[at, :])

    def per_head(at, from_mid, from_cot):
        weights_b, u_b, sums = [], [], []
        aux = aux_ref[:, whole(at)]
        for h in range(heads):
            span = slice(h * slices, (h + 1) * slices)
            inv_tau = aux[h : h + 1]
            logits = from_mid[span] * inv_tau
            weights = jnp.exp(logits - aux[heads + h : heads + h + 1])
            d_weights = from_cot[span] + from_mid[top + h * slices : top + (h + 1) * slices]
            d_weights = d_weights + dn_ref[span, 0:1]
            mean = jnp.sum(weights * d_weights, axis=0, keepdims=True)
            d_logits = weights * (d_weights - mean)
            d_tau = jnp.sum(d_logits * logits, axis=0, keepdims=True)
            sums.append(-d_tau * aux[2 * heads + h : 2 * heads + h + 1])
            weights_b.append(weights.astype(bf16))
            u_b.append((d_logits * inv_tau).astype(bf16))
        c_sum = jnp.concatenate(sums, axis=0)
        c_high = c_sum.astype(bf16).astype(f32)
        u_b.append(jnp.concatenate([c_high, c_sum - c_high], axis=0).astype(bf16))
        return jnp.concatenate(weights_b, axis=0), jnp.concatenate(u_b, axis=0), sums

    def outputs(at, weights_b, u_b, sums):
        d_mid = nn(yt[...], jnp.concatenate([weights_b, u_b[0:hm]], axis=0))
        d_mid = [
            (d_mid[h * depth : (h + 1) * depth] + temp * sums[h]).astype(bf16)
            for h in range(heads)
        ]
        d_mid = jnp.concatenate(d_mid, axis=0)
        dmt_ref[:, whole(at)] = d_mid
        grad_acc[...] += nn(d_mid, feats_ref[at, :])
        small_acc[...] += nn(u_b, mid_ref[whole(at), :])

    ready = products(pieces[0])
    for i, at in enumerate(pieces):
        current = ready
        if i + 1 < len(pieces):
            ready = products(pieces[i + 1])
        outputs(at, *per_head(at, *current))

    @pl.when(step == pl.num_programs(0) - 1)
    def _():
        grad = grad_acc[...].T
        u_part = jnp.where(same_block(hm, width, slices, depth), small_acc[0:hm, :], 0.0)
        u_part = fold_rows(u_part, heads, slices)
        c_part = small_acc[hm : hm + heads, :] + small_acc[hm + heads : hm + 2 * heads, :]
        c_part = jnp.where(same_block(heads, width, 1, depth), c_part, 0.0)
        c_part = jnp.sum(c_part, axis=0, keepdims=True)

        def fold_lanes(x):
            total = x[:, 0:128]
            for j in range(1, width // 128):
                total = total + x[:, j * 128 : (j + 1) * 128]
            shift = 64
            while shift >= depth:
                total = total + pltpu.roll(total, shift, 1)
                shift //= 2
            return total

        u_part = fold_lanes(u_part)
        c_part = fold_lanes(jnp.broadcast_to(c_part, (slices, width)))
        where_lane = cols_of((slices, 128))
        extra = jnp.where(where_lane < depth, u_part, c_part)
        rows = width // group
        more = slices // group
        for j in range(group):
            pack[j, 0:rows, :] = grad[j * rows : (j + 1) * rows]
            pack[j, rows : rows + more, 0:128] = extra[j * more : (j + 1) * more]
            pack[j, rows : rows + more, 128:] = jnp.zeros((more, width - 128), f32)
        place = group_place()
        for k, send in enumerate((send0, send1, send2, send3)):
            send[...] = pack[place ^ k]


def rows_kernel(wt_ref, dmt_ref, mw_ref, w_mid_ref, _, attended_ref, feats_grad_ref, token_ref):
    block = attended_ref.shape[0]
    at = pl.ds(pl.multiple_of(pl.program_id(0) * block, block), block)
    token_ref[...] = jnp.zeros_like(token_ref)
    attended_ref[...] = tn(wt_ref[:, at], mw_ref[...]).astype(bf16)
    feats_grad_ref[...] = lax.dot_general(
        dmt_ref[:, at], w_mid_ref[...], (((0,), (1,)), ((), ())), preferred_element_type=f32
    ).astype(bf16)


def grad_out_kernel(own_ref, other_ref, mixed_t_ref, grad_out_ref, token_ref, whole):
    token_ref[...] = jnp.zeros_like(token_ref)
    place = group_place() & 1
    rows = own_ref.shape[0]
    for k, part in enumerate((own_ref, other_ref)):
        whole[pl.ds(pl.multiple_of((place ^ k) * rows, 8), rows), :] = part[...]
    high, low = two_pieces(whole[...])
    mixed_t = mixed_t_ref[...]
    grad_out_ref[...] = nn(mixed_t, high) + nn(mixed_t, low)


def finish_kernel(depth, m0, m1, m2, m3, grad_mid_ref, slice_ref, temp_ref, extra):
    place = group_place()
    slices = slice_ref.shape[1]
    more = slices // group
    rows = m0.shape[0] - more
    for k, part in enumerate((m0, m1, m2, m3)):
        at = pl.ds(pl.multiple_of((place ^ k) * rows, 8), rows)
        grad_mid_ref[at, :] = part[0:rows, :]
        extra[pl.ds(pl.multiple_of((place ^ k) * more, 8), more), :] = part[rows:, 0:128]
    turned = extra[...].T
    slice_ref[...] = turned[0:depth, 0:slices]
    temp_ref[...] = extra[0:1, depth : 2 * depth]


def full(shape):
    zeros = (0,) * len(shape)
    return pl.BlockSpec(shape, lambda *_: zeros)


def params(mebibytes, grid=True):
    semantics = ("arbitrary",) if grid else None
    return pltpu.CompilerParams(
        dimension_semantics=semantics, vmem_limit_bytes=mebibytes * mib
    )


def cost(flops, moved, transcendentals=0):
    return pl.CostEstimate(flops=flops, bytes_accessed=moved, transcendentals=transcendentals)


def exchange(x, k, count):
    return lax.ppermute(x, "node", [(i, i ^ k) for i in range(count)])


def sum_kernel(count, *refs):
    total = refs[0][...] + refs[count - 1][...]
    if count == 4:
        total = total + (refs[1][...] + refs[2][...])
    refs[-1][...] = total


def sum_behind(parts, *before):
    return pl.pallas_call(
        functools.partial(sum_kernel, len(parts)),
        out_shape=jax.ShapeDtypeStruct(parts[0].shape, f32),
        in_specs=[pl.BlockSpec(memory_space=pltpu.VMEM)] * len(parts)
        + [pl.BlockSpec(memory_space=pl.ANY)] * len(before),
        out_specs=pl.BlockSpec(memory_space=pltpu.VMEM),
        compiler_params=params(2, False),
        cost_estimate=cost(3 * parts[0].size, 5 * parts[0].size * 4),
    )(*parts, *before)


def scatter_group(parts, count):
    got = [parts[0]] + [exchange(parts[k], k, count) for k in range(1, group)]
    return (got[0] + got[1]) + (got[2] + got[3])


def sum_stage(total, stride, others, count, *before):
    got = [total] + [exchange(total, stride * j, count) for j in range(others, 0, -1)]
    if before:
        return sum_behind(got, *before)
    if others == 1:
        return got[0] + got[1]
    return (got[0] + got[3]) + (got[1] + got[2])


def sum_over_groups(total, stride, count, *before):
    while stride < count:
        others = 3 if count // stride % 4 == 0 else 1
        total = sum_stage(total, stride, others, count, *before)
        stride *= others + 1
    return total


def gather_group(total, count):
    return [total] + [exchange(total, k, count) for k in range(1, group)]


def shards(count, feats, cotangent, valid, owned, w_mid, w_slice, temp_vec, w_qkv, w_out):
    rows, width = feats.shape
    depth, slices = w_slice.shape
    heads = width // depth
    hm = heads * slices
    unit = 2 * rows * width * width
    smem = pl.BlockSpec(memory_space=pltpu.SMEM)

    def blocks(size):
        return (rows // size,), pl.BlockSpec((size, width), lambda i: (i, 0))

    def like(shape, dtype):
        return jax.ShapeDtypeStruct(shape, dtype)

    def far(x):
        return pltpu.with_memory_space_constraint(x, pltpu.HBM)

    near = pltpu.VMEM
    whole = pl.BlockSpec(memory_space=pltpu.VMEM)

    temp = temp_vec.reshape(1, depth)
    half = (2 * slices + 8, 128)
    wide = (hm // 2, width)
    block = min(2048, rows)
    grid, by_rows = blocks(block)
    mid, wt, aux, sw, sb, w_cat, keep, send, wc_keep, wc_send = pl.pallas_call(
        functools.partial(stats_kernel, heads, slices),
        grid=grid,
        in_specs=[
            smem,
            pl.BlockSpec((1, block), lambda i: (0, i)),
            by_rows,
            by_rows,
            full((width, width)),
            full((depth, slices)),
            full((1, depth)),
            full((width, width)),
            full((3, depth, depth)),
        ],
        out_specs=[whole] * 10,
        out_shape=[
            near((rows, width), bf16),
            near((hm, rows), bf16),
            near((3 * heads, rows), f32),
            near((hm + 16, width), bf16),
            near((width, hm), bf16),
            near((depth, 128), bf16),
            near(half, f32),
            near(half, f32),
            near(wide, f32),
            near(wide, f32),
        ],
        scratch_shapes=[
            pltpu.VMEM((hm, width), f32),
            pltpu.VMEM((hm, 128), f32),
            pltpu.VMEM((hm, width), f32),
            pltpu.VMEM((2,) + half, f32),
        ],
        compiler_params=params(32),
        cost_estimate=cost(4 * unit, rows * width * 8, rows * hm),
    )(owned, *map(far, (valid.reshape(1, rows), feats, cotangent, w_mid, w_slice, temp, w_out, w_qkv)))

    own = keep + exchange(send, 1, count)
    wc_got = exchange(wc_send, 1, count)
    own = sum_stage(own, 2, 3, count)
    wc_sum = sum_behind([wc_keep, wc_got], own)
    wc_got = exchange(wc_sum, 2, count)
    own = sum_over_groups(own, 8, count)
    wc_sum = sum_behind([wc_sum, wc_got], own)
    other = exchange(own, 1, count)
    strides = [stride for stride in (1 << i for i in range(2, 30)) if stride < count]
    for stride in strides[:-1]:
        wc_got = exchange(wc_sum, stride, count)
        if stride != strides[-2]:
            wc_sum = wc_sum + wc_got

    mw, mixed_t, dr, drt, dn, grad_qkv = pl.pallas_call(
        functools.partial(tokens_kernel, heads, slices),
        out_shape=[
            near((hm, width), bf16),
            near((width, hm), bf16),
            near((hm, width), bf16),
            near((width, hm), bf16),
            near((hm, 128), f32),
            like((3, depth, depth), f32),
        ],
        scratch_shapes=[pltpu.VMEM((2,) + half, f32)],
        compiler_params=params(16, False),
        cost_estimate=cost(30 * width**3, 4 * width * width * 4, hm * hm),
    )(own, other, w_cat, w_out)
    wc_sum = sum_behind([wc_sum, wc_got], mw)
    wc_got = exchange(wc_sum, strides[-1], count)

    larger = (width // group + slices // group, width)
    block = min(2048, rows)
    grid, by_rows = blocks(block)
    dmt, *sends = pl.pallas_call(
        functools.partial(backward_kernel, heads, slices),
        grid=grid,
        in_specs=[whole, whole, by_rows, by_rows]
        + [whole] * 7
        + [pl.BlockSpec(memory_space=pl.ANY)],
        out_specs=[whole] * (1 + group),
        out_shape=[near((width, rows), bf16)] + [near(larger, f32)] * group,
        scratch_shapes=[
            pltpu.VMEM((2 * hm + 16, width), bf16),
            pltpu.VMEM((width, 2 * hm), bf16),
            pltpu.VMEM((width, width), f32),
            pltpu.VMEM((hm + 16, width), f32),
            pltpu.VMEM((group,) + larger, f32),
        ],
        compiler_params=params(32),
        cost_estimate=cost(8 * unit, rows * width * 8, rows * hm),
    )(aux, mid, cotangent, feats, sw, sb, mw, dr, drt, dn, temp, wc_sum)

    mid_total = scatter_group(sends, count)
    wc_sum = sum_behind([wc_sum, wc_got], sends[1])
    wc_other = exchange(wc_sum, 1, count)

    block = min(1024, rows)
    grid, by_rows = blocks(block)
    attended, feats_grad, token = pl.pallas_call(
        rows_kernel,
        grid=grid,
        in_specs=[
            whole,
            whole,
            whole,
            full((width, width)),
            pl.BlockSpec(memory_space=pl.ANY),
        ],
        out_specs=[by_rows, by_rows, full((8, 128))],
        out_shape=[like((rows, width), bf16)] * 2 + [like((8, 128), f32)],
        compiler_params=params(20),
        cost_estimate=cost(2 * unit, rows * width * 8),
    )(wt, dmt, mw, w_mid, mid_total)

    grad_w_out, token_out = pl.pallas_call(
        grad_out_kernel,
        out_shape=[like((width, width), f32), like((8, 128), f32)],
        scratch_shapes=[pltpu.VMEM((hm, width), f32)],
        compiler_params=params(8, False),
        cost_estimate=cost(4 * width**3, 3 * width * width * 4),
    )(wc_sum, wc_other, mixed_t)

    mid_total = sum_over_groups(mid_total, group, count, token, token_out)
    mid_parts = gather_group(mid_total, count)
    grad_w_mid, grad_w_slice, grad_temp = pl.pallas_call(
        functools.partial(finish_kernel, depth),
        out_shape=[
            like((width, width), f32),
            like((depth, slices), f32),
            like((1, depth), f32),
        ],
        scratch_shapes=[pltpu.VMEM((slices, 128), f32)],
        compiler_params=params(8, False),
        cost_estimate=cost(0, 2 * width * width * 4),
    )(*mid_parts)
    return (
        attended,
        feats_grad,
        grad_w_mid,
        grad_w_out,
        grad_w_slice,
        grad_temp.reshape(depth),
        grad_qkv,
    )


def solution(mesh):
    in_specs = (
        P(("design", "node"), None),
        P(("design", "node"), None),
        P(("design", "node")),
        P(("design", "node")),
        P(),
        P(),
        P(),
        P(),
        P(),
    )
    out_specs = (
        P(("design", "node"), None),
        P(("design", "node"), None),
        P("design", None),
        P("design", None),
        P("design", None),
        P("design"),
        P("design", None, None),
    )
    return jax.shard_map(
        functools.partial(shards, mesh.shape["node"]),
        mesh=mesh,
        in_specs=in_specs,
        out_specs=out_specs,
        check_vma=False,
    )
```

```python
import functools
import math

import jax
import jax.numpy as jnp
from jax import lax
from jax.experimental import pallas as pl
from jax.experimental.pallas import tpu as pltpu
from jax.sharding import PartitionSpec as P

f32 = jnp.float32
bf16 = jnp.bfloat16
eps_norm = 1e-05
exact = lax.Precision.HIGHEST
group = 4
sub_block = 512
mib = 1024 * 1024


def nn(a, b, precision=None):
    return lax.dot_general(
        a, b, (((1,), (0,)), ((), ())), preferred_element_type=f32, precision=precision
    )


def nt(a, b, precision=None):
    return lax.dot_general(
        a, b, (((1,), (1,)), ((), ())), preferred_element_type=f32, precision=precision
    )


def tn(a, b, precision=None):
    return lax.dot_general(
        a, b, (((0,), (0,)), ((), ())), preferred_element_type=f32, precision=precision
    )


def rows_of(shape):
    return lax.broadcasted_iota(jnp.int32, shape, 0)


def cols_of(shape):
    return lax.broadcasted_iota(jnp.int32, shape, 1)


def spread_matrix(width, small):
    shape = (width, small)
    return jnp.where(rows_of(shape) % small == cols_of(shape), 1.0, 0.0).astype(bf16)


def same_block(rows, cols, row_size, col_size):
    shape = (rows, cols)
    return rows_of(shape) // row_size == cols_of(shape) // col_size


def two_pieces(x):
    high = x.astype(bf16)
    return high, (x - high.astype(f32)).astype(bf16)


def fold_rows(x, heads, size):
    total = x[0:size]
    for h in range(1, heads):
        total = total + x[h * size : (h + 1) * size]
    return total


def group_place():
    return lax.axis_index("node") % group


def stats_kernel(
    heads,
    slices,
    owned_ref,
    temp_ref,
    valid_far,
    feats_far,
    cot_far,
    w_mid_far,
    w_slice_far,
    w_out_far,
    w_qkv_far,
    mid_ref,
    wt_ref,
    aux_ref,
    sw_ref,
    sb_ref,
    w_cat_ref,
    keep_ref,
    send_ref,
    wc_keep_ref,
    wc_send_ref,
    feats_ref,
    cot_ref,
    valid_ref,
    w_mid_ref,
    w_slice_ref,
    w_out_ref,
    w_qkv_ref,
    raw_acc,
    norm_acc,
    wc_acc,
    pack,
    sems,
):
    width = w_mid_ref.shape[0]
    depth = width // heads
    hm = heads * slices
    rows = feats_ref.shape[0]
    piece = min(sub_block, rows)
    count = rows // piece
    small = [
        pltpu.make_async_copy(source, target, sems.at[i])
        for i, (source, target) in enumerate(
            (
                (w_slice_far, w_slice_ref),
                (w_qkv_far, w_qkv_ref),
                (w_mid_far, w_mid_ref),
                (valid_far, valid_ref),
                (w_out_far, w_out_ref),
            )
        )
    ]
    feats_in, cot_in = [], []
    for i in range(count):
        at = pl.ds(i * piece, piece)
        for j, (source, target, into) in enumerate(
            ((feats_far, feats_ref, feats_in), (cot_far, cot_ref, cot_in))
        ):
            sem = sems.at[len(small) + 2 * i + j]
            into.append(pltpu.make_async_copy(source.at[at, :], target.at[at, :], sem))
    for copy in small[:3] + feats_in[:1] + small[3:] + cot_in[:1]:
        copy.start()
    for i in range(1, count):
        feats_in[i].start()
        cot_in[i].start()

    raw_acc[...] = jnp.zeros_like(raw_acc)
    norm_acc[...] = jnp.zeros_like(norm_acc)
    wc_acc[...] = jnp.zeros_like(wc_acc)
    spread_d = spread_matrix(width, depth)
    spread_m = spread_matrix(hm, slices)
    temp = jnp.broadcast_to(temp_ref[...].astype(f32), (16, depth)).astype(bf16)
    small[0].wait()
    w_slice = w_slice_ref[...]
    half = nt(spread_m, w_slice).astype(bf16)
    full = nt(half, spread_d)
    sw_ref[0:hm, :] = jnp.where(same_block(hm, width, slices, depth), full, 0.0).astype(bf16)
    half = nn(spread_d, w_slice).astype(bf16)
    full = nt(half, spread_m)
    sb_ref[...] = jnp.where(same_block(width, hm, depth, slices), full, 0.0).astype(bf16)
    full = nt(temp, spread_d)
    sw_ref[hm : hm + 16, :] = jnp.where(same_block(16, width, 1, depth), full, 0.0).astype(bf16)
    small[1].wait()
    w_cat = jnp.zeros((depth, 128), f32)
    for i in range(3):
        place_at = jnp.where(rows_of((depth, 128)) + i * depth == cols_of((depth, 128)), 1.0, 0.0)
        w_cat = w_cat + nn(w_qkv_ref[i], place_at.astype(bf16))
    w_cat_ref[...] = w_cat.astype(bf16)
    small[2].wait()
    small[3].wait()
    small[4].wait()
    owned = owned_ref[0]

    def products(i):
        at = slice(i * piece, (i + 1) * piece)
        feats_in[i].wait()
        mid = nn(feats_ref[at, :], w_mid_ref[...]).astype(bf16)
        mid_ref[at, :] = mid
        return mid, nt(sw_ref[...], mid)

    def statistics(i, mid, scores):
        at = slice(i * piece, (i + 1) * piece)
        zsum = scores[hm : hm + heads]
        small = jnp.exp(-jnp.abs(zsum))
        inv_tau = 1.0 / (0.5 + (jnp.maximum(zsum, 0.0) + jnp.log(1.0 + small)))
        sig = jnp.where(zsum >= 0.0, 1.0, small) / (1.0 + small)
        position = i * piece + cols_of((1, piece))
        live = (valid_ref[:, at] > 0) & (position < owned)
        live_f = live.astype(f32)
        rounded, sums, logs = [], [], []
        for h in range(heads):
            span = slice(h * slices, (h + 1) * slices)
            logits = scores[span] * inv_tau[h : h + 1]
            peak = jnp.max(logits, axis=0, keepdims=True)
            expo = jnp.exp(logits - peak)
            total = jnp.sum(expo, axis=0, keepdims=True)
            weights = expo * (live_f / total)
            rounded.append(weights.astype(bf16))
            lanes = weights[:, 0:128]
            for c in range(1, piece // 128):
                lanes = lanes + weights[:, c * 128 : (c + 1) * 128]
            sums.append(lanes)
            logs.append(jnp.where(live, peak + jnp.log(total), jnp.inf))
        wt = jnp.concatenate(rounded, axis=0)
        wt_ref[:, at] = wt
        norm_acc[...] += jnp.concatenate(sums, axis=0)
        aux_ref[:, at] = jnp.concatenate([inv_tau] + logs + [sig * inv_tau], axis=0)
        raw_acc[...] += nn(wt, mid)
        cot_in[i].wait()
        wc_acc[...] += nn(wt, cot_ref[at, :])

    ready = products(0)
    for i in range(count):
        current = ready
        if i + 1 < count:
            ready = products(i + 1)
        statistics(i, *current)

    diagonal = same_block(hm, width, slices, depth)
    raw = fold_rows(jnp.where(diagonal, raw_acc[...], 0.0), heads, slices)
    high, low = two_pieces(wc_acc[...])
    w_out = w_out_ref[...]
    mixed = nt(high, w_out) + nt(low, w_out)
    mixed = fold_rows(jnp.where(diagonal, mixed, 0.0), heads, slices)
    norm = jnp.sum(norm_acc[...].T, axis=0, keepdims=True)
    first = rows_of((8, 128)) == 0
    for j in range(2):
        part = slice(j * 128, (j + 1) * 128)
        pack[j, 0:slices, :] = raw[:, part]
        pack[j, slices : 2 * slices, :] = mixed[:, part]
        pack[j, 2 * slices :, :] = jnp.where(first, norm[:, part], 0.0)
    place = group_place()
    keep_ref[...] = pack[place & 1]
    send_ref[...] = pack[(place & 1) ^ 1]
    rows = hm // 2
    for k, out in enumerate((wc_keep_ref, wc_send_ref)):
        out[...] = wc_acc[pl.ds(pl.multiple_of(((place & 1) ^ k) * rows, 8), rows), :]


def lanes_at(x, lane, *where):
    place = cols_of(x.shape) // lane
    total = jnp.zeros_like(x)
    for value, at, to in where:
        shift = (to - at) * lane % 128
        moved = pltpu.roll(value, shift, 1) if shift else value
        total = jnp.where(place == to, moved, total)
    return total.astype(bf16)


def split(x):
    high = x.astype(bf16).astype(f32)
    return high, x - high


def tokens_kernel(
    heads,
    slices,
    own_ref,
    got_ref,
    w_cat_ref,
    w_out_ref,
    mw_ref,
    mixed_t_ref,
    dr_ref,
    drt_ref,
    dn_ref,
    grad_qkv_ref,
    pack,
):
    width = w_out_ref.shape[0]
    depth = width // heads
    hm = heads * slices
    place = group_place() & 1
    pack[place] = own_ref[...]
    pack[place ^ 1] = got_ref[...]
    per = 128 // depth

    def compact(first):
        pieces = []
        for h in range(heads):
            x = pack[h // per, first : first + slices, :]
            shift = (h % per) * depth
            pieces.append(pltpu.roll(x, 128 - shift, 1) if shift else x)
        x = jnp.concatenate(pieces, axis=0)
        return jnp.where(cols_of(x.shape) < depth, x, 0.0)

    raw = compact(0)
    d_mixed = compact(slices)
    norm = jnp.concatenate([pack[j, 2 * slices :, :].T[:, 0:1] for j in range(2)], axis=0)
    inverse = 1.0 / (norm + eps_norm)
    tokens = raw * inverse
    w_cat = w_cat_ref[...]

    t_high, rest = split(tokens)
    t_low, rest = split(rest)
    left = lanes_at(tokens, depth, (t_high, 0, 0), (t_low, 0, 1), (rest, 0, 2))
    blank = jnp.zeros((128 - 3 * depth, 128), bf16)
    qkv = nn(left, jnp.concatenate([w_cat, w_cat, w_cat, blank], axis=0))
    high, low = split(qkv)
    q_left = lanes_at(qkv, depth, (high, 0, 0), (high, 0, 1), (low, 0, 2))
    k_right = lanes_at(qkv, depth, (high, 1, 0), (low, 1, 1), (high, 1, 2))
    v_right = lanes_at(qkv, depth, (high, 2, 0), (low, 2, 1), (high, 2, 2))
    q_pair = lanes_at(qkv, depth, (high, 0, 0), (low, 0, 1))
    k_pair = lanes_at(qkv, depth, (high, 1, 0), (low, 1, 1))
    v_pair = lanes_at(qkv, depth, (high, 2, 0), (low, 2, 1))
    g_high, g_low = split(d_mixed)
    g_left = lanes_at(qkv, depth, (g_high, 0, 0), (g_high, 0, 1), (g_low, 0, 2))
    g_pair = lanes_at(qkv, depth, (g_high, 0, 0), (g_low, 0, 1))

    def times_pair(dot, x, pair):
        x_high, x_low = two_pieces(x)
        both = dot(x_high, pair)
        low_part = dot(x_low, pair)
        total = both + pltpu.roll(both, 128 - depth, 1) + low_part
        return jnp.where(cols_of(total.shape) < depth, total, 0.0)

    blocks = same_block(hm, hm, slices, slices)
    scale = 1.0 / math.sqrt(depth)
    scores = jnp.where(blocks, nt(q_left, k_right) * scale, -jnp.inf)
    expo = jnp.exp(scores - jnp.max(scores, axis=1, keepdims=True))
    probs = expo * (1.0 / jnp.sum(expo, axis=1, keepdims=True))
    mixed_b = times_pair(nn, probs, v_pair).astype(bf16)

    spread_d = jnp.where(
        (rows_of((width, 128)) % depth == cols_of((width, 128))), 1.0, 0.0
    ).astype(bf16)
    diagonal = same_block(hm, width, slices, depth)
    diagonal_t = same_block(width, hm, depth, slices)
    mixed_block = jnp.where(diagonal, nt(mixed_b, spread_d), 0.0).astype(bf16)
    mw_ref[...] = nn(mixed_block, w_out_ref[...]).astype(bf16)
    mixed_t_ref[...] = jnp.where(diagonal_t, nt(spread_d, mixed_b), 0.0).astype(bf16)

    d_probs = nt(g_left, v_right)
    d_v = times_pair(tn, probs, g_pair)
    d_scores = probs * (d_probs - jnp.sum(probs * d_probs, axis=1, keepdims=True)) * scale
    d_q = times_pair(nn, d_scores, k_pair)
    d_k = times_pair(tn, d_scores, q_pair)
    d_qkv = d_q + pltpu.roll(d_k, depth, 1) + pltpu.roll(d_v, 2 * depth, 1)
    d_high, d_low = two_pieces(d_qkv)
    d_tokens = nt(d_high, w_cat) + nt(d_low, w_cat)
    raw = raw[:, 0:depth]
    d_raw_b = (d_tokens * inverse).astype(bf16)
    d_norm = -jnp.sum(d_tokens * raw, axis=1, keepdims=True) * inverse * inverse
    dn_ref[...] = jnp.broadcast_to(d_norm, dn_ref.shape)
    spread_d = spread_matrix(width, depth)
    dr_ref[...] = jnp.where(diagonal, nt(d_raw_b, spread_d), 0.0).astype(bf16)
    drt_ref[...] = jnp.where(diagonal_t, nt(spread_d, d_raw_b), 0.0).astype(bf16)

    t_high, t_low = two_pieces(tokens)
    grads = tn(t_high, d_high) + tn(t_high, d_low) + tn(t_low, d_high)
    for i in range(3):
        at = pltpu.roll(grads, 128 - i * depth, 1) if i else grads
        grad_qkv_ref[i] = at[0:depth, 0:depth]


def backward_kernel(
    heads,
    slices,
    aux_ref,
    mid_ref,
    cot_ref,
    feats_ref,
    sw_ref,
    sb_ref,
    mw_ref,
    dr_ref,
    drt_ref,
    dn_ref,
    temp_ref,
    _,
    dmt_ref,
    send0,
    send1,
    send2,
    send3,
    lhs,
    yt,
    grad_acc,
    small_acc,
    pack,
):
    width = mid_ref.shape[1]
    depth = width // heads
    hm = heads * slices
    block = feats_ref.shape[0]
    top = hm + 16

    grad_acc[...] = jnp.zeros_like(grad_acc)
    small_acc[...] = jnp.zeros_like(small_acc)
    lhs[0:top, :] = sw_ref[...]
    lhs[top:, :] = dr_ref[...]
    yt[:, 0:hm] = drt_ref[...]
    yt[:, hm:] = sb_ref[...]

    temp = jnp.broadcast_to(temp_ref[...].astype(f32), (16, depth)).astype(bf16)
    same = (rows_of((depth, depth)) == cols_of((depth, depth))).astype(f32).astype(bf16)
    temp = nt(same, temp)[:, 0:1]
    piece = min(sub_block, block)
    pieces = [slice(i * piece, (i + 1) * piece) for i in range(block // piece)]

    def products(at):
        return nt(lhs[...], mid_ref[at, :]), nt(mw_ref[...], cot_ref[at, :])

    def per_head(at, from_mid, from_cot):
        weights_b, u_b, sums = [], [], []
        aux = aux_ref[:, at]
        for h in range(heads):
            span = slice(h * slices, (h + 1) * slices)
            inv_tau = aux[h : h + 1]
            logits = from_mid[span] * inv_tau
            weights = jnp.exp(logits - aux[heads + h : heads + h + 1])
            d_weights = from_cot[span] + from_mid[top + h * slices : top + (h + 1) * slices]
            d_weights = d_weights + dn_ref[span, 0:1]
            mean = jnp.sum(weights * d_weights, axis=0, keepdims=True)
            d_logits = weights * (d_weights - mean)
            d_tau = jnp.sum(d_logits * logits, axis=0, keepdims=True)
            sums.append(-d_tau * aux[2 * heads + h : 2 * heads + h + 1])
            weights_b.append(weights.astype(bf16))
            u_b.append((d_logits * inv_tau).astype(bf16))
        c_sum = jnp.concatenate(sums, axis=0)
        c_high = c_sum.astype(bf16).astype(f32)
        u_b.append(jnp.concatenate([c_high, c_sum - c_high], axis=0).astype(bf16))
        return jnp.concatenate(weights_b, axis=0), jnp.concatenate(u_b, axis=0), sums

    def outputs(at, weights_b, u_b, sums):
        d_mid = nn(yt[...], jnp.concatenate([weights_b, u_b[0:hm]], axis=0))
        d_mid = [
            (d_mid[h * depth : (h + 1) * depth] + temp * sums[h]).astype(bf16)
            for h in range(heads)
        ]
        d_mid = jnp.concatenate(d_mid, axis=0)
        dmt_ref[:, at] = d_mid
        grad_acc[...] += nn(d_mid, feats_ref[at, :])
        small_acc[...] += nn(u_b, mid_ref[at, :])

    ready = products(pieces[0])
    for i, at in enumerate(pieces):
        current = ready
        if i + 1 < len(pieces):
            ready = products(pieces[i + 1])
        outputs(at, *per_head(at, *current))

    grad = grad_acc[...].T
    u_part = jnp.where(same_block(hm, width, slices, depth), small_acc[0:hm, :], 0.0)
    u_part = fold_rows(u_part, heads, slices)
    c_part = small_acc[hm : hm + heads, :] + small_acc[hm + heads : hm + 2 * heads, :]
    c_part = jnp.where(same_block(heads, width, 1, depth), c_part, 0.0)
    c_part = jnp.sum(c_part, axis=0, keepdims=True)

    def fold_lanes(x):
        total = x[:, 0:128]
        for j in range(1, width // 128):
            total = total + x[:, j * 128 : (j + 1) * 128]
        shift = 64
        while shift >= depth:
            total = total + pltpu.roll(total, shift, 1)
            shift //= 2
        return total

    u_part = fold_lanes(u_part)
    c_part = fold_lanes(jnp.broadcast_to(c_part, (slices, width)))
    where_lane = cols_of((slices, 128))
    extra = jnp.where(where_lane < depth, u_part, c_part)
    rows = width // group
    more = slices // group
    for j in range(group):
        pack[j, 0:rows, :] = grad[j * rows : (j + 1) * rows]
        pack[j, rows : rows + more, 0:128] = extra[j * more : (j + 1) * more]
        pack[j, rows : rows + more, 128:] = jnp.zeros((more, width - 128), f32)
    place = group_place()
    for k, send in enumerate((send0, send1, send2, send3)):
        send[...] = pack[place ^ k]


def rows_kernel(wt_ref, dmt_ref, mw_ref, w_mid_ref, _, attended_ref, feats_grad_ref, token_ref):
    block = attended_ref.shape[0]
    at = pl.ds(pl.multiple_of(pl.program_id(0) * block, block), block)
    token_ref[...] = jnp.zeros_like(token_ref)
    attended_ref[...] = tn(wt_ref[:, at], mw_ref[...]).astype(bf16)
    feats_grad_ref[...] = lax.dot_general(
        dmt_ref[:, at], w_mid_ref[...], (((0,), (1,)), ((), ())), preferred_element_type=f32
    ).astype(bf16)


def grad_out_kernel(own_ref, other_ref, mixed_t_ref, grad_out_ref, token_ref, whole):
    token_ref[...] = jnp.zeros_like(token_ref)
    place = group_place() & 1
    rows = own_ref.shape[0]
    for k, part in enumerate((own_ref, other_ref)):
        whole[pl.ds(pl.multiple_of((place ^ k) * rows, 8), rows), :] = part[...]
    high, low = two_pieces(whole[...])
    mixed_t = mixed_t_ref[...]
    grad_out_ref[...] = nn(mixed_t, high) + nn(mixed_t, low)


def finish_kernel(depth, m0, m1, m2, m3, grad_mid_ref, slice_ref, temp_ref, extra):
    place = group_place()
    slices = slice_ref.shape[1]
    more = slices // group
    rows = m0.shape[0] - more
    for k, part in enumerate((m0, m1, m2, m3)):
        at = pl.ds(pl.multiple_of((place ^ k) * rows, 8), rows)
        grad_mid_ref[at, :] = part[0:rows, :]
        extra[pl.ds(pl.multiple_of((place ^ k) * more, 8), more), :] = part[rows:, 0:128]
    turned = extra[...].T
    slice_ref[...] = turned[0:depth, 0:slices]
    temp_ref[...] = extra[0:1, depth : 2 * depth]


def full(shape):
    zeros = (0,) * len(shape)
    return pl.BlockSpec(shape, lambda *_: zeros)


def params(mebibytes, grid=True):
    semantics = ("arbitrary",) if grid else None
    return pltpu.CompilerParams(
        dimension_semantics=semantics, vmem_limit_bytes=mebibytes * mib
    )


def cost(flops, moved, transcendentals=0):
    return pl.CostEstimate(flops=flops, bytes_accessed=moved, transcendentals=transcendentals)


def exchange(x, k, count):
    return lax.ppermute(x, "node", [(i, i ^ k) for i in range(count)])


def sum_kernel(count, *refs):
    total = refs[0][...] + refs[count - 1][...]
    if count == 4:
        total = total + (refs[1][...] + refs[2][...])
    refs[-1][...] = total


def sum_behind(parts, *before):
    return pl.pallas_call(
        functools.partial(sum_kernel, len(parts)),
        out_shape=jax.ShapeDtypeStruct(parts[0].shape, f32),
        in_specs=[pl.BlockSpec(memory_space=pltpu.VMEM)] * len(parts)
        + [pl.BlockSpec(memory_space=pl.ANY)] * len(before),
        out_specs=pl.BlockSpec(memory_space=pltpu.VMEM),
        compiler_params=params(2, False),
        cost_estimate=cost(3 * parts[0].size, 5 * parts[0].size * 4),
    )(*parts, *before)


def scatter_group(parts, count):
    got = [parts[0]] + [exchange(parts[k], k, count) for k in range(1, group)]
    return (got[0] + got[1]) + (got[2] + got[3])


def sum_stage(total, stride, others, count, *before):
    got = [total] + [exchange(total, stride * j, count) for j in range(others, 0, -1)]
    if before:
        return sum_behind(got, *before)
    if others == 1:
        return got[0] + got[1]
    return (got[0] + got[3]) + (got[1] + got[2])


def sum_over_groups(total, stride, count, *before):
    while stride < count:
        others = 3 if count // stride % 4 == 0 else 1
        total = sum_stage(total, stride, others, count, *before)
        stride *= others + 1
    return total


def gather_group(total, count):
    return [total] + [exchange(total, k, count) for k in range(1, group)]


def shards(count, feats, cotangent, valid, owned, w_mid, w_slice, temp_vec, w_qkv, w_out):
    rows, width = feats.shape
    depth, slices = w_slice.shape
    heads = width // depth
    hm = heads * slices
    unit = 2 * rows * width * width
    smem = pl.BlockSpec(memory_space=pltpu.SMEM)

    def blocks(size):
        return (rows // size,), pl.BlockSpec((size, width), lambda i: (i, 0))

    def like(shape, dtype):
        return jax.ShapeDtypeStruct(shape, dtype)

    def far(x):
        return pltpu.with_memory_space_constraint(x, pltpu.HBM)

    near = pltpu.VMEM
    whole = pl.BlockSpec(memory_space=pltpu.VMEM)

    temp = temp_vec.reshape(1, depth)
    half = (2 * slices + 8, 128)
    wide = (hm // 2, width)
    inputs = (valid.reshape(1, rows), feats, cotangent, w_mid, w_slice, w_out, w_qkv)
    pieces = rows // min(sub_block, rows)
    (
        mid,
        wt,
        aux,
        sw,
        sb,
        w_cat,
        keep,
        send,
        wc_keep,
        wc_send,
        feats_near,
        cot_near,
    ) = pl.pallas_call(
        functools.partial(stats_kernel, heads, slices),
        in_specs=[smem, whole] + [pl.BlockSpec(memory_space=pltpu.HBM)] * len(inputs),
        out_specs=[whole] * 12,
        out_shape=[
            near((rows, width), bf16),
            near((hm, rows), bf16),
            near((3 * heads, rows), f32),
            near((hm + 16, width), bf16),
            near((width, hm), bf16),
            near((depth, 128), bf16),
            near(half, f32),
            near(half, f32),
            near(wide, f32),
            near(wide, f32),
            near((rows, width), bf16),
            near((rows, width), bf16),
        ],
        scratch_shapes=[
            pltpu.VMEM((1, rows), jnp.int32),
            pltpu.VMEM((width, width), bf16),
            pltpu.VMEM((depth, slices), bf16),
            pltpu.VMEM((width, width), bf16),
            pltpu.VMEM((3, depth, depth), bf16),
            pltpu.VMEM((hm, width), f32),
            pltpu.VMEM((hm, 128), f32),
            pltpu.VMEM((hm, width), f32),
            pltpu.VMEM((2,) + half, f32),
            pltpu.SemaphoreType.DMA((5 + 2 * pieces,)),
        ],
        compiler_params=params(24, False),
        cost_estimate=cost(4 * unit, rows * width * 8, rows * hm),
    )(owned, far(temp), *map(far, inputs))

    own = keep + exchange(send, 1, count)
    wc_got = exchange(wc_send, 1, count)
    own = sum_stage(own, 2, 3, count)
    own = sum_over_groups(own, 8, count)
    other = exchange(own, 1, count)
    wc_sum = sum_behind([wc_keep, wc_got], own)
    wc_got = exchange(wc_sum, 2, count)

    mw, mixed_t, dr, drt, dn, grad_qkv = pl.pallas_call(
        functools.partial(tokens_kernel, heads, slices),
        out_shape=[
            near((hm, width), bf16),
            near((width, hm), bf16),
            near((hm, width), bf16),
            near((width, hm), bf16),
            near((hm, 128), f32),
            like((3, depth, depth), f32),
        ],
        scratch_shapes=[pltpu.VMEM((2,) + half, f32)],
        compiler_params=params(16, False),
        cost_estimate=cost(30 * width**3, 4 * width * width * 4, hm * hm),
    )(own, other, w_cat, w_out)
    wc_sum = sum_behind([wc_sum, wc_got], mw)
    stride = 4
    while stride < count // 2:
        if stride > 4:
            wc_sum = wc_sum + wc_got
        wc_got = exchange(wc_sum, stride, count)
        stride *= 2

    larger = (width // group + slices // group, width)
    dmt, *sends = pl.pallas_call(
        functools.partial(backward_kernel, heads, slices),
        in_specs=[whole] * 11 + [pl.BlockSpec(memory_space=pl.ANY)],
        out_specs=[whole] * (1 + group),
        out_shape=[near((width, rows), bf16)] + [near(larger, f32)] * group,
        scratch_shapes=[
            pltpu.VMEM((2 * hm + 16, width), bf16),
            pltpu.VMEM((width, 2 * hm), bf16),
            pltpu.VMEM((width, width), f32),
            pltpu.VMEM((hm + 16, width), f32),
            pltpu.VMEM((group,) + larger, f32),
        ],
        compiler_params=params(24, False),
        cost_estimate=cost(8 * unit, rows * width * 8, rows * hm),
    )(aux, mid, cot_near, feats_near, sw, sb, mw, dr, drt, dn, temp, wc_sum)

    mid_total = scatter_group(sends, count)
    wc_sum = sum_behind([wc_sum, wc_got], sends[1])
    wc_got = exchange(wc_sum, count // 2, count)
    wc_sum = sum_behind([wc_sum, wc_got], mid_total)
    wc_other = exchange(wc_sum, 1, count)

    block = min(1024, rows)
    grid, by_rows = blocks(block)
    attended, feats_grad, token = pl.pallas_call(
        rows_kernel,
        grid=grid,
        in_specs=[
            whole,
            whole,
            whole,
            full((width, width)),
            pl.BlockSpec(memory_space=pl.ANY),
        ],
        out_specs=[by_rows, by_rows, full((8, 128))],
        out_shape=[like((rows, width), bf16)] * 2 + [like((8, 128), f32)],
        compiler_params=params(20),
        cost_estimate=cost(2 * unit, rows * width * 8),
    )(wt, dmt, mw, w_mid, mid_total)

    grad_w_out, token_out = pl.pallas_call(
        grad_out_kernel,
        out_shape=[like((width, width), f32), like((8, 128), f32)],
        scratch_shapes=[pltpu.VMEM((hm, width), f32)],
        compiler_params=params(8, False),
        cost_estimate=cost(4 * width**3, 3 * width * width * 4),
    )(wc_sum, wc_other, mixed_t)

    mid_total = sum_over_groups(mid_total, group, count, token, token_out)
    mid_parts = gather_group(mid_total, count)
    grad_w_mid, grad_w_slice, grad_temp = pl.pallas_call(
        functools.partial(finish_kernel, depth),
        out_shape=[
            like((width, width), f32),
            like((depth, slices), f32),
            like((1, depth), f32),
        ],
        scratch_shapes=[pltpu.VMEM((slices, 128), f32)],
        compiler_params=params(8, False),
        cost_estimate=cost(0, 2 * width * width * 4),
    )(*mid_parts)
    return (
        attended,
        feats_grad,
        grad_w_mid,
        grad_w_out,
        grad_w_slice,
        grad_temp.reshape(depth),
        grad_qkv,
    )


def solution(mesh):
    in_specs = (
        P(("design", "node"), None),
        P(("design", "node"), None),
        P(("design", "node")),
        P(("design", "node")),
        P(),
        P(),
        P(),
        P(),
        P(),
    )
    out_specs = (
        P(("design", "node"), None),
        P(("design", "node"), None),
        P("design", None),
        P("design", None),
        P("design", None),
        P("design"),
        P("design", None, None),
    )
    return jax.shard_map(
        functools.partial(shards, mesh.shape["node"]),
        mesh=mesh,
        in_specs=in_specs,
        out_specs=out_specs,
        check_vma=False,
    )
```

```python
import functools
import math

import jax
import jax.numpy as jnp
from jax import lax
from jax.experimental import pallas as pl
from jax.experimental.pallas import tpu as pltpu
from jax.sharding import PartitionSpec as P

f32 = jnp.float32
bf16 = jnp.bfloat16
eps_norm = 1e-05
exact = lax.Precision.HIGHEST
group = 4
sub_block = 512
mib = 1024 * 1024


def nn(a, b, precision=None):
    return lax.dot_general(
        a, b, (((1,), (0,)), ((), ())), preferred_element_type=f32, precision=precision
    )


def nt(a, b, precision=None):
    return lax.dot_general(
        a, b, (((1,), (1,)), ((), ())), preferred_element_type=f32, precision=precision
    )


def tn(a, b, precision=None):
    return lax.dot_general(
        a, b, (((0,), (0,)), ((), ())), preferred_element_type=f32, precision=precision
    )


def log2(size):
    return size.bit_length() - 1


def rows_of(shape):
    return lax.broadcasted_iota(jnp.int32, shape, 0)


def cols_of(shape):
    return lax.broadcasted_iota(jnp.int32, shape, 1)


def spread_matrix(width, small):
    shape = (width, small)
    return jnp.where((rows_of(shape) & (small - 1)) == cols_of(shape), 1.0, 0.0).astype(bf16)


def same_block(rows, cols, row_size, col_size):
    shape = (rows, cols)
    return rows_of(shape) >> log2(row_size) == cols_of(shape) >> log2(col_size)


def two_pieces(x):
    high = x.astype(bf16)
    return high, (x - high.astype(f32)).astype(bf16)


def fold_rows(x, heads, size):
    total = x[0:size]
    for h in range(1, heads):
        total = total + x[h * size : (h + 1) * size]
    return total


def group_place():
    return lax.axis_index("node") % group


def stats_kernel(
    heads,
    slices,
    owned_ref,
    temp_ref,
    valid_far,
    feats_far,
    cot_far,
    w_mid_far,
    w_slice_far,
    w_out_far,
    w_qkv_far,
    mid_ref,
    wt_ref,
    aux_ref,
    sw_ref,
    sb_ref,
    w_cat_ref,
    keep_ref,
    send_ref,
    wc_keep_ref,
    wc_send_ref,
    feats_ref,
    cot_ref,
    valid_ref,
    w_mid_ref,
    w_slice_ref,
    w_out_ref,
    w_qkv_ref,
    raw_acc,
    norm_acc,
    wc_acc,
    pack,
    sems,
):
    width = w_mid_ref.shape[0]
    depth = width // heads
    hm = heads * slices
    rows = feats_ref.shape[0]
    piece = min(sub_block, rows)
    count = rows // piece
    small = [
        pltpu.make_async_copy(source, target, sems.at[i])
        for i, (source, target) in enumerate(
            (
                (w_slice_far, w_slice_ref),
                (w_qkv_far, w_qkv_ref),
                (w_mid_far, w_mid_ref),
                (valid_far, valid_ref),
                (w_out_far, w_out_ref),
            )
        )
    ]
    feats_in, cot_in = [], []
    for i in range(count):
        at = pl.ds(i * piece, piece)
        for j, (source, target, into) in enumerate(
            ((feats_far, feats_ref, feats_in), (cot_far, cot_ref, cot_in))
        ):
            sem = sems.at[len(small) + 2 * i + j]
            into.append(pltpu.make_async_copy(source.at[at, :], target.at[at, :], sem))
    for copy in small[:3] + feats_in[:1] + small[3:] + cot_in[:1]:
        copy.start()
    for i in range(1, count):
        feats_in[i].start()
        cot_in[i].start()

    raw_acc[...] = jnp.zeros_like(raw_acc)
    norm_acc[...] = jnp.zeros_like(norm_acc)
    wc_acc[...] = jnp.zeros_like(wc_acc)
    spread_d = spread_matrix(width, depth)
    spread_m = spread_matrix(hm, slices)
    temp = jnp.broadcast_to(temp_ref[...].astype(f32), (16, depth)).astype(bf16)
    small[0].wait()
    w_slice = w_slice_ref[...]
    half = nt(spread_m, w_slice).astype(bf16)
    full = nt(half, spread_d)
    sw_ref[0:hm, :] = jnp.where(same_block(hm, width, slices, depth), full, 0.0).astype(bf16)
    half = nn(spread_d, w_slice).astype(bf16)
    full = nt(half, spread_m)
    sb_ref[...] = jnp.where(same_block(width, hm, depth, slices), full, 0.0).astype(bf16)
    full = nt(temp, spread_d)
    sw_ref[hm : hm + 16, :] = jnp.where(same_block(16, width, 1, depth), full, 0.0).astype(bf16)
    small[1].wait()
    w_cat = jnp.zeros((depth, 128), f32)
    for i in range(3):
        place_at = jnp.where(rows_of((depth, 128)) + i * depth == cols_of((depth, 128)), 1.0, 0.0)
        w_cat = w_cat + nn(w_qkv_ref[i], place_at.astype(bf16))
    w_cat_ref[...] = w_cat.astype(bf16)
    small[2].wait()
    small[3].wait()
    small[4].wait()
    owned = owned_ref[0]

    def products(i):
        at = slice(i * piece, (i + 1) * piece)
        mid = nn(feats_ref[at, :], w_mid_ref[...]).astype(bf16)
        mid_ref[at, :] = mid
        return mid, nt(sw_ref[...], mid)

    def statistics(i, mid, scores):
        at = slice(i * piece, (i + 1) * piece)
        zsum = scores[hm : hm + heads]
        small = jnp.exp(-jnp.abs(zsum))
        inv_tau = 1.0 / (0.5 + (jnp.maximum(zsum, 0.0) + jnp.log(1.0 + small)))
        sig = jnp.where(zsum >= 0.0, 1.0, small) / (1.0 + small)
        position = i * piece + cols_of((1, piece))
        live = (valid_ref[:, at] > 0) & (position < owned)
        live_f = live.astype(f32)
        rounded, sums, logs = [], [], []
        for h in range(heads):
            span = slice(h * slices, (h + 1) * slices)
            logits = scores[span] * inv_tau[h : h + 1]
            peak = jnp.max(logits, axis=0, keepdims=True)
            expo = jnp.exp(logits - peak)
            total = jnp.sum(expo, axis=0, keepdims=True)
            weights = expo * (live_f / total)
            rounded.append(weights.astype(bf16))
            lanes = weights[:, 0:128]
            for c in range(1, piece // 128):
                lanes = lanes + weights[:, c * 128 : (c + 1) * 128]
            sums.append(lanes)
            logs.append(jnp.where(live, peak + jnp.log(total), jnp.inf))
        wt = jnp.concatenate(rounded, axis=0)
        wt_ref[:, at] = wt
        norm_acc[...] += jnp.concatenate(sums, axis=0)
        aux_ref[:, at] = jnp.concatenate([inv_tau] + logs + [sig * inv_tau], axis=0)
        raw_acc[...] += nn(wt, mid)
        wc_acc[...] += nn(wt, cot_ref[at, :])

    feats_in[0].wait()
    ready = products(0)
    for i in range(count):
        current = ready
        cot_in[i].wait()
        if i + 1 < count:
            feats_in[i + 1].wait()
            ready = products(i + 1)
        statistics(i, *current)

    diagonal = same_block(hm, width, slices, depth)
    raw = fold_rows(jnp.where(diagonal, raw_acc[...], 0.0), heads, slices)
    high, low = two_pieces(wc_acc[...])
    w_out = w_out_ref[...]
    mixed = nt(high, w_out) + nt(low, w_out)
    mixed = fold_rows(jnp.where(diagonal, mixed, 0.0), heads, slices)
    norm = jnp.sum(norm_acc[...].T, axis=0, keepdims=True)
    first = rows_of((8, 128)) == 0
    for j in range(2):
        part = slice(j * 128, (j + 1) * 128)
        pack[j, 0:slices, :] = raw[:, part]
        pack[j, slices : 2 * slices, :] = mixed[:, part]
        pack[j, 2 * slices :, :] = jnp.where(first, norm[:, part], 0.0)
    place = group_place()
    keep_ref[...] = pack[place & 1]
    send_ref[...] = pack[(place & 1) ^ 1]
    rows = hm // 2
    for k, out in enumerate((wc_keep_ref, wc_send_ref)):
        out[...] = wc_acc[pl.ds(pl.multiple_of(((place & 1) ^ k) * rows, 8), rows), :]


def lanes_at(x, lane, *where):
    place = cols_of(x.shape) >> log2(lane)
    total = jnp.zeros_like(x)
    for value, at, to in where:
        shift = (to - at) * lane % 128
        moved = pltpu.roll(value, shift, 1) if shift else value
        total = jnp.where(place == to, moved, total)
    return total.astype(bf16)


def split(x):
    high = x.astype(bf16).astype(f32)
    return high, x - high


def tokens_kernel(
    heads,
    slices,
    own_ref,
    got_ref,
    w_cat_ref,
    w_out_ref,
    mw_ref,
    mixed_t_ref,
    dr_ref,
    drt_ref,
    dn_ref,
    grad_qkv_ref,
    pack,
):
    width = w_out_ref.shape[0]
    depth = width // heads
    hm = heads * slices
    place = group_place() & 1
    pack[place] = own_ref[...]
    pack[place ^ 1] = got_ref[...]
    per = 128 // depth

    def compact(first):
        pieces = []
        for h in range(heads):
            x = pack[h // per, first : first + slices, :]
            shift = (h % per) * depth
            pieces.append(pltpu.roll(x, 128 - shift, 1) if shift else x)
        x = jnp.concatenate(pieces, axis=0)
        return jnp.where(cols_of(x.shape) < depth, x, 0.0)

    raw = compact(0)
    d_mixed = compact(slices)
    norm = jnp.concatenate([pack[j, 2 * slices :, :].T[:, 0:1] for j in range(2)], axis=0)
    inverse = 1.0 / (norm + eps_norm)
    tokens = raw * inverse
    w_cat = w_cat_ref[...]

    t_high, rest = split(tokens)
    t_low, rest = split(rest)
    left = lanes_at(tokens, depth, (t_high, 0, 0), (t_low, 0, 1), (rest, 0, 2))
    blank = jnp.zeros((128 - 3 * depth, 128), bf16)
    qkv = nn(left, jnp.concatenate([w_cat, w_cat, w_cat, blank], axis=0))
    high, low = split(qkv)
    q_left = lanes_at(qkv, depth, (high, 0, 0), (high, 0, 1), (low, 0, 2))
    k_right = lanes_at(qkv, depth, (high, 1, 0), (low, 1, 1), (high, 1, 2))
    v_right = lanes_at(qkv, depth, (high, 2, 0), (low, 2, 1), (high, 2, 2))
    q_pair = lanes_at(qkv, depth, (high, 0, 0), (low, 0, 1))
    k_pair = lanes_at(qkv, depth, (high, 1, 0), (low, 1, 1))
    v_pair = lanes_at(qkv, depth, (high, 2, 0), (low, 2, 1))
    g_high, g_low = split(d_mixed)
    g_left = lanes_at(qkv, depth, (g_high, 0, 0), (g_high, 0, 1), (g_low, 0, 2))
    g_pair = lanes_at(qkv, depth, (g_high, 0, 0), (g_low, 0, 1))

    def times_pair(dot, x, pair):
        x_high, x_low = two_pieces(x)
        both = dot(x_high, pair)
        low_part = dot(x_low, pair)
        total = both + pltpu.roll(both, 128 - depth, 1) + low_part
        return jnp.where(cols_of(total.shape) < depth, total, 0.0)

    blocks = same_block(hm, hm, slices, slices)
    scale = 1.0 / math.sqrt(depth)
    scores = jnp.where(blocks, nt(q_left, k_right) * scale, -jnp.inf)
    expo = jnp.exp(scores - jnp.max(scores, axis=1, keepdims=True))
    probs = expo * (1.0 / jnp.sum(expo, axis=1, keepdims=True))
    mixed_b = times_pair(nn, probs, v_pair).astype(bf16)

    spread_d = jnp.where(
        (rows_of((width, 128)) & (depth - 1)) == cols_of((width, 128)), 1.0, 0.0
    ).astype(bf16)
    diagonal = same_block(hm, width, slices, depth)
    diagonal_t = same_block(width, hm, depth, slices)
    mixed_block = jnp.where(diagonal, nt(mixed_b, spread_d), 0.0).astype(bf16)
    mw_ref[...] = nn(mixed_block, w_out_ref[...]).astype(bf16)
    mixed_t_ref[...] = jnp.where(diagonal_t, nt(spread_d, mixed_b), 0.0).astype(bf16)

    d_probs = nt(g_left, v_right)
    d_v = times_pair(tn, probs, g_pair)
    d_scores = probs * (d_probs - jnp.sum(probs * d_probs, axis=1, keepdims=True)) * scale
    d_q = times_pair(nn, d_scores, k_pair)
    d_k = times_pair(tn, d_scores, q_pair)
    d_qkv = d_q + pltpu.roll(d_k, depth, 1) + pltpu.roll(d_v, 2 * depth, 1)
    d_high, d_low = two_pieces(d_qkv)
    d_tokens = nt(d_high, w_cat) + nt(d_low, w_cat)
    raw = raw[:, 0:depth]
    d_raw_b = (d_tokens * inverse).astype(bf16)
    d_norm = -jnp.sum(d_tokens * raw, axis=1, keepdims=True) * inverse * inverse
    dn_ref[...] = jnp.broadcast_to(d_norm, dn_ref.shape)
    spread_d = spread_matrix(width, depth)
    dr_ref[...] = jnp.where(diagonal, nt(d_raw_b, spread_d), 0.0).astype(bf16)
    drt_ref[...] = jnp.where(diagonal_t, nt(spread_d, d_raw_b), 0.0).astype(bf16)

    t_high, t_low = two_pieces(tokens)
    grads = tn(t_high, d_high) + tn(t_high, d_low) + tn(t_low, d_high)
    for i in range(3):
        at = pltpu.roll(grads, 128 - i * depth, 1) if i else grads
        grad_qkv_ref[i] = at[0:depth, 0:depth]


def backward_kernel(
    heads,
    slices,
    aux_ref,
    mid_ref,
    cot_ref,
    feats_ref,
    sw_ref,
    sb_ref,
    mw_ref,
    dr_ref,
    drt_ref,
    dn_ref,
    temp_ref,
    _,
    dmt_ref,
    send0,
    send1,
    send2,
    send3,
    lhs,
    yt,
    grad_acc,
    small_acc,
    pack,
):
    width = mid_ref.shape[1]
    depth = width // heads
    hm = heads * slices
    block = feats_ref.shape[0]
    top = hm + 16

    grad_acc[...] = jnp.zeros_like(grad_acc)
    small_acc[...] = jnp.zeros_like(small_acc)
    lhs[0:top, :] = sw_ref[...]
    lhs[top:, :] = dr_ref[...]
    yt[:, 0:hm] = drt_ref[...]
    yt[:, hm:] = sb_ref[...]

    temp = jnp.broadcast_to(temp_ref[...].astype(f32), (16, depth)).astype(bf16)
    same = (rows_of((depth, depth)) == cols_of((depth, depth))).astype(f32).astype(bf16)
    temp = nt(same, temp)[:, 0:1]
    piece = min(2 * sub_block, block)
    pieces = [slice(i * piece, (i + 1) * piece) for i in range(block // piece)]

    def products(at):
        return nt(lhs[...], mid_ref[at, :]), nt(mw_ref[...], cot_ref[at, :])

    def per_head(at, from_mid, from_cot):
        weights_b, u_b, sums = [], [], []
        aux = aux_ref[:, at]
        for h in range(heads):
            span = slice(h * slices, (h + 1) * slices)
            inv_tau = aux[h : h + 1]
            logits = from_mid[span] * inv_tau
            weights = jnp.exp(logits - aux[heads + h : heads + h + 1])
            d_weights = from_cot[span] + from_mid[top + h * slices : top + (h + 1) * slices]
            d_weights = d_weights + dn_ref[span, 0:1]
            mean = jnp.sum(weights * d_weights, axis=0, keepdims=True)
            d_logits = weights * (d_weights - mean)
            d_tau = jnp.sum(d_logits * logits, axis=0, keepdims=True)
            sums.append(-d_tau * aux[2 * heads + h : 2 * heads + h + 1])
            weights_b.append(weights.astype(bf16))
            u_b.append((d_logits * inv_tau).astype(bf16))
        c_sum = jnp.concatenate(sums, axis=0)
        c_high = c_sum.astype(bf16).astype(f32)
        u_b.append(jnp.concatenate([c_high, c_sum - c_high], axis=0).astype(bf16))
        return jnp.concatenate(weights_b, axis=0), jnp.concatenate(u_b, axis=0), sums

    def outputs(at, weights_b, u_b, sums):
        d_mid = nn(yt[...], jnp.concatenate([weights_b, u_b[0:hm]], axis=0))
        d_mid = [
            (d_mid[h * depth : (h + 1) * depth] + temp * sums[h]).astype(bf16)
            for h in range(heads)
        ]
        d_mid = jnp.concatenate(d_mid, axis=0)
        dmt_ref[:, at] = d_mid
        grad_acc[...] += nn(d_mid, feats_ref[at, :])
        small_acc[...] += nn(u_b, mid_ref[at, :])

    ready = products(pieces[0])
    for i, at in enumerate(pieces):
        current = ready
        if i + 1 < len(pieces):
            ready = products(pieces[i + 1])
        outputs(at, *per_head(at, *current))

    grad = grad_acc[...].T
    u_part = jnp.where(same_block(hm, width, slices, depth), small_acc[0:hm, :], 0.0)
    u_part = fold_rows(u_part, heads, slices)
    c_part = small_acc[hm : hm + heads, :] + small_acc[hm + heads : hm + 2 * heads, :]
    c_part = jnp.where(same_block(heads, width, 1, depth), c_part, 0.0)
    c_part = jnp.sum(c_part, axis=0, keepdims=True)

    def fold_lanes(x):
        total = x[:, 0:128]
        for j in range(1, width // 128):
            total = total + x[:, j * 128 : (j + 1) * 128]
        shift = 64
        while shift >= depth:
            total = total + pltpu.roll(total, shift, 1)
            shift //= 2
        return total

    u_part = fold_lanes(u_part)
    c_part = fold_lanes(jnp.broadcast_to(c_part, (slices, width)))
    where_lane = cols_of((slices, 128))
    extra = jnp.where(where_lane < depth, u_part, c_part)
    rows = width // group
    more = slices // group
    for j in range(group):
        pack[j, 0:rows, :] = grad[j * rows : (j + 1) * rows]
        pack[j, rows : rows + more, 0:128] = extra[j * more : (j + 1) * more]
        pack[j, rows : rows + more, 128:] = jnp.zeros((more, width - 128), f32)
    place = group_place()
    for k, send in enumerate((send0, send1, send2, send3)):
        send[...] = pack[place ^ k]


def rows_kernel(wt_ref, dmt_ref, mw_ref, w_mid_ref, _, attended_ref, feats_grad_ref, token_ref):
    block = attended_ref.shape[0]
    at = pl.ds(pl.multiple_of(pl.program_id(0) * block, block), block)
    token_ref[...] = jnp.zeros_like(token_ref)
    attended_ref[...] = tn(wt_ref[:, at], mw_ref[...]).astype(bf16)
    feats_grad_ref[...] = lax.dot_general(
        dmt_ref[:, at], w_mid_ref[...], (((0,), (1,)), ((), ())), preferred_element_type=f32
    ).astype(bf16)


def grad_out_kernel(own_ref, other_ref, mixed_t_ref, _, grad_out_ref, token_ref, whole):
    token_ref[...] = jnp.zeros_like(token_ref)
    place = group_place() & 1
    rows = own_ref.shape[0]
    for k, part in enumerate((own_ref, other_ref)):
        whole[pl.ds(pl.multiple_of((place ^ k) * rows, 8), rows), :] = part[...]
    high, low = two_pieces(whole[...])
    mixed_t = mixed_t_ref[...]
    grad_out_ref[...] = nn(mixed_t, high) + nn(mixed_t, low)


def finish_kernel(depth, m0, m1, m2, m3, _, grad_mid_ref, slice_ref, temp_ref, extra):
    place = group_place()
    slices = slice_ref.shape[1]
    more = slices // group
    rows = m0.shape[0] - more
    for k, part in enumerate((m0, m1, m2, m3)):
        at = pl.ds(pl.multiple_of((place ^ k) * rows, 8), rows)
        grad_mid_ref[at, :] = part[0:rows, :]
        extra[pl.ds(pl.multiple_of((place ^ k) * more, 8), more), :] = part[rows:, 0:128]
    turned = extra[...].T
    slice_ref[...] = turned[0:depth, 0:slices]
    temp_ref[...] = extra[0:1, depth : 2 * depth]


def full(shape):
    zeros = (0,) * len(shape)
    return pl.BlockSpec(shape, lambda *_: zeros)


def params(mebibytes, grid=True):
    semantics = ("arbitrary",) if grid else None
    return pltpu.CompilerParams(
        dimension_semantics=semantics, vmem_limit_bytes=mebibytes * mib
    )


def cost(flops, moved, transcendentals=0):
    return pl.CostEstimate(flops=flops, bytes_accessed=moved, transcendentals=transcendentals)


def exchange(x, k, count):
    return lax.ppermute(x, "node", [(i, i ^ k) for i in range(count)])


def sum_kernel(count, *refs):
    total = refs[0][...] + refs[count - 1][...]
    if count == 4:
        total = total + (refs[1][...] + refs[2][...])
    refs[-1][...] = total


def sum_behind(parts, *before):
    return pl.pallas_call(
        functools.partial(sum_kernel, len(parts)),
        out_shape=jax.ShapeDtypeStruct(parts[0].shape, f32),
        in_specs=[pl.BlockSpec(memory_space=pltpu.VMEM)] * len(parts)
        + [pl.BlockSpec(memory_space=pl.ANY)] * len(before),
        out_specs=pl.BlockSpec(memory_space=pltpu.VMEM),
        compiler_params=params(2, False),
        cost_estimate=cost(3 * parts[0].size, 5 * parts[0].size * 4),
    )(*parts, *before)


def scatter_group(parts, count):
    got = [parts[0]] + [exchange(parts[k], k, count) for k in range(1, group)]
    return (got[0] + got[1]) + (got[2] + got[3])


def sum_stage(total, stride, others, count, *before):
    got = [total] + [exchange(total, stride * j, count) for j in range(others, 0, -1)]
    if before:
        return sum_behind(got, *before)
    if others == 1:
        return got[0] + got[1]
    return (got[0] + got[3]) + (got[1] + got[2])


def sum_over_groups(total, stride, count, *before):
    while stride < count:
        others = 3 if count // stride % 4 == 0 else 1
        total = sum_stage(total, stride, others, count, *before)
        stride *= others + 1
    return total


def gather_group(total, count):
    return [total] + [exchange(total, k, count) for k in range(1, group)]


def shards(count, feats, cotangent, valid, owned, w_mid, w_slice, temp_vec, w_qkv, w_out):
    rows, width = feats.shape
    depth, slices = w_slice.shape
    heads = width // depth
    hm = heads * slices
    unit = 2 * rows * width * width
    smem = pl.BlockSpec(memory_space=pltpu.SMEM)

    def blocks(size):
        return (rows // size,), pl.BlockSpec((size, width), lambda i: (i, 0))

    def like(shape, dtype):
        return jax.ShapeDtypeStruct(shape, dtype)

    def far(x):
        return pltpu.with_memory_space_constraint(x, pltpu.HBM)

    near = pltpu.VMEM
    whole = pl.BlockSpec(memory_space=pltpu.VMEM)

    temp = temp_vec.reshape(1, depth)
    half = (2 * slices + 8, 128)
    wide = (hm // 2, width)
    inputs = (valid.reshape(1, rows), feats, cotangent, w_mid, w_slice, w_out, w_qkv)
    pieces = rows // min(sub_block, rows)
    (
        mid,
        wt,
        aux,
        sw,
        sb,
        w_cat,
        keep,
        send,
        wc_keep,
        wc_send,
        feats_near,
        cot_near,
    ) = pl.pallas_call(
        functools.partial(stats_kernel, heads, slices),
        in_specs=[smem, whole] + [pl.BlockSpec(memory_space=pltpu.HBM)] * len(inputs),
        out_specs=[whole] * 12,
        out_shape=[
            near((rows, width), bf16),
            near((hm, rows), bf16),
            near((3 * heads, rows), f32),
            near((hm + 16, width), bf16),
            near((width, hm), bf16),
            near((depth, 128), bf16),
            near(half, f32),
            near(half, f32),
            near(wide, f32),
            near(wide, f32),
            near((rows, width), bf16),
            near((rows, width), bf16),
        ],
        scratch_shapes=[
            pltpu.VMEM((1, rows), jnp.int32),
            pltpu.VMEM((width, width), bf16),
            pltpu.VMEM((depth, slices), bf16),
            pltpu.VMEM((width, width), bf16),
            pltpu.VMEM((3, depth, depth), bf16),
            pltpu.VMEM((hm, width), f32),
            pltpu.VMEM((hm, 128), f32),
            pltpu.VMEM((hm, width), f32),
            pltpu.VMEM((2,) + half, f32),
            pltpu.SemaphoreType.DMA((5 + 2 * pieces,)),
        ],
        compiler_params=params(24, False),
        cost_estimate=cost(4 * unit, rows * width * 8, rows * hm),
    )(owned, far(temp), *map(far, inputs))

    own = keep + exchange(send, 1, count)
    wc_got = exchange(wc_send, 1, count)
    own = sum_stage(own, 2, 3, count)
    own = sum_over_groups(own, 8, count)
    other = exchange(own, 1, count)
    wc_sum = sum_behind([wc_keep, wc_got], own)
    wc_got = exchange(wc_sum, 2, count)

    mw, mixed_t, dr, drt, dn, grad_qkv = pl.pallas_call(
        functools.partial(tokens_kernel, heads, slices),
        out_shape=[
            near((hm, width), bf16),
            near((width, hm), bf16),
            near((hm, width), bf16),
            near((width, hm), bf16),
            near((hm, 128), f32),
            like((3, depth, depth), f32),
        ],
        scratch_shapes=[pltpu.VMEM((2,) + half, f32)],
        compiler_params=params(16, False),
        cost_estimate=cost(30 * width**3, 4 * width * width * 4, hm * hm),
    )(own, other, w_cat, w_out)
    wc_sum = sum_behind([wc_sum, wc_got], mw)
    stride = 4
    while stride < count // 2:
        if stride > 4:
            wc_sum = wc_sum + wc_got
        wc_got = exchange(wc_sum, stride, count)
        stride *= 2

    larger = (width // group + slices // group, width)
    dmt, *sends = pl.pallas_call(
        functools.partial(backward_kernel, heads, slices),
        in_specs=[whole] * 11 + [pl.BlockSpec(memory_space=pl.ANY)],
        out_specs=[whole] * (1 + group),
        out_shape=[near((width, rows), bf16)] + [near(larger, f32)] * group,
        scratch_shapes=[
            pltpu.VMEM((2 * hm + 16, width), bf16),
            pltpu.VMEM((width, 2 * hm), bf16),
            pltpu.VMEM((width, width), f32),
            pltpu.VMEM((hm + 16, width), f32),
            pltpu.VMEM((group,) + larger, f32),
        ],
        compiler_params=params(24, False),
        cost_estimate=cost(8 * unit, rows * width * 8, rows * hm),
    )(aux, mid, cot_near, feats_near, sw, sb, mw, dr, drt, dn, temp, wc_sum)

    mid_total = scatter_group(sends, count)
    wc_sum = sum_behind([wc_sum, wc_got], sends[1])
    wc_got = exchange(wc_sum, count // 2, count)

    block = min(1024, rows)
    grid, by_rows = blocks(block)
    attended, feats_grad, token = pl.pallas_call(
        rows_kernel,
        grid=grid,
        in_specs=[
            whole,
            whole,
            whole,
            full((width, width)),
            pl.BlockSpec(memory_space=pl.ANY),
        ],
        out_specs=[by_rows, by_rows, full((8, 128))],
        out_shape=[like((rows, width), bf16)] * 2 + [like((8, 128), f32)],
        compiler_params=params(20),
        cost_estimate=cost(2 * unit, rows * width * 8),
    )(wt, dmt, mw, w_mid, mid_total)

    wc_sum = sum_behind([wc_sum, wc_got], token)
    wc_other = exchange(wc_sum, 1, count)
    mid_total = sum_over_groups(mid_total, group, count, token)
    grad_w_out, token = pl.pallas_call(
        grad_out_kernel,
        out_shape=[like((width, width), f32), like((8, 128), f32)],
        in_specs=[whole] * 3 + [pl.BlockSpec(memory_space=pl.ANY)],
        out_specs=[whole] * 2,
        scratch_shapes=[pltpu.VMEM((hm, width), f32)],
        compiler_params=params(8, False),
        cost_estimate=cost(4 * width**3, 3 * width * width * 4),
    )(wc_sum, wc_other, mixed_t, mid_total)

    mid_parts = gather_group(mid_total, count)
    grad_w_mid, grad_w_slice, grad_temp = pl.pallas_call(
        functools.partial(finish_kernel, depth),
        in_specs=[whole] * group + [pl.BlockSpec(memory_space=pl.ANY)],
        out_specs=[whole] * 3,
        out_shape=[
            like((width, width), f32),
            like((depth, slices), f32),
            like((1, depth), f32),
        ],
        scratch_shapes=[pltpu.VMEM((slices, 128), f32)],
        compiler_params=params(8, False),
        cost_estimate=cost(0, 2 * width * width * 4),
    )(*mid_parts, token)
    return (
        attended,
        feats_grad,
        grad_w_mid,
        grad_w_out,
        grad_w_slice,
        grad_temp.reshape(depth),
        grad_qkv,
    )


def solution(mesh):
    in_specs = (
        P(("design", "node"), None),
        P(("design", "node"), None),
        P(("design", "node")),
        P(("design", "node")),
        P(),
        P(),
        P(),
        P(),
        P(),
    )
    out_specs = (
        P(("design", "node"), None),
        P(("design", "node"), None),
        P("design", None),
        P("design", None),
        P("design", None),
        P("design"),
        P("design", None, None),
    )
    return jax.shard_map(
        functools.partial(shards, mesh.shape["node"]),
        mesh=mesh,
        in_specs=in_specs,
        out_specs=out_specs,
        check_vma=False,
    )
```

```python
import functools
import math

import jax
import jax.numpy as jnp
from jax import lax
from jax.experimental import pallas as pl
from jax.experimental.pallas import tpu as pltpu
from jax.sharding import PartitionSpec as P

f32 = jnp.float32
bf16 = jnp.bfloat16
eps_norm = 1e-05
exact = lax.Precision.HIGHEST
group = 4
sub_block = 512
mib = 1024 * 1024


def nn(a, b, precision=None):
    return lax.dot_general(
        a, b, (((1,), (0,)), ((), ())), preferred_element_type=f32, precision=precision
    )


def nt(a, b, precision=None):
    return lax.dot_general(
        a, b, (((1,), (1,)), ((), ())), preferred_element_type=f32, precision=precision
    )


def tn(a, b, precision=None):
    return lax.dot_general(
        a, b, (((0,), (0,)), ((), ())), preferred_element_type=f32, precision=precision
    )


def log2(size):
    return size.bit_length() - 1


def rows_of(shape):
    return lax.broadcasted_iota(jnp.int32, shape, 0)


def cols_of(shape):
    return lax.broadcasted_iota(jnp.int32, shape, 1)


def spread_matrix(width, small):
    shape = (width, small)
    return jnp.where((rows_of(shape) & (small - 1)) == cols_of(shape), 1.0, 0.0).astype(bf16)


def same_block(rows, cols, row_size, col_size):
    shape = (rows, cols)
    return rows_of(shape) >> log2(row_size) == cols_of(shape) >> log2(col_size)


def two_pieces(x):
    high = x.astype(bf16)
    return high, (x - high.astype(f32)).astype(bf16)


def fold_rows(x, heads, size):
    total = x[0:size]
    for h in range(1, heads):
        total = total + x[h * size : (h + 1) * size]
    return total


def group_place():
    return lax.axis_index("node") % group


def stats_kernel(
    heads,
    slices,
    owned_ref,
    temp_ref,
    valid_far,
    feats_far,
    cot_far,
    w_mid_far,
    w_slice_far,
    w_out_far,
    w_qkv_far,
    mid_ref,
    wt_ref,
    aux_ref,
    sw_ref,
    sb_ref,
    w_cat_ref,
    keep_ref,
    send_ref,
    wc_keep_ref,
    wc_send_ref,
    feats_ref,
    cot_ref,
    valid_ref,
    w_mid_ref,
    w_slice_ref,
    w_out_ref,
    w_qkv_ref,
    raw_acc,
    norm_acc,
    wc_acc,
    pack,
    sems,
):
    width = w_mid_ref.shape[0]
    depth = width // heads
    hm = heads * slices
    rows = feats_ref.shape[0]
    piece = min(sub_block, rows)
    count = rows // piece
    small = [
        pltpu.make_async_copy(source, target, sems.at[i])
        for i, (source, target) in enumerate(
            (
                (w_slice_far, w_slice_ref),
                (w_qkv_far, w_qkv_ref),
                (w_mid_far, w_mid_ref),
                (valid_far, valid_ref),
                (w_out_far, w_out_ref),
            )
        )
    ]
    first, rest = pl.ds(0, piece), pl.ds(piece, rows - piece)
    large = [
        pltpu.make_async_copy(source, target, sems.at[len(small) + i])
        for i, (source, target) in enumerate(
            (
                (feats_far.at[first, :], feats_ref.at[first, :]),
                (feats_far.at[rest, :], feats_ref.at[rest, :]),
                (cot_far, cot_ref),
            )
        )
    ]
    for copy in small[:3] + large[:1] + small[3:] + large[1:]:
        copy.start()

    raw_acc[...] = jnp.zeros_like(raw_acc)
    norm_acc[...] = jnp.zeros_like(norm_acc)
    wc_acc[...] = jnp.zeros_like(wc_acc)
    spread_d = spread_matrix(width, depth)
    spread_m = spread_matrix(hm, slices)
    temp = jnp.broadcast_to(temp_ref[...].astype(f32), (16, depth)).astype(bf16)
    small[0].wait()
    w_slice = w_slice_ref[...]
    half = nt(spread_m, w_slice).astype(bf16)
    full = nt(half, spread_d)
    sw_ref[0:hm, :] = jnp.where(same_block(hm, width, slices, depth), full, 0.0).astype(bf16)
    half = nn(spread_d, w_slice).astype(bf16)
    full = nt(half, spread_m)
    sb_ref[...] = jnp.where(same_block(width, hm, depth, slices), full, 0.0).astype(bf16)
    full = nt(temp, spread_d)
    sw_ref[hm : hm + 16, :] = jnp.where(same_block(16, width, 1, depth), full, 0.0).astype(bf16)
    small[1].wait()
    w_cat = jnp.zeros((depth, 128), f32)
    for i in range(3):
        place_at = jnp.where(rows_of((depth, 128)) + i * depth == cols_of((depth, 128)), 1.0, 0.0)
        w_cat = w_cat + nn(w_qkv_ref[i], place_at.astype(bf16))
    w_cat_ref[...] = w_cat.astype(bf16)
    small[2].wait()
    small[3].wait()
    small[4].wait()
    owned = owned_ref[0]

    def products(i):
        at = slice(i * piece, (i + 1) * piece)
        mid = nn(feats_ref[at, :], w_mid_ref[...]).astype(bf16)
        mid_ref[at, :] = mid
        return mid, nt(sw_ref[...], mid)

    def statistics(i, mid, scores):
        at = slice(i * piece, (i + 1) * piece)
        zsum = scores[hm : hm + heads]
        small = jnp.exp(-jnp.abs(zsum))
        inv_tau = 1.0 / (0.5 + (jnp.maximum(zsum, 0.0) + jnp.log(1.0 + small)))
        sig = jnp.where(zsum >= 0.0, 1.0, small) / (1.0 + small)
        position = i * piece + cols_of((1, piece))
        live = (valid_ref[:, at] > 0) & (position < owned)
        live_f = live.astype(f32)
        rounded, sums, logs = [], [], []
        for h in range(heads):
            span = slice(h * slices, (h + 1) * slices)
            logits = scores[span] * inv_tau[h : h + 1]
            peak = jnp.max(logits, axis=0, keepdims=True)
            expo = jnp.exp(logits - peak)
            total = jnp.sum(expo, axis=0, keepdims=True)
            weights = expo * (live_f / total)
            rounded.append(weights.astype(bf16))
            lanes = weights[:, 0:128]
            for c in range(1, piece // 128):
                lanes = lanes + weights[:, c * 128 : (c + 1) * 128]
            sums.append(lanes)
            logs.append(jnp.where(live, peak + jnp.log(total), jnp.inf))
        wt = jnp.concatenate(rounded, axis=0)
        wt_ref[:, at] = wt
        norm_acc[...] += jnp.concatenate(sums, axis=0)
        aux_ref[:, at] = jnp.concatenate([inv_tau] + logs + [sig * inv_tau], axis=0)
        raw_acc[...] += nn(wt, mid)
        wc_acc[...] += nn(wt, cot_ref[at, :])

    large[0].wait()
    ready = products(0)
    large[1].wait()
    large[2].wait()
    for i in range(count):
        current = ready
        if i + 1 < count:
            ready = products(i + 1)
        statistics(i, *current)

    diagonal = same_block(hm, width, slices, depth)
    raw = fold_rows(jnp.where(diagonal, raw_acc[...], 0.0), heads, slices)
    high, low = two_pieces(wc_acc[...])
    w_out = w_out_ref[...]
    mixed = nt(high, w_out) + nt(low, w_out)
    mixed = fold_rows(jnp.where(diagonal, mixed, 0.0), heads, slices)
    norm = jnp.sum(norm_acc[...].T, axis=0, keepdims=True)
    first = rows_of((8, 128)) == 0
    for j in range(2):
        part = slice(j * 128, (j + 1) * 128)
        pack[j, 0:slices, :] = raw[:, part]
        pack[j, slices : 2 * slices, :] = mixed[:, part]
        pack[j, 2 * slices :, :] = jnp.where(first, norm[:, part], 0.0)
    place = group_place()
    keep_ref[...] = pack[place & 1]
    send_ref[...] = pack[(place & 1) ^ 1]
    rows = hm // 2
    for k, out in enumerate((wc_keep_ref, wc_send_ref)):
        out[...] = wc_acc[pl.ds(pl.multiple_of(((place & 1) ^ k) * rows, 8), rows), :]


def lanes_at(x, lane, *where):
    place = cols_of(x.shape) >> log2(lane)
    total = jnp.zeros_like(x)
    for value, at, to in where:
        shift = (to - at) * lane % 128
        moved = pltpu.roll(value, shift, 1) if shift else value
        total = jnp.where(place == to, moved, total)
    return total.astype(bf16)


def split(x):
    high = x.astype(bf16).astype(f32)
    return high, x - high


def tokens_kernel(
    heads,
    slices,
    own_ref,
    got_ref,
    w_cat_ref,
    w_out_ref,
    mw_ref,
    mixed_t_ref,
    dr_ref,
    drt_ref,
    dn_ref,
    grad_qkv_ref,
    pack,
):
    width = w_out_ref.shape[0]
    depth = width // heads
    hm = heads * slices
    place = group_place() & 1
    pack[place] = own_ref[...]
    pack[place ^ 1] = got_ref[...]
    per = 128 // depth

    def compact(first):
        pieces = []
        for h in range(heads):
            x = pack[h // per, first : first + slices, :]
            shift = (h % per) * depth
            pieces.append(pltpu.roll(x, 128 - shift, 1) if shift else x)
        x = jnp.concatenate(pieces, axis=0)
        return jnp.where(cols_of(x.shape) < depth, x, 0.0)

    raw = compact(0)
    d_mixed = compact(slices)
    norm = jnp.concatenate([pack[j, 2 * slices :, :].T[:, 0:1] for j in range(2)], axis=0)
    inverse = 1.0 / (norm + eps_norm)
    tokens = raw * inverse
    w_cat = w_cat_ref[...]

    t_high, rest = split(tokens)
    t_low, rest = split(rest)
    left = lanes_at(tokens, depth, (t_high, 0, 0), (t_low, 0, 1), (rest, 0, 2))
    blank = jnp.zeros((128 - 3 * depth, 128), bf16)
    qkv = nn(left, jnp.concatenate([w_cat, w_cat, w_cat, blank], axis=0))
    high, low = split(qkv)
    q_left = lanes_at(qkv, depth, (high, 0, 0), (high, 0, 1), (low, 0, 2))
    k_right = lanes_at(qkv, depth, (high, 1, 0), (low, 1, 1), (high, 1, 2))
    v_right = lanes_at(qkv, depth, (high, 2, 0), (low, 2, 1), (high, 2, 2))
    q_pair = lanes_at(qkv, depth, (high, 0, 0), (low, 0, 1))
    k_pair = lanes_at(qkv, depth, (high, 1, 0), (low, 1, 1))
    v_pair = lanes_at(qkv, depth, (high, 2, 0), (low, 2, 1))
    g_high, g_low = split(d_mixed)
    g_left = lanes_at(qkv, depth, (g_high, 0, 0), (g_high, 0, 1), (g_low, 0, 2))
    g_pair = lanes_at(qkv, depth, (g_high, 0, 0), (g_low, 0, 1))

    def times_pair(dot, x, pair):
        x_high, x_low = two_pieces(x)
        both = dot(x_high, pair)
        low_part = dot(x_low, pair)
        total = both + pltpu.roll(both, 128 - depth, 1) + low_part
        return jnp.where(cols_of(total.shape) < depth, total, 0.0)

    blocks = same_block(hm, hm, slices, slices)
    scale = 1.0 / math.sqrt(depth)
    scores = jnp.where(blocks, nt(q_left, k_right) * scale, -jnp.inf)
    expo = jnp.exp(scores - jnp.max(scores, axis=1, keepdims=True))
    probs = expo * (1.0 / jnp.sum(expo, axis=1, keepdims=True))
    mixed_b = times_pair(nn, probs, v_pair).astype(bf16)

    spread_d = jnp.where(
        (rows_of((width, 128)) & (depth - 1)) == cols_of((width, 128)), 1.0, 0.0
    ).astype(bf16)
    diagonal = same_block(hm, width, slices, depth)
    diagonal_t = same_block(width, hm, depth, slices)
    mixed_block = jnp.where(diagonal, nt(mixed_b, spread_d), 0.0).astype(bf16)
    mw_ref[...] = nn(mixed_block, w_out_ref[...]).astype(bf16)
    mixed_t_ref[...] = jnp.where(diagonal_t, nt(spread_d, mixed_b), 0.0).astype(bf16)

    d_probs = nt(g_left, v_right)
    d_v = times_pair(tn, probs, g_pair)
    d_scores = probs * (d_probs - jnp.sum(probs * d_probs, axis=1, keepdims=True)) * scale
    d_q = times_pair(nn, d_scores, k_pair)
    d_k = times_pair(tn, d_scores, q_pair)
    d_qkv = d_q + pltpu.roll(d_k, depth, 1) + pltpu.roll(d_v, 2 * depth, 1)
    d_high, d_low = two_pieces(d_qkv)
    d_tokens = nt(d_high, w_cat) + nt(d_low, w_cat)
    raw = raw[:, 0:depth]
    d_raw_b = (d_tokens * inverse).astype(bf16)
    d_norm = -jnp.sum(d_tokens * raw, axis=1, keepdims=True) * inverse * inverse
    dn_ref[...] = jnp.broadcast_to(d_norm, dn_ref.shape)
    spread_d = spread_matrix(width, depth)
    dr_ref[...] = jnp.where(diagonal, nt(d_raw_b, spread_d), 0.0).astype(bf16)
    drt_ref[...] = jnp.where(diagonal_t, nt(spread_d, d_raw_b), 0.0).astype(bf16)

    t_high, t_low = two_pieces(tokens)
    grads = tn(t_high, d_high) + tn(t_high, d_low) + tn(t_low, d_high)
    for i in range(3):
        at = pltpu.roll(grads, 128 - i * depth, 1) if i else grads
        grad_qkv_ref[i] = at[0:depth, 0:depth]


def backward_kernel(
    heads,
    slices,
    aux_ref,
    mid_ref,
    cot_ref,
    feats_ref,
    sw_ref,
    sb_ref,
    mw_ref,
    dr_ref,
    drt_ref,
    dn_ref,
    temp_ref,
    _,
    dmt_ref,
    send0,
    send1,
    send2,
    send3,
    lhs,
    yt,
    grad_acc,
    small_acc,
    pack,
):
    width = mid_ref.shape[1]
    depth = width // heads
    hm = heads * slices
    block = feats_ref.shape[0]
    top = hm + 16

    grad_acc[...] = jnp.zeros_like(grad_acc)
    small_acc[...] = jnp.zeros_like(small_acc)
    lhs[0:top, :] = sw_ref[...]
    lhs[top:, :] = dr_ref[...]
    yt[:, 0:hm] = drt_ref[...]
    yt[:, hm:] = sb_ref[...]

    temp = jnp.broadcast_to(temp_ref[...].astype(f32), (16, depth)).astype(bf16)
    same = (rows_of((depth, depth)) == cols_of((depth, depth))).astype(f32).astype(bf16)
    temp = nt(same, temp)[:, 0:1]
    piece = min(2 * sub_block, block)
    pieces = [slice(i * piece, (i + 1) * piece) for i in range(block // piece)]

    def products(at):
        return nt(lhs[...], mid_ref[at, :]), nt(mw_ref[...], cot_ref[at, :])

    def per_head(at, from_mid, from_cot):
        weights_b, u_b, sums = [], [], []
        aux = aux_ref[:, at]
        for h in range(heads):
            span = slice(h * slices, (h + 1) * slices)
            inv_tau = aux[h : h + 1]
            logits = from_mid[span] * inv_tau
            weights = jnp.exp(logits - aux[heads + h : heads + h + 1])
            d_weights = from_cot[span] + from_mid[top + h * slices : top + (h + 1) * slices]
            d_weights = d_weights + dn_ref[span, 0:1]
            mean = jnp.sum(weights * d_weights, axis=0, keepdims=True)
            d_logits = weights * (d_weights - mean)
            d_tau = jnp.sum(d_logits * logits, axis=0, keepdims=True)
            sums.append(-d_tau * aux[2 * heads + h : 2 * heads + h + 1])
            weights_b.append(weights.astype(bf16))
            u_b.append((d_logits * inv_tau).astype(bf16))
        c_sum = jnp.concatenate(sums, axis=0)
        c_high = c_sum.astype(bf16).astype(f32)
        u_b.append(jnp.concatenate([c_high, c_sum - c_high], axis=0).astype(bf16))
        return jnp.concatenate(weights_b, axis=0), jnp.concatenate(u_b, axis=0), sums

    def outputs(at, weights_b, u_b, sums):
        d_mid = nn(yt[...], jnp.concatenate([weights_b, u_b[0:hm]], axis=0))
        d_mid = [
            (d_mid[h * depth : (h + 1) * depth] + temp * sums[h]).astype(bf16)
            for h in range(heads)
        ]
        d_mid = jnp.concatenate(d_mid, axis=0)
        dmt_ref[:, at] = d_mid
        grad_acc[...] += nn(d_mid, feats_ref[at, :])
        small_acc[...] += nn(u_b, mid_ref[at, :])

    ready = products(pieces[0])
    for i, at in enumerate(pieces):
        current = ready
        if i + 1 < len(pieces):
            ready = products(pieces[i + 1])
        outputs(at, *per_head(at, *current))

    grad = grad_acc[...].T
    u_part = jnp.where(same_block(hm, width, slices, depth), small_acc[0:hm, :], 0.0)
    u_part = fold_rows(u_part, heads, slices)
    c_part = small_acc[hm : hm + heads, :] + small_acc[hm + heads : hm + 2 * heads, :]
    c_part = jnp.where(same_block(heads, width, 1, depth), c_part, 0.0)
    c_part = jnp.sum(c_part, axis=0, keepdims=True)

    def fold_lanes(x):
        total = x[:, 0:128]
        for j in range(1, width // 128):
            total = total + x[:, j * 128 : (j + 1) * 128]
        shift = 64
        while shift >= depth:
            total = total + pltpu.roll(total, shift, 1)
            shift //= 2
        return total

    u_part = fold_lanes(u_part)
    c_part = fold_lanes(jnp.broadcast_to(c_part, (slices, width)))
    where_lane = cols_of((slices, 128))
    extra = jnp.where(where_lane < depth, u_part, c_part)
    rows = width // group
    more = slices // group
    for j in range(group):
        pack[j, 0:rows, :] = grad[j * rows : (j + 1) * rows]
        pack[j, rows : rows + more, 0:128] = extra[j * more : (j + 1) * more]
        pack[j, rows : rows + more, 128:] = jnp.zeros((more, width - 128), f32)
    place = group_place()
    for k, send in enumerate((send0, send1, send2, send3)):
        send[...] = pack[place ^ k]


def rows_kernel(wt_ref, dmt_ref, mw_ref, w_mid_ref, _, attended_ref, feats_grad_ref, token_ref):
    block = attended_ref.shape[0]
    at = pl.ds(pl.multiple_of(pl.program_id(0) * block, block), block)
    token_ref[...] = jnp.zeros_like(token_ref)
    attended_ref[...] = tn(wt_ref[:, at], mw_ref[...]).astype(bf16)
    feats_grad_ref[...] = lax.dot_general(
        dmt_ref[:, at], w_mid_ref[...], (((0,), (1,)), ((), ())), preferred_element_type=f32
    ).astype(bf16)


def grad_out_kernel(own_ref, other_ref, mixed_t_ref, _, grad_out_ref, token_ref, whole):
    token_ref[...] = jnp.zeros_like(token_ref)
    place = group_place() & 1
    rows = own_ref.shape[0]
    for k, part in enumerate((own_ref, other_ref)):
        whole[pl.ds(pl.multiple_of((place ^ k) * rows, 8), rows), :] = part[...]
    high, low = two_pieces(whole[...])
    mixed_t = mixed_t_ref[...]
    grad_out_ref[...] = nn(mixed_t, high) + nn(mixed_t, low)


def finish_kernel(depth, m0, m1, m2, m3, _, grad_mid_ref, slice_ref, temp_ref, extra):
    place = group_place()
    slices = slice_ref.shape[1]
    more = slices // group
    rows = m0.shape[0] - more
    for k, part in enumerate((m0, m1, m2, m3)):
        at = pl.ds(pl.multiple_of((place ^ k) * rows, 8), rows)
        grad_mid_ref[at, :] = part[0:rows, :]
        extra[pl.ds(pl.multiple_of((place ^ k) * more, 8), more), :] = part[rows:, 0:128]
    turned = extra[...].T
    slice_ref[...] = turned[0:depth, 0:slices]
    temp_ref[...] = extra[0:1, depth : 2 * depth]


def full(shape):
    zeros = (0,) * len(shape)
    return pl.BlockSpec(shape, lambda *_: zeros)


def params(mebibytes, grid=True):
    semantics = ("arbitrary",) if grid else None
    return pltpu.CompilerParams(
        dimension_semantics=semantics, vmem_limit_bytes=mebibytes * mib
    )


def cost(flops, moved, transcendentals=0):
    return pl.CostEstimate(flops=flops, bytes_accessed=moved, transcendentals=transcendentals)


def exchange(x, k, count):
    return lax.ppermute(x, "node", [(i, i ^ k) for i in range(count)])


def sum_kernel(count, *refs):
    total = refs[0][...] + refs[count - 1][...]
    if count == 4:
        total = total + (refs[1][...] + refs[2][...])
    refs[-1][...] = total


def sum_behind(parts, *before):
    return pl.pallas_call(
        functools.partial(sum_kernel, len(parts)),
        out_shape=jax.ShapeDtypeStruct(parts[0].shape, f32),
        in_specs=[pl.BlockSpec(memory_space=pltpu.VMEM)] * len(parts)
        + [pl.BlockSpec(memory_space=pl.ANY)] * len(before),
        out_specs=pl.BlockSpec(memory_space=pltpu.VMEM),
        compiler_params=params(2, False),
        cost_estimate=cost(3 * parts[0].size, 5 * parts[0].size * 4),
    )(*parts, *before)


def scatter_group(parts, count):
    got = [parts[0]] + [exchange(parts[k], k, count) for k in range(1, group)]
    return (got[0] + got[1]) + (got[2] + got[3])


def sum_stage(total, stride, others, count, *before):
    got = [total] + [exchange(total, stride * j, count) for j in range(others, 0, -1)]
    if before:
        return sum_behind(got, *before)
    if others == 1:
        return got[0] + got[1]
    return (got[0] + got[3]) + (got[1] + got[2])


def sum_over_groups(total, stride, count, *before):
    while stride < count:
        others = 3 if count // stride % 4 == 0 else 1
        total = sum_stage(total, stride, others, count, *before)
        stride *= others + 1
    return total


def gather_group(total, count):
    return [total] + [exchange(total, k, count) for k in range(1, group)]


def shards(count, feats, cotangent, valid, owned, w_mid, w_slice, temp_vec, w_qkv, w_out):
    rows, width = feats.shape
    depth, slices = w_slice.shape
    heads = width // depth
    hm = heads * slices
    unit = 2 * rows * width * width
    smem = pl.BlockSpec(memory_space=pltpu.SMEM)

    def blocks(size):
        return (rows // size,), pl.BlockSpec((size, width), lambda i: (i, 0))

    def like(shape, dtype):
        return jax.ShapeDtypeStruct(shape, dtype)

    def far(x):
        return pltpu.with_memory_space_constraint(x, pltpu.HBM)

    near = pltpu.VMEM
    whole = pl.BlockSpec(memory_space=pltpu.VMEM)

    temp = temp_vec.reshape(1, depth)
    half = (2 * slices + 8, 128)
    wide = (hm // 2, width)
    inputs = (valid.reshape(1, rows), feats, cotangent, w_mid, w_slice, w_out, w_qkv)
    (
        mid,
        wt,
        aux,
        sw,
        sb,
        w_cat,
        keep,
        send,
        wc_keep,
        wc_send,
        feats_near,
        cot_near,
    ) = pl.pallas_call(
        functools.partial(stats_kernel, heads, slices),
        in_specs=[smem, whole] + [pl.BlockSpec(memory_space=pltpu.HBM)] * len(inputs),
        out_specs=[whole] * 12,
        out_shape=[
            near((rows, width), bf16),
            near((hm, rows), bf16),
            near((3 * heads, rows), f32),
            near((hm + 16, width), bf16),
            near((width, hm), bf16),
            near((depth, 128), bf16),
            near(half, f32),
            near(half, f32),
            near(wide, f32),
            near(wide, f32),
            near((rows, width), bf16),
            near((rows, width), bf16),
        ],
        scratch_shapes=[
            pltpu.VMEM((1, rows), jnp.int32),
            pltpu.VMEM((width, width), bf16),
            pltpu.VMEM((depth, slices), bf16),
            pltpu.VMEM((width, width), bf16),
            pltpu.VMEM((3, depth, depth), bf16),
            pltpu.VMEM((hm, width), f32),
            pltpu.VMEM((hm, 128), f32),
            pltpu.VMEM((hm, width), f32),
            pltpu.VMEM((2,) + half, f32),
            pltpu.SemaphoreType.DMA((8,)),
        ],
        compiler_params=params(24, False),
        cost_estimate=cost(4 * unit, rows * width * 8, rows * hm),
    )(owned, far(temp), *map(far, inputs))

    own = keep + exchange(send, 1, count)
    wc_got = exchange(wc_send, 1, count)
    wc_sum = sum_behind([wc_keep, wc_got], own)
    own = sum_stage(own, 2, 3, count)
    wc_got = exchange(wc_sum, 2, count)
    wc_sum = sum_behind([wc_sum, wc_got], own)
    own = sum_over_groups(own, 8, count)
    other = exchange(own, 1, count)
    stride = 4
    while stride < count // 2:
        wc_got = exchange(wc_sum, stride, count)
        stride *= 2
        if stride < count // 2:
            wc_sum = wc_sum + wc_got

    mw, mixed_t, dr, drt, dn, grad_qkv = pl.pallas_call(
        functools.partial(tokens_kernel, heads, slices),
        out_shape=[
            near((hm, width), bf16),
            near((width, hm), bf16),
            near((hm, width), bf16),
            near((width, hm), bf16),
            near((hm, 128), f32),
            like((3, depth, depth), f32),
        ],
        scratch_shapes=[pltpu.VMEM((2,) + half, f32)],
        compiler_params=params(16, False),
        cost_estimate=cost(3 * width**3, 4 * width * width * 4, hm * hm),
    )(own, other, w_cat, w_out)
    larger = (width // group + slices // group, width)
    dmt, *sends = pl.pallas_call(
        functools.partial(backward_kernel, heads, slices),
        in_specs=[whole] * 11 + [pl.BlockSpec(memory_space=pl.ANY)],
        out_specs=[whole] * (1 + group),
        out_shape=[near((width, rows), bf16)] + [near(larger, f32)] * group,
        scratch_shapes=[
            pltpu.VMEM((2 * hm + 16, width), bf16),
            pltpu.VMEM((width, 2 * hm), bf16),
            pltpu.VMEM((width, width), f32),
            pltpu.VMEM((hm + 16, width), f32),
            pltpu.VMEM((group,) + larger, f32),
        ],
        compiler_params=params(24, False),
        cost_estimate=cost(width**3, rows * width, rows),
    )(aux, mid, cot_near, feats_near, sw, sb, mw, dr, drt, dn, temp, wc_sum)

    mid_total = scatter_group(sends, count)
    wc_sum = sum_behind([wc_sum, wc_got], sends[1])
    wc_got = exchange(wc_sum, count // 2, count)

    block = min(1024, rows)
    grid, by_rows = blocks(block)
    attended, feats_grad, token = pl.pallas_call(
        rows_kernel,
        grid=grid,
        in_specs=[
            whole,
            whole,
            whole,
            full((width, width)),
            pl.BlockSpec(memory_space=pl.ANY),
        ],
        out_specs=[by_rows, by_rows, full((8, 128))],
        out_shape=[like((rows, width), bf16)] * 2 + [like((8, 128), f32)],
        compiler_params=params(20),
        cost_estimate=cost(2 * unit, rows * width * 8),
    )(wt, dmt, mw, w_mid, mid_total)

    wc_sum = sum_behind([wc_sum, wc_got], token)
    wc_other = exchange(wc_sum, 1, count)
    mid_total = sum_over_groups(mid_total, group, count, token)
    grad_w_out, token = pl.pallas_call(
        grad_out_kernel,
        out_shape=[like((width, width), f32), like((8, 128), f32)],
        in_specs=[whole] * 3 + [pl.BlockSpec(memory_space=pl.ANY)],
        out_specs=[whole] * 2,
        scratch_shapes=[pltpu.VMEM((hm, width), f32)],
        compiler_params=params(8, False),
        cost_estimate=cost(4 * width**3, 3 * width * width * 4),
    )(wc_sum, wc_other, mixed_t, mid_total)

    mid_parts = gather_group(mid_total, count)
    grad_w_mid, grad_w_slice, grad_temp = pl.pallas_call(
        functools.partial(finish_kernel, depth),
        in_specs=[whole] * group + [pl.BlockSpec(memory_space=pl.ANY)],
        out_specs=[whole] * 3,
        out_shape=[
            like((width, width), f32),
            like((depth, slices), f32),
            like((1, depth), f32),
        ],
        scratch_shapes=[pltpu.VMEM((slices, 128), f32)],
        compiler_params=params(8, False),
        cost_estimate=cost(0, 2 * width * width * 4),
    )(*mid_parts, token)
    return (
        attended,
        feats_grad,
        grad_w_mid,
        grad_w_out,
        grad_w_slice,
        grad_temp.reshape(depth),
        grad_qkv,
    )


def solution(mesh):
    in_specs = (
        P(("design", "node"), None),
        P(("design", "node"), None),
        P(("design", "node")),
        P(("design", "node")),
        P(),
        P(),
        P(),
        P(),
        P(),
    )
    out_specs = (
        P(("design", "node"), None),
        P(("design", "node"), None),
        P("design", None),
        P("design", None),
        P("design", None),
        P("design"),
        P("design", None, None),
    )
    return jax.shard_map(
        functools.partial(shards, mesh.shape["node"]),
        mesh=mesh,
        in_specs=in_specs,
        out_specs=out_specs,
        check_vma=False,
    )
```

```python
import functools
import math

import jax
import jax.numpy as jnp
from jax import lax
from jax.experimental import pallas as pl
from jax.experimental.pallas import tpu as pltpu
from jax.sharding import PartitionSpec as P

f32 = jnp.float32
bf16 = jnp.bfloat16
eps_norm = 1e-05
exact = lax.Precision.HIGHEST
group = 4
sub_block = 512
mib = 1024 * 1024


def nn(a, b, precision=None):
    return lax.dot_general(
        a, b, (((1,), (0,)), ((), ())), preferred_element_type=f32, precision=precision
    )


def nt(a, b, precision=None):
    return lax.dot_general(
        a, b, (((1,), (1,)), ((), ())), preferred_element_type=f32, precision=precision
    )


def tn(a, b, precision=None):
    return lax.dot_general(
        a, b, (((0,), (0,)), ((), ())), preferred_element_type=f32, precision=precision
    )


def log2(size):
    return size.bit_length() - 1


def rows_of(shape):
    return lax.broadcasted_iota(jnp.int32, shape, 0)


def cols_of(shape):
    return lax.broadcasted_iota(jnp.int32, shape, 1)


def spread_matrix(width, small):
    shape = (width, small)
    return jnp.where((rows_of(shape) & (small - 1)) == cols_of(shape), 1.0, 0.0).astype(bf16)


def same_block(rows, cols, row_size, col_size):
    shape = (rows, cols)
    return rows_of(shape) >> log2(row_size) == cols_of(shape) >> log2(col_size)


def two_pieces(x):
    high = x.astype(bf16)
    return high, (x - high.astype(f32)).astype(bf16)


def fold_rows(x, heads, size):
    total = x[0:size]
    for h in range(1, heads):
        total = total + x[h * size : (h + 1) * size]
    return total


def group_place():
    return lax.axis_index("node") % group


def stats_kernel(
    heads,
    slices,
    owned_ref,
    temp_ref,
    valid_far,
    feats_far,
    cot_far,
    w_mid_far,
    w_slice_far,
    w_out_far,
    mid_ref,
    wt_ref,
    aux_ref,
    sw_ref,
    keep_ref,
    send_ref,
    wc_keep_ref,
    wc_send_ref,
    feats_ref,
    cot_ref,
    valid_ref,
    w_mid_ref,
    w_slice_ref,
    w_out_ref,
    raw_acc,
    norm_acc,
    wc_acc,
    pack,
    sems,
):
    width = w_mid_ref.shape[0]
    depth = width // heads
    hm = heads * slices
    rows = feats_ref.shape[0]
    piece = min(sub_block, rows)
    count = rows // piece
    small = [
        pltpu.make_async_copy(source, target, sems.at[i])
        for i, (source, target) in enumerate(
            (
                (w_slice_far, w_slice_ref),
                (w_mid_far, w_mid_ref),
                (valid_far, valid_ref),
                (w_out_far, w_out_ref),
            )
        )
    ]
    first, rest = pl.ds(0, piece), pl.ds(piece, rows - piece)
    large = [
        pltpu.make_async_copy(source, target, sems.at[len(small) + i])
        for i, (source, target) in enumerate(
            (
                (feats_far.at[first, :], feats_ref.at[first, :]),
                (feats_far.at[rest, :], feats_ref.at[rest, :]),
                (cot_far, cot_ref),
            )
        )
    ]
    for copy in small[:2] + large[:1] + small[2:] + large[1:]:
        copy.start()

    raw_acc[...] = jnp.zeros_like(raw_acc)
    norm_acc[...] = jnp.zeros_like(norm_acc)
    wc_acc[...] = jnp.zeros_like(wc_acc)
    spread_d = spread_matrix(width, depth)
    spread_m = spread_matrix(hm, slices)
    for copy in small + large[:1]:
        copy.wait()
    temp = jnp.broadcast_to(temp_ref[...].astype(f32), (16, depth)).astype(bf16)
    half = nt(spread_m, w_slice_ref[...]).astype(bf16)
    full = nt(half, spread_d)
    sw_ref[0:hm, :] = jnp.where(same_block(hm, width, slices, depth), full, 0.0).astype(bf16)
    full = nt(temp, spread_d)
    sw_ref[hm : hm + 16, :] = jnp.where(same_block(16, width, 1, depth), full, 0.0).astype(bf16)
    owned = owned_ref[0]

    def products(i):
        at = slice(i * piece, (i + 1) * piece)
        mid = nn(feats_ref[at, :], w_mid_ref[...]).astype(bf16)
        mid_ref[at, :] = mid
        return mid, nt(sw_ref[...], mid)

    def statistics(i, mid, scores):
        at = slice(i * piece, (i + 1) * piece)
        zsum = scores[hm : hm + heads]
        small = jnp.exp(-jnp.abs(zsum))
        inv_tau = 1.0 / (0.5 + (jnp.maximum(zsum, 0.0) + jnp.log(1.0 + small)))
        sig = jnp.where(zsum >= 0.0, 1.0, small) / (1.0 + small)
        position = i * piece + cols_of((1, piece))
        live = (valid_ref[:, at] > 0) & (position < owned)
        live_f = live.astype(f32)
        rounded, sums, logs = [], [], []
        for h in range(heads):
            span = slice(h * slices, (h + 1) * slices)
            logits = scores[span] * inv_tau[h : h + 1]
            peak = jnp.max(logits, axis=0, keepdims=True)
            expo = jnp.exp(logits - peak)
            total = jnp.sum(expo, axis=0, keepdims=True)
            weights = expo * (live_f / total)
            rounded.append(weights.astype(bf16))
            lanes = weights[:, 0:128]
            for c in range(1, piece // 128):
                lanes = lanes + weights[:, c * 128 : (c + 1) * 128]
            sums.append(lanes)
            logs.append(jnp.where(live, peak + jnp.log(total), jnp.inf))
        wt = jnp.concatenate(rounded, axis=0)
        wt_ref[:, at] = wt
        norm_acc[...] += jnp.concatenate(sums, axis=0)
        aux_ref[:, at] = jnp.concatenate([inv_tau] + logs + [sig * inv_tau], axis=0)
        raw_acc[...] += nn(wt, mid)
        wc_acc[...] += nn(wt, cot_ref[at, :])

    ready = products(0)
    large[1].wait()
    large[2].wait()
    for i in range(count):
        current = ready
        if i + 1 < count:
            ready = products(i + 1)
        statistics(i, *current)

    diagonal = same_block(hm, width, slices, depth)
    raw = fold_rows(jnp.where(diagonal, raw_acc[...], 0.0), heads, slices)
    high, low = two_pieces(wc_acc[...])
    w_out = w_out_ref[...]
    mixed = nt(high, w_out) + nt(low, w_out)
    mixed = fold_rows(jnp.where(diagonal, mixed, 0.0), heads, slices)
    norm = jnp.sum(norm_acc[...].T, axis=0, keepdims=True)
    first = rows_of((8, 128)) == 0
    for j in range(2):
        part = slice(j * 128, (j + 1) * 128)
        pack[j, 0:slices, :] = raw[:, part]
        pack[j, slices : 2 * slices, :] = mixed[:, part]
        pack[j, 2 * slices :, :] = jnp.where(first, norm[:, part], 0.0)
    place = group_place()
    keep_ref[...] = pack[place & 1]
    send_ref[...] = pack[(place & 1) ^ 1]
    rows = hm // 2
    for k, out in enumerate((wc_keep_ref, wc_send_ref)):
        out[...] = wc_acc[pl.ds(pl.multiple_of(((place & 1) ^ k) * rows, 8), rows), :]


def between_kernel(
    heads,
    slices,
    mid_ref,
    sw_ref,
    aux_ref,
    w_slice_ref,
    w_qkv_ref,
    _,
    logits_ref,
    weights_ref,
    sb_ref,
    w_cat_ref,
    token_ref,
):
    depth = w_slice_ref.shape[0]
    width = heads * depth
    hm = heads * slices
    rows = mid_ref.shape[0]
    piece = min(sub_block, rows)
    token_ref[...] = jnp.zeros_like(token_ref)
    spread_d = spread_matrix(width, depth)
    spread_m = spread_matrix(hm, slices)
    half = nn(spread_d, w_slice_ref[...]).astype(bf16)
    full = nt(half, spread_m)
    sb_ref[...] = jnp.where(same_block(width, hm, depth, slices), full, 0.0).astype(bf16)
    w_cat = jnp.zeros((depth, 128), f32)
    for i in range(3):
        place_at = jnp.where(rows_of((depth, 128)) + i * depth == cols_of((depth, 128)), 1.0, 0.0)
        w_cat = w_cat + nn(w_qkv_ref[i], place_at.astype(bf16))
    w_cat_ref[...] = w_cat.astype(bf16)
    for i in range(rows // piece):
        at = slice(i * piece, (i + 1) * piece)
        scores = nt(sw_ref[0:hm, :], mid_ref[at, :])
        for h in range(heads):
            span = slice(h * slices, (h + 1) * slices)
            logits = scores[span] * aux_ref[h : h + 1, at]
            logits_ref[span, at] = logits
            weights_ref[span, at] = jnp.exp(logits - aux_ref[heads + h : heads + h + 1, at])


def lanes_at(x, lane, *where):
    place = cols_of(x.shape) >> log2(lane)
    total = jnp.zeros_like(x)
    for value, at, to in where:
        shift = (to - at) * lane % 128
        moved = pltpu.roll(value, shift, 1) if shift else value
        total = jnp.where(place == to, moved, total)
    return total.astype(bf16)


def split(x):
    high = x.astype(bf16).astype(f32)
    return high, x - high


def tokens_kernel(
    heads,
    slices,
    own_ref,
    got_ref,
    w_cat_ref,
    w_out_ref,
    mw_ref,
    mixed_t_ref,
    dr_ref,
    drt_ref,
    dn_ref,
    grad_qkv_ref,
    pack,
):
    width = w_out_ref.shape[0]
    depth = width // heads
    hm = heads * slices
    place = group_place() & 1
    pack[place] = own_ref[...]
    pack[place ^ 1] = got_ref[...]
    per = 128 // depth

    def compact(first):
        pieces = []
        for h in range(heads):
            x = pack[h // per, first : first + slices, :]
            shift = (h % per) * depth
            pieces.append(pltpu.roll(x, 128 - shift, 1) if shift else x)
        x = jnp.concatenate(pieces, axis=0)
        return jnp.where(cols_of(x.shape) < depth, x, 0.0)

    raw = compact(0)
    d_mixed = compact(slices)
    norm = jnp.concatenate([pack[j, 2 * slices :, :].T[:, 0:1] for j in range(2)], axis=0)
    inverse = 1.0 / (norm + eps_norm)
    tokens = raw * inverse
    w_cat = w_cat_ref[...]

    t_high, rest = split(tokens)
    t_low, rest = split(rest)
    left = lanes_at(tokens, depth, (t_high, 0, 0), (t_low, 0, 1), (rest, 0, 2))
    blank = jnp.zeros((128 - 3 * depth, 128), bf16)
    qkv = nn(left, jnp.concatenate([w_cat, w_cat, w_cat, blank], axis=0))
    high, low = split(qkv)
    q_left = lanes_at(qkv, depth, (high, 0, 0), (high, 0, 1), (low, 0, 2))
    k_right = lanes_at(qkv, depth, (high, 1, 0), (low, 1, 1), (high, 1, 2))
    v_right = lanes_at(qkv, depth, (high, 2, 0), (low, 2, 1), (high, 2, 2))
    q_pair = lanes_at(qkv, depth, (high, 0, 0), (low, 0, 1))
    k_pair = lanes_at(qkv, depth, (high, 1, 0), (low, 1, 1))
    v_pair = lanes_at(qkv, depth, (high, 2, 0), (low, 2, 1))
    g_high, g_low = split(d_mixed)
    g_left = lanes_at(qkv, depth, (g_high, 0, 0), (g_high, 0, 1), (g_low, 0, 2))
    g_pair = lanes_at(qkv, depth, (g_high, 0, 0), (g_low, 0, 1))

    def times_pair(dot, x, pair):
        x_high, x_low = two_pieces(x)
        both = dot(x_high, pair)
        low_part = dot(x_low, pair)
        total = both + pltpu.roll(both, 128 - depth, 1) + low_part
        return jnp.where(cols_of(total.shape) < depth, total, 0.0)

    blocks = same_block(hm, hm, slices, slices)
    scale = 1.0 / math.sqrt(depth)
    scores = jnp.where(blocks, nt(q_left, k_right) * scale, -jnp.inf)
    expo = jnp.exp(scores - jnp.max(scores, axis=1, keepdims=True))
    probs = expo * (1.0 / jnp.sum(expo, axis=1, keepdims=True))
    mixed_b = times_pair(nn, probs, v_pair).astype(bf16)

    spread_d = jnp.where(
        (rows_of((width, 128)) & (depth - 1)) == cols_of((width, 128)), 1.0, 0.0
    ).astype(bf16)
    diagonal = same_block(hm, width, slices, depth)
    diagonal_t = same_block(width, hm, depth, slices)
    mixed_block = jnp.where(diagonal, nt(mixed_b, spread_d), 0.0).astype(bf16)
    mw_ref[...] = nn(mixed_block, w_out_ref[...]).astype(bf16)
    mixed_t_ref[...] = jnp.where(diagonal_t, nt(spread_d, mixed_b), 0.0).astype(bf16)

    d_probs = nt(g_left, v_right)
    d_v = times_pair(tn, probs, g_pair)
    d_scores = probs * (d_probs - jnp.sum(probs * d_probs, axis=1, keepdims=True)) * scale
    d_q = times_pair(nn, d_scores, k_pair)
    d_k = times_pair(tn, d_scores, q_pair)
    d_qkv = d_q + pltpu.roll(d_k, depth, 1) + pltpu.roll(d_v, 2 * depth, 1)
    d_high, d_low = two_pieces(d_qkv)
    d_tokens = nt(d_high, w_cat) + nt(d_low, w_cat)
    raw = raw[:, 0:depth]
    d_raw_b = (d_tokens * inverse).astype(bf16)
    d_norm = -jnp.sum(d_tokens * raw, axis=1, keepdims=True) * inverse * inverse
    dn_ref[...] = jnp.broadcast_to(d_norm, dn_ref.shape)
    spread_d = spread_matrix(width, depth)
    dr_ref[...] = jnp.where(diagonal, nt(d_raw_b, spread_d), 0.0).astype(bf16)
    drt_ref[...] = jnp.where(diagonal_t, nt(spread_d, d_raw_b), 0.0).astype(bf16)

    t_high, t_low = two_pieces(tokens)
    grads = tn(t_high, d_high) + tn(t_high, d_low) + tn(t_low, d_high)
    for i in range(3):
        at = pltpu.roll(grads, 128 - i * depth, 1) if i else grads
        grad_qkv_ref[i] = at[0:depth, 0:depth]


def backward_kernel(
    heads,
    slices,
    aux_ref,
    wt_ref,
    logits_ref,
    weights_ref,
    mid_ref,
    cot_ref,
    feats_ref,
    sb_ref,
    mw_ref,
    dr_ref,
    drt_ref,
    dn_ref,
    temp_ref,
    _,
    dmt_ref,
    send0,
    send1,
    send2,
    send3,
    yt,
    grad_acc,
    small_acc,
    pack,
):
    width = mid_ref.shape[1]
    depth = width // heads
    hm = heads * slices
    block = feats_ref.shape[0]

    grad_acc[...] = jnp.zeros_like(grad_acc)
    small_acc[...] = jnp.zeros_like(small_acc)
    yt[:, 0:hm] = drt_ref[...]
    yt[:, hm:] = sb_ref[...]

    temp = jnp.broadcast_to(temp_ref[...].astype(f32), (16, depth)).astype(bf16)
    same = (rows_of((depth, depth)) == cols_of((depth, depth))).astype(f32).astype(bf16)
    temp = nt(same, temp)[:, 0:1]
    piece = min(sub_block, block)
    pieces = [slice(i * piece, (i + 1) * piece) for i in range(block // piece)]

    def products(at):
        return nt(dr_ref[...], mid_ref[at, :]) + nt(mw_ref[...], cot_ref[at, :])

    def per_head(at, products):
        u_b, sums = [], []
        aux = aux_ref[:, at]
        for h in range(heads):
            span = slice(h * slices, (h + 1) * slices)
            inv_tau = aux[h : h + 1]
            logits = logits_ref[span, at]
            weights = weights_ref[span, at]
            d_weights = products[span] + dn_ref[span, 0:1]
            mean = jnp.sum(weights * d_weights, axis=0, keepdims=True)
            d_logits = weights * (d_weights - mean)
            d_tau = jnp.sum(d_logits * logits, axis=0, keepdims=True)
            sums.append(-d_tau * aux[2 * heads + h : 2 * heads + h + 1])
            u_b.append((d_logits * inv_tau).astype(bf16))
        c_sum = jnp.concatenate(sums, axis=0)
        c_high = c_sum.astype(bf16).astype(f32)
        u_b.append(jnp.concatenate([c_high, c_sum - c_high], axis=0).astype(bf16))
        return jnp.concatenate(u_b, axis=0), sums

    def outputs(at, u_b, sums):
        d_mid = nn(yt[...], jnp.concatenate([wt_ref[:, at], u_b[0:hm]], axis=0))
        d_mid = [
            (d_mid[h * depth : (h + 1) * depth] + temp * sums[h]).astype(bf16)
            for h in range(heads)
        ]
        d_mid = jnp.concatenate(d_mid, axis=0)
        dmt_ref[:, at] = d_mid
        grad_acc[...] += nn(d_mid, feats_ref[at, :])
        small_acc[...] += nn(u_b, mid_ref[at, :])

    ready = products(pieces[0])
    for i, at in enumerate(pieces):
        current = ready
        if i + 1 < len(pieces):
            ready = products(pieces[i + 1])
        outputs(at, *per_head(at, current))

    grad = grad_acc[...].T
    u_part = jnp.where(same_block(hm, width, slices, depth), small_acc[0:hm, :], 0.0)
    u_part = fold_rows(u_part, heads, slices)
    c_part = small_acc[hm : hm + heads, :] + small_acc[hm + heads : hm + 2 * heads, :]
    c_part = jnp.where(same_block(heads, width, 1, depth), c_part, 0.0)
    c_part = jnp.sum(c_part, axis=0, keepdims=True)

    def fold_lanes(x):
        total = x[:, 0:128]
        for j in range(1, width // 128):
            total = total + x[:, j * 128 : (j + 1) * 128]
        shift = 64
        while shift >= depth:
            total = total + pltpu.roll(total, shift, 1)
            shift //= 2
        return total

    u_part = fold_lanes(u_part)
    c_part = fold_lanes(jnp.broadcast_to(c_part, (slices, width)))
    where_lane = cols_of((slices, 128))
    extra = jnp.where(where_lane < depth, u_part, c_part)
    rows = width // group
    more = slices // group
    for j in range(group):
        pack[j, 0:rows, :] = grad[j * rows : (j + 1) * rows]
        pack[j, rows : rows + more, 0:128] = extra[j * more : (j + 1) * more]
        pack[j, rows : rows + more, 128:] = jnp.zeros((more, width - 128), f32)
    place = group_place()
    for k, send in enumerate((send0, send1, send2, send3)):
        send[...] = pack[place ^ k]


def rows_kernel(wt_ref, dmt_ref, mw_ref, w_mid_ref, _, attended_ref, feats_grad_ref, token_ref):
    block = attended_ref.shape[0]
    at = pl.ds(pl.multiple_of(pl.program_id(0) * block, block), block)
    token_ref[...] = jnp.zeros_like(token_ref)
    attended_ref[...] = tn(wt_ref[:, at], mw_ref[...]).astype(bf16)
    feats_grad_ref[...] = lax.dot_general(
        dmt_ref[:, at], w_mid_ref[...], (((0,), (1,)), ((), ())), preferred_element_type=f32
    ).astype(bf16)


def grad_out_kernel(own_ref, other_ref, mixed_t_ref, grad_out_ref, token_ref, whole):
    token_ref[...] = jnp.zeros_like(token_ref)
    place = group_place() & 1
    rows = own_ref.shape[0]
    for k, part in enumerate((own_ref, other_ref)):
        whole[pl.ds(pl.multiple_of((place ^ k) * rows, 8), rows), :] = part[...]
    high, low = two_pieces(whole[...])
    mixed_t = mixed_t_ref[...]
    grad_out_ref[...] = nn(mixed_t, high) + nn(mixed_t, low)


def finish_kernel(depth, m0, m1, m2, m3, grad_mid_ref, slice_ref, temp_ref, extra):
    place = group_place()
    slices = slice_ref.shape[1]
    more = slices // group
    rows = m0.shape[0] - more
    for k, part in enumerate((m0, m1, m2, m3)):
        at = pl.ds(pl.multiple_of((place ^ k) * rows, 8), rows)
        grad_mid_ref[at, :] = part[0:rows, :]
        extra[pl.ds(pl.multiple_of((place ^ k) * more, 8), more), :] = part[rows:, 0:128]
    turned = extra[...].T
    slice_ref[...] = turned[0:depth, 0:slices]
    temp_ref[...] = extra[0:1, depth : 2 * depth]


def full(shape):
    zeros = (0,) * len(shape)
    return pl.BlockSpec(shape, lambda *_: zeros)


def params(mebibytes, grid=True):
    semantics = ("arbitrary",) if grid else None
    return pltpu.CompilerParams(
        dimension_semantics=semantics, vmem_limit_bytes=mebibytes * mib
    )


def cost(flops, moved, transcendentals=0):
    return pl.CostEstimate(flops=flops, bytes_accessed=moved, transcendentals=transcendentals)


def exchange(x, k, count):
    return lax.ppermute(x, "node", [(i, i ^ k) for i in range(count)])


def sum_kernel(count, *refs):
    total = refs[0][...] + refs[count - 1][...]
    if count == 4:
        total = total + (refs[1][...] + refs[2][...])
    refs[-1][...] = total


def sum_behind(parts, *before):
    return pl.pallas_call(
        functools.partial(sum_kernel, len(parts)),
        out_shape=jax.ShapeDtypeStruct(parts[0].shape, f32),
        in_specs=[pl.BlockSpec(memory_space=pltpu.VMEM)] * len(parts)
        + [pl.BlockSpec(memory_space=pl.ANY)] * len(before),
        out_specs=pl.BlockSpec(memory_space=pltpu.VMEM),
        compiler_params=params(2, False),
        cost_estimate=cost(3 * parts[0].size, 5 * parts[0].size * 4),
    )(*parts, *before)


def scatter_group(parts, count):
    got = [parts[0]] + [exchange(parts[k], k, count) for k in range(1, group)]
    return (got[0] + got[1]) + (got[2] + got[3])


def sum_stage(total, stride, others, count, *before):
    parts = [total] + [exchange(total, stride * j, count) for j in range(others, 0, -1)]
    if before:
        return sum_behind(parts, *before)
    if others == 1:
        return parts[0] + parts[1]
    return (parts[0] + parts[3]) + (parts[1] + parts[2])


def sum_over_groups(total, stride, count, *before):
    while stride < count:
        others = 3 if count // stride % 4 == 0 else 1
        total = sum_stage(total, stride, others, count, *before)
        stride *= others + 1
    return total


def gather_group(total, count):
    return [total] + [exchange(total, k, count) for k in range(1, group)]


def shards(count, feats, cotangent, valid, owned, w_mid, w_slice, temp_vec, w_qkv, w_out):
    rows, width = feats.shape
    depth, slices = w_slice.shape
    heads = width // depth
    hm = heads * slices
    unit = 2 * rows * width * width
    smem = pl.BlockSpec(memory_space=pltpu.SMEM)

    def blocks(size):
        return (rows // size,), pl.BlockSpec((size, width), lambda i: (i, 0))

    def like(shape, dtype):
        return jax.ShapeDtypeStruct(shape, dtype)

    def far(x):
        return pltpu.with_memory_space_constraint(x, pltpu.HBM)

    near = pltpu.VMEM
    whole = pl.BlockSpec(memory_space=pltpu.VMEM)

    temp = temp_vec.reshape(1, depth)
    half = (2 * slices + 8, 128)
    wide = (hm // 2, width)
    inputs = (valid.reshape(1, rows), feats, cotangent, w_mid, w_slice, w_out)
    (
        mid,
        wt,
        aux,
        sw,
        keep,
        send,
        wc_keep,
        wc_send,
        feats_near,
        cot_near,
    ) = pl.pallas_call(
        functools.partial(stats_kernel, heads, slices),
        in_specs=[smem, whole] + [pl.BlockSpec(memory_space=pltpu.HBM)] * len(inputs),
        out_specs=[whole] * 10,
        out_shape=[
            near((rows, width), bf16),
            near((hm, rows), bf16),
            near((3 * heads, rows), f32),
            near((hm + 16, width), bf16),
            near(half, f32),
            near(half, f32),
            near(wide, f32),
            near(wide, f32),
            near((rows, width), bf16),
            near((rows, width), bf16),
        ],
        scratch_shapes=[
            pltpu.VMEM((1, rows), jnp.int32),
            pltpu.VMEM((width, width), bf16),
            pltpu.VMEM((depth, slices), bf16),
            pltpu.VMEM((width, width), bf16),
            pltpu.VMEM((hm, width), f32),
            pltpu.VMEM((hm, 128), f32),
            pltpu.VMEM((hm, width), f32),
            pltpu.VMEM((2,) + half, f32),
            pltpu.SemaphoreType.DMA((7,)),
        ],
        compiler_params=params(24, False),
        cost_estimate=cost(4 * unit, rows * width * 8, rows * hm),
    )(owned, far(temp), *map(far, inputs))

    own = keep + exchange(send, 1, count)
    wc_got = exchange(wc_send, 1, count)
    wc_sum = sum_behind([wc_keep, wc_got], own)
    logits, weights, sb, w_cat, token = pl.pallas_call(
        functools.partial(between_kernel, heads, slices),
        in_specs=[whole] * 5 + [pl.BlockSpec(memory_space=pl.ANY)],
        out_specs=[whole] * 5,
        out_shape=[
            near((hm, rows), f32),
            near((hm, rows), f32),
            near((width, hm), bf16),
            near((depth, 128), bf16),
            near((8, 128), f32),
        ],
        compiler_params=params(16, False),
        cost_estimate=cost(unit // 10, rows, rows),
    )(mid, sw, aux, w_slice, w_qkv, wc_sum)
    own = sum_stage(own, 2, 3, count)
    wc_got = exchange(wc_sum, 2, count)
    wc_sum = sum_behind([wc_sum, wc_got], own)
    own = sum_over_groups(own, 8, count, token)
    other = exchange(own, 1, count)
    stride = 4
    while stride < count // 2:
        wc_got = exchange(wc_sum, stride, count)
        stride *= 2
        if stride < count // 2:
            wc_sum = wc_sum + wc_got

    mw, mixed_t, dr, drt, dn, grad_qkv = pl.pallas_call(
        functools.partial(tokens_kernel, heads, slices),
        out_shape=[
            near((hm, width), bf16),
            near((width, hm), bf16),
            near((hm, width), bf16),
            near((width, hm), bf16),
            near((hm, 128), f32),
            like((3, depth, depth), f32),
        ],
        scratch_shapes=[pltpu.VMEM((2,) + half, f32)],
        compiler_params=params(16, False),
        cost_estimate=cost(100 * width**3, 4 * width * width * 4, hm * hm),
    )(own, other, w_cat, w_out)
    wc_sum = sum_behind([wc_sum, wc_got], mw)
    wc_got = exchange(wc_sum, count // 2, count)
    larger = (width // group + slices // group, width)
    dmt, *sends = pl.pallas_call(
        functools.partial(backward_kernel, heads, slices),
        in_specs=[whole] * 13 + [pl.BlockSpec(memory_space=pl.ANY)],
        out_specs=[whole] * (1 + group),
        out_shape=[near((width, rows), bf16)] + [near(larger, f32)] * group,
        scratch_shapes=[
            pltpu.VMEM((width, 2 * hm), bf16),
            pltpu.VMEM((width, width), f32),
            pltpu.VMEM((hm + 16, width), f32),
            pltpu.VMEM((group,) + larger, f32),
        ],
        compiler_params=params(24, False),
        cost_estimate=cost(unit, rows * width, rows),
    )(aux, wt, logits, weights, mid, cot_near, feats_near, sb, mw, dr, drt, dn, temp, wc_sum)

    mid_total = scatter_group(sends, count)
    wc_sum = sum_behind([wc_sum, wc_got], sends[1])
    wc_other = exchange(wc_sum, 1, count)

    block = min(1024, rows)
    grid, by_rows = blocks(block)
    attended, feats_grad, token = pl.pallas_call(
        rows_kernel,
        grid=grid,
        in_specs=[
            whole,
            whole,
            whole,
            full((width, width)),
            pl.BlockSpec(memory_space=pl.ANY),
        ],
        out_specs=[by_rows, by_rows, full((8, 128))],
        out_shape=[like((rows, width), bf16)] * 2 + [like((8, 128), f32)],
        compiler_params=params(20),
        cost_estimate=cost(2 * unit, rows * width * 8),
    )(wt, dmt, mw, w_mid, mid_total)

    grad_w_out, token_out = pl.pallas_call(
        grad_out_kernel,
        out_shape=[like((width, width), f32), like((8, 128), f32)],
        scratch_shapes=[pltpu.VMEM((hm, width), f32)],
        compiler_params=params(8, False),
        cost_estimate=cost(4 * width**3, 3 * width * width * 4),
    )(wc_sum, wc_other, mixed_t)
    mid_total = sum_over_groups(mid_total, group, count, token, token_out)

    mid_parts = gather_group(mid_total, count)
    grad_w_mid, grad_w_slice, grad_temp = pl.pallas_call(
        functools.partial(finish_kernel, depth),
        out_shape=[
            like((width, width), f32),
            like((depth, slices), f32),
            like((1, depth), f32),
        ],
        scratch_shapes=[pltpu.VMEM((slices, 128), f32)],
        compiler_params=params(8, False),
        cost_estimate=cost(0, 2 * width * width * 4),
    )(*mid_parts)
    return (
        attended,
        feats_grad,
        grad_w_mid,
        grad_w_out,
        grad_w_slice,
        grad_temp.reshape(depth),
        grad_qkv,
    )


def solution(mesh):
    in_specs = (
        P(("design", "node"), None),
        P(("design", "node"), None),
        P(("design", "node")),
        P(("design", "node")),
        P(),
        P(),
        P(),
        P(),
        P(),
    )
    out_specs = (
        P(("design", "node"), None),
        P(("design", "node"), None),
        P("design", None),
        P("design", None),
        P("design", None),
        P("design"),
        P("design", None, None),
    )
    return jax.shard_map(
        functools.partial(shards, mesh.shape["node"]),
        mesh=mesh,
        in_specs=in_specs,
        out_specs=out_specs,
        check_vma=False,
    )
```

```python
import functools
import math

import jax
import jax.numpy as jnp
from jax import lax
from jax.experimental import pallas as pl
from jax.experimental.pallas import tpu as pltpu
from jax.sharding import PartitionSpec as P

f32 = jnp.float32
bf16 = jnp.bfloat16
eps_norm = 1e-05
exact = lax.Precision.HIGHEST
group = 4
sub_block = 512
mib = 1024 * 1024


def nn(a, b, precision=None):
    return lax.dot_general(
        a, b, (((1,), (0,)), ((), ())), preferred_element_type=f32, precision=precision
    )


def nt(a, b, precision=None):
    return lax.dot_general(
        a, b, (((1,), (1,)), ((), ())), preferred_element_type=f32, precision=precision
    )


def tn(a, b, precision=None):
    return lax.dot_general(
        a, b, (((0,), (0,)), ((), ())), preferred_element_type=f32, precision=precision
    )


def log2(size):
    return size.bit_length() - 1


def rows_of(shape):
    return lax.broadcasted_iota(jnp.int32, shape, 0)


def cols_of(shape):
    return lax.broadcasted_iota(jnp.int32, shape, 1)


def spread_matrix(width, small):
    shape = (width, small)
    return jnp.where((rows_of(shape) & (small - 1)) == cols_of(shape), 1.0, 0.0).astype(bf16)


def same_block(rows, cols, row_size, col_size):
    shape = (rows, cols)
    return rows_of(shape) >> log2(row_size) == cols_of(shape) >> log2(col_size)


def two_pieces(x):
    high = x.astype(bf16)
    return high, (x - high.astype(f32)).astype(bf16)


def fold_rows(x, heads, size):
    total = x[0:size]
    for h in range(1, heads):
        total = total + x[h * size : (h + 1) * size]
    return total


def group_place():
    return lax.axis_index("node") % group


def stats_kernel(
    heads,
    slices,
    owned_ref,
    temp_ref,
    valid_far,
    feats_far,
    cot_far,
    w_mid_far,
    w_slice_far,
    w_out_far,
    mid_ref,
    wt_ref,
    aux_ref,
    sw_ref,
    keep_ref,
    send_ref,
    wc_keep_ref,
    wc_send_ref,
    feats_ref,
    cot_ref,
    valid_ref,
    w_mid_ref,
    w_slice_ref,
    w_out_ref,
    raw_acc,
    norm_acc,
    wc_acc,
    pack,
    sems,
):
    width = w_mid_ref.shape[0]
    depth = width // heads
    hm = heads * slices
    rows = feats_ref.shape[0]
    piece = min(sub_block, rows)
    count = rows // piece
    small = [
        pltpu.make_async_copy(source, target, sems.at[i])
        for i, (source, target) in enumerate(
            (
                (w_slice_far, w_slice_ref),
                (w_mid_far, w_mid_ref),
                (valid_far, valid_ref),
                (w_out_far, w_out_ref),
            )
        )
    ]
    first, rest = pl.ds(0, piece), pl.ds(piece, rows - piece)
    large = [
        pltpu.make_async_copy(source, target, sems.at[len(small) + i])
        for i, (source, target) in enumerate(
            (
                (feats_far.at[first, :], feats_ref.at[first, :]),
                (feats_far.at[rest, :], feats_ref.at[rest, :]),
                (cot_far, cot_ref),
            )
        )
    ]
    for copy in small[:2] + large[:1] + small[2:] + large[1:]:
        copy.start()

    raw_acc[...] = jnp.zeros_like(raw_acc)
    norm_acc[...] = jnp.zeros_like(norm_acc)
    wc_acc[...] = jnp.zeros_like(wc_acc)
    spread_d = spread_matrix(width, depth)
    spread_m = spread_matrix(hm, slices)
    for copy in small + large[:1]:
        copy.wait()
    temp = jnp.broadcast_to(temp_ref[...].astype(f32), (16, depth)).astype(bf16)
    half = nt(spread_m, w_slice_ref[...]).astype(bf16)
    full = nt(half, spread_d)
    sw_ref[0:hm, :] = jnp.where(same_block(hm, width, slices, depth), full, 0.0).astype(bf16)
    full = nt(temp, spread_d)
    sw_ref[hm : hm + 16, :] = jnp.where(same_block(16, width, 1, depth), full, 0.0).astype(bf16)
    owned = owned_ref[0]

    def products(i):
        at = slice(i * piece, (i + 1) * piece)
        mid = nn(feats_ref[at, :], w_mid_ref[...]).astype(bf16)
        mid_ref[at, :] = mid
        return mid, nt(sw_ref[...], mid)

    def statistics(i, mid, scores):
        at = slice(i * piece, (i + 1) * piece)
        zsum = scores[hm : hm + heads]
        small = jnp.exp(-jnp.abs(zsum))
        inv_tau = 1.0 / (0.5 + (jnp.maximum(zsum, 0.0) + jnp.log(1.0 + small)))
        sig = jnp.where(zsum >= 0.0, 1.0, small) / (1.0 + small)
        position = i * piece + cols_of((1, piece))
        live = (valid_ref[:, at] > 0) & (position < owned)
        live_f = live.astype(f32)
        rounded, sums, logs = [], [], []
        for h in range(heads):
            span = slice(h * slices, (h + 1) * slices)
            logits = scores[span] * inv_tau[h : h + 1]
            peak = jnp.max(logits, axis=0, keepdims=True)
            expo = jnp.exp(logits - peak)
            total = jnp.sum(expo, axis=0, keepdims=True)
            weights = expo * (live_f / total)
            rounded.append(weights.astype(bf16))
            lanes = weights[:, 0:128]
            for c in range(1, piece // 128):
                lanes = lanes + weights[:, c * 128 : (c + 1) * 128]
            sums.append(lanes)
            logs.append(jnp.where(live, peak + jnp.log(total), jnp.inf))
        wt = jnp.concatenate(rounded, axis=0)
        wt_ref[:, at] = wt
        norm_acc[...] += jnp.concatenate(sums, axis=0)
        aux_ref[:, at] = jnp.concatenate([inv_tau] + logs + [sig * inv_tau], axis=0)
        raw_acc[...] += nn(wt, mid)
        wc_acc[...] += nn(wt, cot_ref[at, :])

    ready = products(0)
    large[1].wait()
    large[2].wait()
    for i in range(count):
        current = ready
        if i + 1 < count:
            ready = products(i + 1)
        statistics(i, *current)

    diagonal = same_block(hm, width, slices, depth)
    raw = fold_rows(jnp.where(diagonal, raw_acc[...], 0.0), heads, slices)
    high, low = two_pieces(wc_acc[...])
    w_out = w_out_ref[...]
    mixed = nt(high, w_out) + nt(low, w_out)
    mixed = fold_rows(jnp.where(diagonal, mixed, 0.0), heads, slices)
    norm = jnp.sum(norm_acc[...].T, axis=0, keepdims=True)
    first = rows_of((8, 128)) == 0
    for j in range(2):
        part = slice(j * 128, (j + 1) * 128)
        pack[j, 0:slices, :] = raw[:, part]
        pack[j, slices : 2 * slices, :] = mixed[:, part]
        pack[j, 2 * slices :, :] = jnp.where(first, norm[:, part], 0.0)
    place = group_place()
    keep_ref[...] = pack[place & 1]
    send_ref[...] = pack[(place & 1) ^ 1]
    rows = hm // 2
    for k, out in enumerate((wc_keep_ref, wc_send_ref)):
        out[...] = wc_acc[pl.ds(pl.multiple_of(((place & 1) ^ k) * rows, 8), rows), :]


def between_kernel(
    heads,
    slices,
    mid_ref,
    sw_ref,
    aux_ref,
    w_slice_ref,
    w_qkv_ref,
    _,
    logits_ref,
    weights_ref,
    sb_ref,
    w_cat_ref,
    token_ref,
):
    depth = w_slice_ref.shape[0]
    width = heads * depth
    hm = heads * slices
    rows = mid_ref.shape[0]
    piece = min(sub_block, rows)
    token_ref[...] = jnp.zeros_like(token_ref)
    spread_d = spread_matrix(width, depth)
    spread_m = spread_matrix(hm, slices)
    half = nn(spread_d, w_slice_ref[...]).astype(bf16)
    full = nt(half, spread_m)
    sb_ref[...] = jnp.where(same_block(width, hm, depth, slices), full, 0.0).astype(bf16)
    w_cat = jnp.zeros((depth, 128), f32)
    for i in range(3):
        place_at = jnp.where(rows_of((depth, 128)) + i * depth == cols_of((depth, 128)), 1.0, 0.0)
        w_cat = w_cat + nn(w_qkv_ref[i], place_at.astype(bf16))
    w_cat_ref[...] = w_cat.astype(bf16)
    for i in range(rows // piece):
        at = slice(i * piece, (i + 1) * piece)
        scores = nt(sw_ref[0:hm, :], mid_ref[at, :])
        for h in range(heads):
            span = slice(h * slices, (h + 1) * slices)
            logits = scores[span] * aux_ref[h : h + 1, at]
            logits_ref[span, at] = logits
            weights_ref[span, at] = jnp.exp(logits - aux_ref[heads + h : heads + h + 1, at])


def lanes_at(x, lane, *where):
    place = cols_of(x.shape) >> log2(lane)
    total = jnp.zeros_like(x)
    for value, at, to in where:
        shift = (to - at) * lane % 128
        moved = pltpu.roll(value, shift, 1) if shift else value
        total = jnp.where(place == to, moved, total)
    return total.astype(bf16)


def split(x):
    high = x.astype(bf16).astype(f32)
    return high, x - high


def tokens_kernel(
    heads,
    slices,
    own_ref,
    got_ref,
    w_cat_ref,
    w_out_ref,
    mw_ref,
    mixed_t_ref,
    dr_ref,
    drt_ref,
    dn_ref,
    grad_qkv_ref,
    pack,
):
    width = w_out_ref.shape[0]
    depth = width // heads
    hm = heads * slices
    place = group_place() & 1
    pack[place] = own_ref[...]
    pack[place ^ 1] = got_ref[...]
    per = 128 // depth

    def compact(first):
        pieces = []
        for h in range(heads):
            x = pack[h // per, first : first + slices, :]
            shift = (h % per) * depth
            pieces.append(pltpu.roll(x, 128 - shift, 1) if shift else x)
        x = jnp.concatenate(pieces, axis=0)
        return jnp.where(cols_of(x.shape) < depth, x, 0.0)

    raw = compact(0)
    d_mixed = compact(slices)
    norm = jnp.concatenate([pack[j, 2 * slices :, :].T[:, 0:1] for j in range(2)], axis=0)
    inverse = 1.0 / (norm + eps_norm)
    tokens = raw * inverse
    w_cat = w_cat_ref[...]

    t_high, rest = split(tokens)
    t_low, rest = split(rest)
    left = lanes_at(tokens, depth, (t_high, 0, 0), (t_low, 0, 1), (rest, 0, 2))
    blank = jnp.zeros((128 - 3 * depth, 128), bf16)
    qkv = nn(left, jnp.concatenate([w_cat, w_cat, w_cat, blank], axis=0))
    high, low = split(qkv)
    q_left = lanes_at(qkv, depth, (high, 0, 0), (high, 0, 1), (low, 0, 2))
    k_right = lanes_at(qkv, depth, (high, 1, 0), (low, 1, 1), (high, 1, 2))
    v_right = lanes_at(qkv, depth, (high, 2, 0), (low, 2, 1), (high, 2, 2))
    q_pair = lanes_at(qkv, depth, (high, 0, 0), (low, 0, 1))
    k_pair = lanes_at(qkv, depth, (high, 1, 0), (low, 1, 1))
    v_pair = lanes_at(qkv, depth, (high, 2, 0), (low, 2, 1))
    g_high, g_low = split(d_mixed)
    g_left = lanes_at(qkv, depth, (g_high, 0, 0), (g_high, 0, 1), (g_low, 0, 2))
    g_pair = lanes_at(qkv, depth, (g_high, 0, 0), (g_low, 0, 1))

    def times_pair(dot, x, pair):
        x_high, x_low = two_pieces(x)
        both = dot(x_high, pair)
        low_part = dot(x_low, pair)
        total = both + pltpu.roll(both, 128 - depth, 1) + low_part
        return jnp.where(cols_of(total.shape) < depth, total, 0.0)

    blocks = same_block(hm, hm, slices, slices)
    scale = 1.0 / math.sqrt(depth)
    scores = jnp.where(blocks, nt(q_left, k_right) * scale, -jnp.inf)
    expo = jnp.exp(scores - jnp.max(scores, axis=1, keepdims=True))
    probs = expo * (1.0 / jnp.sum(expo, axis=1, keepdims=True))
    mixed_b = times_pair(nn, probs, v_pair).astype(bf16)

    spread_d = jnp.where(
        (rows_of((width, 128)) & (depth - 1)) == cols_of((width, 128)), 1.0, 0.0
    ).astype(bf16)
    diagonal = same_block(hm, width, slices, depth)
    diagonal_t = same_block(width, hm, depth, slices)
    mixed_block = jnp.where(diagonal, nt(mixed_b, spread_d), 0.0).astype(bf16)
    mw_ref[...] = nn(mixed_block, w_out_ref[...]).astype(bf16)
    mixed_t_ref[...] = jnp.where(diagonal_t, nt(spread_d, mixed_b), 0.0).astype(bf16)

    d_probs = nt(g_left, v_right)
    d_v = times_pair(tn, probs, g_pair)
    d_scores = probs * (d_probs - jnp.sum(probs * d_probs, axis=1, keepdims=True)) * scale
    d_q = times_pair(nn, d_scores, k_pair)
    d_k = times_pair(tn, d_scores, q_pair)
    d_qkv = d_q + pltpu.roll(d_k, depth, 1) + pltpu.roll(d_v, 2 * depth, 1)
    d_high, d_low = two_pieces(d_qkv)
    d_tokens = nt(d_high, w_cat) + nt(d_low, w_cat)
    raw = raw[:, 0:depth]
    d_raw_b = (d_tokens * inverse).astype(bf16)
    d_norm = -jnp.sum(d_tokens * raw, axis=1, keepdims=True) * inverse * inverse
    dn_ref[...] = jnp.broadcast_to(d_norm, dn_ref.shape)
    spread_d = spread_matrix(width, depth)
    dr_ref[...] = jnp.where(diagonal, nt(d_raw_b, spread_d), 0.0).astype(bf16)
    drt_ref[...] = jnp.where(diagonal_t, nt(spread_d, d_raw_b), 0.0).astype(bf16)

    t_high, t_low = two_pieces(tokens)
    grads = tn(t_high, d_high) + tn(t_high, d_low) + tn(t_low, d_high)
    for i in range(3):
        at = pltpu.roll(grads, 128 - i * depth, 1) if i else grads
        grad_qkv_ref[i] = at[0:depth, 0:depth]


def backward_kernel(
    heads,
    slices,
    aux_ref,
    wt_ref,
    logits_ref,
    weights_ref,
    mid_ref,
    cot_ref,
    feats_ref,
    sb_ref,
    mw_ref,
    dr_ref,
    drt_ref,
    dn_ref,
    temp_ref,
    _,
    dmt_ref,
    send0,
    send1,
    send2,
    send3,
    yt,
    grad_acc,
    small_acc,
    pack,
):
    width = mid_ref.shape[1]
    depth = width // heads
    hm = heads * slices
    block = feats_ref.shape[0]

    grad_acc[...] = jnp.zeros_like(grad_acc)
    small_acc[...] = jnp.zeros_like(small_acc)
    yt[:, 0:hm] = drt_ref[...]
    yt[:, hm:] = sb_ref[...]

    temp = jnp.broadcast_to(temp_ref[...].astype(f32), (16, depth)).astype(bf16)
    same = (rows_of((depth, depth)) == cols_of((depth, depth))).astype(f32).astype(bf16)
    temp = nt(same, temp)[:, 0:1]
    piece = min(sub_block, block)
    pieces = [slice(i * piece, (i + 1) * piece) for i in range(block // piece)]

    def products(at):
        return nt(dr_ref[...], mid_ref[at, :]) + nt(mw_ref[...], cot_ref[at, :])

    def per_head(at, products):
        u_b, sums = [], []
        aux = aux_ref[:, at]
        for h in range(heads):
            span = slice(h * slices, (h + 1) * slices)
            inv_tau = aux[h : h + 1]
            logits = logits_ref[span, at]
            weights = weights_ref[span, at]
            d_weights = products[span] + dn_ref[span, 0:1]
            mean = jnp.sum(weights * d_weights, axis=0, keepdims=True)
            d_logits = weights * (d_weights - mean)
            d_tau = jnp.sum(d_logits * logits, axis=0, keepdims=True)
            sums.append(-d_tau * aux[2 * heads + h : 2 * heads + h + 1])
            u_b.append((d_logits * inv_tau).astype(bf16))
        c_sum = jnp.concatenate(sums, axis=0)
        c_high = c_sum.astype(bf16).astype(f32)
        u_b.append(jnp.concatenate([c_high, c_sum - c_high], axis=0).astype(bf16))
        return jnp.concatenate(u_b, axis=0), sums

    def outputs(at, u_b, sums):
        d_mid = nn(yt[...], jnp.concatenate([wt_ref[:, at], u_b[0:hm]], axis=0))
        d_mid = [
            (d_mid[h * depth : (h + 1) * depth] + temp * sums[h]).astype(bf16)
            for h in range(heads)
        ]
        d_mid = jnp.concatenate(d_mid, axis=0)
        dmt_ref[:, at] = d_mid
        grad_acc[...] += nn(d_mid, feats_ref[at, :])
        small_acc[...] += nn(u_b, mid_ref[at, :])

    ready = products(pieces[0])
    for i, at in enumerate(pieces):
        current = ready
        if i + 1 < len(pieces):
            ready = products(pieces[i + 1])
        outputs(at, *per_head(at, current))

    grad = grad_acc[...].T
    u_part = jnp.where(same_block(hm, width, slices, depth), small_acc[0:hm, :], 0.0)
    u_part = fold_rows(u_part, heads, slices)
    c_part = small_acc[hm : hm + heads, :] + small_acc[hm + heads : hm + 2 * heads, :]
    c_part = jnp.where(same_block(heads, width, 1, depth), c_part, 0.0)
    c_part = jnp.sum(c_part, axis=0, keepdims=True)

    def fold_lanes(x):
        total = x[:, 0:128]
        for j in range(1, width // 128):
            total = total + x[:, j * 128 : (j + 1) * 128]
        shift = 64
        while shift >= depth:
            total = total + pltpu.roll(total, shift, 1)
            shift //= 2
        return total

    u_part = fold_lanes(u_part)
    c_part = fold_lanes(jnp.broadcast_to(c_part, (slices, width)))
    where_lane = cols_of((slices, 128))
    extra = jnp.where(where_lane < depth, u_part, c_part)
    rows = width // group
    more = slices // group
    for j in range(group):
        pack[j, 0:rows, :] = grad[j * rows : (j + 1) * rows]
        pack[j, rows : rows + more, 0:128] = extra[j * more : (j + 1) * more]
        pack[j, rows : rows + more, 128:] = jnp.zeros((more, width - 128), f32)
    place = group_place()
    for k, send in enumerate((send0, send1, send2, send3)):
        send[...] = pack[place ^ k]


def rows_kernel(wt_ref, dmt_ref, mw_ref, w_mid_ref, _, attended_ref, feats_grad_ref, token_ref):
    block = attended_ref.shape[0]
    at = pl.ds(pl.multiple_of(pl.program_id(0) * block, block), block)
    token_ref[...] = jnp.zeros_like(token_ref)
    attended_ref[...] = tn(wt_ref[:, at], mw_ref[...]).astype(bf16)
    feats_grad_ref[...] = lax.dot_general(
        dmt_ref[:, at], w_mid_ref[...], (((0,), (1,)), ((), ())), preferred_element_type=f32
    ).astype(bf16)


def grad_out_kernel(own_ref, other_ref, mixed_t_ref, _, grad_out_ref, token_ref, whole):
    token_ref[...] = jnp.zeros_like(token_ref)
    place = group_place() & 1
    rows = own_ref.shape[0]
    for k, part in enumerate((own_ref, other_ref)):
        whole[pl.ds(pl.multiple_of((place ^ k) * rows, 8), rows), :] = part[...]
    high, low = two_pieces(whole[...])
    mixed_t = mixed_t_ref[...]
    grad_out_ref[...] = nn(mixed_t, high) + nn(mixed_t, low)


def finish_kernel(depth, m0, m1, m2, m3, _, grad_mid_ref, slice_ref, temp_ref, extra):
    place = group_place()
    slices = slice_ref.shape[1]
    more = slices // group
    rows = m0.shape[0] - more
    for k, part in enumerate((m0, m1, m2, m3)):
        at = pl.ds(pl.multiple_of((place ^ k) * rows, 8), rows)
        grad_mid_ref[at, :] = part[0:rows, :]
        extra[pl.ds(pl.multiple_of((place ^ k) * more, 8), more), :] = part[rows:, 0:128]
    turned = extra[...].T
    slice_ref[...] = turned[0:depth, 0:slices]
    temp_ref[...] = extra[0:1, depth : 2 * depth]


def full(shape):
    zeros = (0,) * len(shape)
    return pl.BlockSpec(shape, lambda *_: zeros)


def params(mebibytes, grid=True):
    semantics = ("arbitrary",) if grid else None
    return pltpu.CompilerParams(
        dimension_semantics=semantics, vmem_limit_bytes=mebibytes * mib
    )


def cost(flops, moved, transcendentals=0):
    return pl.CostEstimate(flops=flops, bytes_accessed=moved, transcendentals=transcendentals)


def exchange(x, k, count):
    return lax.ppermute(x, "node", [(i, i ^ k) for i in range(count)])


def sum_kernel(count, *refs):
    total = refs[0][...] + refs[count - 1][...]
    if count == 4:
        total = total + (refs[1][...] + refs[2][...])
    refs[-1][...] = total


def sum_behind(parts, *before):
    return pl.pallas_call(
        functools.partial(sum_kernel, len(parts)),
        out_shape=jax.ShapeDtypeStruct(parts[0].shape, f32),
        in_specs=[pl.BlockSpec(memory_space=pltpu.VMEM)] * len(parts)
        + [pl.BlockSpec(memory_space=pl.ANY)] * len(before),
        out_specs=pl.BlockSpec(memory_space=pltpu.VMEM),
        compiler_params=params(2, False),
        cost_estimate=cost(3 * parts[0].size, 5 * parts[0].size * 4),
    )(*parts, *before)


def scatter_group(parts, count):
    got = [parts[0]] + [exchange(parts[k], k, count) for k in range(1, group)]
    return (got[0] + got[1]) + (got[2] + got[3])


def sum_stage(total, stride, others, count, *before):
    parts = [total] + [exchange(total, stride * j, count) for j in range(others, 0, -1)]
    if before:
        return sum_behind(parts, *before)
    if others == 1:
        return parts[0] + parts[1]
    return (parts[0] + parts[3]) + (parts[1] + parts[2])


def sum_over_groups(total, stride, count, *before):
    while stride < count:
        others = 3 if count // stride % 4 == 0 else 1
        total = sum_stage(total, stride, others, count, *before)
        stride *= others + 1
    return total


def gather_group(total, count):
    return [total] + [exchange(total, k, count) for k in range(1, group)]


def shards(count, feats, cotangent, valid, owned, w_mid, w_slice, temp_vec, w_qkv, w_out):
    rows, width = feats.shape
    depth, slices = w_slice.shape
    heads = width // depth
    hm = heads * slices
    unit = 2 * rows * width * width
    smem = pl.BlockSpec(memory_space=pltpu.SMEM)

    def blocks(size):
        return (rows // size,), pl.BlockSpec((size, width), lambda i: (i, 0))

    def like(shape, dtype):
        return jax.ShapeDtypeStruct(shape, dtype)

    def far(x):
        return pltpu.with_memory_space_constraint(x, pltpu.HBM)

    near = pltpu.VMEM
    whole = pl.BlockSpec(memory_space=pltpu.VMEM)

    temp = temp_vec.reshape(1, depth)
    half = (2 * slices + 8, 128)
    wide = (hm // 2, width)
    inputs = (valid.reshape(1, rows), feats, cotangent, w_mid, w_slice, w_out)
    (
        mid,
        wt,
        aux,
        sw,
        keep,
        send,
        wc_keep,
        wc_send,
        feats_near,
        cot_near,
    ) = pl.pallas_call(
        functools.partial(stats_kernel, heads, slices),
        in_specs=[smem, whole] + [pl.BlockSpec(memory_space=pltpu.HBM)] * len(inputs),
        out_specs=[whole] * 10,
        out_shape=[
            near((rows, width), bf16),
            near((hm, rows), bf16),
            near((3 * heads, rows), f32),
            near((hm + 16, width), bf16),
            near(half, f32),
            near(half, f32),
            near(wide, f32),
            near(wide, f32),
            near((rows, width), bf16),
            near((rows, width), bf16),
        ],
        scratch_shapes=[
            pltpu.VMEM((1, rows), jnp.int32),
            pltpu.VMEM((width, width), bf16),
            pltpu.VMEM((depth, slices), bf16),
            pltpu.VMEM((width, width), bf16),
            pltpu.VMEM((hm, width), f32),
            pltpu.VMEM((hm, 128), f32),
            pltpu.VMEM((hm, width), f32),
            pltpu.VMEM((2,) + half, f32),
            pltpu.SemaphoreType.DMA((7,)),
        ],
        compiler_params=params(24, False),
        cost_estimate=cost(4 * unit, rows * width * 8, rows * hm),
    )(owned, far(temp), *map(far, inputs))

    own = keep + exchange(send, 1, count)
    wc_got = exchange(wc_send, 1, count)
    wc_sum = sum_behind([wc_keep, wc_got], own)
    logits, weights, sb, w_cat, token = pl.pallas_call(
        functools.partial(between_kernel, heads, slices),
        in_specs=[whole] * 5 + [pl.BlockSpec(memory_space=pl.ANY)],
        out_specs=[whole] * 5,
        out_shape=[
            near((hm, rows), f32),
            near((hm, rows), f32),
            near((width, hm), bf16),
            near((depth, 128), bf16),
            near((8, 128), f32),
        ],
        compiler_params=params(16, False),
        cost_estimate=cost(unit // 10, rows, rows),
    )(mid, sw, aux, w_slice, w_qkv, wc_sum)
    own = sum_stage(own, 2, 3, count)
    wc_got = exchange(wc_sum, count // 2, count)
    wc_sum = sum_behind([wc_sum, wc_got], own)
    own = sum_over_groups(own, 8, count, token)
    other = exchange(own, 1, count)
    wc_got = exchange(wc_sum, 2, count)
    stride = 8
    while stride < count // 2:
        wc_sum = wc_sum + wc_got
        wc_got = exchange(wc_sum, stride, count)
        stride *= 2

    mw, mixed_t, dr, drt, dn, grad_qkv = pl.pallas_call(
        functools.partial(tokens_kernel, heads, slices),
        out_shape=[
            near((hm, width), bf16),
            near((width, hm), bf16),
            near((hm, width), bf16),
            near((width, hm), bf16),
            near((hm, 128), f32),
            like((3, depth, depth), f32),
        ],
        scratch_shapes=[pltpu.VMEM((2,) + half, f32)],
        compiler_params=params(16, False),
        cost_estimate=cost(30 * width**3, 4 * width * width * 4, hm * hm),
    )(own, other, w_cat, w_out)
    larger = (width // group + slices // group, width)
    dmt, *sends = pl.pallas_call(
        functools.partial(backward_kernel, heads, slices),
        in_specs=[whole] * 13 + [pl.BlockSpec(memory_space=pl.ANY)],
        out_specs=[whole] * (1 + group),
        out_shape=[near((width, rows), bf16)] + [near(larger, f32)] * group,
        scratch_shapes=[
            pltpu.VMEM((width, 2 * hm), bf16),
            pltpu.VMEM((width, width), f32),
            pltpu.VMEM((hm + 16, width), f32),
            pltpu.VMEM((group,) + larger, f32),
        ],
        compiler_params=params(24, False),
        cost_estimate=cost(unit, rows * width, rows),
    )(aux, wt, logits, weights, mid, cot_near, feats_near, sb, mw, dr, drt, dn, temp, wc_sum)

    mid_total = scatter_group(sends, count)
    wc_sum = sum_behind([wc_sum, wc_got], sends[1])
    wc_got = exchange(wc_sum, 4, count)

    block = min(1024, rows)
    grid, by_rows = blocks(block)
    attended, feats_grad, token = pl.pallas_call(
        rows_kernel,
        grid=grid,
        in_specs=[
            whole,
            whole,
            whole,
            full((width, width)),
            pl.BlockSpec(memory_space=pl.ANY),
        ],
        out_specs=[by_rows, by_rows, full((8, 128))],
        out_shape=[like((rows, width), bf16)] * 2 + [like((8, 128), f32)],
        compiler_params=params(20),
        cost_estimate=cost(2 * unit, rows * width * 8),
    )(wt, dmt, mw, w_mid, mid_total)

    wc_sum = sum_behind([wc_sum, wc_got], token)
    wc_other = exchange(wc_sum, 1, count)
    mid_total = sum_over_groups(mid_total, group, count, token)
    grad_w_out, token_out = pl.pallas_call(
        grad_out_kernel,
        in_specs=[whole] * 3 + [pl.BlockSpec(memory_space=pl.ANY)],
        out_specs=[whole] * 2,
        out_shape=[like((width, width), f32), like((8, 128), f32)],
        scratch_shapes=[pltpu.VMEM((hm, width), f32)],
        compiler_params=params(8, False),
        cost_estimate=cost(4 * width**3, 3 * width * width * 4),
    )(wc_sum, wc_other, mixed_t, mid_total)

    mid_parts = gather_group(mid_total, count)
    grad_w_mid, grad_w_slice, grad_temp = pl.pallas_call(
        functools.partial(finish_kernel, depth),
        in_specs=[whole] * group + [pl.BlockSpec(memory_space=pl.ANY)],
        out_specs=[whole] * 3,
        out_shape=[
            like((width, width), f32),
            like((depth, slices), f32),
            like((1, depth), f32),
        ],
        scratch_shapes=[pltpu.VMEM((slices, 128), f32)],
        compiler_params=params(8, False),
        cost_estimate=cost(0, 2 * width * width * 4),
    )(*mid_parts, token_out)
    return (
        attended,
        feats_grad,
        grad_w_mid,
        grad_w_out,
        grad_w_slice,
        grad_temp.reshape(depth),
        grad_qkv,
    )


def solution(mesh):
    in_specs = (
        P(("design", "node"), None),
        P(("design", "node"), None),
        P(("design", "node")),
        P(("design", "node")),
        P(),
        P(),
        P(),
        P(),
        P(),
    )
    out_specs = (
        P(("design", "node"), None),
        P(("design", "node"), None),
        P("design", None),
        P("design", None),
        P("design", None),
        P("design"),
        P("design", None, None),
    )
    return jax.shard_map(
        functools.partial(shards, mesh.shape["node"]),
        mesh=mesh,
        in_specs=in_specs,
        out_specs=out_specs,
        check_vma=False,
    )
```

```python
import functools
import math

import jax
import jax.numpy as jnp
from jax import lax
from jax.experimental import pallas as pl
from jax.experimental.pallas import tpu as pltpu
from jax.sharding import PartitionSpec as P

f32 = jnp.float32
bf16 = jnp.bfloat16
eps_norm = 1e-05
exact = lax.Precision.HIGHEST
group = 4
sub_block = 512
mib = 1024 * 1024


def nn(a, b, precision=None):
    return lax.dot_general(
        a, b, (((1,), (0,)), ((), ())), preferred_element_type=f32, precision=precision
    )


def nt(a, b, precision=None):
    return lax.dot_general(
        a, b, (((1,), (1,)), ((), ())), preferred_element_type=f32, precision=precision
    )


def tn(a, b, precision=None):
    return lax.dot_general(
        a, b, (((0,), (0,)), ((), ())), preferred_element_type=f32, precision=precision
    )


def log2(size):
    return size.bit_length() - 1


def rows_of(shape):
    return lax.broadcasted_iota(jnp.int32, shape, 0)


def cols_of(shape):
    return lax.broadcasted_iota(jnp.int32, shape, 1)


def spread_matrix(width, small):
    shape = (width, small)
    return jnp.where((rows_of(shape) & (small - 1)) == cols_of(shape), 1.0, 0.0).astype(bf16)


def same_block(rows, cols, row_size, col_size):
    shape = (rows, cols)
    return rows_of(shape) >> log2(row_size) == cols_of(shape) >> log2(col_size)


def two_pieces(x):
    high = x.astype(bf16)
    return high, (x - high.astype(f32)).astype(bf16)


def fold_rows(x, heads, size):
    total = x[0:size]
    for h in range(1, heads):
        total = total + x[h * size : (h + 1) * size]
    return total


def group_place():
    return lax.axis_index("node") % group


def stats_kernel(
    heads,
    slices,
    owned_ref,
    temp_ref,
    valid_far,
    feats_far,
    cot_far,
    w_mid_far,
    w_slice_far,
    w_out_far,
    mid_ref,
    wt_ref,
    aux_ref,
    sw_ref,
    keep_ref,
    send_ref,
    wc_keep_ref,
    wc_send_ref,
    feats_ref,
    cot_ref,
    valid_ref,
    w_mid_ref,
    w_slice_ref,
    w_out_ref,
    raw_acc,
    norm_acc,
    wc_acc,
    pack,
    sems,
):
    width = w_mid_ref.shape[0]
    depth = width // heads
    hm = heads * slices
    rows = feats_ref.shape[0]
    piece = min(sub_block, rows)
    count = rows // piece
    small = [
        pltpu.make_async_copy(source, target, sems.at[i])
        for i, (source, target) in enumerate(
            (
                (w_slice_far, w_slice_ref),
                (w_mid_far, w_mid_ref),
                (valid_far, valid_ref),
                (w_out_far, w_out_ref),
            )
        )
    ]
    first, rest = pl.ds(0, piece), pl.ds(piece, rows - piece)
    large = [
        pltpu.make_async_copy(source, target, sems.at[len(small) + i])
        for i, (source, target) in enumerate(
            (
                (feats_far.at[first, :], feats_ref.at[first, :]),
                (feats_far.at[rest, :], feats_ref.at[rest, :]),
                (cot_far, cot_ref),
            )
        )
    ]
    for copy in small[:2] + large[:1] + small[2:] + large[1:]:
        copy.start()

    raw_acc[...] = jnp.zeros_like(raw_acc)
    norm_acc[...] = jnp.zeros_like(norm_acc)
    wc_acc[...] = jnp.zeros_like(wc_acc)
    spread_d = spread_matrix(width, depth)
    spread_m = spread_matrix(hm, slices)
    for copy in small + large[:1]:
        copy.wait()
    temp = jnp.broadcast_to(temp_ref[...].astype(f32), (16, depth)).astype(bf16)
    half = nt(spread_m, w_slice_ref[...]).astype(bf16)
    full = nt(half, spread_d)
    sw_ref[0:hm, :] = jnp.where(same_block(hm, width, slices, depth), full, 0.0).astype(bf16)
    full = nt(temp, spread_d)
    sw_ref[hm : hm + 16, :] = jnp.where(same_block(16, width, 1, depth), full, 0.0).astype(bf16)
    owned = owned_ref[0]

    def products(i):
        at = slice(i * piece, (i + 1) * piece)
        mid = nn(feats_ref[at, :], w_mid_ref[...]).astype(bf16)
        mid_ref[at, :] = mid
        return mid, nt(sw_ref[...], mid)

    def statistics(i, mid, scores):
        at = slice(i * piece, (i + 1) * piece)
        zsum = scores[hm : hm + heads]
        small = jnp.exp(-jnp.abs(zsum))
        inv_tau = 1.0 / (0.5 + (jnp.maximum(zsum, 0.0) + jnp.log(1.0 + small)))
        sig = jnp.where(zsum >= 0.0, 1.0, small) / (1.0 + small)
        position = i * piece + cols_of((1, piece))
        live = (valid_ref[:, at] > 0) & (position < owned)
        live_f = live.astype(f32)
        rounded, sums, logs = [], [], []
        for h in range(heads):
            span = slice(h * slices, (h + 1) * slices)
            logits = scores[span] * inv_tau[h : h + 1]
            peak = jnp.max(logits, axis=0, keepdims=True)
            expo = jnp.exp(logits - peak)
            total = jnp.sum(expo, axis=0, keepdims=True)
            weights = expo * (live_f / total)
            rounded.append(weights.astype(bf16))
            lanes = weights[:, 0:128]
            for c in range(1, piece // 128):
                lanes = lanes + weights[:, c * 128 : (c + 1) * 128]
            sums.append(lanes)
            logs.append(jnp.where(live, peak + jnp.log(total), jnp.inf))
        wt = jnp.concatenate(rounded, axis=0)
        wt_ref[:, at] = wt
        norm_acc[...] += jnp.concatenate(sums, axis=0)
        aux_ref[:, at] = jnp.concatenate([inv_tau] + logs + [sig * inv_tau], axis=0)
        raw_acc[...] += nn(wt, mid)
        wc_acc[...] += nn(wt, cot_ref[at, :])

    ready = products(0)
    large[1].wait()
    large[2].wait()
    for i in range(count):
        current = ready
        if i + 1 < count:
            ready = products(i + 1)
        statistics(i, *current)

    diagonal = same_block(hm, width, slices, depth)
    raw = fold_rows(jnp.where(diagonal, raw_acc[...], 0.0), heads, slices)
    high, low = two_pieces(wc_acc[...])
    w_out = w_out_ref[...]
    mixed = nt(high, w_out) + nt(low, w_out)
    mixed = fold_rows(jnp.where(diagonal, mixed, 0.0), heads, slices)
    norm = jnp.sum(norm_acc[...].T, axis=0, keepdims=True)
    first = rows_of((8, 128)) == 0
    for j in range(2):
        part = slice(j * 128, (j + 1) * 128)
        pack[j, 0:slices, :] = raw[:, part]
        pack[j, slices : 2 * slices, :] = mixed[:, part]
        pack[j, 2 * slices :, :] = jnp.where(first, norm[:, part], 0.0)
    place = group_place()
    keep_ref[...] = pack[place & 1]
    send_ref[...] = pack[(place & 1) ^ 1]
    rows = hm // 2
    for k, out in enumerate((wc_keep_ref, wc_send_ref)):
        out[...] = wc_acc[pl.ds(pl.multiple_of(((place & 1) ^ k) * rows, 8), rows), :]


def between_kernel(
    heads,
    slices,
    mid_ref,
    sw_ref,
    aux_ref,
    w_slice_ref,
    w_qkv_ref,
    _,
    logits_ref,
    weights_ref,
    sb_ref,
    w_cat_ref,
    token_ref,
):
    depth = w_slice_ref.shape[0]
    width = heads * depth
    hm = heads * slices
    rows = mid_ref.shape[0]
    piece = min(sub_block, rows)
    token_ref[...] = jnp.zeros_like(token_ref)
    spread_d = spread_matrix(width, depth)
    spread_m = spread_matrix(hm, slices)
    half = nn(spread_d, w_slice_ref[...]).astype(bf16)
    full = nt(half, spread_m)
    sb_ref[...] = jnp.where(same_block(width, hm, depth, slices), full, 0.0).astype(bf16)
    w_cat = jnp.zeros((depth, 128), f32)
    for i in range(3):
        place_at = jnp.where(rows_of((depth, 128)) + i * depth == cols_of((depth, 128)), 1.0, 0.0)
        w_cat = w_cat + nn(w_qkv_ref[i], place_at.astype(bf16))
    w_cat_ref[...] = w_cat.astype(bf16)
    for i in range(rows // piece):
        at = slice(i * piece, (i + 1) * piece)
        scores = nt(sw_ref[0:hm, :], mid_ref[at, :])
        for h in range(heads):
            span = slice(h * slices, (h + 1) * slices)
            logits = scores[span] * aux_ref[h : h + 1, at]
            logits_ref[span, at] = logits
            weights_ref[span, at] = jnp.exp(logits - aux_ref[heads + h : heads + h + 1, at])


def lanes_at(x, lane, *where):
    place = cols_of(x.shape) >> log2(lane)
    total = jnp.zeros_like(x)
    for value, at, to in where:
        shift = (to - at) * lane % 128
        moved = pltpu.roll(value, shift, 1) if shift else value
        total = jnp.where(place == to, moved, total)
    return total.astype(bf16)


def split(x):
    high = x.astype(bf16).astype(f32)
    return high, x - high


def tokens_kernel(
    heads,
    slices,
    own_ref,
    got_ref,
    w_cat_ref,
    w_out_ref,
    mw_ref,
    mixed_t_ref,
    dr_ref,
    drt_ref,
    dn_ref,
    grad_qkv_ref,
    pack,
):
    width = w_out_ref.shape[0]
    depth = width // heads
    hm = heads * slices
    place = group_place() & 1
    pack[place] = own_ref[...]
    pack[place ^ 1] = got_ref[...]
    per = 128 // depth

    def compact(first):
        pieces = []
        for h in range(heads):
            x = pack[h // per, first : first + slices, :]
            shift = (h % per) * depth
            pieces.append(pltpu.roll(x, 128 - shift, 1) if shift else x)
        x = jnp.concatenate(pieces, axis=0)
        return jnp.where(cols_of(x.shape) < depth, x, 0.0)

    raw = compact(0)
    d_mixed = compact(slices)
    norm = jnp.concatenate([pack[j, 2 * slices :, :].T[:, 0:1] for j in range(2)], axis=0)
    inverse = 1.0 / (norm + eps_norm)
    tokens = raw * inverse
    w_cat = w_cat_ref[...]

    t_high, rest = split(tokens)
    t_low, rest = split(rest)
    left = lanes_at(tokens, depth, (t_high, 0, 0), (t_low, 0, 1), (rest, 0, 2))
    blank = jnp.zeros((128 - 3 * depth, 128), bf16)
    qkv = nn(left, jnp.concatenate([w_cat, w_cat, w_cat, blank], axis=0))
    high, low = split(qkv)
    q_left = lanes_at(qkv, depth, (high, 0, 0), (high, 0, 1), (low, 0, 2))
    k_right = lanes_at(qkv, depth, (high, 1, 0), (low, 1, 1), (high, 1, 2))
    v_right = lanes_at(qkv, depth, (high, 2, 0), (low, 2, 1), (high, 2, 2))
    q_pair = lanes_at(qkv, depth, (high, 0, 0), (low, 0, 1))
    k_pair = lanes_at(qkv, depth, (high, 1, 0), (low, 1, 1))
    v_pair = lanes_at(qkv, depth, (high, 2, 0), (low, 2, 1))
    g_high, g_low = split(d_mixed)
    g_left = lanes_at(qkv, depth, (g_high, 0, 0), (g_high, 0, 1), (g_low, 0, 2))
    g_pair = lanes_at(qkv, depth, (g_high, 0, 0), (g_low, 0, 1))

    def times_pair(dot, x, pair):
        x_high, x_low = two_pieces(x)
        both = dot(x_high, pair)
        low_part = dot(x_low, pair)
        total = both + pltpu.roll(both, 128 - depth, 1) + low_part
        return jnp.where(cols_of(total.shape) < depth, total, 0.0)

    blocks = same_block(hm, hm, slices, slices)
    scale = 1.0 / math.sqrt(depth)
    scores = jnp.where(blocks, nt(q_left, k_right) * scale, -jnp.inf)
    expo = jnp.exp(scores - jnp.max(scores, axis=1, keepdims=True))
    probs = expo * (1.0 / jnp.sum(expo, axis=1, keepdims=True))
    mixed_b = times_pair(nn, probs, v_pair).astype(bf16)

    spread_d = jnp.where(
        (rows_of((width, 128)) & (depth - 1)) == cols_of((width, 128)), 1.0, 0.0
    ).astype(bf16)
    diagonal = same_block(hm, width, slices, depth)
    diagonal_t = same_block(width, hm, depth, slices)
    mixed_block = jnp.where(diagonal, nt(mixed_b, spread_d), 0.0).astype(bf16)
    mw_ref[...] = nn(mixed_block, w_out_ref[...]).astype(bf16)
    mixed_t_ref[...] = jnp.where(diagonal_t, nt(spread_d, mixed_b), 0.0).astype(bf16)

    d_probs = nt(g_left, v_right)
    d_v = times_pair(tn, probs, g_pair)
    d_scores = probs * (d_probs - jnp.sum(probs * d_probs, axis=1, keepdims=True)) * scale
    d_q = times_pair(nn, d_scores, k_pair)
    d_k = times_pair(tn, d_scores, q_pair)
    d_qkv = d_q + pltpu.roll(d_k, depth, 1) + pltpu.roll(d_v, 2 * depth, 1)
    d_high, d_low = two_pieces(d_qkv)
    d_tokens = nt(d_high, w_cat) + nt(d_low, w_cat)
    raw = raw[:, 0:depth]
    d_raw_b = (d_tokens * inverse).astype(bf16)
    d_norm = -jnp.sum(d_tokens * raw, axis=1, keepdims=True) * inverse * inverse
    dn_ref[...] = jnp.broadcast_to(d_norm, dn_ref.shape)
    spread_d = spread_matrix(width, depth)
    dr_ref[...] = jnp.where(diagonal, nt(d_raw_b, spread_d), 0.0).astype(bf16)
    drt_ref[...] = jnp.where(diagonal_t, nt(spread_d, d_raw_b), 0.0).astype(bf16)

    t_high, t_low = two_pieces(tokens)
    grads = tn(t_high, d_high) + tn(t_high, d_low) + tn(t_low, d_high)
    for i in range(3):
        at = pltpu.roll(grads, 128 - i * depth, 1) if i else grads
        grad_qkv_ref[i] = at[0:depth, 0:depth]


def backward_kernel(
    heads,
    slices,
    aux_ref,
    wt_ref,
    logits_ref,
    weights_ref,
    mid_ref,
    cot_ref,
    feats_ref,
    sb_ref,
    mw_ref,
    dr_ref,
    drt_ref,
    dn_ref,
    temp_ref,
    _,
    dmt_ref,
    send0,
    send1,
    send2,
    send3,
    yt,
    grad_acc,
    small_acc,
    pack,
):
    width = mid_ref.shape[1]
    depth = width // heads
    hm = heads * slices
    block = feats_ref.shape[0]

    grad_acc[...] = jnp.zeros_like(grad_acc)
    small_acc[...] = jnp.zeros_like(small_acc)
    yt[:, 0:hm] = drt_ref[...]
    yt[:, hm:] = sb_ref[...]

    temp = jnp.broadcast_to(temp_ref[...].astype(f32), (16, depth)).astype(bf16)
    same = (rows_of((depth, depth)) == cols_of((depth, depth))).astype(f32).astype(bf16)
    temp = nt(same, temp)[:, 0:1]
    piece = min(sub_block, block)
    pieces = [slice(i * piece, (i + 1) * piece) for i in range(block // piece)]

    def products(at):
        return nt(dr_ref[...], mid_ref[at, :]) + nt(mw_ref[...], cot_ref[at, :])

    def per_head(at, products):
        u_b, sums = [], []
        aux = aux_ref[:, at]
        for h in range(heads):
            span = slice(h * slices, (h + 1) * slices)
            inv_tau = aux[h : h + 1]
            logits = logits_ref[span, at]
            weights = weights_ref[span, at]
            d_weights = products[span] + dn_ref[span, 0:1]
            mean = jnp.sum(weights * d_weights, axis=0, keepdims=True)
            d_logits = weights * (d_weights - mean)
            d_tau = jnp.sum(d_logits * logits, axis=0, keepdims=True)
            sums.append(-d_tau * aux[2 * heads + h : 2 * heads + h + 1])
            u_b.append((d_logits * inv_tau).astype(bf16))
        c_sum = jnp.concatenate(sums, axis=0)
        c_high = c_sum.astype(bf16).astype(f32)
        u_b.append(jnp.concatenate([c_high, c_sum - c_high], axis=0).astype(bf16))
        return jnp.concatenate(u_b, axis=0), sums

    def outputs(at, u_b, sums):
        d_mid = nn(yt[...], jnp.concatenate([wt_ref[:, at], u_b[0:hm]], axis=0))
        d_mid = [
            (d_mid[h * depth : (h + 1) * depth] + temp * sums[h]).astype(bf16)
            for h in range(heads)
        ]
        d_mid = jnp.concatenate(d_mid, axis=0)
        dmt_ref[:, at] = d_mid
        grad_acc[...] += nn(d_mid, feats_ref[at, :])
        small_acc[...] += nn(u_b, mid_ref[at, :])

    ready = products(pieces[0])
    for i, at in enumerate(pieces):
        current = ready
        if i + 1 < len(pieces):
            ready = products(pieces[i + 1])
        outputs(at, *per_head(at, current))

    grad = grad_acc[...].T
    u_part = jnp.where(same_block(hm, width, slices, depth), small_acc[0:hm, :], 0.0)
    u_part = fold_rows(u_part, heads, slices)
    c_part = small_acc[hm : hm + heads, :] + small_acc[hm + heads : hm + 2 * heads, :]
    c_part = jnp.where(same_block(heads, width, 1, depth), c_part, 0.0)
    c_part = jnp.sum(c_part, axis=0, keepdims=True)

    def fold_lanes(x):
        total = x[:, 0:128]
        for j in range(1, width // 128):
            total = total + x[:, j * 128 : (j + 1) * 128]
        shift = 64
        while shift >= depth:
            total = total + pltpu.roll(total, shift, 1)
            shift //= 2
        return total

    u_part = fold_lanes(u_part)
    c_part = fold_lanes(jnp.broadcast_to(c_part, (slices, width)))
    where_lane = cols_of((slices, 128))
    extra = jnp.where(where_lane < depth, u_part, c_part)
    rows = width // group
    more = slices // group
    for j in range(group):
        pack[j, 0:rows, :] = grad[j * rows : (j + 1) * rows]
        pack[j, rows : rows + more, 0:128] = extra[j * more : (j + 1) * more]
        pack[j, rows : rows + more, 128:] = jnp.zeros((more, width - 128), f32)
    place = group_place()
    for k, send in enumerate((send0, send1, send2, send3)):
        send[...] = pack[place ^ k]


def rows_kernel(wt_ref, dmt_ref, mw_ref, w_mid_ref, _, attended_ref, feats_grad_ref, token_ref):
    block = attended_ref.shape[0]
    at = pl.ds(pl.multiple_of(pl.program_id(0) * block, block), block)
    token_ref[...] = jnp.zeros_like(token_ref)
    attended_ref[...] = tn(wt_ref[:, at], mw_ref[...]).astype(bf16)
    feats_grad_ref[...] = lax.dot_general(
        dmt_ref[:, at], w_mid_ref[...], (((0,), (1,)), ((), ())), preferred_element_type=f32
    ).astype(bf16)


def grad_out_kernel(own_ref, other_ref, mixed_t_ref, _, grad_out_ref, token_ref, whole):
    token_ref[...] = jnp.zeros_like(token_ref)
    place = group_place() & 1
    rows = own_ref.shape[0]
    for k, part in enumerate((own_ref, other_ref)):
        whole[pl.ds(pl.multiple_of((place ^ k) * rows, 8), rows), :] = part[...]
    high, low = two_pieces(whole[...])
    mixed_t = mixed_t_ref[...]
    grad_out_ref[...] = nn(mixed_t, high) + nn(mixed_t, low)


def finish_kernel(depth, m0, m1, m2, m3, _, grad_mid_ref, slice_ref, temp_ref, extra):
    place = group_place()
    slices = slice_ref.shape[1]
    more = slices // group
    rows = m0.shape[0] - more
    for k, part in enumerate((m0, m1, m2, m3)):
        at = pl.ds(pl.multiple_of((place ^ k) * rows, 8), rows)
        grad_mid_ref[at, :] = part[0:rows, :]
        extra[pl.ds(pl.multiple_of((place ^ k) * more, 8), more), :] = part[rows:, 0:128]
    turned = extra[...].T
    slice_ref[...] = turned[0:depth, 0:slices]
    temp_ref[...] = extra[0:1, depth : 2 * depth]


def full(shape):
    zeros = (0,) * len(shape)
    return pl.BlockSpec(shape, lambda *_: zeros)


def params(mebibytes, grid=True):
    semantics = ("arbitrary",) if grid else None
    return pltpu.CompilerParams(
        dimension_semantics=semantics, vmem_limit_bytes=mebibytes * mib
    )


def cost(flops, moved, transcendentals=0):
    return pl.CostEstimate(flops=flops, bytes_accessed=moved, transcendentals=transcendentals)


def exchange(x, k, count):
    return lax.ppermute(x, "node", [(i, i ^ k) for i in range(count)])


def sum_kernel(count, *refs):
    total = refs[0][...] + refs[count - 1][...]
    if count == 4:
        total = total + (refs[1][...] + refs[2][...])
    refs[-1][...] = total


def sum_behind(parts, *before):
    return pl.pallas_call(
        functools.partial(sum_kernel, len(parts)),
        out_shape=jax.ShapeDtypeStruct(parts[0].shape, f32),
        in_specs=[pl.BlockSpec(memory_space=pltpu.VMEM)] * len(parts)
        + [pl.BlockSpec(memory_space=pl.ANY)] * len(before),
        out_specs=pl.BlockSpec(memory_space=pltpu.VMEM),
        compiler_params=params(2, False),
        cost_estimate=cost(3 * parts[0].size, 5 * parts[0].size * 4),
    )(*parts, *before)


def scatter_group(parts, count):
    got = [parts[0]] + [exchange(parts[k], k, count) for k in range(1, group)]
    return (got[0] + got[1]) + (got[2] + got[3])


def sum_stage(total, stride, others, count, *before):
    parts = [total] + [exchange(total, stride * j, count) for j in range(others, 0, -1)]
    if before:
        return sum_behind(parts, *before)
    if others == 1:
        return parts[0] + parts[1]
    return (parts[0] + parts[3]) + (parts[1] + parts[2])


def sum_over_groups(total, stride, count, *before):
    while stride < count:
        others = 3 if count // stride % 4 == 0 else 1
        total = sum_stage(total, stride, others, count, *before)
        stride *= others + 1
    return total


def gather_group(total, count):
    return [total] + [exchange(total, k, count) for k in range(1, group)]


def shards(count, feats, cotangent, valid, owned, w_mid, w_slice, temp_vec, w_qkv, w_out):
    rows, width = feats.shape
    depth, slices = w_slice.shape
    heads = width // depth
    hm = heads * slices
    unit = 2 * rows * width * width
    smem = pl.BlockSpec(memory_space=pltpu.SMEM)

    def blocks(size):
        return (rows // size,), pl.BlockSpec((size, width), lambda i: (i, 0))

    def like(shape, dtype):
        return jax.ShapeDtypeStruct(shape, dtype)

    def far(x):
        return pltpu.with_memory_space_constraint(x, pltpu.HBM)

    near = pltpu.VMEM
    whole = pl.BlockSpec(memory_space=pltpu.VMEM)

    temp = temp_vec.reshape(1, depth)
    half = (2 * slices + 8, 128)
    wide = (hm // 2, width)
    inputs = (valid.reshape(1, rows), feats, cotangent, w_mid, w_slice, w_out)
    (
        mid,
        wt,
        aux,
        sw,
        keep,
        send,
        wc_keep,
        wc_send,
        feats_near,
        cot_near,
    ) = pl.pallas_call(
        functools.partial(stats_kernel, heads, slices),
        in_specs=[smem, whole] + [pl.BlockSpec(memory_space=pltpu.HBM)] * len(inputs),
        out_specs=[whole] * 10,
        out_shape=[
            near((rows, width), bf16),
            near((hm, rows), bf16),
            near((3 * heads, rows), f32),
            near((hm + 16, width), bf16),
            near(half, f32),
            near(half, f32),
            near(wide, f32),
            near(wide, f32),
            near((rows, width), bf16),
            near((rows, width), bf16),
        ],
        scratch_shapes=[
            pltpu.VMEM((1, rows), jnp.int32),
            pltpu.VMEM((width, width), bf16),
            pltpu.VMEM((depth, slices), bf16),
            pltpu.VMEM((width, width), bf16),
            pltpu.VMEM((hm, width), f32),
            pltpu.VMEM((hm, 128), f32),
            pltpu.VMEM((hm, width), f32),
            pltpu.VMEM((2,) + half, f32),
            pltpu.SemaphoreType.DMA((7,)),
        ],
        compiler_params=params(24, False),
        cost_estimate=cost(4 * unit, rows * width * 8, rows * hm),
    )(owned, far(temp), *map(far, inputs))

    own = keep + exchange(send, 1, count)
    wc_got = exchange(wc_send, 1, count)
    wc_sum = sum_behind([wc_keep, wc_got], own)
    logits, weights, sb, w_cat, token = pl.pallas_call(
        functools.partial(between_kernel, heads, slices),
        in_specs=[whole] * 5 + [pl.BlockSpec(memory_space=pl.ANY)],
        out_specs=[whole] * 5,
        out_shape=[
            near((hm, rows), f32),
            near((hm, rows), f32),
            near((width, hm), bf16),
            near((depth, 128), bf16),
            near((8, 128), f32),
        ],
        compiler_params=params(16, False),
        cost_estimate=cost(3 * unit, rows, rows),
    )(mid, sw, aux, w_slice, w_qkv, own)
    own = sum_stage(own, 2, 3, count, token)
    wc_got = exchange(wc_sum, 2, count)
    wc_sum = sum_behind([wc_sum, wc_got], own)
    own = sum_over_groups(own, 8, count)
    other = exchange(own, 1, count)
    stride = 8
    wc_got = exchange(wc_sum, stride, count)
    while 2 * stride < count:
        wc_sum = wc_sum + wc_got
        stride *= 2
        wc_got = exchange(wc_sum, stride, count)

    mw, mixed_t, dr, drt, dn, grad_qkv = pl.pallas_call(
        functools.partial(tokens_kernel, heads, slices),
        out_shape=[
            near((hm, width), bf16),
            near((width, hm), bf16),
            near((hm, width), bf16),
            near((width, hm), bf16),
            near((hm, 128), f32),
            like((3, depth, depth), f32),
        ],
        scratch_shapes=[pltpu.VMEM((2,) + half, f32)],
        compiler_params=params(16, False),
        cost_estimate=cost(3 * width**3, 4 * width * width * 4, hm * hm),
    )(own, other, w_cat, w_out)
    larger = (width // group + slices // group, width)
    dmt, *sends = pl.pallas_call(
        functools.partial(backward_kernel, heads, slices),
        in_specs=[whole] * 13 + [pl.BlockSpec(memory_space=pl.ANY)],
        out_specs=[whole] * (1 + group),
        out_shape=[near((width, rows), bf16)] + [near(larger, f32)] * group,
        scratch_shapes=[
            pltpu.VMEM((width, 2 * hm), bf16),
            pltpu.VMEM((width, width), f32),
            pltpu.VMEM((hm + 16, width), f32),
            pltpu.VMEM((group,) + larger, f32),
        ],
        compiler_params=params(24, False),
        cost_estimate=cost(unit * 3 // 10, rows * width, rows),
    )(aux, wt, logits, weights, mid, cot_near, feats_near, sb, mw, dr, drt, dn, temp, wc_sum)

    mid_total = scatter_group(sends, count)
    wc_sum = sum_behind([wc_sum, wc_got], sends[1])
    wc_got = exchange(wc_sum, 4, count)

    block = min(1024, rows)
    grid, by_rows = blocks(block)
    attended, feats_grad, token = pl.pallas_call(
        rows_kernel,
        grid=grid,
        in_specs=[
            whole,
            whole,
            whole,
            full((width, width)),
            pl.BlockSpec(memory_space=pl.ANY),
        ],
        out_specs=[by_rows, by_rows, full((8, 128))],
        out_shape=[like((rows, width), bf16)] * 2 + [like((8, 128), f32)],
        compiler_params=params(20),
        cost_estimate=cost(2 * unit, rows * width * 8),
    )(wt, dmt, mw, w_mid, mid_total)

    wc_sum = sum_behind([wc_sum, wc_got], token)
    wc_other = exchange(wc_sum, 1, count)
    mid_total = sum_over_groups(mid_total, group, count, token)
    grad_w_out, token_out = pl.pallas_call(
        grad_out_kernel,
        in_specs=[whole] * 3 + [pl.BlockSpec(memory_space=pl.ANY)],
        out_specs=[whole] * 2,
        out_shape=[like((width, width), f32), like((8, 128), f32)],
        scratch_shapes=[pltpu.VMEM((hm, width), f32)],
        compiler_params=params(8, False),
        cost_estimate=cost(4 * width**3, 3 * width * width * 4),
    )(wc_sum, wc_other, mixed_t, mid_total)

    mid_parts = gather_group(mid_total, count)
    grad_w_mid, grad_w_slice, grad_temp = pl.pallas_call(
        functools.partial(finish_kernel, depth),
        in_specs=[whole] * group + [pl.BlockSpec(memory_space=pl.ANY)],
        out_specs=[whole] * 3,
        out_shape=[
            like((width, width), f32),
            like((depth, slices), f32),
            like((1, depth), f32),
        ],
        scratch_shapes=[pltpu.VMEM((slices, 128), f32)],
        compiler_params=params(8, False),
        cost_estimate=cost(0, 2 * width * width * 4),
    )(*mid_parts, token_out)
    return (
        attended,
        feats_grad,
        grad_w_mid,
        grad_w_out,
        grad_w_slice,
        grad_temp.reshape(depth),
        grad_qkv,
    )


def solution(mesh):
    in_specs = (
        P(("design", "node"), None),
        P(("design", "node"), None),
        P(("design", "node")),
        P(("design", "node")),
        P(),
        P(),
        P(),
        P(),
        P(),
    )
    out_specs = (
        P(("design", "node"), None),
        P(("design", "node"), None),
        P("design", None),
        P("design", None),
        P("design", None),
        P("design"),
        P("design", None, None),
    )
    return jax.shard_map(
        functools.partial(shards, mesh.shape["node"]),
        mesh=mesh,
        in_specs=in_specs,
        out_specs=out_specs,
        check_vma=False,
    )
```

```python
import functools
import math

import jax
import jax.numpy as jnp
from jax import lax
from jax.experimental import pallas as pl
from jax.experimental.pallas import tpu as pltpu
from jax.sharding import PartitionSpec as P

f32 = jnp.float32
bf16 = jnp.bfloat16
eps_norm = 1e-05
exact = lax.Precision.HIGHEST
group = 4
sub_block = 512
mib = 1024 * 1024


def nn(a, b, precision=None):
    return lax.dot_general(
        a, b, (((1,), (0,)), ((), ())), preferred_element_type=f32, precision=precision
    )


def nt(a, b, precision=None):
    return lax.dot_general(
        a, b, (((1,), (1,)), ((), ())), preferred_element_type=f32, precision=precision
    )


def tn(a, b, precision=None):
    return lax.dot_general(
        a, b, (((0,), (0,)), ((), ())), preferred_element_type=f32, precision=precision
    )


def log2(size):
    return size.bit_length() - 1


def rows_of(shape):
    return lax.broadcasted_iota(jnp.int32, shape, 0)


def cols_of(shape):
    return lax.broadcasted_iota(jnp.int32, shape, 1)


def spread_matrix(width, small):
    shape = (width, small)
    return jnp.where((rows_of(shape) & (small - 1)) == cols_of(shape), 1.0, 0.0).astype(bf16)


def same_block(rows, cols, row_size, col_size):
    shape = (rows, cols)
    return rows_of(shape) >> log2(row_size) == cols_of(shape) >> log2(col_size)


def two_pieces(x):
    high = x.astype(bf16)
    return high, (x - high.astype(f32)).astype(bf16)


def fold_rows(x, heads, size):
    total = x[0:size]
    for h in range(1, heads):
        total = total + x[h * size : (h + 1) * size]
    return total


def group_place():
    return lax.axis_index("node") % group


def stats_kernel(
    heads,
    slices,
    owned_ref,
    temp_ref,
    valid_far,
    feats_far,
    cot_far,
    w_mid_far,
    w_slice_far,
    w_out_far,
    mid_ref,
    wt_ref,
    aux_ref,
    sw_ref,
    keep_ref,
    send_ref,
    wc_keep_ref,
    wc_send_ref,
    feats_ref,
    cot_ref,
    valid_ref,
    w_mid_ref,
    w_slice_ref,
    w_out_ref,
    raw_acc,
    norm_acc,
    wc_acc,
    pack,
    sems,
):
    width = w_mid_ref.shape[0]
    depth = width // heads
    hm = heads * slices
    rows = feats_ref.shape[0]
    piece = min(2 * sub_block, rows)
    count = rows // piece
    small = [
        pltpu.make_async_copy(source, target, sems.at[i])
        for i, (source, target) in enumerate(
            (
                (w_slice_far, w_slice_ref),
                (w_mid_far, w_mid_ref),
                (valid_far, valid_ref),
                (w_out_far, w_out_ref),
            )
        )
    ]
    first, rest = pl.ds(0, piece), pl.ds(piece, rows - piece)
    large = [
        pltpu.make_async_copy(source, target, sems.at[len(small) + i])
        for i, (source, target) in enumerate(
            (
                (feats_far.at[first, :], feats_ref.at[first, :]),
                (feats_far.at[rest, :], feats_ref.at[rest, :]),
                (cot_far, cot_ref),
            )
        )
    ]
    for copy in small[:2] + large[:1] + small[2:] + large[1:]:
        copy.start()

    raw_acc[...] = jnp.zeros_like(raw_acc)
    norm_acc[...] = jnp.zeros_like(norm_acc)
    wc_acc[...] = jnp.zeros_like(wc_acc)
    spread_d = spread_matrix(width, depth)
    spread_m = spread_matrix(hm, slices)
    for copy in small + large[:1]:
        copy.wait()
    temp = jnp.broadcast_to(temp_ref[...].astype(f32), (16, depth)).astype(bf16)
    half = nt(spread_m, w_slice_ref[...]).astype(bf16)
    full = nt(half, spread_d)
    sw_ref[0:hm, :] = jnp.where(same_block(hm, width, slices, depth), full, 0.0).astype(bf16)
    full = nt(temp, spread_d)
    sw_ref[hm : hm + 16, :] = jnp.where(same_block(16, width, 1, depth), full, 0.0).astype(bf16)
    owned = owned_ref[0]

    def products(i):
        at = slice(i * piece, (i + 1) * piece)
        mid = nn(feats_ref[at, :], w_mid_ref[...]).astype(bf16)
        mid_ref[at, :] = mid
        return mid, nt(sw_ref[...], mid)

    def statistics(i, mid, scores):
        at = slice(i * piece, (i + 1) * piece)
        zsum = scores[hm : hm + heads]
        small = jnp.exp(-jnp.abs(zsum))
        inv_tau = 1.0 / (0.5 + (jnp.maximum(zsum, 0.0) + jnp.log(1.0 + small)))
        sig = jnp.where(zsum >= 0.0, 1.0, small) / (1.0 + small)
        position = i * piece + cols_of((1, piece))
        live = (valid_ref[:, at] > 0) & (position < owned)
        live_f = live.astype(f32)
        rounded, sums, logs = [], [], []
        for h in range(heads):
            span = slice(h * slices, (h + 1) * slices)
            logits = scores[span] * inv_tau[h : h + 1]
            peak = jnp.max(logits, axis=0, keepdims=True)
            expo = jnp.exp(logits - peak)
            total = jnp.sum(expo, axis=0, keepdims=True)
            weights = expo * (live_f / total)
            rounded.append(weights.astype(bf16))
            lanes = weights[:, 0:128]
            for c in range(1, piece // 128):
                lanes = lanes + weights[:, c * 128 : (c + 1) * 128]
            sums.append(lanes)
            logs.append(jnp.where(live, peak + jnp.log(total), jnp.inf))
        wt = jnp.concatenate(rounded, axis=0)
        wt_ref[:, at] = wt
        norm_acc[...] += jnp.concatenate(sums, axis=0)
        aux_ref[:, at] = jnp.concatenate([inv_tau] + logs + [sig * inv_tau], axis=0)
        raw_acc[...] += nn(wt, mid)
        wc_acc[...] += nn(wt, cot_ref[at, :])

    ready = products(0)
    large[1].wait()
    large[2].wait()
    for i in range(count):
        current = ready
        if i + 1 < count:
            ready = products(i + 1)
        statistics(i, *current)

    diagonal = same_block(hm, width, slices, depth)
    raw = fold_rows(jnp.where(diagonal, raw_acc[...], 0.0), heads, slices)
    high, low = two_pieces(wc_acc[...])
    w_out = w_out_ref[...]
    mixed = nt(high, w_out) + nt(low, w_out)
    mixed = fold_rows(jnp.where(diagonal, mixed, 0.0), heads, slices)
    norm = jnp.sum(norm_acc[...].T, axis=0, keepdims=True)
    first = rows_of((8, 128)) == 0
    for j in range(2):
        part = slice(j * 128, (j + 1) * 128)
        pack[j, 0:slices, :] = raw[:, part]
        pack[j, slices : 2 * slices, :] = mixed[:, part]
        pack[j, 2 * slices :, :] = jnp.where(first, norm[:, part], 0.0)
    place = group_place()
    keep_ref[...] = pack[place & 1]
    send_ref[...] = pack[(place & 1) ^ 1]
    rows = hm // 2
    for k, out in enumerate((wc_keep_ref, wc_send_ref)):
        out[...] = wc_acc[pl.ds(pl.multiple_of(((place & 1) ^ k) * rows, 8), rows), :]


def between_kernel(
    heads,
    slices,
    mid_ref,
    sw_ref,
    aux_ref,
    w_slice_ref,
    w_qkv_ref,
    _,
    logits_ref,
    weights_ref,
    sb_ref,
    w_cat_ref,
    token_ref,
):
    depth = w_slice_ref.shape[0]
    width = heads * depth
    hm = heads * slices
    rows = mid_ref.shape[0]
    piece = min(sub_block, rows)
    token_ref[...] = jnp.zeros_like(token_ref)
    spread_d = spread_matrix(width, depth)
    spread_m = spread_matrix(hm, slices)
    half = nn(spread_d, w_slice_ref[...]).astype(bf16)
    full = nt(half, spread_m)
    sb_ref[...] = jnp.where(same_block(width, hm, depth, slices), full, 0.0).astype(bf16)
    w_cat = jnp.zeros((depth, 128), f32)
    for i in range(3):
        place_at = jnp.where(rows_of((depth, 128)) + i * depth == cols_of((depth, 128)), 1.0, 0.0)
        w_cat = w_cat + nn(w_qkv_ref[i], place_at.astype(bf16))
    w_cat_ref[...] = w_cat.astype(bf16)
    for i in range(rows // piece):
        at = slice(i * piece, (i + 1) * piece)
        scores = nt(sw_ref[0:hm, :], mid_ref[at, :])
        for h in range(heads):
            span = slice(h * slices, (h + 1) * slices)
            logits = scores[span] * aux_ref[h : h + 1, at]
            logits_ref[span, at] = logits
            weights_ref[span, at] = jnp.exp(logits - aux_ref[heads + h : heads + h + 1, at])


def lanes_at(x, lane, *where):
    place = cols_of(x.shape) >> log2(lane)
    total = jnp.zeros_like(x)
    for value, at, to in where:
        shift = (to - at) * lane % 128
        moved = pltpu.roll(value, shift, 1) if shift else value
        total = jnp.where(place == to, moved, total)
    return total.astype(bf16)


def split(x):
    high = x.astype(bf16).astype(f32)
    return high, x - high


def tokens_kernel(
    heads,
    slices,
    own_ref,
    got_ref,
    w_cat_ref,
    w_out_ref,
    mw_ref,
    dr_ref,
    drt_ref,
    dn_ref,
    mixed_ref,
    tokens_ref,
    d_qkv_ref,
    pack,
):
    width = w_out_ref.shape[0]
    depth = width // heads
    hm = heads * slices
    place = group_place() & 1
    pack[place] = own_ref[...]
    pack[place ^ 1] = got_ref[...]
    per = 128 // depth

    def compact(first):
        pieces = []
        for h in range(heads):
            x = pack[h // per, first : first + slices, :]
            shift = (h % per) * depth
            pieces.append(pltpu.roll(x, 128 - shift, 1) if shift else x)
        x = jnp.concatenate(pieces, axis=0)
        return jnp.where(cols_of(x.shape) < depth, x, 0.0)

    raw = compact(0)
    d_mixed = compact(slices)
    norm = jnp.concatenate([pack[j, 2 * slices :, :].T[:, 0:1] for j in range(2)], axis=0)
    inverse = 1.0 / (norm + eps_norm)
    tokens = raw * inverse
    w_cat = w_cat_ref[...]

    t_high, rest = split(tokens)
    t_low, rest = split(rest)
    left = lanes_at(tokens, depth, (t_high, 0, 0), (t_low, 0, 1), (rest, 0, 2))
    blank = jnp.zeros((128 - 3 * depth, 128), bf16)
    qkv = nn(left, jnp.concatenate([w_cat, w_cat, w_cat, blank], axis=0))
    high, low = split(qkv)
    q_left = lanes_at(qkv, depth, (high, 0, 0), (high, 0, 1), (low, 0, 2))
    k_right = lanes_at(qkv, depth, (high, 1, 0), (low, 1, 1), (high, 1, 2))
    v_right = lanes_at(qkv, depth, (high, 2, 0), (low, 2, 1), (high, 2, 2))
    q_pair = lanes_at(qkv, depth, (high, 0, 0), (low, 0, 1))
    k_pair = lanes_at(qkv, depth, (high, 1, 0), (low, 1, 1))
    v_pair = lanes_at(qkv, depth, (high, 2, 0), (low, 2, 1))
    g_high, g_low = split(d_mixed)
    g_left = lanes_at(qkv, depth, (g_high, 0, 0), (g_high, 0, 1), (g_low, 0, 2))
    g_pair = lanes_at(qkv, depth, (g_high, 0, 0), (g_low, 0, 1))

    def times_pair(dot, x, pair):
        x_high, x_low = two_pieces(x)
        both = dot(x_high, pair)
        low_part = dot(x_low, pair)
        total = both + pltpu.roll(both, 128 - depth, 1) + low_part
        return jnp.where(cols_of(total.shape) < depth, total, 0.0)

    blocks = same_block(hm, hm, slices, slices)
    scale = 1.0 / math.sqrt(depth)
    scores = jnp.where(blocks, nt(q_left, k_right) * scale, -jnp.inf)
    expo = jnp.exp(scores - jnp.max(scores, axis=1, keepdims=True))
    probs = expo * (1.0 / jnp.sum(expo, axis=1, keepdims=True))
    mixed_b = times_pair(nn, probs, v_pair).astype(bf16)

    spread_d = jnp.where(
        (rows_of((width, 128)) & (depth - 1)) == cols_of((width, 128)), 1.0, 0.0
    ).astype(bf16)
    diagonal = same_block(hm, width, slices, depth)
    diagonal_t = same_block(width, hm, depth, slices)
    mixed_block = jnp.where(diagonal, nt(mixed_b, spread_d), 0.0).astype(bf16)
    mw_ref[...] = nn(mixed_block, w_out_ref[...]).astype(bf16)
    mixed_ref[...] = mixed_b
    tokens_ref[...] = tokens

    d_probs = nt(g_left, v_right)
    d_v = times_pair(tn, probs, g_pair)
    d_scores = probs * (d_probs - jnp.sum(probs * d_probs, axis=1, keepdims=True)) * scale
    d_q = times_pair(nn, d_scores, k_pair)
    d_k = times_pair(tn, d_scores, q_pair)
    d_qkv = d_q + pltpu.roll(d_k, depth, 1) + pltpu.roll(d_v, 2 * depth, 1)
    d_qkv_ref[...] = d_qkv
    d_high, d_low = two_pieces(d_qkv)
    d_tokens = nt(d_high, w_cat) + nt(d_low, w_cat)
    raw = raw[:, 0:depth]
    d_raw_b = (d_tokens * inverse).astype(bf16)
    d_norm = -jnp.sum(d_tokens * raw, axis=1, keepdims=True) * inverse * inverse
    dn_ref[...] = jnp.broadcast_to(d_norm, dn_ref.shape)
    spread_d = spread_matrix(width, depth)
    dr_ref[...] = jnp.where(diagonal, nt(d_raw_b, spread_d), 0.0).astype(bf16)
    drt_ref[...] = jnp.where(diagonal_t, nt(spread_d, d_raw_b), 0.0).astype(bf16)


def backward_kernel(
    heads,
    slices,
    aux_ref,
    wt_ref,
    logits_ref,
    weights_ref,
    mid_ref,
    cot_ref,
    feats_ref,
    sb_ref,
    mw_ref,
    dr_ref,
    drt_ref,
    dn_ref,
    temp_ref,
    _,
    dmt_ref,
    send0,
    send1,
    send2,
    send3,
    yt,
    grad_acc,
    small_acc,
    pack,
):
    width = mid_ref.shape[1]
    depth = width // heads
    hm = heads * slices
    block = feats_ref.shape[0]

    grad_acc[...] = jnp.zeros_like(grad_acc)
    small_acc[...] = jnp.zeros_like(small_acc)
    yt[:, 0:hm] = drt_ref[...]
    yt[:, hm:] = sb_ref[...]

    temp = jnp.broadcast_to(temp_ref[...].astype(f32), (16, depth)).astype(bf16)
    same = (rows_of((depth, depth)) == cols_of((depth, depth))).astype(f32).astype(bf16)
    temp = nt(same, temp)[:, 0:1]
    piece = min(sub_block, block)
    pieces = [slice(i * piece, (i + 1) * piece) for i in range(block // piece)]

    def products(at):
        return nt(dr_ref[...], mid_ref[at, :]) + nt(mw_ref[...], cot_ref[at, :])

    def per_head(at, products):
        u_b, sums = [], []
        aux = aux_ref[:, at]
        for h in range(heads):
            span = slice(h * slices, (h + 1) * slices)
            inv_tau = aux[h : h + 1]
            logits = logits_ref[span, at]
            weights = weights_ref[span, at]
            d_weights = products[span] + dn_ref[span, 0:1]
            mean = jnp.sum(weights * d_weights, axis=0, keepdims=True)
            d_logits = weights * (d_weights - mean)
            d_tau = jnp.sum(d_logits * logits, axis=0, keepdims=True)
            sums.append(-d_tau * aux[2 * heads + h : 2 * heads + h + 1])
            u_b.append((d_logits * inv_tau).astype(bf16))
        c_sum = jnp.concatenate(sums, axis=0)
        c_high = c_sum.astype(bf16).astype(f32)
        u_b.append(jnp.concatenate([c_high, c_sum - c_high], axis=0).astype(bf16))
        return jnp.concatenate(u_b, axis=0), sums

    def outputs(at, u_b, sums):
        d_mid = nn(yt[...], jnp.concatenate([wt_ref[:, at], u_b[0:hm]], axis=0))
        d_mid = [
            (d_mid[h * depth : (h + 1) * depth] + temp * sums[h]).astype(bf16)
            for h in range(heads)
        ]
        d_mid = jnp.concatenate(d_mid, axis=0)
        dmt_ref[:, at] = d_mid
        grad_acc[...] += nn(d_mid, feats_ref[at, :])
        small_acc[...] += nn(u_b, mid_ref[at, :])

    ready = products(pieces[0])
    for i, at in enumerate(pieces):
        current = ready
        if i + 1 < len(pieces):
            ready = products(pieces[i + 1])
        outputs(at, *per_head(at, current))

    grad = grad_acc[...].T
    u_part = jnp.where(same_block(hm, width, slices, depth), small_acc[0:hm, :], 0.0)
    u_part = fold_rows(u_part, heads, slices)
    c_part = small_acc[hm : hm + heads, :] + small_acc[hm + heads : hm + 2 * heads, :]
    c_part = jnp.where(same_block(heads, width, 1, depth), c_part, 0.0)
    c_part = jnp.sum(c_part, axis=0, keepdims=True)

    def fold_lanes(x):
        total = x[:, 0:128]
        for j in range(1, width // 128):
            total = total + x[:, j * 128 : (j + 1) * 128]
        shift = 64
        while shift >= depth:
            total = total + pltpu.roll(total, shift, 1)
            shift //= 2
        return total

    u_part = fold_lanes(u_part)
    c_part = fold_lanes(jnp.broadcast_to(c_part, (slices, width)))
    where_lane = cols_of((slices, 128))
    extra = jnp.where(where_lane < depth, u_part, c_part)
    rows = width // group
    more = slices // group
    for j in range(group):
        pack[j, 0:rows, :] = grad[j * rows : (j + 1) * rows]
        pack[j, rows : rows + more, 0:128] = extra[j * more : (j + 1) * more]
        pack[j, rows : rows + more, 128:] = jnp.zeros((more, width - 128), f32)
    place = group_place()
    for k, send in enumerate((send0, send1, send2, send3)):
        send[...] = pack[place ^ k]


def rows_kernel(wt_ref, dmt_ref, mw_ref, w_mid_ref, _, attended_ref, feats_grad_ref, token_ref):
    block = attended_ref.shape[0]
    at = pl.ds(pl.multiple_of(pl.program_id(0) * block, block), block)
    token_ref[...] = jnp.zeros_like(token_ref)
    attended_ref[...] = tn(wt_ref[:, at], mw_ref[...]).astype(bf16)
    feats_grad_ref[...] = lax.dot_general(
        dmt_ref[:, at], w_mid_ref[...], (((0,), (1,)), ((), ())), preferred_element_type=f32
    ).astype(bf16)


def grad_out_kernel(
    heads,
    slices,
    own_ref,
    other_ref,
    mixed_ref,
    tokens_ref,
    d_qkv_ref,
    _,
    grad_out_ref,
    grad_qkv_ref,
    token_ref,
    whole,
):
    token_ref[...] = jnp.zeros_like(token_ref)
    hm = heads * slices
    depth = grad_qkv_ref.shape[1]
    width = heads * depth
    t_high, t_low = two_pieces(tokens_ref[...])
    d_high, d_low = two_pieces(d_qkv_ref[...])
    grads = tn(t_high, d_high) + tn(t_high, d_low) + tn(t_low, d_high)
    for i in range(3):
        at = pltpu.roll(grads, 128 - i * depth, 1) if i else grads
        grad_qkv_ref[i] = at[0:depth, 0:depth]
    spread_d = jnp.where(
        (rows_of((width, 128)) & (depth - 1)) == cols_of((width, 128)), 1.0, 0.0
    ).astype(bf16)
    diagonal_t = same_block(width, hm, depth, slices)
    mixed_t = jnp.where(diagonal_t, nt(spread_d, mixed_ref[...]), 0.0).astype(bf16)
    place = group_place() & 1
    rows = own_ref.shape[0]
    for k, part in enumerate((own_ref, other_ref)):
        whole[pl.ds(pl.multiple_of((place ^ k) * rows, 8), rows), :] = part[...]
    high, low = two_pieces(whole[...])
    grad_out_ref[...] = nn(mixed_t, high) + nn(mixed_t, low)


def finish_kernel(depth, m0, m1, m2, m3, _, grad_mid_ref, slice_ref, temp_ref, extra):
    place = group_place()
    slices = slice_ref.shape[1]
    more = slices // group
    rows = m0.shape[0] - more
    for k, part in enumerate((m0, m1, m2, m3)):
        at = pl.ds(pl.multiple_of((place ^ k) * rows, 8), rows)
        grad_mid_ref[at, :] = part[0:rows, :]
        extra[pl.ds(pl.multiple_of((place ^ k) * more, 8), more), :] = part[rows:, 0:128]
    turned = extra[...].T
    slice_ref[...] = turned[0:depth, 0:slices]
    temp_ref[...] = extra[0:1, depth : 2 * depth]


def full(shape):
    zeros = (0,) * len(shape)
    return pl.BlockSpec(shape, lambda *_: zeros)


def params(mebibytes, grid=True):
    semantics = ("arbitrary",) if grid else None
    return pltpu.CompilerParams(
        dimension_semantics=semantics, vmem_limit_bytes=mebibytes * mib
    )


def cost(flops, moved, transcendentals=0):
    return pl.CostEstimate(flops=flops, bytes_accessed=moved, transcendentals=transcendentals)


def exchange(x, k, count):
    return lax.ppermute(x, "node", [(i, i ^ k) for i in range(count)])


def sum_kernel(count, *refs):
    total = refs[0][...] + refs[count - 1][...]
    if count == 4:
        total = total + (refs[1][...] + refs[2][...])
    refs[-1][...] = total


def sum_behind(parts, *before):
    return pl.pallas_call(
        functools.partial(sum_kernel, len(parts)),
        out_shape=jax.ShapeDtypeStruct(parts[0].shape, f32),
        in_specs=[pl.BlockSpec(memory_space=pltpu.VMEM)] * len(parts)
        + [pl.BlockSpec(memory_space=pl.ANY)] * len(before),
        out_specs=pl.BlockSpec(memory_space=pltpu.VMEM),
        compiler_params=params(2, False),
        cost_estimate=cost(3 * parts[0].size, 5 * parts[0].size * 4),
    )(*parts, *before)


def scatter_group(parts, count):
    got = [parts[0]] + [exchange(parts[k], k, count) for k in range(1, group)]
    return (got[0] + got[1]) + (got[2] + got[3])


def sum_stage(total, stride, others, count, *before):
    parts = [total] + [exchange(total, stride * j, count) for j in range(others, 0, -1)]
    if before:
        return sum_behind(parts, *before)
    if others == 1:
        return parts[0] + parts[1]
    return (parts[0] + parts[3]) + (parts[1] + parts[2])


def sum_over_groups(total, stride, count, *before):
    while stride < count:
        others = 3 if count // stride % 4 == 0 else 1
        total = sum_stage(total, stride, others, count, *before)
        stride *= others + 1
    return total


def gather_group(total, count):
    return [total] + [exchange(total, k, count) for k in range(1, group)]


def shards(count, feats, cotangent, valid, owned, w_mid, w_slice, temp_vec, w_qkv, w_out):
    rows, width = feats.shape
    depth, slices = w_slice.shape
    heads = width // depth
    hm = heads * slices
    unit = 2 * rows * width * width
    smem = pl.BlockSpec(memory_space=pltpu.SMEM)

    def blocks(size):
        return (rows // size,), pl.BlockSpec((size, width), lambda i: (i, 0))

    def like(shape, dtype):
        return jax.ShapeDtypeStruct(shape, dtype)

    def far(x):
        return pltpu.with_memory_space_constraint(x, pltpu.HBM)

    near = pltpu.VMEM
    whole = pl.BlockSpec(memory_space=pltpu.VMEM)

    temp = temp_vec.reshape(1, depth)
    half = (2 * slices + 8, 128)
    wide = (hm // 2, width)
    inputs = (valid.reshape(1, rows), feats, cotangent, w_mid, w_slice, w_out)
    (
        mid,
        wt,
        aux,
        sw,
        keep,
        send,
        wc_keep,
        wc_send,
        feats_near,
        cot_near,
    ) = pl.pallas_call(
        functools.partial(stats_kernel, heads, slices),
        in_specs=[smem, whole] + [pl.BlockSpec(memory_space=pltpu.HBM)] * len(inputs),
        out_specs=[whole] * 10,
        out_shape=[
            near((rows, width), bf16),
            near((hm, rows), bf16),
            near((3 * heads, rows), f32),
            near((hm + 16, width), bf16),
            near(half, f32),
            near(half, f32),
            near(wide, f32),
            near(wide, f32),
            near((rows, width), bf16),
            near((rows, width), bf16),
        ],
        scratch_shapes=[
            pltpu.VMEM((1, rows), jnp.int32),
            pltpu.VMEM((width, width), bf16),
            pltpu.VMEM((depth, slices), bf16),
            pltpu.VMEM((width, width), bf16),
            pltpu.VMEM((hm, width), f32),
            pltpu.VMEM((hm, 128), f32),
            pltpu.VMEM((hm, width), f32),
            pltpu.VMEM((2,) + half, f32),
            pltpu.SemaphoreType.DMA((7,)),
        ],
        compiler_params=params(24, False),
        cost_estimate=cost(4 * unit, rows * width * 8, rows * hm),
    )(owned, far(temp), *map(far, inputs))

    own = keep + exchange(send, 1, count)
    wc_got = exchange(wc_send, 1, count)
    wc_sum = sum_behind([wc_keep, wc_got], own)
    logits, weights, sb, w_cat, token = pl.pallas_call(
        functools.partial(between_kernel, heads, slices),
        in_specs=[whole] * 5 + [pl.BlockSpec(memory_space=pl.ANY)],
        out_specs=[whole] * 5,
        out_shape=[
            near((hm, rows), f32),
            near((hm, rows), f32),
            near((width, hm), bf16),
            near((depth, 128), bf16),
            near((8, 128), f32),
        ],
        compiler_params=params(16, False),
        cost_estimate=cost(3 * unit, rows, rows),
    )(mid, sw, aux, w_slice, w_qkv, own)
    own = sum_stage(own, 2, 3, count, token)
    wc_got = exchange(wc_sum, 2, count)
    wc_sum = sum_behind([wc_sum, wc_got], own)
    own = sum_over_groups(own, 8, count)
    other = exchange(own, 1, count)
    stride = 4
    wc_got = exchange(wc_sum, stride, count)
    while 4 * stride < count:
        wc_sum = wc_sum + wc_got
        stride *= 2
        wc_got = exchange(wc_sum, stride, count)

    mw, dr, drt, dn, mixed, tokens, d_qkv = pl.pallas_call(
        functools.partial(tokens_kernel, heads, slices),
        out_shape=[
            near((hm, width), bf16),
            near((hm, width), bf16),
            near((width, hm), bf16),
            near((hm, 128), f32),
            near((hm, 128), bf16),
            near((hm, 128), f32),
            near((hm, 128), f32),
        ],
        scratch_shapes=[pltpu.VMEM((2,) + half, f32)],
        compiler_params=params(16, False),
        cost_estimate=cost(3 * width**3, 4 * width * width * 4, hm * hm),
    )(own, other, w_cat, w_out)
    larger = (width // group + slices // group, width)
    dmt, *sends = pl.pallas_call(
        functools.partial(backward_kernel, heads, slices),
        in_specs=[whole] * 13 + [pl.BlockSpec(memory_space=pl.ANY)],
        out_specs=[whole] * (1 + group),
        out_shape=[near((width, rows), bf16)] + [near(larger, f32)] * group,
        scratch_shapes=[
            pltpu.VMEM((width, 2 * hm), bf16),
            pltpu.VMEM((width, width), f32),
            pltpu.VMEM((hm + 16, width), f32),
            pltpu.VMEM((group,) + larger, f32),
        ],
        compiler_params=params(24, False),
        cost_estimate=cost(unit * 3 // 10, rows * width, rows),
    )(aux, wt, logits, weights, mid, cot_near, feats_near, sb, mw, dr, drt, dn, temp, wc_sum)

    mid_total = scatter_group(sends, count)
    wc_sum = sum_behind([wc_sum, wc_got], sends[1])
    wc_got = exchange(wc_sum, count // 2, count)

    block = min(1024, rows)
    grid, by_rows = blocks(block)
    attended, feats_grad, token = pl.pallas_call(
        rows_kernel,
        grid=grid,
        in_specs=[
            whole,
            whole,
            whole,
            full((width, width)),
            pl.BlockSpec(memory_space=pl.ANY),
        ],
        out_specs=[by_rows, by_rows, full((8, 128))],
        out_shape=[like((rows, width), bf16)] * 2 + [like((8, 128), f32)],
        compiler_params=params(20),
        cost_estimate=cost(2 * unit, rows * width * 8),
    )(wt, dmt, mw, w_mid, mid_total)

    wc_sum = sum_behind([wc_sum, wc_got], token)
    wc_other = exchange(wc_sum, 1, count)
    mid_total = sum_over_groups(mid_total, group, count, token)
    grad_w_out, grad_qkv, token_out = pl.pallas_call(
        functools.partial(grad_out_kernel, heads, slices),
        in_specs=[whole] * 5 + [pl.BlockSpec(memory_space=pl.ANY)],
        out_specs=[whole] * 3,
        out_shape=[
            like((width, width), f32),
            like((3, depth, depth), f32),
            like((8, 128), f32),
        ],
        scratch_shapes=[pltpu.VMEM((hm, width), f32)],
        compiler_params=params(8, False),
        cost_estimate=cost(4 * width**3, 3 * width * width * 4),
    )(wc_sum, wc_other, mixed, tokens, d_qkv, mid_total)

    mid_parts = gather_group(mid_total, count)
    grad_w_mid, grad_w_slice, grad_temp = pl.pallas_call(
        functools.partial(finish_kernel, depth),
        in_specs=[whole] * group + [pl.BlockSpec(memory_space=pl.ANY)],
        out_specs=[whole] * 3,
        out_shape=[
            like((width, width), f32),
            like((depth, slices), f32),
            like((1, depth), f32),
        ],
        scratch_shapes=[pltpu.VMEM((slices, 128), f32)],
        compiler_params=params(8, False),
        cost_estimate=cost(0, 2 * width * width * 4),
    )(*mid_parts, token_out)
    return (
        attended,
        feats_grad,
        grad_w_mid,
        grad_w_out,
        grad_w_slice,
        grad_temp.reshape(depth),
        grad_qkv,
    )


def solution(mesh):
    in_specs = (
        P(("design", "node"), None),
        P(("design", "node"), None),
        P(("design", "node")),
        P(("design", "node")),
        P(),
        P(),
        P(),
        P(),
        P(),
    )
    out_specs = (
        P(("design", "node"), None),
        P(("design", "node"), None),
        P("design", None),
        P("design", None),
        P("design", None),
        P("design"),
        P("design", None, None),
    )
    return jax.shard_map(
        functools.partial(shards, mesh.shape["node"]),
        mesh=mesh,
        in_specs=in_specs,
        out_specs=out_specs,
        check_vma=False,
    )
```

```python
import functools
import math

import jax
import jax.numpy as jnp
from jax import lax
from jax.experimental import pallas as pl
from jax.experimental.pallas import tpu as pltpu
from jax.sharding import PartitionSpec as P

f32 = jnp.float32
bf16 = jnp.bfloat16
eps_norm = 1e-05
exact = lax.Precision.HIGHEST
group = 4
sub_block = 512
mib = 1024 * 1024


def nn(a, b, precision=None):
    return lax.dot_general(
        a, b, (((1,), (0,)), ((), ())), preferred_element_type=f32, precision=precision
    )


def nt(a, b, precision=None):
    return lax.dot_general(
        a, b, (((1,), (1,)), ((), ())), preferred_element_type=f32, precision=precision
    )


def tn(a, b, precision=None):
    return lax.dot_general(
        a, b, (((0,), (0,)), ((), ())), preferred_element_type=f32, precision=precision
    )


def log2(size):
    return size.bit_length() - 1


def rows_of(shape):
    return lax.broadcasted_iota(jnp.int32, shape, 0)


def cols_of(shape):
    return lax.broadcasted_iota(jnp.int32, shape, 1)


def spread_matrix(width, small):
    shape = (width, small)
    return jnp.where((rows_of(shape) & (small - 1)) == cols_of(shape), 1.0, 0.0).astype(bf16)


def same_block(rows, cols, row_size, col_size):
    shape = (rows, cols)
    return rows_of(shape) >> log2(row_size) == cols_of(shape) >> log2(col_size)


def two_pieces(x):
    high = x.astype(bf16)
    return high, (x - high.astype(f32)).astype(bf16)


def fold_rows(x, heads, size):
    total = x[0:size]
    for h in range(1, heads):
        total = total + x[h * size : (h + 1) * size]
    return total


def group_place():
    return lax.axis_index("node") % group


def stats_kernel(
    heads,
    slices,
    owned_ref,
    temp_ref,
    valid_far,
    feats_far,
    cot_far,
    w_mid_far,
    w_slice_far,
    w_out_far,
    mid_ref,
    wt_ref,
    aux_ref,
    sw_ref,
    keep_ref,
    send_ref,
    wc_keep_ref,
    wc_send_ref,
    feats_ref,
    cot_ref,
    valid_ref,
    w_mid_ref,
    w_slice_ref,
    w_out_ref,
    raw_acc,
    norm_acc,
    wc_acc,
    pack,
    sems,
):
    width = w_mid_ref.shape[0]
    depth = width // heads
    hm = heads * slices
    rows = feats_ref.shape[0]
    piece = min(4 * sub_block, rows)
    count = rows // piece
    small = [
        pltpu.make_async_copy(source, target, sems.at[i])
        for i, (source, target) in enumerate(
            (
                (w_slice_far, w_slice_ref),
                (w_mid_far, w_mid_ref),
                (valid_far, valid_ref),
                (w_out_far, w_out_ref),
            )
        )
    ]
    first, rest = pl.ds(0, piece), pl.ds(piece, rows - piece)
    large = [
        pltpu.make_async_copy(source, target, sems.at[len(small) + i])
        for i, (source, target) in enumerate(
            (
                (feats_far.at[first, :], feats_ref.at[first, :]),
                (feats_far.at[rest, :], feats_ref.at[rest, :]),
                (cot_far, cot_ref),
            )
        )
    ]
    for copy in small[:2] + large[:1] + small[2:] + large[1:]:
        copy.start()

    raw_acc[...] = jnp.zeros_like(raw_acc)
    norm_acc[...] = jnp.zeros_like(norm_acc)
    wc_acc[...] = jnp.zeros_like(wc_acc)
    spread_d = spread_matrix(width, depth)
    spread_m = spread_matrix(hm, slices)
    for copy in small + large[:1]:
        copy.wait()
    temp = jnp.broadcast_to(temp_ref[...].astype(f32), (16, depth)).astype(bf16)
    half = nt(spread_m, w_slice_ref[...]).astype(bf16)
    full = nt(half, spread_d)
    sw_ref[0:hm, :] = jnp.where(same_block(hm, width, slices, depth), full, 0.0).astype(bf16)
    full = nt(temp, spread_d)
    sw_ref[hm : hm + 16, :] = jnp.where(same_block(16, width, 1, depth), full, 0.0).astype(bf16)
    owned = owned_ref[0]

    def products(i):
        at = slice(i * piece, (i + 1) * piece)
        mid = nn(feats_ref[at, :], w_mid_ref[...]).astype(bf16)
        mid_ref[at, :] = mid
        return mid, nt(sw_ref[...], mid)

    def statistics(i, mid, scores):
        at = slice(i * piece, (i + 1) * piece)
        zsum = scores[hm : hm + heads]
        small = jnp.exp(-jnp.abs(zsum))
        inv_tau = 1.0 / (0.5 + (jnp.maximum(zsum, 0.0) + jnp.log(1.0 + small)))
        sig = jnp.where(zsum >= 0.0, 1.0, small) / (1.0 + small)
        position = i * piece + cols_of((1, piece))
        live = (valid_ref[:, at] > 0) & (position < owned)
        live_f = live.astype(f32)
        rounded, sums, logs = [], [], []
        for h in range(heads):
            span = slice(h * slices, (h + 1) * slices)
            logits = scores[span] * inv_tau[h : h + 1]
            peak = jnp.max(logits, axis=0, keepdims=True)
            expo = jnp.exp(logits - peak)
            total = jnp.sum(expo, axis=0, keepdims=True)
            weights = expo * (live_f / total)
            rounded.append(weights.astype(bf16))
            lanes = weights[:, 0:128]
            for c in range(1, piece // 128):
                lanes = lanes + weights[:, c * 128 : (c + 1) * 128]
            sums.append(lanes)
            logs.append(jnp.where(live, peak + jnp.log(total), jnp.inf))
        wt = jnp.concatenate(rounded, axis=0)
        wt_ref[:, at] = wt
        norm_acc[...] += jnp.concatenate(sums, axis=0)
        aux_ref[:, at] = jnp.concatenate([inv_tau] + logs + [sig * inv_tau], axis=0)
        raw_acc[...] += nn(wt, mid)
        wc_acc[...] += nn(wt, cot_ref[at, :])

    ready = products(0)
    large[1].wait()
    large[2].wait()
    for i in range(count):
        current = ready
        if i + 1 < count:
            ready = products(i + 1)
        statistics(i, *current)

    diagonal = same_block(hm, width, slices, depth)
    raw = fold_rows(jnp.where(diagonal, raw_acc[...], 0.0), heads, slices)
    high, low = two_pieces(wc_acc[...])
    w_out = w_out_ref[...]
    mixed = nt(high, w_out) + nt(low, w_out)
    mixed = fold_rows(jnp.where(diagonal, mixed, 0.0), heads, slices)
    norm = jnp.sum(norm_acc[...].T, axis=0, keepdims=True)
    first = rows_of((8, 128)) == 0
    for j in range(2):
        part = slice(j * 128, (j + 1) * 128)
        pack[j, 0:slices, :] = raw[:, part]
        pack[j, slices : 2 * slices, :] = mixed[:, part]
        pack[j, 2 * slices :, :] = jnp.where(first, norm[:, part], 0.0)
    place = group_place()
    keep_ref[...] = pack[place & 1]
    send_ref[...] = pack[(place & 1) ^ 1]
    rows = hm // 2
    for k, out in enumerate((wc_keep_ref, wc_send_ref)):
        out[...] = wc_acc[pl.ds(pl.multiple_of(((place & 1) ^ k) * rows, 8), rows), :]


def between_kernel(
    heads,
    slices,
    mid_ref,
    sw_ref,
    aux_ref,
    w_slice_ref,
    w_qkv_ref,
    _,
    logits_ref,
    weights_ref,
    sb_ref,
    w_cat_ref,
    token_ref,
):
    depth = w_slice_ref.shape[0]
    width = heads * depth
    hm = heads * slices
    rows = mid_ref.shape[0]
    piece = min(sub_block, rows)
    token_ref[...] = jnp.zeros_like(token_ref)
    spread_d = spread_matrix(width, depth)
    spread_m = spread_matrix(hm, slices)
    half = nn(spread_d, w_slice_ref[...]).astype(bf16)
    full = nt(half, spread_m)
    sb_ref[...] = jnp.where(same_block(width, hm, depth, slices), full, 0.0).astype(bf16)
    w_cat = jnp.zeros((depth, 128), f32)
    for i in range(3):
        place_at = jnp.where(rows_of((depth, 128)) + i * depth == cols_of((depth, 128)), 1.0, 0.0)
        w_cat = w_cat + nn(w_qkv_ref[i], place_at.astype(bf16))
    w_cat_ref[...] = w_cat.astype(bf16)
    for i in range(rows // piece):
        at = slice(i * piece, (i + 1) * piece)
        scores = nt(sw_ref[0:hm, :], mid_ref[at, :])
        for h in range(heads):
            span = slice(h * slices, (h + 1) * slices)
            logits = scores[span] * aux_ref[h : h + 1, at]
            logits_ref[span, at] = logits
            weights_ref[span, at] = jnp.exp(logits - aux_ref[heads + h : heads + h + 1, at])


def lanes_at(x, lane, *where):
    place = cols_of(x.shape) >> log2(lane)
    total = jnp.zeros_like(x)
    for value, at, to in where:
        shift = (to - at) * lane % 128
        moved = pltpu.roll(value, shift, 1) if shift else value
        total = jnp.where(place == to, moved, total)
    return total.astype(bf16)


def split(x):
    high = x.astype(bf16).astype(f32)
    return high, x - high


def tokens_kernel(
    heads,
    slices,
    own_ref,
    got_ref,
    w_cat_ref,
    w_out_ref,
    mw_ref,
    dr_ref,
    drt_ref,
    dn_ref,
    mixed_ref,
    tokens_ref,
    d_qkv_ref,
    pack,
):
    width = w_out_ref.shape[0]
    depth = width // heads
    hm = heads * slices
    place = group_place() & 1
    pack[place] = own_ref[...]
    pack[place ^ 1] = got_ref[...]
    per = 128 // depth

    def compact(first):
        pieces = []
        for h in range(heads):
            x = pack[h // per, first : first + slices, :]
            shift = (h % per) * depth
            pieces.append(pltpu.roll(x, 128 - shift, 1) if shift else x)
        x = jnp.concatenate(pieces, axis=0)
        return jnp.where(cols_of(x.shape) < depth, x, 0.0)

    raw = compact(0)
    d_mixed = compact(slices)
    norm = jnp.concatenate([pack[j, 2 * slices :, :].T[:, 0:1] for j in range(2)], axis=0)
    inverse = 1.0 / (norm + eps_norm)
    tokens = raw * inverse
    w_cat = w_cat_ref[...]

    t_high, rest = split(tokens)
    t_low, rest = split(rest)
    left = lanes_at(tokens, depth, (t_high, 0, 0), (t_low, 0, 1), (rest, 0, 2))
    blank = jnp.zeros((128 - 3 * depth, 128), bf16)
    qkv = nn(left, jnp.concatenate([w_cat, w_cat, w_cat, blank], axis=0))
    high, low = split(qkv)
    q_left = lanes_at(qkv, depth, (high, 0, 0), (high, 0, 1), (low, 0, 2))
    k_right = lanes_at(qkv, depth, (high, 1, 0), (low, 1, 1), (high, 1, 2))
    v_right = lanes_at(qkv, depth, (high, 2, 0), (low, 2, 1), (high, 2, 2))
    q_pair = lanes_at(qkv, depth, (high, 0, 0), (low, 0, 1))
    k_pair = lanes_at(qkv, depth, (high, 1, 0), (low, 1, 1))
    v_pair = lanes_at(qkv, depth, (high, 2, 0), (low, 2, 1))
    g_high, g_low = split(d_mixed)
    g_left = lanes_at(qkv, depth, (g_high, 0, 0), (g_high, 0, 1), (g_low, 0, 2))
    g_pair = lanes_at(qkv, depth, (g_high, 0, 0), (g_low, 0, 1))

    def times_pair(dot, x, pair):
        x_high, x_low = two_pieces(x)
        both = dot(x_high, pair)
        low_part = dot(x_low, pair)
        total = both + pltpu.roll(both, 128 - depth, 1) + low_part
        return jnp.where(cols_of(total.shape) < depth, total, 0.0)

    blocks = same_block(hm, hm, slices, slices)
    scale = 1.0 / math.sqrt(depth)
    scores = jnp.where(blocks, nt(q_left, k_right) * scale, -jnp.inf)
    expo = jnp.exp(scores - jnp.max(scores, axis=1, keepdims=True))
    probs = expo * (1.0 / jnp.sum(expo, axis=1, keepdims=True))
    mixed_b = times_pair(nn, probs, v_pair).astype(bf16)

    spread_d = jnp.where(
        (rows_of((width, 128)) & (depth - 1)) == cols_of((width, 128)), 1.0, 0.0
    ).astype(bf16)
    diagonal = same_block(hm, width, slices, depth)
    diagonal_t = same_block(width, hm, depth, slices)
    mixed_block = jnp.where(diagonal, nt(mixed_b, spread_d), 0.0).astype(bf16)
    mw_ref[...] = nn(mixed_block, w_out_ref[...]).astype(bf16)
    mixed_ref[...] = mixed_b
    tokens_ref[...] = tokens

    d_probs = nt(g_left, v_right)
    d_v = times_pair(tn, probs, g_pair)
    d_scores = probs * (d_probs - jnp.sum(probs * d_probs, axis=1, keepdims=True)) * scale
    d_q = times_pair(nn, d_scores, k_pair)
    d_k = times_pair(tn, d_scores, q_pair)
    d_qkv = d_q + pltpu.roll(d_k, depth, 1) + pltpu.roll(d_v, 2 * depth, 1)
    d_qkv_ref[...] = d_qkv
    d_high, d_low = two_pieces(d_qkv)
    d_tokens = nt(d_high, w_cat) + nt(d_low, w_cat)
    raw = raw[:, 0:depth]
    d_raw_b = (d_tokens * inverse).astype(bf16)
    d_norm = -jnp.sum(d_tokens * raw, axis=1, keepdims=True) * inverse * inverse
    dn_ref[...] = jnp.broadcast_to(d_norm, dn_ref.shape)
    spread_d = spread_matrix(width, depth)
    dr_ref[...] = jnp.where(diagonal, nt(d_raw_b, spread_d), 0.0).astype(bf16)
    drt_ref[...] = jnp.where(diagonal_t, nt(spread_d, d_raw_b), 0.0).astype(bf16)


def backward_kernel(
    heads,
    slices,
    aux_ref,
    wt_ref,
    logits_ref,
    weights_ref,
    mid_ref,
    cot_ref,
    feats_ref,
    sb_ref,
    mw_ref,
    dr_ref,
    drt_ref,
    dn_ref,
    temp_ref,
    _,
    dmt_ref,
    send0,
    send1,
    send2,
    send3,
    yt,
    grad_acc,
    small_acc,
    pack,
):
    width = mid_ref.shape[1]
    depth = width // heads
    hm = heads * slices
    block = feats_ref.shape[0]

    grad_acc[...] = jnp.zeros_like(grad_acc)
    small_acc[...] = jnp.zeros_like(small_acc)
    yt[:, 0:hm] = drt_ref[...]
    yt[:, hm:] = sb_ref[...]

    temp = jnp.broadcast_to(temp_ref[...].astype(f32), (16, depth)).astype(bf16)
    same = (rows_of((depth, depth)) == cols_of((depth, depth))).astype(f32).astype(bf16)
    temp = nt(same, temp)[:, 0:1]
    piece = min(2 * sub_block, block)
    pieces = [slice(i * piece, (i + 1) * piece) for i in range(block // piece)]

    def products(at):
        return nt(dr_ref[...], mid_ref[at, :]) + nt(mw_ref[...], cot_ref[at, :])

    def per_head(at, products):
        u_b, sums = [], []
        aux = aux_ref[:, at]
        for h in range(heads):
            span = slice(h * slices, (h + 1) * slices)
            inv_tau = aux[h : h + 1]
            logits = logits_ref[span, at]
            weights = weights_ref[span, at]
            d_weights = products[span] + dn_ref[span, 0:1]
            mean = jnp.sum(weights * d_weights, axis=0, keepdims=True)
            d_logits = weights * (d_weights - mean)
            d_tau = jnp.sum(d_logits * logits, axis=0, keepdims=True)
            sums.append(-d_tau * aux[2 * heads + h : 2 * heads + h + 1])
            u_b.append((d_logits * inv_tau).astype(bf16))
        c_sum = jnp.concatenate(sums, axis=0)
        c_high = c_sum.astype(bf16).astype(f32)
        u_b.append(jnp.concatenate([c_high, c_sum - c_high], axis=0).astype(bf16))
        return jnp.concatenate(u_b, axis=0), sums

    def outputs(at, u_b, sums):
        d_mid = nn(yt[...], jnp.concatenate([wt_ref[:, at], u_b[0:hm]], axis=0))
        d_mid = [
            (d_mid[h * depth : (h + 1) * depth] + temp * sums[h]).astype(bf16)
            for h in range(heads)
        ]
        d_mid = jnp.concatenate(d_mid, axis=0)
        dmt_ref[:, at] = d_mid
        grad_acc[...] += nn(d_mid, feats_ref[at, :])
        small_acc[...] += nn(u_b, mid_ref[at, :])

    ready = products(pieces[0])
    for i, at in enumerate(pieces):
        current = ready
        if i + 1 < len(pieces):
            ready = products(pieces[i + 1])
        outputs(at, *per_head(at, current))

    grad = grad_acc[...].T
    u_part = jnp.where(same_block(hm, width, slices, depth), small_acc[0:hm, :], 0.0)
    u_part = fold_rows(u_part, heads, slices)
    c_part = small_acc[hm : hm + heads, :] + small_acc[hm + heads : hm + 2 * heads, :]
    c_part = jnp.where(same_block(heads, width, 1, depth), c_part, 0.0)
    c_part = jnp.sum(c_part, axis=0, keepdims=True)

    def fold_lanes(x):
        total = x[:, 0:128]
        for j in range(1, width // 128):
            total = total + x[:, j * 128 : (j + 1) * 128]
        shift = 64
        while shift >= depth:
            total = total + pltpu.roll(total, shift, 1)
            shift //= 2
        return total

    u_part = fold_lanes(u_part)
    c_part = fold_lanes(jnp.broadcast_to(c_part, (slices, width)))
    where_lane = cols_of((slices, 128))
    extra = jnp.where(where_lane < depth, u_part, c_part)
    rows = width // group
    more = slices // group
    for j in range(group):
        pack[j, 0:rows, :] = grad[j * rows : (j + 1) * rows]
        pack[j, rows : rows + more, 0:128] = extra[j * more : (j + 1) * more]
        pack[j, rows : rows + more, 128:] = jnp.zeros((more, width - 128), f32)
    place = group_place()
    for k, send in enumerate((send0, send1, send2, send3)):
        send[...] = pack[place ^ k]


def rows_kernel(wt_ref, dmt_ref, mw_ref, w_mid_ref, _, attended_ref, feats_grad_ref, token_ref):
    block = attended_ref.shape[0]
    at = pl.ds(pl.multiple_of(pl.program_id(0) * block, block), block)
    token_ref[...] = jnp.zeros_like(token_ref)
    attended_ref[...] = tn(wt_ref[:, at], mw_ref[...]).astype(bf16)
    feats_grad_ref[...] = lax.dot_general(
        dmt_ref[:, at], w_mid_ref[...], (((0,), (1,)), ((), ())), preferred_element_type=f32
    ).astype(bf16)


def grad_out_kernel(
    heads,
    slices,
    own_ref,
    other_ref,
    mixed_ref,
    tokens_ref,
    d_qkv_ref,
    _,
    grad_out_ref,
    grad_qkv_ref,
    token_ref,
    whole,
):
    token_ref[...] = jnp.zeros_like(token_ref)
    hm = heads * slices
    depth = grad_qkv_ref.shape[1]
    width = heads * depth
    t_high, t_low = two_pieces(tokens_ref[...])
    d_high, d_low = two_pieces(d_qkv_ref[...])
    grads = tn(t_high, d_high) + tn(t_high, d_low) + tn(t_low, d_high)
    for i in range(3):
        at = pltpu.roll(grads, 128 - i * depth, 1) if i else grads
        grad_qkv_ref[i] = at[0:depth, 0:depth]
    spread_d = jnp.where(
        (rows_of((width, 128)) & (depth - 1)) == cols_of((width, 128)), 1.0, 0.0
    ).astype(bf16)
    diagonal_t = same_block(width, hm, depth, slices)
    mixed_t = jnp.where(diagonal_t, nt(spread_d, mixed_ref[...]), 0.0).astype(bf16)
    place = group_place() & 1
    rows = own_ref.shape[0]
    for k, part in enumerate((own_ref, other_ref)):
        whole[pl.ds(pl.multiple_of((place ^ k) * rows, 8), rows), :] = part[...]
    high, low = two_pieces(whole[...])
    grad_out_ref[...] = nn(mixed_t, high) + nn(mixed_t, low)


def finish_kernel(depth, m0, m1, m2, m3, _, grad_mid_ref, slice_ref, temp_ref, extra):
    place = group_place()
    slices = slice_ref.shape[1]
    more = slices // group
    rows = m0.shape[0] - more
    for k, part in enumerate((m0, m1, m2, m3)):
        at = pl.ds(pl.multiple_of((place ^ k) * rows, 8), rows)
        grad_mid_ref[at, :] = part[0:rows, :]
        extra[pl.ds(pl.multiple_of((place ^ k) * more, 8), more), :] = part[rows:, 0:128]
    turned = extra[...].T
    slice_ref[...] = turned[0:depth, 0:slices]
    temp_ref[...] = extra[0:1, depth : 2 * depth]


def full(shape):
    zeros = (0,) * len(shape)
    return pl.BlockSpec(shape, lambda *_: zeros)


def params(mebibytes, grid=True):
    semantics = ("arbitrary",) if grid else None
    return pltpu.CompilerParams(
        dimension_semantics=semantics, vmem_limit_bytes=mebibytes * mib
    )


def cost(flops, moved, transcendentals=0):
    return pl.CostEstimate(flops=flops, bytes_accessed=moved, transcendentals=transcendentals)


def exchange(x, k, count):
    return lax.ppermute(x, "node", [(i, i ^ k) for i in range(count)])


def sum_kernel(count, *refs):
    total = refs[0][...] + refs[count - 1][...]
    if count == 4:
        total = total + (refs[1][...] + refs[2][...])
    refs[-1][...] = total


def sum_behind(parts, *before):
    return pl.pallas_call(
        functools.partial(sum_kernel, len(parts)),
        out_shape=jax.ShapeDtypeStruct(parts[0].shape, f32),
        in_specs=[pl.BlockSpec(memory_space=pltpu.VMEM)] * len(parts)
        + [pl.BlockSpec(memory_space=pl.ANY)] * len(before),
        out_specs=pl.BlockSpec(memory_space=pltpu.VMEM),
        compiler_params=params(2, False),
        cost_estimate=cost(3 * parts[0].size, 5 * parts[0].size * 4),
    )(*parts, *before)


def scatter_group(parts, count):
    got = [parts[0]] + [exchange(parts[k], k, count) for k in range(1, group)]
    return (got[0] + got[1]) + (got[2] + got[3])


def sum_stage(total, stride, others, count, *before):
    parts = [total] + [exchange(total, stride * j, count) for j in range(others, 0, -1)]
    if before:
        return sum_behind(parts, *before)
    if others == 1:
        return parts[0] + parts[1]
    return (parts[0] + parts[3]) + (parts[1] + parts[2])


def sum_over_groups(total, stride, count, *before):
    while stride < count:
        others = 3 if count // stride % 4 == 0 else 1
        total = sum_stage(total, stride, others, count, *before)
        stride *= others + 1
    return total


def gather_group(total, count):
    return [total] + [exchange(total, k, count) for k in range(1, group)]


def shards(count, feats, cotangent, valid, owned, w_mid, w_slice, temp_vec, w_qkv, w_out):
    rows, width = feats.shape
    depth, slices = w_slice.shape
    heads = width // depth
    hm = heads * slices
    unit = 2 * rows * width * width
    smem = pl.BlockSpec(memory_space=pltpu.SMEM)

    def blocks(size):
        return (rows // size,), pl.BlockSpec((size, width), lambda i: (i, 0))

    def like(shape, dtype):
        return jax.ShapeDtypeStruct(shape, dtype)

    def far(x):
        return pltpu.with_memory_space_constraint(x, pltpu.HBM)

    near = pltpu.VMEM
    whole = pl.BlockSpec(memory_space=pltpu.VMEM)

    temp = temp_vec.reshape(1, depth)
    half = (2 * slices + 8, 128)
    wide = (hm // 2, width)
    inputs = (valid.reshape(1, rows), feats, cotangent, w_mid, w_slice, w_out)
    (
        mid,
        wt,
        aux,
        sw,
        keep,
        send,
        wc_keep,
        wc_send,
        feats_near,
        cot_near,
    ) = pl.pallas_call(
        functools.partial(stats_kernel, heads, slices),
        in_specs=[smem, whole] + [pl.BlockSpec(memory_space=pltpu.HBM)] * len(inputs),
        out_specs=[whole] * 10,
        out_shape=[
            near((rows, width), bf16),
            near((hm, rows), bf16),
            near((3 * heads, rows), f32),
            near((hm + 16, width), bf16),
            near(half, f32),
            near(half, f32),
            near(wide, f32),
            near(wide, f32),
            near((rows, width), bf16),
            near((rows, width), bf16),
        ],
        scratch_shapes=[
            pltpu.VMEM((1, rows), jnp.int32),
            pltpu.VMEM((width, width), bf16),
            pltpu.VMEM((depth, slices), bf16),
            pltpu.VMEM((width, width), bf16),
            pltpu.VMEM((hm, width), f32),
            pltpu.VMEM((hm, 128), f32),
            pltpu.VMEM((hm, width), f32),
            pltpu.VMEM((2,) + half, f32),
            pltpu.SemaphoreType.DMA((7,)),
        ],
        compiler_params=params(24, False),
        cost_estimate=cost(4 * unit, rows * width * 8, rows * hm),
    )(owned, far(temp), *map(far, inputs))

    own = keep + exchange(send, 1, count)
    wc_got = exchange(wc_send, 1, count)
    wc_sum = sum_behind([wc_keep, wc_got], own)
    logits, weights, sb, w_cat, token = pl.pallas_call(
        functools.partial(between_kernel, heads, slices),
        in_specs=[whole] * 5 + [pl.BlockSpec(memory_space=pl.ANY)],
        out_specs=[whole] * 5,
        out_shape=[
            near((hm, rows), f32),
            near((hm, rows), f32),
            near((width, hm), bf16),
            near((depth, 128), bf16),
            near((8, 128), f32),
        ],
        compiler_params=params(16, False),
        cost_estimate=cost(3 * unit, rows, rows),
    )(mid, sw, aux, w_slice, w_qkv, own)
    own = sum_stage(own, 2, 3, count, token)
    wc_got = exchange(wc_sum, 2, count)
    wc_sum = sum_behind([wc_sum, wc_got], own)
    own = sum_over_groups(own, 8, count)
    other = exchange(own, 1, count)
    stride = 4
    wc_got = exchange(wc_sum, stride, count)
    while 4 * stride < count:
        wc_sum = wc_sum + wc_got
        stride *= 2
        wc_got = exchange(wc_sum, stride, count)

    mw, dr, drt, dn, mixed, tokens, d_qkv = pl.pallas_call(
        functools.partial(tokens_kernel, heads, slices),
        out_shape=[
            near((hm, width), bf16),
            near((hm, width), bf16),
            near((width, hm), bf16),
            near((hm, 128), f32),
            near((hm, 128), bf16),
            near((hm, 128), f32),
            near((hm, 128), f32),
        ],
        scratch_shapes=[pltpu.VMEM((2,) + half, f32)],
        compiler_params=params(16, False),
        cost_estimate=cost(3 * width**3, 4 * width * width * 4, hm * hm),
    )(own, other, w_cat, w_out)
    larger = (width // group + slices // group, width)
    dmt, *sends = pl.pallas_call(
        functools.partial(backward_kernel, heads, slices),
        in_specs=[whole] * 13 + [pl.BlockSpec(memory_space=pl.ANY)],
        out_specs=[whole] * (1 + group),
        out_shape=[near((width, rows), bf16)] + [near(larger, f32)] * group,
        scratch_shapes=[
            pltpu.VMEM((width, 2 * hm), bf16),
            pltpu.VMEM((width, width), f32),
            pltpu.VMEM((hm + 16, width), f32),
            pltpu.VMEM((group,) + larger, f32),
        ],
        compiler_params=params(24, False),
        cost_estimate=cost(unit * 3 // 10, rows * width, rows),
    )(aux, wt, logits, weights, mid, cot_near, feats_near, sb, mw, dr, drt, dn, temp, wc_sum)

    mid_total = scatter_group(sends, count)
    wc_sum = sum_behind([wc_sum, wc_got], sends[1])
    wc_got = exchange(wc_sum, count // 2, count)

    block = min(1024, rows)
    grid, by_rows = blocks(block)
    attended, feats_grad, token = pl.pallas_call(
        rows_kernel,
        grid=grid,
        in_specs=[
            whole,
            whole,
            whole,
            full((width, width)),
            pl.BlockSpec(memory_space=pl.ANY),
        ],
        out_specs=[by_rows, by_rows, full((8, 128))],
        out_shape=[like((rows, width), bf16)] * 2 + [like((8, 128), f32)],
        compiler_params=params(20),
        cost_estimate=cost(2 * unit, rows * width * 8),
    )(wt, dmt, mw, w_mid, mid_total)

    wc_sum = sum_behind([wc_sum, wc_got], token)
    wc_other = exchange(wc_sum, 1, count)
    mid_total = sum_over_groups(mid_total, group, count, token)
    grad_w_out, grad_qkv, token_out = pl.pallas_call(
        functools.partial(grad_out_kernel, heads, slices),
        in_specs=[whole] * 5 + [pl.BlockSpec(memory_space=pl.ANY)],
        out_specs=[whole] * 3,
        out_shape=[
            like((width, width), f32),
            like((3, depth, depth), f32),
            like((8, 128), f32),
        ],
        scratch_shapes=[pltpu.VMEM((hm, width), f32)],
        compiler_params=params(8, False),
        cost_estimate=cost(4 * width**3, 3 * width * width * 4),
    )(wc_sum, wc_other, mixed, tokens, d_qkv, mid_total)

    mid_parts = gather_group(mid_total, count)
    grad_w_mid, grad_w_slice, grad_temp = pl.pallas_call(
        functools.partial(finish_kernel, depth),
        in_specs=[whole] * group + [pl.BlockSpec(memory_space=pl.ANY)],
        out_specs=[whole] * 3,
        out_shape=[
            like((width, width), f32),
            like((depth, slices), f32),
            like((1, depth), f32),
        ],
        scratch_shapes=[pltpu.VMEM((slices, 128), f32)],
        compiler_params=params(8, False),
        cost_estimate=cost(0, 2 * width * width * 4),
    )(*mid_parts, token_out)
    return (
        attended,
        feats_grad,
        grad_w_mid,
        grad_w_out,
        grad_w_slice,
        grad_temp.reshape(depth),
        grad_qkv,
    )


def solution(mesh):
    in_specs = (
        P(("design", "node"), None),
        P(("design", "node"), None),
        P(("design", "node")),
        P(("design", "node")),
        P(),
        P(),
        P(),
        P(),
        P(),
    )
    out_specs = (
        P(("design", "node"), None),
        P(("design", "node"), None),
        P("design", None),
        P("design", None),
        P("design", None),
        P("design"),
        P("design", None, None),
    )
    return jax.shard_map(
        functools.partial(shards, mesh.shape["node"]),
        mesh=mesh,
        in_specs=in_specs,
        out_specs=out_specs,
        check_vma=False,
    )
```

```python
import functools
import math

import jax
import jax.numpy as jnp
from jax import lax
from jax.experimental import pallas as pl
from jax.experimental.pallas import tpu as pltpu
from jax.sharding import PartitionSpec as P

f32 = jnp.float32
bf16 = jnp.bfloat16
eps_norm = 1e-05
exact = lax.Precision.HIGHEST
group = 4
sub_block = 512
mib = 1024 * 1024


def nn(a, b, precision=None):
    return lax.dot_general(
        a, b, (((1,), (0,)), ((), ())), preferred_element_type=f32, precision=precision
    )


def nt(a, b, precision=None):
    return lax.dot_general(
        a, b, (((1,), (1,)), ((), ())), preferred_element_type=f32, precision=precision
    )


def tn(a, b, precision=None):
    return lax.dot_general(
        a, b, (((0,), (0,)), ((), ())), preferred_element_type=f32, precision=precision
    )


def log2(size):
    return size.bit_length() - 1


def rows_of(shape):
    return lax.broadcasted_iota(jnp.int32, shape, 0)


def cols_of(shape):
    return lax.broadcasted_iota(jnp.int32, shape, 1)


def spread_matrix(width, small):
    shape = (width, small)
    return jnp.where((rows_of(shape) & (small - 1)) == cols_of(shape), 1.0, 0.0).astype(bf16)


def same_block(rows, cols, row_size, col_size):
    shape = (rows, cols)
    return rows_of(shape) >> log2(row_size) == cols_of(shape) >> log2(col_size)


def two_pieces(x):
    high = x.astype(bf16)
    return high, (x - high.astype(f32)).astype(bf16)


def fold_rows(x, heads, size):
    total = x[0:size]
    for h in range(1, heads):
        total = total + x[h * size : (h + 1) * size]
    return total


def group_place():
    return lax.axis_index("node") % group


def stats_kernel(
    heads,
    slices,
    owned_ref,
    temp_ref,
    valid_far,
    feats_far,
    cot_far,
    w_mid_far,
    w_slice_far,
    w_out_far,
    mid_ref,
    wt_ref,
    aux_ref,
    sw_ref,
    keep_ref,
    send_ref,
    wc_keep_ref,
    wc_send_ref,
    feats_ref,
    cot_ref,
    valid_ref,
    w_mid_ref,
    w_slice_ref,
    w_out_ref,
    raw_acc,
    norm_acc,
    wc_acc,
    pack,
    sems,
):
    width = w_mid_ref.shape[0]
    depth = width // heads
    hm = heads * slices
    rows = feats_ref.shape[0]
    piece = min(2 * sub_block, rows)
    count = rows // piece
    small = [
        pltpu.make_async_copy(source, target, sems.at[i])
        for i, (source, target) in enumerate(
            (
                (w_slice_far, w_slice_ref),
                (w_mid_far, w_mid_ref),
                (valid_far, valid_ref),
                (w_out_far, w_out_ref),
            )
        )
    ]
    first, rest = pl.ds(0, piece), pl.ds(piece, rows - piece)
    large = [
        pltpu.make_async_copy(source, target, sems.at[len(small) + i])
        for i, (source, target) in enumerate(
            (
                (feats_far.at[first, :], feats_ref.at[first, :]),
                (feats_far.at[rest, :], feats_ref.at[rest, :]),
                (cot_far, cot_ref),
            )
        )
    ]
    for copy in small[:2] + large[:1] + small[2:] + large[1:]:
        copy.start()

    raw_acc[...] = jnp.zeros_like(raw_acc)
    norm_acc[...] = jnp.zeros_like(norm_acc)
    wc_acc[...] = jnp.zeros_like(wc_acc)
    spread_d = spread_matrix(width, depth)
    spread_m = spread_matrix(hm, slices)
    for copy in small[:2] + large[:1]:
        copy.wait()
    temp = jnp.broadcast_to(temp_ref[...].astype(f32), (16, depth)).astype(bf16)
    half = nt(spread_m, w_slice_ref[...]).astype(bf16)
    full = nt(half, spread_d)
    sw_ref[0:hm, :] = jnp.where(same_block(hm, width, slices, depth), full, 0.0).astype(bf16)
    full = nt(temp, spread_d)
    sw_ref[hm : hm + 16, :] = jnp.where(same_block(16, width, 1, depth), full, 0.0).astype(bf16)
    owned = owned_ref[0]

    def products(i):
        at = slice(i * piece, (i + 1) * piece)
        mid = nn(feats_ref[at, :], w_mid_ref[...]).astype(bf16)
        mid_ref[at, :] = mid
        return mid, nt(sw_ref[...], mid)

    def statistics(i, mid, scores):
        at = slice(i * piece, (i + 1) * piece)
        zsum = scores[hm : hm + heads]
        small = jnp.exp(-jnp.abs(zsum))
        inv_tau = 1.0 / (0.5 + (jnp.maximum(zsum, 0.0) + jnp.log(1.0 + small)))
        sig = jnp.where(zsum >= 0.0, 1.0, small) / (1.0 + small)
        position = i * piece + cols_of((1, piece))
        live = (valid_ref[:, at] > 0) & (position < owned)
        live_f = live.astype(f32)
        rounded, sums, logs = [], [], []
        for h in range(heads):
            span = slice(h * slices, (h + 1) * slices)
            logits = scores[span] * inv_tau[h : h + 1]
            peak = jnp.max(logits, axis=0, keepdims=True)
            expo = jnp.exp(logits - peak)
            total = jnp.sum(expo, axis=0, keepdims=True)
            weights = expo * (live_f / total)
            rounded.append(weights.astype(bf16))
            lanes = weights[:, 0:128]
            for c in range(1, piece // 128):
                lanes = lanes + weights[:, c * 128 : (c + 1) * 128]
            sums.append(lanes)
            logs.append(jnp.where(live, peak + jnp.log(total), jnp.inf))
        wt = jnp.concatenate(rounded, axis=0)
        wt_ref[:, at] = wt
        norm_acc[...] += jnp.concatenate(sums, axis=0)
        aux_ref[:, at] = jnp.concatenate([inv_tau] + logs + [sig * inv_tau], axis=0)
        raw_acc[...] += nn(wt, mid)
        wc_acc[...] += nn(wt, cot_ref[at, :])

    ready = products(0)
    for copy in small[2:] + large[1:]:
        copy.wait()
    for i in range(count):
        current = ready
        if i + 1 < count:
            ready = products(i + 1)
        statistics(i, *current)

    diagonal = same_block(hm, width, slices, depth)
    raw = fold_rows(jnp.where(diagonal, raw_acc[...], 0.0), heads, slices)
    high, low = two_pieces(wc_acc[...])
    w_out = w_out_ref[...]
    mixed = nt(high, w_out) + nt(low, w_out)
    mixed = fold_rows(jnp.where(diagonal, mixed, 0.0), heads, slices)
    norm = jnp.sum(norm_acc[...].T, axis=0, keepdims=True)
    first = rows_of((8, 128)) == 0
    for j in range(2):
        part = slice(j * 128, (j + 1) * 128)
        pack[j, 0:slices, :] = raw[:, part]
        pack[j, slices : 2 * slices, :] = mixed[:, part]
        pack[j, 2 * slices :, :] = jnp.where(first, norm[:, part], 0.0)
    place = group_place()
    keep_ref[...] = pack[place & 1]
    send_ref[...] = pack[(place & 1) ^ 1]
    rows = hm // 2
    for k, out in enumerate((wc_keep_ref, wc_send_ref)):
        out[...] = wc_acc[pl.ds(pl.multiple_of(((place & 1) ^ k) * rows, 8), rows), :]


def between_kernel(
    heads,
    slices,
    mid_ref,
    sw_ref,
    aux_ref,
    w_slice_ref,
    w_qkv_ref,
    _,
    logits_ref,
    weights_ref,
    sb_ref,
    w_cat_ref,
    token_ref,
):
    depth = w_slice_ref.shape[0]
    width = heads * depth
    hm = heads * slices
    rows = mid_ref.shape[0]
    piece = min(sub_block, rows)
    token_ref[...] = jnp.zeros_like(token_ref)
    spread_d = spread_matrix(width, depth)
    spread_m = spread_matrix(hm, slices)
    half = nn(spread_d, w_slice_ref[...]).astype(bf16)
    full = nt(half, spread_m)
    sb_ref[...] = jnp.where(same_block(width, hm, depth, slices), full, 0.0).astype(bf16)
    w_cat = jnp.zeros((depth, 128), f32)
    for i in range(3):
        place_at = jnp.where(rows_of((depth, 128)) + i * depth == cols_of((depth, 128)), 1.0, 0.0)
        w_cat = w_cat + nn(w_qkv_ref[i], place_at.astype(bf16))
    w_cat_ref[...] = w_cat.astype(bf16)
    for i in range(rows // piece):
        at = slice(i * piece, (i + 1) * piece)
        scores = nt(sw_ref[0:hm, :], mid_ref[at, :])
        for h in range(heads):
            span = slice(h * slices, (h + 1) * slices)
            logits = scores[span] * aux_ref[h : h + 1, at]
            logits_ref[span, at] = logits
            weights_ref[span, at] = jnp.exp(logits - aux_ref[heads + h : heads + h + 1, at])


def lanes_at(x, lane, *where):
    place = cols_of(x.shape) >> log2(lane)
    total = jnp.zeros_like(x)
    for value, at, to in where:
        shift = (to - at) * lane % 128
        moved = pltpu.roll(value, shift, 1) if shift else value
        total = jnp.where(place == to, moved, total)
    return total.astype(bf16)


def split(x):
    high = x.astype(bf16).astype(f32)
    return high, x - high


def tokens_kernel(
    heads,
    slices,
    own_ref,
    got_ref,
    w_cat_ref,
    w_out_ref,
    mw_ref,
    dr_ref,
    drt_ref,
    dn_ref,
    mixed_ref,
    tokens_ref,
    d_qkv_ref,
    pack,
):
    width = w_out_ref.shape[0]
    depth = width // heads
    hm = heads * slices
    place = group_place() & 1
    pack[place] = own_ref[...]
    pack[place ^ 1] = got_ref[...]
    per = 128 // depth

    def compact(first):
        pieces = []
        for h in range(heads):
            x = pack[h // per, first : first + slices, :]
            shift = (h % per) * depth
            pieces.append(pltpu.roll(x, 128 - shift, 1) if shift else x)
        x = jnp.concatenate(pieces, axis=0)
        return jnp.where(cols_of(x.shape) < depth, x, 0.0)

    raw = compact(0)
    d_mixed = compact(slices)
    norm = jnp.concatenate([pack[j, 2 * slices :, :].T[:, 0:1] for j in range(2)], axis=0)
    inverse = 1.0 / (norm + eps_norm)
    tokens = raw * inverse
    w_cat = w_cat_ref[...]

    t_high, rest = split(tokens)
    t_low, rest = split(rest)
    left = lanes_at(tokens, depth, (t_high, 0, 0), (t_low, 0, 1), (rest, 0, 2))
    blank = jnp.zeros((128 - 3 * depth, 128), bf16)
    qkv = nn(left, jnp.concatenate([w_cat, w_cat, w_cat, blank], axis=0))
    high, low = split(qkv)
    q_left = lanes_at(qkv, depth, (high, 0, 0), (high, 0, 1), (low, 0, 2))
    k_right = lanes_at(qkv, depth, (high, 1, 0), (low, 1, 1), (high, 1, 2))
    v_right = lanes_at(qkv, depth, (high, 2, 0), (low, 2, 1), (high, 2, 2))
    q_pair = lanes_at(qkv, depth, (high, 0, 0), (low, 0, 1))
    k_pair = lanes_at(qkv, depth, (high, 1, 0), (low, 1, 1))
    v_pair = lanes_at(qkv, depth, (high, 2, 0), (low, 2, 1))
    g_high, g_low = split(d_mixed)
    g_left = lanes_at(qkv, depth, (g_high, 0, 0), (g_high, 0, 1), (g_low, 0, 2))
    g_pair = lanes_at(qkv, depth, (g_high, 0, 0), (g_low, 0, 1))

    def times_pair(dot, x, pair):
        x_high, x_low = two_pieces(x)
        both = dot(x_high, pair)
        low_part = dot(x_low, pair)
        total = both + pltpu.roll(both, 128 - depth, 1) + low_part
        return jnp.where(cols_of(total.shape) < depth, total, 0.0)

    blocks = same_block(hm, hm, slices, slices)
    scale = 1.0 / math.sqrt(depth)
    scores = jnp.where(blocks, nt(q_left, k_right) * scale, -jnp.inf)
    expo = jnp.exp(scores - jnp.max(scores, axis=1, keepdims=True))
    probs = expo * (1.0 / jnp.sum(expo, axis=1, keepdims=True))
    mixed_b = times_pair(nn, probs, v_pair).astype(bf16)

    spread_d = jnp.where(
        (rows_of((width, 128)) & (depth - 1)) == cols_of((width, 128)), 1.0, 0.0
    ).astype(bf16)
    diagonal = same_block(hm, width, slices, depth)
    diagonal_t = same_block(width, hm, depth, slices)
    mixed_block = jnp.where(diagonal, nt(mixed_b, spread_d), 0.0).astype(bf16)
    mw_ref[...] = nn(mixed_block, w_out_ref[...]).astype(bf16)
    mixed_ref[...] = mixed_b
    tokens_ref[...] = tokens

    d_probs = nt(g_left, v_right)
    d_v = times_pair(tn, probs, g_pair)
    d_scores = probs * (d_probs - jnp.sum(probs * d_probs, axis=1, keepdims=True)) * scale
    d_q = times_pair(nn, d_scores, k_pair)
    d_k = times_pair(tn, d_scores, q_pair)
    d_qkv = d_q + pltpu.roll(d_k, depth, 1) + pltpu.roll(d_v, 2 * depth, 1)
    d_qkv_ref[...] = d_qkv
    d_high, d_low = two_pieces(d_qkv)
    d_tokens = nt(d_high, w_cat) + nt(d_low, w_cat)
    raw = raw[:, 0:depth]
    d_raw_b = (d_tokens * inverse).astype(bf16)
    d_norm = -jnp.sum(d_tokens * raw, axis=1, keepdims=True) * inverse * inverse
    dn_ref[...] = jnp.broadcast_to(d_norm, dn_ref.shape)
    spread_d = spread_matrix(width, depth)
    dr_ref[...] = jnp.where(diagonal, nt(d_raw_b, spread_d), 0.0).astype(bf16)
    drt_ref[...] = jnp.where(diagonal_t, nt(spread_d, d_raw_b), 0.0).astype(bf16)


def backward_kernel(
    heads,
    slices,
    aux_ref,
    wt_ref,
    logits_ref,
    weights_ref,
    mid_ref,
    cot_ref,
    feats_ref,
    sb_ref,
    mw_ref,
    dr_ref,
    drt_ref,
    dn_ref,
    temp_ref,
    _,
    dmt_ref,
    send0,
    send1,
    send2,
    send3,
    yt,
    grad_acc,
    small_acc,
    pack,
):
    width = mid_ref.shape[1]
    depth = width // heads
    hm = heads * slices
    block = feats_ref.shape[0]

    grad_acc[...] = jnp.zeros_like(grad_acc)
    small_acc[...] = jnp.zeros_like(small_acc)
    yt[:, 0:hm] = drt_ref[...]
    yt[:, hm:] = sb_ref[...]

    temp = jnp.broadcast_to(temp_ref[...].astype(f32), (16, depth)).astype(bf16)
    same = (rows_of((depth, depth)) == cols_of((depth, depth))).astype(f32).astype(bf16)
    temp = nt(same, temp)[:, 0:1]
    piece = min(2 * sub_block, block)
    pieces = [slice(i * piece, (i + 1) * piece) for i in range(block // piece)]

    def products(at):
        return nt(dr_ref[...], mid_ref[at, :]) + nt(mw_ref[...], cot_ref[at, :])

    def per_head(at, products):
        u_b, sums = [], []
        aux = aux_ref[:, at]
        for h in range(heads):
            span = slice(h * slices, (h + 1) * slices)
            inv_tau = aux[h : h + 1]
            logits = logits_ref[span, at]
            weights = weights_ref[span, at]
            d_weights = products[span] + dn_ref[span, 0:1]
            mean = jnp.sum(weights * d_weights, axis=0, keepdims=True)
            d_logits = weights * (d_weights - mean)
            d_tau = jnp.sum(d_logits * logits, axis=0, keepdims=True)
            sums.append(-d_tau * aux[2 * heads + h : 2 * heads + h + 1])
            u_b.append((d_logits * inv_tau).astype(bf16))
        c_sum = jnp.concatenate(sums, axis=0)
        c_high = c_sum.astype(bf16).astype(f32)
        u_b.append(jnp.concatenate([c_high, c_sum - c_high], axis=0).astype(bf16))
        return jnp.concatenate(u_b, axis=0), sums

    def outputs(at, u_b, sums):
        d_mid = nn(yt[...], jnp.concatenate([wt_ref[:, at], u_b[0:hm]], axis=0))
        d_mid = [
            (d_mid[h * depth : (h + 1) * depth] + temp * sums[h]).astype(bf16)
            for h in range(heads)
        ]
        d_mid = jnp.concatenate(d_mid, axis=0)
        dmt_ref[:, at] = d_mid
        grad_acc[...] += nn(d_mid, feats_ref[at, :])
        small_acc[...] += nn(u_b, mid_ref[at, :])

    ready = products(pieces[0])
    for i, at in enumerate(pieces):
        current = ready
        if i + 1 < len(pieces):
            ready = products(pieces[i + 1])
        outputs(at, *per_head(at, current))

    grad = grad_acc[...].T
    u_part = jnp.where(same_block(hm, width, slices, depth), small_acc[0:hm, :], 0.0)
    u_part = fold_rows(u_part, heads, slices)
    c_part = small_acc[hm : hm + heads, :] + small_acc[hm + heads : hm + 2 * heads, :]
    c_part = jnp.where(same_block(heads, width, 1, depth), c_part, 0.0)
    c_part = jnp.sum(c_part, axis=0, keepdims=True)

    def fold_lanes(x):
        total = x[:, 0:128]
        for j in range(1, width // 128):
            total = total + x[:, j * 128 : (j + 1) * 128]
        shift = 64
        while shift >= depth:
            total = total + pltpu.roll(total, shift, 1)
            shift //= 2
        return total

    u_part = fold_lanes(u_part)
    c_part = fold_lanes(jnp.broadcast_to(c_part, (slices, width)))
    where_lane = cols_of((slices, 128))
    extra = jnp.where(where_lane < depth, u_part, c_part)
    rows = width // group
    more = slices // group
    for j in range(group):
        pack[j, 0:rows, :] = grad[j * rows : (j + 1) * rows]
        pack[j, rows : rows + more, 0:128] = extra[j * more : (j + 1) * more]
        pack[j, rows : rows + more, 128:] = jnp.zeros((more, width - 128), f32)
    place = group_place()
    for k, send in enumerate((send0, send1, send2, send3)):
        send[...] = pack[place ^ k]


def rows_kernel(wt_ref, dmt_ref, mw_ref, w_mid_ref, _, attended_ref, feats_grad_ref, token_ref):
    block = attended_ref.shape[0]
    at = pl.ds(pl.multiple_of(pl.program_id(0) * block, block), block)
    token_ref[...] = jnp.zeros_like(token_ref)
    attended_ref[...] = tn(wt_ref[:, at], mw_ref[...]).astype(bf16)
    feats_grad_ref[...] = lax.dot_general(
        dmt_ref[:, at], w_mid_ref[...], (((0,), (1,)), ((), ())), preferred_element_type=f32
    ).astype(bf16)


def grad_out_kernel(
    heads,
    slices,
    own_ref,
    other_ref,
    mixed_ref,
    tokens_ref,
    d_qkv_ref,
    _,
    grad_out_ref,
    grad_qkv_ref,
    token_ref,
    whole,
):
    token_ref[...] = jnp.zeros_like(token_ref)
    hm = heads * slices
    depth = grad_qkv_ref.shape[1]
    width = heads * depth
    t_high, t_low = two_pieces(tokens_ref[...])
    d_high, d_low = two_pieces(d_qkv_ref[...])
    grads = tn(t_high, d_high) + tn(t_high, d_low) + tn(t_low, d_high)
    for i in range(3):
        at = pltpu.roll(grads, 128 - i * depth, 1) if i else grads
        grad_qkv_ref[i] = at[0:depth, 0:depth]
    spread_d = jnp.where(
        (rows_of((width, 128)) & (depth - 1)) == cols_of((width, 128)), 1.0, 0.0
    ).astype(bf16)
    diagonal_t = same_block(width, hm, depth, slices)
    mixed_t = jnp.where(diagonal_t, nt(spread_d, mixed_ref[...]), 0.0).astype(bf16)
    place = group_place() & 1
    rows = own_ref.shape[0]
    for k, part in enumerate((own_ref, other_ref)):
        whole[pl.ds(pl.multiple_of((place ^ k) * rows, 8), rows), :] = part[...]
    high, low = two_pieces(whole[...])
    grad_out_ref[...] = nn(mixed_t, high) + nn(mixed_t, low)


def finish_kernel(depth, m0, m1, m2, m3, _, grad_mid_ref, slice_ref, temp_ref, extra):
    place = group_place()
    slices = slice_ref.shape[1]
    more = slices // group
    rows = m0.shape[0] - more
    for k, part in enumerate((m0, m1, m2, m3)):
        at = pl.ds(pl.multiple_of((place ^ k) * rows, 8), rows)
        grad_mid_ref[at, :] = part[0:rows, :]
        extra[pl.ds(pl.multiple_of((place ^ k) * more, 8), more), :] = part[rows:, 0:128]
    turned = extra[...].T
    slice_ref[...] = turned[0:depth, 0:slices]
    temp_ref[...] = extra[0:1, depth : 2 * depth]


def full(shape):
    zeros = (0,) * len(shape)
    return pl.BlockSpec(shape, lambda *_: zeros)


def params(mebibytes, grid=True):
    semantics = ("arbitrary",) if grid else None
    return pltpu.CompilerParams(
        dimension_semantics=semantics, vmem_limit_bytes=mebibytes * mib
    )


def cost(flops, moved, transcendentals=0):
    return pl.CostEstimate(flops=flops, bytes_accessed=moved, transcendentals=transcendentals)


def exchange(x, k, count):
    return lax.ppermute(x, "node", [(i, i ^ k) for i in range(count)])


def sum_kernel(count, *refs):
    total = refs[0][...] + refs[count - 1][...]
    if count == 4:
        total = total + (refs[1][...] + refs[2][...])
    refs[-1][...] = total


def sum_behind(parts, *before):
    return pl.pallas_call(
        functools.partial(sum_kernel, len(parts)),
        out_shape=jax.ShapeDtypeStruct(parts[0].shape, f32),
        in_specs=[pl.BlockSpec(memory_space=pltpu.VMEM)] * len(parts)
        + [pl.BlockSpec(memory_space=pl.ANY)] * len(before),
        out_specs=pl.BlockSpec(memory_space=pltpu.VMEM),
        compiler_params=params(2, False),
        cost_estimate=cost(3 * parts[0].size, 5 * parts[0].size * 4),
    )(*parts, *before)


def scatter_group(parts, count):
    got = [parts[0]] + [exchange(parts[k], k, count) for k in range(1, group)]
    return (got[0] + got[1]) + (got[2] + got[3])


def sum_stage(total, stride, others, count, *before):
    parts = [total] + [exchange(total, stride * j, count) for j in range(others, 0, -1)]
    if before:
        return sum_behind(parts, *before)
    if others == 1:
        return parts[0] + parts[1]
    return (parts[0] + parts[3]) + (parts[1] + parts[2])


def sum_over_groups(total, stride, count, *before):
    while stride < count:
        others = 3 if count // stride % 4 == 0 else 1
        total = sum_stage(total, stride, others, count, *before)
        stride *= others + 1
    return total


def gather_group(total, count):
    return [total] + [exchange(total, k, count) for k in range(1, group)]


def shards(count, feats, cotangent, valid, owned, w_mid, w_slice, temp_vec, w_qkv, w_out):
    rows, width = feats.shape
    depth, slices = w_slice.shape
    heads = width // depth
    hm = heads * slices
    unit = 2 * rows * width * width
    smem = pl.BlockSpec(memory_space=pltpu.SMEM)

    def blocks(size):
        return (rows // size,), pl.BlockSpec((size, width), lambda i: (i, 0))

    def like(shape, dtype):
        return jax.ShapeDtypeStruct(shape, dtype)

    def far(x):
        return pltpu.with_memory_space_constraint(x, pltpu.HBM)

    near = pltpu.VMEM
    whole = pl.BlockSpec(memory_space=pltpu.VMEM)

    temp = temp_vec.reshape(1, depth)
    half = (2 * slices + 8, 128)
    wide = (hm // 2, width)
    inputs = (valid.reshape(1, rows), feats, cotangent, w_mid, w_slice, w_out)
    (
        mid,
        wt,
        aux,
        sw,
        keep,
        send,
        wc_keep,
        wc_send,
        feats_near,
        cot_near,
    ) = pl.pallas_call(
        functools.partial(stats_kernel, heads, slices),
        in_specs=[smem, whole] + [pl.BlockSpec(memory_space=pltpu.HBM)] * len(inputs),
        out_specs=[whole] * 10,
        out_shape=[
            near((rows, width), bf16),
            near((hm, rows), bf16),
            near((3 * heads, rows), f32),
            near((hm + 16, width), bf16),
            near(half, f32),
            near(half, f32),
            near(wide, f32),
            near(wide, f32),
            near((rows, width), bf16),
            near((rows, width), bf16),
        ],
        scratch_shapes=[
            pltpu.VMEM((1, rows), jnp.int32),
            pltpu.VMEM((width, width), bf16),
            pltpu.VMEM((depth, slices), bf16),
            pltpu.VMEM((width, width), bf16),
            pltpu.VMEM((hm, width), f32),
            pltpu.VMEM((hm, 128), f32),
            pltpu.VMEM((hm, width), f32),
            pltpu.VMEM((2,) + half, f32),
            pltpu.SemaphoreType.DMA((7,)),
        ],
        compiler_params=params(24, False),
        cost_estimate=cost(4 * unit, rows * width * 8, rows * hm),
    )(owned, far(temp), *map(far, inputs))

    own = keep + exchange(send, 1, count)
    wc_got = exchange(wc_send, 1, count)
    wc_sum = sum_behind([wc_keep, wc_got], own)
    logits, weights, sb, w_cat, token = pl.pallas_call(
        functools.partial(between_kernel, heads, slices),
        in_specs=[whole] * 5 + [pl.BlockSpec(memory_space=pl.ANY)],
        out_specs=[whole] * 5,
        out_shape=[
            near((hm, rows), f32),
            near((hm, rows), f32),
            near((width, hm), bf16),
            near((depth, 128), bf16),
            near((8, 128), f32),
        ],
        compiler_params=params(16, False),
        cost_estimate=cost(3 * unit, rows, rows),
    )(mid, sw, aux, w_slice, w_qkv, own)
    own = sum_stage(own, 2, 3, count, token)
    wc_got = exchange(wc_sum, 2, count)
    wc_sum = sum_behind([wc_sum, wc_got], own)
    own = sum_over_groups(own, 8, count)
    other = exchange(own, 1, count)
    stride = 4
    wc_got = exchange(wc_sum, stride, count)
    while 4 * stride < count:
        wc_sum = wc_sum + wc_got
        stride *= 2
        wc_got = exchange(wc_sum, stride, count)

    mw, dr, drt, dn, mixed, tokens, d_qkv = pl.pallas_call(
        functools.partial(tokens_kernel, heads, slices),
        out_shape=[
            near((hm, width), bf16),
            near((hm, width), bf16),
            near((width, hm), bf16),
            near((hm, 128), f32),
            near((hm, 128), bf16),
            near((hm, 128), f32),
            near((hm, 128), f32),
        ],
        scratch_shapes=[pltpu.VMEM((2,) + half, f32)],
        compiler_params=params(16, False),
        cost_estimate=cost(3 * width**3, 4 * width * width * 4, hm * hm),
    )(own, other, w_cat, w_out)
    larger = (width // group + slices // group, width)
    dmt, *sends = pl.pallas_call(
        functools.partial(backward_kernel, heads, slices),
        in_specs=[whole] * 13 + [pl.BlockSpec(memory_space=pl.ANY)],
        out_specs=[whole] * (1 + group),
        out_shape=[near((width, rows), bf16)] + [near(larger, f32)] * group,
        scratch_shapes=[
            pltpu.VMEM((width, 2 * hm), bf16),
            pltpu.VMEM((width, width), f32),
            pltpu.VMEM((hm + 16, width), f32),
            pltpu.VMEM((group,) + larger, f32),
        ],
        compiler_params=params(24, False),
        cost_estimate=cost(unit * 3 // 10, rows * width, rows),
    )(aux, wt, logits, weights, mid, cot_near, feats_near, sb, mw, dr, drt, dn, temp, wc_sum)

    mid_total = scatter_group(sends, count)
    wc_sum = sum_behind([wc_sum, wc_got], sends[1])
    wc_got = exchange(wc_sum, count // 2, count)

    block = min(1024, rows)
    grid, by_rows = blocks(block)
    attended, feats_grad, token = pl.pallas_call(
        rows_kernel,
        grid=grid,
        in_specs=[
            whole,
            whole,
            whole,
            full((width, width)),
            pl.BlockSpec(memory_space=pl.ANY),
        ],
        out_specs=[by_rows, by_rows, full((8, 128))],
        out_shape=[like((rows, width), bf16)] * 2 + [like((8, 128), f32)],
        compiler_params=params(20),
        cost_estimate=cost(2 * unit, rows * width * 8),
    )(wt, dmt, mw, w_mid, mid_total)

    wc_sum = sum_behind([wc_sum, wc_got], token)
    wc_other = exchange(wc_sum, 1, count)
    mid_total = sum_over_groups(mid_total, group, count, token)
    grad_w_out, grad_qkv, token_out = pl.pallas_call(
        functools.partial(grad_out_kernel, heads, slices),
        in_specs=[whole] * 5 + [pl.BlockSpec(memory_space=pl.ANY)],
        out_specs=[whole] * 3,
        out_shape=[
            like((width, width), f32),
            like((3, depth, depth), f32),
            like((8, 128), f32),
        ],
        scratch_shapes=[pltpu.VMEM((hm, width), f32)],
        compiler_params=params(8, False),
        cost_estimate=cost(4 * width**3, 3 * width * width * 4),
    )(wc_sum, wc_other, mixed, tokens, d_qkv, mid_total)

    mid_parts = gather_group(mid_total, count)
    grad_w_mid, grad_w_slice, grad_temp = pl.pallas_call(
        functools.partial(finish_kernel, depth),
        in_specs=[whole] * group + [pl.BlockSpec(memory_space=pl.ANY)],
        out_specs=[whole] * 3,
        out_shape=[
            like((width, width), f32),
            like((depth, slices), f32),
            like((1, depth), f32),
        ],
        scratch_shapes=[pltpu.VMEM((slices, 128), f32)],
        compiler_params=params(8, False),
        cost_estimate=cost(0, 2 * width * width * 4),
    )(*mid_parts, token_out)
    return (
        attended,
        feats_grad,
        grad_w_mid,
        grad_w_out,
        grad_w_slice,
        grad_temp.reshape(depth),
        grad_qkv,
    )


def solution(mesh):
    in_specs = (
        P(("design", "node"), None),
        P(("design", "node"), None),
        P(("design", "node")),
        P(("design", "node")),
        P(),
        P(),
        P(),
        P(),
        P(),
    )
    out_specs = (
        P(("design", "node"), None),
        P(("design", "node"), None),
        P("design", None),
        P("design", None),
        P("design", None),
        P("design"),
        P("design", None, None),
    )
    return jax.shard_map(
        functools.partial(shards, mesh.shape["node"]),
        mesh=mesh,
        in_specs=in_specs,
        out_specs=out_specs,
        check_vma=False,
    )
```

```python
import functools
import math

import jax
import jax.numpy as jnp
from jax import lax
from jax.experimental import pallas as pl
from jax.experimental.pallas import tpu as pltpu
from jax.sharding import PartitionSpec as P

f32 = jnp.float32
bf16 = jnp.bfloat16
eps_norm = 1e-05
exact = lax.Precision.HIGHEST
group = 4
sub_block = 512
mib = 1024 * 1024


def nn(a, b, precision=None):
    return lax.dot_general(
        a, b, (((1,), (0,)), ((), ())), preferred_element_type=f32, precision=precision
    )


def nt(a, b, precision=None):
    return lax.dot_general(
        a, b, (((1,), (1,)), ((), ())), preferred_element_type=f32, precision=precision
    )


def tn(a, b, precision=None):
    return lax.dot_general(
        a, b, (((0,), (0,)), ((), ())), preferred_element_type=f32, precision=precision
    )


def log2(size):
    return size.bit_length() - 1


def rows_of(shape):
    return lax.broadcasted_iota(jnp.int32, shape, 0)


def cols_of(shape):
    return lax.broadcasted_iota(jnp.int32, shape, 1)


def spread_matrix(width, small):
    shape = (width, small)
    return jnp.where((rows_of(shape) & (small - 1)) == cols_of(shape), 1.0, 0.0).astype(bf16)


def same_block(rows, cols, row_size, col_size):
    shape = (rows, cols)
    return rows_of(shape) >> log2(row_size) == cols_of(shape) >> log2(col_size)


def two_pieces(x):
    high = x.astype(bf16)
    return high, (x - high.astype(f32)).astype(bf16)


def fold_rows(x, heads, size):
    total = x[0:size]
    for h in range(1, heads):
        total = total + x[h * size : (h + 1) * size]
    return total


def group_place():
    return lax.axis_index("node") % group


def stats_kernel(
    heads,
    slices,
    owned_ref,
    temp_ref,
    valid_far,
    feats_far,
    cot_far,
    w_mid_far,
    w_slice_far,
    w_out_far,
    mid_ref,
    wt_ref,
    aux_ref,
    sw_ref,
    keep_ref,
    send_ref,
    wc_keep_ref,
    wc_send_ref,
    feats_ref,
    cot_ref,
    valid_ref,
    w_mid_ref,
    w_slice_ref,
    w_out_ref,
    raw_acc,
    norm_acc,
    wc_acc,
    pack,
    sems,
):
    width = w_mid_ref.shape[0]
    depth = width // heads
    hm = heads * slices
    rows = feats_ref.shape[0]
    piece = min(2 * sub_block, rows)
    count = rows // piece
    small = [
        pltpu.make_async_copy(source, target, sems.at[i])
        for i, (source, target) in enumerate(
            (
                (w_slice_far, w_slice_ref),
                (w_mid_far, w_mid_ref),
                (valid_far, valid_ref),
                (w_out_far, w_out_ref),
            )
        )
    ]
    first, rest = pl.ds(0, piece), pl.ds(piece, rows - piece)
    large = [
        pltpu.make_async_copy(source, target, sems.at[len(small) + i])
        for i, (source, target) in enumerate(
            (
                (feats_far.at[first, :], feats_ref.at[first, :]),
                (feats_far.at[rest, :], feats_ref.at[rest, :]),
                (cot_far, cot_ref),
            )
        )
    ]
    for copy in small[:2] + large[:1] + small[2:] + large[1:]:
        copy.start()

    raw_acc[...] = jnp.zeros_like(raw_acc)
    norm_acc[...] = jnp.zeros_like(norm_acc)
    wc_acc[...] = jnp.zeros_like(wc_acc)
    spread_d = spread_matrix(width, depth)
    spread_m = spread_matrix(hm, slices)
    for copy in small[:2] + large[:1]:
        copy.wait()
    temp = jnp.broadcast_to(temp_ref[...].astype(f32), (16, depth)).astype(bf16)
    half = nt(spread_m, w_slice_ref[...]).astype(bf16)
    full = nt(half, spread_d)
    sw_ref[0:hm, :] = jnp.where(same_block(hm, width, slices, depth), full, 0.0).astype(bf16)
    full = nt(temp, spread_d)
    sw_ref[hm : hm + 16, :] = jnp.where(same_block(16, width, 1, depth), full, 0.0).astype(bf16)
    owned = owned_ref[0]

    def products(i):
        at = slice(i * piece, (i + 1) * piece)
        mid = nn(feats_ref[at, :], w_mid_ref[...]).astype(bf16)
        mid_ref[at, :] = mid
        return mid, nt(sw_ref[...], mid)

    def statistics(i, mid, scores):
        at = slice(i * piece, (i + 1) * piece)
        zsum = scores[hm : hm + heads]
        small = jnp.exp(-jnp.abs(zsum))
        inv_tau = 1.0 / (0.5 + (jnp.maximum(zsum, 0.0) + jnp.log(1.0 + small)))
        sig = jnp.where(zsum >= 0.0, 1.0, small) / (1.0 + small)
        position = i * piece + cols_of((1, piece))
        live = (valid_ref[:, at] > 0) & (position < owned)
        live_f = live.astype(f32)
        rounded, sums, logs = [], [], []
        for h in range(heads):
            span = slice(h * slices, (h + 1) * slices)
            logits = scores[span] * inv_tau[h : h + 1]
            peak = jnp.max(logits, axis=0, keepdims=True)
            expo = jnp.exp(logits - peak)
            total = jnp.sum(expo, axis=0, keepdims=True)
            weights = expo * (live_f / total)
            rounded.append(weights.astype(bf16))
            lanes = weights[:, 0:128]
            for c in range(1, piece // 128):
                lanes = lanes + weights[:, c * 128 : (c + 1) * 128]
            sums.append(lanes)
            logs.append(jnp.where(live, peak + jnp.log(total), jnp.inf))
        wt = jnp.concatenate(rounded, axis=0)
        wt_ref[:, at] = wt
        norm_acc[...] += jnp.concatenate(sums, axis=0)
        aux_ref[:, at] = jnp.concatenate([inv_tau] + logs + [sig * inv_tau], axis=0)
        raw_acc[...] += nn(wt, mid)
        wc_acc[...] += nn(wt, cot_ref[at, :])

    ready = products(0)
    for copy in small[2:] + large[1:]:
        copy.wait()
    for i in range(count):
        current = ready
        if i + 1 < count:
            ready = products(i + 1)
        statistics(i, *current)

    diagonal = same_block(hm, width, slices, depth)
    raw = fold_rows(jnp.where(diagonal, raw_acc[...], 0.0), heads, slices)
    high, low = two_pieces(wc_acc[...])
    w_out = w_out_ref[...]
    mixed = nt(high, w_out) + nt(low, w_out)
    mixed = fold_rows(jnp.where(diagonal, mixed, 0.0), heads, slices)
    norm = jnp.sum(norm_acc[...].T, axis=0, keepdims=True)
    first = rows_of((8, 128)) == 0
    for j in range(2):
        part = slice(j * 128, (j + 1) * 128)
        pack[j, 0:slices, :] = raw[:, part]
        pack[j, slices : 2 * slices, :] = mixed[:, part]
        pack[j, 2 * slices :, :] = jnp.where(first, norm[:, part], 0.0)
    place = group_place()
    keep_ref[...] = pack[place & 1]
    send_ref[...] = pack[(place & 1) ^ 1]
    rows = hm // 2
    for k, out in enumerate((wc_keep_ref, wc_send_ref)):
        out[...] = wc_acc[pl.ds(pl.multiple_of(((place & 1) ^ k) * rows, 8), rows), :]


def between_kernel(
    heads,
    slices,
    mid_ref,
    sw_ref,
    aux_ref,
    w_slice_ref,
    w_qkv_ref,
    _,
    logits_ref,
    weights_ref,
    sb_ref,
    w_cat_ref,
    token_ref,
):
    depth = w_slice_ref.shape[0]
    width = heads * depth
    hm = heads * slices
    rows = mid_ref.shape[0]
    piece = min(sub_block, rows)
    token_ref[...] = jnp.zeros_like(token_ref)
    spread_d = spread_matrix(width, depth)
    spread_m = spread_matrix(hm, slices)
    half = nn(spread_d, w_slice_ref[...]).astype(bf16)
    full = nt(half, spread_m)
    sb_ref[...] = jnp.where(same_block(width, hm, depth, slices), full, 0.0).astype(bf16)
    w_cat = jnp.zeros((depth, 128), f32)
    for i in range(3):
        place_at = jnp.where(rows_of((depth, 128)) + i * depth == cols_of((depth, 128)), 1.0, 0.0)
        w_cat = w_cat + nn(w_qkv_ref[i], place_at.astype(bf16))
    w_cat_ref[...] = w_cat.astype(bf16)
    for i in range(rows // piece):
        at = slice(i * piece, (i + 1) * piece)
        scores = nt(sw_ref[0:hm, :], mid_ref[at, :])
        for h in range(heads):
            span = slice(h * slices, (h + 1) * slices)
            logits = scores[span] * aux_ref[h : h + 1, at]
            logits_ref[span, at] = logits
            weights_ref[span, at] = jnp.exp(logits - aux_ref[heads + h : heads + h + 1, at])


def lanes_at(x, lane, *where):
    place = cols_of(x.shape) >> log2(lane)
    total = jnp.zeros_like(x)
    for value, at, to in where:
        shift = (to - at) * lane % 128
        moved = pltpu.roll(value, shift, 1) if shift else value
        total = jnp.where(place == to, moved, total)
    return total.astype(bf16)


def split(x):
    high = x.astype(bf16).astype(f32)
    return high, x - high


def tokens_kernel(
    heads,
    slices,
    own_ref,
    got_ref,
    w_cat_ref,
    w_out_ref,
    mw_ref,
    dr_ref,
    drt_ref,
    dn_ref,
    mixed_ref,
    tokens_ref,
    d_qkv_ref,
    pack,
):
    width = w_out_ref.shape[0]
    depth = width // heads
    hm = heads * slices
    place = group_place() & 1
    pack[place] = own_ref[...]
    pack[place ^ 1] = got_ref[...]
    per = 128 // depth

    def compact(first):
        pieces = []
        for h in range(heads):
            x = pack[h // per, first : first + slices, :]
            shift = (h % per) * depth
            pieces.append(pltpu.roll(x, 128 - shift, 1) if shift else x)
        x = jnp.concatenate(pieces, axis=0)
        return jnp.where(cols_of(x.shape) < depth, x, 0.0)

    raw = compact(0)
    d_mixed = compact(slices)
    norm = jnp.concatenate([pack[j, 2 * slices :, :].T[:, 0:1] for j in range(2)], axis=0)
    inverse = 1.0 / (norm + eps_norm)
    tokens = raw * inverse
    w_cat = w_cat_ref[...]

    t_high, rest = split(tokens)
    t_low, rest = split(rest)
    left = lanes_at(tokens, depth, (t_high, 0, 0), (t_low, 0, 1), (rest, 0, 2))
    blank = jnp.zeros((128 - 3 * depth, 128), bf16)
    qkv = nn(left, jnp.concatenate([w_cat, w_cat, w_cat, blank], axis=0))
    high, low = split(qkv)
    q_left = lanes_at(qkv, depth, (high, 0, 0), (high, 0, 1), (low, 0, 2))
    k_right = lanes_at(qkv, depth, (high, 1, 0), (low, 1, 1), (high, 1, 2))
    v_right = lanes_at(qkv, depth, (high, 2, 0), (low, 2, 1), (high, 2, 2))
    q_pair = lanes_at(qkv, depth, (high, 0, 0), (low, 0, 1))
    k_pair = lanes_at(qkv, depth, (high, 1, 0), (low, 1, 1))
    v_pair = lanes_at(qkv, depth, (high, 2, 0), (low, 2, 1))
    g_high, g_low = split(d_mixed)
    g_left = lanes_at(qkv, depth, (g_high, 0, 0), (g_high, 0, 1), (g_low, 0, 2))
    g_pair = lanes_at(qkv, depth, (g_high, 0, 0), (g_low, 0, 1))

    def times_pair(dot, x, pair):
        x_high, x_low = two_pieces(x)
        both = dot(x_high, pair)
        low_part = dot(x_low, pair)
        total = both + pltpu.roll(both, 128 - depth, 1) + low_part
        return jnp.where(cols_of(total.shape) < depth, total, 0.0)

    blocks = same_block(hm, hm, slices, slices)
    scale = 1.0 / math.sqrt(depth)
    scores = jnp.where(blocks, nt(q_left, k_right) * scale, -jnp.inf)
    expo = jnp.exp(scores - jnp.max(scores, axis=1, keepdims=True))
    probs = expo * (1.0 / jnp.sum(expo, axis=1, keepdims=True))
    mixed_b = times_pair(nn, probs, v_pair).astype(bf16)

    spread_d = jnp.where(
        (rows_of((width, 128)) & (depth - 1)) == cols_of((width, 128)), 1.0, 0.0
    ).astype(bf16)
    diagonal = same_block(hm, width, slices, depth)
    diagonal_t = same_block(width, hm, depth, slices)
    mixed_block = jnp.where(diagonal, nt(mixed_b, spread_d), 0.0).astype(bf16)
    mw_ref[...] = nn(mixed_block, w_out_ref[...]).astype(bf16)
    mixed_ref[...] = mixed_b
    tokens_ref[...] = tokens

    d_probs = nt(g_left, v_right)
    d_v = times_pair(tn, probs, g_pair)
    d_scores = probs * (d_probs - jnp.sum(probs * d_probs, axis=1, keepdims=True)) * scale
    d_q = times_pair(nn, d_scores, k_pair)
    d_k = times_pair(tn, d_scores, q_pair)
    d_qkv = d_q + pltpu.roll(d_k, depth, 1) + pltpu.roll(d_v, 2 * depth, 1)
    d_qkv_ref[...] = d_qkv
    d_high, d_low = two_pieces(d_qkv)
    d_tokens = nt(d_high, w_cat) + nt(d_low, w_cat)
    raw = raw[:, 0:depth]
    d_raw_b = (d_tokens * inverse).astype(bf16)
    d_norm = -jnp.sum(d_tokens * raw, axis=1, keepdims=True) * inverse * inverse
    dn_ref[...] = jnp.broadcast_to(d_norm, dn_ref.shape)
    spread_d = spread_matrix(width, depth)
    dr_ref[...] = jnp.where(diagonal, nt(d_raw_b, spread_d), 0.0).astype(bf16)
    drt_ref[...] = jnp.where(diagonal_t, nt(spread_d, d_raw_b), 0.0).astype(bf16)


def backward_kernel(
    heads,
    slices,
    aux_ref,
    wt_ref,
    logits_ref,
    weights_ref,
    mid_ref,
    cot_ref,
    feats_ref,
    sb_ref,
    mw_ref,
    dr_ref,
    drt_ref,
    dn_ref,
    temp_ref,
    _,
    dmt_ref,
    send0,
    send1,
    send2,
    send3,
    yt,
    grad_acc,
    small_acc,
    pack,
):
    width = mid_ref.shape[1]
    depth = width // heads
    hm = heads * slices
    block = feats_ref.shape[0]

    grad_acc[...] = jnp.zeros_like(grad_acc)
    small_acc[...] = jnp.zeros_like(small_acc)
    yt[:, 0:hm] = drt_ref[...]
    yt[:, hm:] = sb_ref[...]

    temp = jnp.broadcast_to(temp_ref[...].astype(f32), (16, depth)).astype(bf16)
    same = (rows_of((depth, depth)) == cols_of((depth, depth))).astype(f32).astype(bf16)
    temp = nt(same, temp)[:, 0:1]
    piece = min(2 * sub_block, block)
    pieces = [slice(i * piece, (i + 1) * piece) for i in range(block // piece)]

    def products(at):
        return nt(dr_ref[...], mid_ref[at, :]) + nt(mw_ref[...], cot_ref[at, :])

    def per_head(at, products):
        u_b, sums = [], []
        aux = aux_ref[:, at]
        for h in range(heads):
            span = slice(h * slices, (h + 1) * slices)
            inv_tau = aux[h : h + 1]
            logits = logits_ref[span, at]
            weights = weights_ref[span, at]
            d_weights = products[span] + dn_ref[span, 0:1]
            mean = jnp.sum(weights * d_weights, axis=0, keepdims=True)
            d_logits = weights * (d_weights - mean)
            d_tau = jnp.sum(d_logits * logits, axis=0, keepdims=True)
            sums.append(-d_tau * aux[2 * heads + h : 2 * heads + h + 1])
            u_b.append((d_logits * inv_tau).astype(bf16))
        c_sum = jnp.concatenate(sums, axis=0)
        c_high = c_sum.astype(bf16).astype(f32)
        u_b.append(jnp.concatenate([c_high, c_sum - c_high], axis=0).astype(bf16))
        return jnp.concatenate(u_b, axis=0), sums

    def outputs(at, u_b, sums):
        d_mid = nn(yt[...], jnp.concatenate([wt_ref[:, at], u_b[0:hm]], axis=0))
        d_mid = [
            (d_mid[h * depth : (h + 1) * depth] + temp * sums[h]).astype(bf16)
            for h in range(heads)
        ]
        d_mid = jnp.concatenate(d_mid, axis=0)
        dmt_ref[:, at] = d_mid
        grad_acc[...] += nn(d_mid, feats_ref[at, :])
        small_acc[...] += nn(u_b, mid_ref[at, :])

    ready = products(pieces[0])
    for i, at in enumerate(pieces):
        current = ready
        if i + 1 < len(pieces):
            ready = products(pieces[i + 1])
        outputs(at, *per_head(at, current))

    grad = grad_acc[...].T
    u_part = jnp.where(same_block(hm, width, slices, depth), small_acc[0:hm, :], 0.0)
    u_part = fold_rows(u_part, heads, slices)
    c_part = small_acc[hm : hm + heads, :] + small_acc[hm + heads : hm + 2 * heads, :]
    c_part = jnp.where(same_block(heads, width, 1, depth), c_part, 0.0)
    c_part = jnp.sum(c_part, axis=0, keepdims=True)

    def fold_lanes(x):
        total = x[:, 0:128]
        for j in range(1, width // 128):
            total = total + x[:, j * 128 : (j + 1) * 128]
        shift = 64
        while shift >= depth:
            total = total + pltpu.roll(total, shift, 1)
            shift //= 2
        return total

    u_part = fold_lanes(u_part)
    c_part = fold_lanes(jnp.broadcast_to(c_part, (slices, width)))
    where_lane = cols_of((slices, 128))
    extra = jnp.where(where_lane < depth, u_part, c_part)
    rows = width // group
    more = slices // group
    for j in range(group):
        for i in range(width // 128):
            part = grad[j * rows : (j + 1) * rows, i * 128 : (i + 1) * 128]
            pack[j, i * rows : (i + 1) * rows, :] = part
        pack[j, rows * (width // 128) :, :] = extra[j * more : (j + 1) * more]
    place = group_place()
    for k, send in enumerate((send0, send1, send2, send3)):
        send[...] = pack[place ^ k]


def rows_kernel(wt_ref, dmt_ref, mw_ref, w_mid_ref, _, attended_ref, feats_grad_ref, token_ref):
    block = attended_ref.shape[0]
    at = pl.ds(pl.multiple_of(pl.program_id(0) * block, block), block)
    token_ref[...] = jnp.zeros_like(token_ref)
    attended_ref[...] = tn(wt_ref[:, at], mw_ref[...]).astype(bf16)
    feats_grad_ref[...] = lax.dot_general(
        dmt_ref[:, at], w_mid_ref[...], (((0,), (1,)), ((), ())), preferred_element_type=f32
    ).astype(bf16)


def grad_out_kernel(
    heads,
    slices,
    own_ref,
    other_ref,
    mixed_ref,
    tokens_ref,
    d_qkv_ref,
    _,
    grad_out_ref,
    grad_qkv_ref,
    token_ref,
    whole,
):
    token_ref[...] = jnp.zeros_like(token_ref)
    hm = heads * slices
    depth = grad_qkv_ref.shape[1]
    width = heads * depth
    t_high, t_low = two_pieces(tokens_ref[...])
    d_high, d_low = two_pieces(d_qkv_ref[...])
    grads = tn(t_high, d_high) + tn(t_high, d_low) + tn(t_low, d_high)
    for i in range(3):
        at = pltpu.roll(grads, 128 - i * depth, 1) if i else grads
        grad_qkv_ref[i] = at[0:depth, 0:depth]
    spread_d = jnp.where(
        (rows_of((width, 128)) & (depth - 1)) == cols_of((width, 128)), 1.0, 0.0
    ).astype(bf16)
    diagonal_t = same_block(width, hm, depth, slices)
    mixed_t = jnp.where(diagonal_t, nt(spread_d, mixed_ref[...]), 0.0).astype(bf16)
    place = group_place() & 1
    rows = own_ref.shape[0]
    for k, part in enumerate((own_ref, other_ref)):
        whole[pl.ds(pl.multiple_of((place ^ k) * rows, 8), rows), :] = part[...]
    high, low = two_pieces(whole[...])
    grad_out_ref[...] = nn(mixed_t, high) + nn(mixed_t, low)


def finish_kernel(depth, m0, m1, m2, m3, _, grad_mid_ref, slice_ref, temp_ref, extra):
    place = group_place()
    slices = slice_ref.shape[1]
    more = slices // group
    rows, width = grad_mid_ref.shape[0] // group, grad_mid_ref.shape[1]
    for k, part in enumerate((m0, m1, m2, m3)):
        at = pl.ds(pl.multiple_of((place ^ k) * rows, 8), rows)
        for i in range(width // 128):
            grad_mid_ref[at, i * 128 : (i + 1) * 128] = part[i * rows : (i + 1) * rows, :]
        last = part[rows * (width // 128) :, :]
        extra[pl.ds(pl.multiple_of((place ^ k) * more, 8), more), :] = last
    turned = extra[...].T
    slice_ref[...] = turned[0:depth, 0:slices]
    temp_ref[...] = extra[0:1, depth : 2 * depth]


def full(shape):
    zeros = (0,) * len(shape)
    return pl.BlockSpec(shape, lambda *_: zeros)


def params(mebibytes, grid=True):
    semantics = ("arbitrary",) if grid else None
    return pltpu.CompilerParams(
        dimension_semantics=semantics, vmem_limit_bytes=mebibytes * mib
    )


def cost(flops, moved, transcendentals=0):
    return pl.CostEstimate(flops=flops, bytes_accessed=moved, transcendentals=transcendentals)


def exchange(x, k, count):
    return lax.ppermute(x, "node", [(i, i ^ k) for i in range(count)])


def sum_kernel(count, *refs):
    total = refs[0][...] + refs[count - 1][...]
    if count == 4:
        total = total + (refs[1][...] + refs[2][...])
    refs[-1][...] = total


def sum_behind(parts, *before):
    return pl.pallas_call(
        functools.partial(sum_kernel, len(parts)),
        out_shape=jax.ShapeDtypeStruct(parts[0].shape, f32),
        in_specs=[pl.BlockSpec(memory_space=pltpu.VMEM)] * len(parts)
        + [pl.BlockSpec(memory_space=pl.ANY)] * len(before),
        out_specs=pl.BlockSpec(memory_space=pltpu.VMEM),
        compiler_params=params(2, False),
        cost_estimate=cost(3 * parts[0].size, 5 * parts[0].size * 4),
    )(*parts, *before)


def scatter_group(parts, count):
    got = [parts[0]] + [exchange(parts[k], k, count) for k in range(1, group)]
    return (got[0] + got[1]) + (got[2] + got[3])


def sum_stage(total, stride, others, count, *before):
    parts = [total] + [exchange(total, stride * j, count) for j in range(others, 0, -1)]
    if before:
        return sum_behind(parts, *before)
    if others == 1:
        return parts[0] + parts[1]
    return (parts[0] + parts[3]) + (parts[1] + parts[2])


def sum_over_groups(total, stride, count, *before):
    while stride < count:
        others = 3 if count // stride % 4 == 0 else 1
        total = sum_stage(total, stride, others, count, *before)
        stride *= others + 1
    return total


def gather_group(total, count):
    return [total] + [exchange(total, k, count) for k in range(1, group)]


def shards(count, feats, cotangent, valid, owned, w_mid, w_slice, temp_vec, w_qkv, w_out):
    rows, width = feats.shape
    depth, slices = w_slice.shape
    heads = width // depth
    hm = heads * slices
    unit = 2 * rows * width * width
    smem = pl.BlockSpec(memory_space=pltpu.SMEM)

    def blocks(size):
        return (rows // size,), pl.BlockSpec((size, width), lambda i: (i, 0))

    def like(shape, dtype):
        return jax.ShapeDtypeStruct(shape, dtype)

    def far(x):
        return pltpu.with_memory_space_constraint(x, pltpu.HBM)

    near = pltpu.VMEM
    whole = pl.BlockSpec(memory_space=pltpu.VMEM)

    temp = temp_vec.reshape(1, depth)
    half = (2 * slices + 8, 128)
    wide = (hm // 2, width)
    inputs = (valid.reshape(1, rows), feats, cotangent, w_mid, w_slice, w_out)
    (
        mid,
        wt,
        aux,
        sw,
        keep,
        send,
        wc_keep,
        wc_send,
        feats_near,
        cot_near,
    ) = pl.pallas_call(
        functools.partial(stats_kernel, heads, slices),
        in_specs=[smem, whole] + [pl.BlockSpec(memory_space=pltpu.HBM)] * len(inputs),
        out_specs=[whole] * 10,
        out_shape=[
            near((rows, width), bf16),
            near((hm, rows), bf16),
            near((3 * heads, rows), f32),
            near((hm + 16, width), bf16),
            near(half, f32),
            near(half, f32),
            near(wide, f32),
            near(wide, f32),
            near((rows, width), bf16),
            near((rows, width), bf16),
        ],
        scratch_shapes=[
            pltpu.VMEM((1, rows), jnp.int32),
            pltpu.VMEM((width, width), bf16),
            pltpu.VMEM((depth, slices), bf16),
            pltpu.VMEM((width, width), bf16),
            pltpu.VMEM((hm, width), f32),
            pltpu.VMEM((hm, 128), f32),
            pltpu.VMEM((hm, width), f32),
            pltpu.VMEM((2,) + half, f32),
            pltpu.SemaphoreType.DMA((7,)),
        ],
        compiler_params=params(24, False),
        cost_estimate=cost(4 * unit, rows * width * 8, rows * hm),
    )(owned, far(temp), *map(far, inputs))

    own = keep + exchange(send, 1, count)
    wc_got = exchange(wc_send, 1, count)
    wc_sum = sum_behind([wc_keep, wc_got], own)
    logits, weights, sb, w_cat, token = pl.pallas_call(
        functools.partial(between_kernel, heads, slices),
        in_specs=[whole] * 5 + [pl.BlockSpec(memory_space=pl.ANY)],
        out_specs=[whole] * 5,
        out_shape=[
            near((hm, rows), f32),
            near((hm, rows), f32),
            near((width, hm), bf16),
            near((depth, 128), bf16),
            near((8, 128), f32),
        ],
        compiler_params=params(16, False),
        cost_estimate=cost(3 * unit, rows, rows),
    )(mid, sw, aux, w_slice, w_qkv, own)
    own = sum_stage(own, 2, 3, count, token)
    wc_got = exchange(wc_sum, 2, count)
    wc_sum = sum_behind([wc_sum, wc_got], own)
    own = sum_over_groups(own, 8, count)
    other = exchange(own, 1, count)
    stride = 4
    wc_got = exchange(wc_sum, stride, count)
    while 4 * stride < count:
        wc_sum = wc_sum + wc_got
        stride *= 2
        wc_got = exchange(wc_sum, stride, count)

    mw, dr, drt, dn, mixed, tokens, d_qkv = pl.pallas_call(
        functools.partial(tokens_kernel, heads, slices),
        out_shape=[
            near((hm, width), bf16),
            near((hm, width), bf16),
            near((width, hm), bf16),
            near((hm, 128), f32),
            near((hm, 128), bf16),
            near((hm, 128), f32),
            near((hm, 128), f32),
        ],
        scratch_shapes=[pltpu.VMEM((2,) + half, f32)],
        compiler_params=params(16, False),
        cost_estimate=cost(3 * width**3, 4 * width * width * 4, hm * hm),
    )(own, other, w_cat, w_out)
    larger = (width // group * (width // 128) + slices // group, 128)
    dmt, *sends = pl.pallas_call(
        functools.partial(backward_kernel, heads, slices),
        in_specs=[whole] * 13 + [pl.BlockSpec(memory_space=pl.ANY)],
        out_specs=[whole] * (1 + group),
        out_shape=[near((width, rows), bf16)] + [near(larger, f32)] * group,
        scratch_shapes=[
            pltpu.VMEM((width, 2 * hm), bf16),
            pltpu.VMEM((width, width), f32),
            pltpu.VMEM((hm + 16, width), f32),
            pltpu.VMEM((group,) + larger, f32),
        ],
        compiler_params=params(24, False),
        cost_estimate=cost(unit * 3 // 10, rows * width, rows),
    )(aux, wt, logits, weights, mid, cot_near, feats_near, sb, mw, dr, drt, dn, temp, wc_sum)

    mid_total = scatter_group(sends, count)
    wc_sum = sum_behind([wc_sum, wc_got], sends[1])
    wc_got = exchange(wc_sum, count // 2, count)

    block = min(1024, rows)
    grid, by_rows = blocks(block)
    attended, feats_grad, token = pl.pallas_call(
        rows_kernel,
        grid=grid,
        in_specs=[
            whole,
            whole,
            whole,
            full((width, width)),
            pl.BlockSpec(memory_space=pl.ANY),
        ],
        out_specs=[by_rows, by_rows, full((8, 128))],
        out_shape=[like((rows, width), bf16)] * 2 + [like((8, 128), f32)],
        compiler_params=params(20),
        cost_estimate=cost(2 * unit, rows * width * 8),
    )(wt, dmt, mw, w_mid, mid_total)

    wc_sum = sum_behind([wc_sum, wc_got], token)
    wc_other = exchange(wc_sum, 1, count)
    mid_total = sum_over_groups(mid_total, group, count, token)
    grad_w_out, grad_qkv, token_out = pl.pallas_call(
        functools.partial(grad_out_kernel, heads, slices),
        in_specs=[whole] * 5 + [pl.BlockSpec(memory_space=pl.ANY)],
        out_specs=[whole] * 3,
        out_shape=[
            like((width, width), f32),
            like((3, depth, depth), f32),
            like((8, 128), f32),
        ],
        scratch_shapes=[pltpu.VMEM((hm, width), f32)],
        compiler_params=params(8, False),
        cost_estimate=cost(4 * width**3, 3 * width * width * 4),
    )(wc_sum, wc_other, mixed, tokens, d_qkv, mid_total)

    mid_parts = gather_group(mid_total, count)
    grad_w_mid, grad_w_slice, grad_temp = pl.pallas_call(
        functools.partial(finish_kernel, depth),
        in_specs=[whole] * group + [pl.BlockSpec(memory_space=pl.ANY)],
        out_specs=[whole] * 3,
        out_shape=[
            like((width, width), f32),
            like((depth, slices), f32),
            like((1, depth), f32),
        ],
        scratch_shapes=[pltpu.VMEM((slices, 128), f32)],
        compiler_params=params(8, False),
        cost_estimate=cost(0, 2 * width * width * 4),
    )(*mid_parts, token_out)
    return (
        attended,
        feats_grad,
        grad_w_mid,
        grad_w_out,
        grad_w_slice,
        grad_temp.reshape(depth),
        grad_qkv,
    )


def solution(mesh):
    in_specs = (
        P(("design", "node"), None),
        P(("design", "node"), None),
        P(("design", "node")),
        P(("design", "node")),
        P(),
        P(),
        P(),
        P(),
        P(),
    )
    out_specs = (
        P(("design", "node"), None),
        P(("design", "node"), None),
        P("design", None),
        P("design", None),
        P("design", None),
        P("design"),
        P("design", None, None),
    )
    return jax.shard_map(
        functools.partial(shards, mesh.shape["node"]),
        mesh=mesh,
        in_specs=in_specs,
        out_specs=out_specs,
        check_vma=False,
    )
```
